32 devices in a mesh: expert: 16 (over z, y, core), shard: 2 (over x).
Axes of the slice: x: 2, y: 2, z: 4, core: 2. Of those that a mesh axis runs over, the one named last changes fastest.
Arguments:
- tokens: bfloat16 [96, 197, 512], P(('expert', 'shard')), may hold values from -6 to 6
- cotangent: bfloat16 [96, 197, 512], P(('expert', 'shard')), may hold values from -6 to 6
- routes: int32 [96, 197, 2], P(('expert', 'shard')), may hold values from 0 to 31, all different within a row; in each aligned block of 591 rows (0 to 590, 591 to 1181, ..., all dimensions but the last counted through in order) at most 40 rows name the same one
- counts: int32 [32], P(('expert', 'shard')), may hold values from 1 to 3, as said below
- aux_weight: float32 [], replicated, may hold values from 605184 to 1210368
- attn_qkv1: bfloat16 [3, 512, 512], P(None, 'shard'), may hold values from -0.25 to 0.25
- attn_out1: bfloat16 [512, 512], P('shard'), may hold values from -3 to 3
- mlp_in: bfloat16 [512, 2048], P('shard'), may hold values from -0.25 to 0.25
- mlp_out: bfloat16 [2048, 512], P('shard'), may hold values from -0.125 to 0.125
- gains1: bfloat16 [2, 512], P(None, 'shard'), may hold values from 0.5 to 1.5
- attn_qkv2: bfloat16 [3, 512, 512], P(None, 'shard'), may hold values from -0.25 to 0.25
- attn_out2: bfloat16 [512, 512], P('shard'), may hold values from -3 to 3
- router: bfloat16 [512, 32], P('shard'), may hold values from -0.25 to 0.25
- gains2: bfloat16 [2, 512], P(None, 'shard'), may hold values from 0.5 to 1.5
- expert_in: bfloat16 [32, 512, 2048], P('expert'), may hold values from -0.25 to 0.25
- expert_out: bfloat16 [32, 2048, 512], P('expert'), as said below
Outputs:
- output: bfloat16 [96, 197, 512], P(('expert', 'shard'))
- balance_loss: float32 [], replicated
- grad_tokens: float32 [96, 197, 512], P(('expert', 'shard'))
- grad_attn_qkv1: float32 [3, 512, 512], P(None, 'shard')
- grad_attn_out1: float32 [512, 512], P('shard')
- grad_mlp_in: float32 [512, 2048], P('shard')
- grad_mlp_out: float32 [2048, 512], P('shard')
- grad_gains1: float32 [2, 512], P(None, 'shard')
- grad_attn_qkv2: float32 [3, 512, 512], P(None, 'shard')
- grad_attn_out2: float32 [512, 512], P('shard')
- grad_router: float32 [512, 32], P('shard')
- grad_gains2: float32 [2, 512], P(None, 'shard')
- grad_expert_in: float32 [32, 512, 2048], P('expert')
- grad_expert_out: float32 [32, 2048, 512], P('expert')
The draws below stay inside these ranges and needn't reach their ends.
Inputs may be any that keep to these rules, and one draw needn't show every extreme that they name: `counts`: each device holds its images in its first slots, the further slots are padding; some device holds 3 images in every draw. `routes`: each token names two different experts. Among the 591 tokens of one device's slots no expert is named more than 40 times, a bound that some block reaches. `expert_out`: independent entries of mean 0 and standard deviation 40 / sqrt(2048).
All inputs are finite; a program needn't handle non-finite values.
Results may differ from the reference program's by a relative error of at most 0.023.
Values may be sent and summed in bfloat16 or wider, within the bound.
A program may use at most 256 MiB of HBM per device.

```python
import math
from functools import partial
import jax
import jax.numpy as jnp
import numpy as np
from jax import lax

D = 512
HEADS = 8
HDIM = 64
FF = 2048
EXPERTS = 32
SEQ = 197
IMG_CAP = 3
CAP = 40
SLOTS = 96


def draw_counts(key, part):
    first, second = jax.random.split(key)
    devices = SLOTS // IMG_CAP
    drawn = jax.random.randint(first, (devices,), 1, IMG_CAP + 1)
    full_one = jax.random.randint(second, (), 0, devices)
    return jnp.where(jnp.arange(devices) == full_one, IMG_CAP, drawn).astype(jnp.int32)


def draw_expert_out(key, part):
    key = jax.random.fold_in(key, 7)
    values = jax.random.truncated_normal(key, -6.0, 6.0, (EXPERTS, FF, D), jnp.float32)
    return (values * (40.0 / FF ** 0.5)).astype(jnp.bfloat16)


def block_levels(stream_key, dims, shards, smallest, high):
    level = 1.0
    for axis_at, parts in shards:
        heights = jax.random.uniform(jax.random.fold_in(jax.random.fold_in(stream_key, 6), axis_at), (parts,), jnp.float32, smallest / len(shards), high / len(shards))
        level = level * jnp.repeat(jnp.exp(heights), dims[axis_at] // parts).reshape((-1,) + (1,) * (len(dims) - 1 - axis_at))
    return level


def deal_out(rng, own, number, rows, number_of, top, most, lean):
    ranking = jax.random.permutation(rng, number_of)
    heavy_load, usual = load_shares(number_of, rows * top, most, lean, True), load_shares(number_of, rows * top, most, lean, False)
    places = jnp.arange(number_of)

    def named(lengths, turn):
        used = int((lengths > 0).sum())
        fixed = max(1, used // 4)
        moved = fixed + (places - fixed + turn * (used - fixed)) % max(1, number_of - fixed)
        return jnp.zeros((number_of,), jnp.int32).at[ranking[jnp.where(places < fixed, places, moved)]].set(jnp.asarray(lengths, jnp.int32))

    lengths = jnp.where(number % 4 == 0, named(heavy_load, number // 4), named(usual, number - number // 4 - 1))
    mixed = jax.random.permutation(jax.random.fold_in(own, 3), number_of)
    donor, receiver = mixed[0:number_of // 2 * 2:2], mixed[1:number_of // 2 * 2:2]
    room = jnp.minimum(lengths[donor] - 1, most - lengths[receiver]) // 2
    room = jnp.where((donor == ranking[0]) | (receiver == ranking[0]) | (lengths[receiver] == 0), 0, jnp.maximum(room, 0))
    moved = jax.random.randint(jax.random.fold_in(own, 4), (number_of // 2,), 0, 1 << 20) % (room + 1)
    lengths = lengths.at[donor].add(-moved).at[receiver].add(moved)
    members = jnp.searchsorted(jnp.cumsum(lengths), jnp.arange(rows * top), side="right").astype(jnp.int32)
    table = members.reshape(top, rows).T
    table = table[jax.random.permutation(jax.random.fold_in(own, 1), rows)]
    turn = jax.random.randint(jax.random.fold_in(own, 2), (rows, 1), 0, top)
    return jnp.take_along_axis(table, (jnp.arange(top)[None, :] + turn) % top, axis=1)


def load_shares(amount, total, limit, lean, full):
    portions = [(1 << 20) // math.isqrt(standing ** lean) + 1 for standing in range(1, amount + 1)]
    largest = limit if full else min(limit, max(-(-total // amount), total * portions[0] // sum(portions)))
    least = 1 if total - largest >= amount - 1 else 0
    holding, surplus = [largest] + [least] * (amount - 1), total - largest - least * (amount - 1)
    while surplus > 0:
        movable = [i for i in range(1, amount) if holding[i] < largest] or [i for i in range(1, amount) if holding[i] < limit]
        pool, budget = sum([portions[i] for i in movable]), surplus
        for i in movable:
            extra = min(limit - holding[i], max(1, budget * portions[i] // pool), surplus)
            holding[i] = holding[i] + extra
            surplus = surplus - extra
    return np.array(holding)


def bell_draw(key, dims, deviation, reach, cuts=(), kind=jnp.bfloat16):
    loudness = block_levels(key, dims, cuts, -0.22, 0.18) if cuts else 1.0
    values = jax.random.normal(key, dims, jnp.float32) * deviation * loudness
    return jnp.minimum(jnp.maximum(values, -reach), reach).astype(kind)


def setup_inputs(seed: int = 0) -> dict:
    seeds = jax.random.split(jax.random.key(seed), 17)
    tokens = bell_draw(seeds[0], (SLOTS, SEQ, D), 1.0, 6.0, ((0, 32),))
    cotangent = bell_draw(seeds[1], (SLOTS, SEQ, D), 1.0, 6.0, ((0, 32),))
    routes_keys = jax.random.split(jax.random.fold_in(seeds[2], 1), SLOTS * SEQ // (IMG_CAP * SEQ))
    routes_turns = jax.random.permutation(jax.random.fold_in(seeds[2], 3), SLOTS * SEQ // (IMG_CAP * SEQ))
    routes = jax.vmap(lambda own, number: deal_out(jax.random.fold_in(seeds[2], 2), own, number, IMG_CAP * SEQ, EXPERTS, 2, CAP, 1))(routes_keys, routes_turns).reshape((SLOTS, SEQ, 2))
    counts = draw_counts(jax.random.fold_in(seeds[16], 71), 0)
    aux_weight = jnp.clip(jax.random.uniform(seeds[4], (), jnp.float32, 605184.0, 1210368), 605184.0, 1210368)
    attn_qkv1 = bell_draw(seeds[5], (3, D, D), D ** -0.5, 0.25, ((1, 2),))
    attn_out1 = bell_draw(seeds[6], (D, D), (max(D // 128, 1)) ** -0.5, 3.0, ((0, 2),))
    mlp_in = bell_draw(seeds[7], (D, FF), D ** -0.5, 0.25, ((0, 2),))
    mlp_out = bell_draw(seeds[8], (FF, D), FF ** -0.5, 0.125, ((0, 2),))
    gains1 = jnp.clip(1.0 + 0.1 * jax.random.normal(seeds[9], (2, D), jnp.float32), 0.5, 1.5).astype(jnp.bfloat16)
    attn_qkv2 = bell_draw(seeds[10], (3, D, D), D ** -0.5, 0.25, ((1, 2),))
    attn_out2 = bell_draw(seeds[11], (D, D), (max(D // 128, 1)) ** -0.5, 3.0, ((0, 2),))
    router = bell_draw(seeds[12], (D, EXPERTS), D ** -0.5, 0.25, ((0, 2),))
    gains2 = jnp.clip(1.0 + 0.1 * jax.random.normal(seeds[13], (2, D), jnp.float32), 0.5, 1.5).astype(jnp.bfloat16)
    expert_in = bell_draw(seeds[14], (EXPERTS, D, FF), D ** -0.5, 0.25, ((0, 16),))
    expert_out = draw_expert_out(jax.random.fold_in(seeds[16], 71), 0)
    return dict(tokens=tokens, cotangent=cotangent, routes=routes, counts=counts, aux_weight=aux_weight, attn_qkv1=attn_qkv1, attn_out1=attn_out1, mlp_in=mlp_in, mlp_out=mlp_out, gains1=gains1, attn_qkv2=attn_qkv2, attn_out2=attn_out2, router=router, gains2=gains2, expert_in=expert_in, expert_out=expert_out)


EPS = 1e-06
HIGHEST = lax.Precision.HIGHEST

@jax.custom_vjp
def low(v):
    return lax.optimization_barrier(v.astype(jnp.bfloat16)).astype(jnp.float32)

@jax.custom_vjp
def low_back(v):
    return v

def low_keep(v):
    return (low(v), None)

def low_pass(kept, grad):
    return (grad,)

def back_keep(v):
    return (v, None)

def back_low(kept, grad):
    return (low(grad),)
low.defvjp(low_keep, low_pass)
low_back.defvjp(back_keep, back_low)

def layer_norm(values, norm_gain):
    average = lax.optimization_barrier(jnp.mean(values, axis=-1, keepdims=True))
    centered = values - average
    variance = lax.optimization_barrier(jnp.mean(centered * centered, axis=-1, keepdims=True))
    return centered * lax.rsqrt(variance + EPS) * norm_gain

def attention(normed, qkv_weight, out_weight):
    images, seq_len, model_width = normed.shape
    projected = low(low_back(jnp.einsum('bsd,cde->cbse', normed, qkv_weight, precision=HIGHEST)))
    head_vals = projected.reshape(3, images, seq_len, HEADS, HDIM)
    scores = low_back(HDIM ** (-0.5) * jnp.einsum('bqhd,bkhd->bhqk', head_vals[0], head_vals[1], precision=HIGHEST))
    attn_probs = low(jax.nn.softmax(scores, axis=-1))
    mixture = jnp.einsum('bhqk,bkhd->bqhd', attn_probs, head_vals[2], precision=HIGHEST)
    mixture = low(low_back(mixture.reshape(images, seq_len, model_width)))
    return low_back(jnp.einsum('bsd,de->bse', mixture, out_weight, precision=HIGHEST))

def feed_forward(normed, in_weight, out_weight):
    preact = low_back(jnp.einsum('bsd,df->bsf', normed, in_weight, precision=HIGHEST))
    activation = low(jax.nn.gelu(preact, approximate=False))
    return low_back(jnp.einsum('bsf,fd->bsd', activation, out_weight, precision=HIGHEST))

def dense_part(grouped, params):
    qkv_one, out_one, mlp_in, mlp_out, gains_one, qkv_two, out_two, router, gains_two = params
    hidden = grouped + attention(low(layer_norm(grouped, gains_one[0])), qkv_one, out_one)
    block_out = hidden + feed_forward(low(layer_norm(hidden, gains_one[1])), mlp_in, mlp_out)
    hidden_two = block_out + attention(low(layer_norm(block_out, gains_two[0])), qkv_two, out_two)
    routed = low(layer_norm(hidden_two, gains_two[1]))
    logits = low_back(jnp.einsum('bsd,de->bse', routed, router, precision=HIGHEST))
    return (hidden_two, routed, jax.nn.softmax(logits, axis=-1))

def serve_expert(items, routed_flat):
    row_ids, keep_mask, in_weight, out_weight = items
    sent = low_back(routed_flat[row_ids] * keep_mask[:, None])
    preact = low_back(jnp.dot(sent, in_weight, precision=HIGHEST, preferred_element_type=jnp.float32))
    activation = low(jax.nn.gelu(preact, approximate=False))
    return low(low_back(jnp.dot(activation, out_weight, precision=HIGHEST, preferred_element_type=jnp.float32)))

def slot_table(routes, counts):
    devices = counts.shape[0]
    row_count = IMG_CAP * SEQ
    live_images = jnp.arange(IMG_CAP, dtype=jnp.int32)[None, :] < counts[:, None]
    live_tokens = jnp.repeat(live_images, SEQ, axis=1)
    chosen = routes.reshape(devices, row_count * 2)
    live_pairs = jnp.repeat(live_tokens, 2, axis=1)
    onehot = ((chosen[:, :, None] == jnp.arange(EXPERTS, dtype=jnp.int32)[None, None, :]) & live_pairs[:, :, None]).astype(jnp.int32)
    position = lax.optimization_barrier(jnp.sum((jnp.cumsum(onehot, axis=1) - onehot) * onehot, axis=2))
    slot_index = jnp.arange(devices, dtype=jnp.int32)[:, None] * CAP + position
    target = jnp.where(live_pairs, chosen, EXPERTS)
    token_of = (jnp.arange(devices * row_count * 2, dtype=jnp.int32) // 2).reshape(devices, row_count * 2)
    table = jnp.full((EXPERTS, devices * CAP), devices * row_count, jnp.int32)
    table = table.at[target.reshape(-1), slot_index.reshape(-1)].set(token_of.reshape(-1), mode='drop')
    load_count = lax.optimization_barrier(jnp.sum(onehot, axis=(0, 1)))
    return (table, live_tokens, load_count)

def forward(tokens, qkv_one, out_one, mlp_in, mlp_out, gains_one, qkv_two, out_two, router, gains_two, expert_in, expert_out, table, live_tokens, load_count):
    devices = live_tokens.shape[0]
    row_count = IMG_CAP * SEQ
    params = (qkv_one, out_one, mlp_in, mlp_out, gains_one, qkv_two, out_two, router, gains_two)
    grouped = tokens.reshape(devices, IMG_CAP, SEQ, D)
    hidden_two, routed, router_probs = lax.map(jax.checkpoint(partial(dense_part, params=params)), grouped)
    hidden_two = hidden_two.reshape(devices * row_count, D)
    routed = routed.reshape(devices * row_count, D)
    router_probs = router_probs.reshape(devices * row_count, EXPERTS)
    present = table < devices * row_count
    safe_rows = jnp.where(present, table, 0).astype(jnp.int32)
    keep_mask = present.astype(jnp.float32)
    served = lax.map(jax.checkpoint(partial(serve_expert, routed_flat=routed)), (safe_rows, keep_mask, expert_in, expert_out))
    gate_value = router_probs[safe_rows, jnp.arange(EXPERTS, dtype=jnp.int32)[:, None]] * keep_mask
    mixture = jnp.zeros((devices * row_count, D), jnp.float32).at[safe_rows.reshape(-1)].add((gate_value[:, :, None] * served).reshape(-1, D))
    live_rows = live_tokens.reshape(-1).astype(jnp.float32)
    output = (hidden_two + mixture) * live_rows[:, None]
    token_total = jnp.sum(live_rows)
    fraction = load_count.astype(jnp.float32) / (2.0 * token_total)
    mean_prob = lax.optimization_barrier(jnp.sum(router_probs * live_rows[:, None], axis=0)) / token_total
    balance_loss = EXPERTS * jnp.sum(fraction * mean_prob)
    return (output.reshape(tokens.shape), balance_loss)

def reference(tokens, cotangent, routes, counts, aux_weight, attn_qkv1, attn_out1, mlp_in, mlp_out, gains1, attn_qkv2, attn_out2, router, gains2, expert_in, expert_out):
    table, live_tokens, load_count = slot_table(routes, counts)
    floats = tuple((weight.astype(jnp.float32) for weight in (tokens, attn_qkv1, attn_out1, mlp_in, mlp_out, gains1, attn_qkv2, attn_out2, router, gains2, expert_in, expert_out)))
    bound = partial(forward, table=table, live_tokens=live_tokens, load_count=load_count)
    (output, balance_loss), pullback = jax.vjp(bound, *floats)
    grads = pullback((cotangent.astype(jnp.float32), aux_weight))
    return (output.astype(jnp.bfloat16), balance_loss, grads[0], grads[1], grads[2], grads[3], grads[4], grads[5], grads[6], grads[7], grads[8], grads[9], grads[10], grads[11])
```

```python
import functools

import jax
import jax.numpy as jnp
from jax import lax
from jax.experimental import pallas as pl
from jax.experimental.pallas import tpu as pltpu
from jax.sharding import PartitionSpec as P

HEADS = 8
CAP = 40
EPS = 1e-06
NEG = -1e30
LANES = 128
f32 = jnp.float32
bf16 = jnp.bfloat16
ANY = pl.BlockSpec(memory_space=pl.ANY)
VM = pl.BlockSpec(memory_space=pltpu.VMEM)
VMEM_BYTES = 58 << 20


def nn(a, b):
    return lax.dot_general(a, b, (((1,), (0,)), ((), ())), preferred_element_type=f32)


def nt(a, b):
    return lax.dot_general(a, b, (((1,), (1,)), ((), ())), preferred_element_type=f32)


def tn(a, b):
    return lax.dot_general(a, b, (((0,), (0,)), ((), ())), preferred_element_type=f32)


def sds(shape, dtype):
    return jax.ShapeDtypeStruct(shape, dtype)


def padded(seq):
    return -(-seq // 16) * 16


def norm(x):
    xc = x - jnp.mean(x, axis=-1, keepdims=True)
    rs = lax.rsqrt(jnp.mean(xc * xc, axis=-1, keepdims=True) + EPS)
    return xc * rs, rs


def norm_back(dyn, xn, rs, gain):
    dgain = jnp.sum(dyn * xn, axis=0, keepdims=True)
    dxn = dyn * gain
    dv = dxn - jnp.mean(dxn, axis=-1, keepdims=True)
    dv = (dv - xn * jnp.mean(dxn * xn, axis=-1, keepdims=True)) * rs
    return dv, dgain


def gelu_pair(z):
    a = jnp.abs(z)
    t = 1.0 / (1.0 + (0.3275911 * 0.7071067811865476) * a)
    e = jnp.exp(-0.5 * (z * z))
    q = t * (0.127414796 + t * (-0.142248368 + t * (0.7107068705 + t * (-0.7265760135 + t * 0.5307027145))))
    q = q * e
    phi = jnp.where(z >= 0.0, 1.0 - q, q)
    return z * phi, phi + z * (e * 0.3989422804014327)


class Split:
    def __init__(self, shards):
        self.pair = shards == 2
        self.shards = shards

    def gather(self, owns):
        if not self.pair:
            whole = [lax.all_gather(o, "shard", axis=1, tiled=True) for o in owns]
            return whole
        core = lax.axis_index("expert") % 2
        owners = lax.axis_size("expert")
        half = owns[0].shape[1] // 2
        send = jnp.concatenate([lax.dynamic_slice_in_dim(o, core * half, half, 1) for o in owns], axis=0)
        far = lax.ppermute(send, "shard", [(0, 1), (1, 0)])
        near = lax.ppermute(far, "expert", [(i, i ^ 1) for i in range(owners)])
        return list(owns) + [far, near]

    def count(self, owns):
        return owns + 2 if self.pair else owns

    def copies(self, refs, full, sems):
        out = []
        if not self.pair:
            at = 0
            for i, r in enumerate(refs):
                n = r.shape[0]
                out.append(pltpu.make_async_copy(r, full.at[at:at + n], sems.at[i]))
                at += n
            return out
        me = lax.axis_index("shard")
        core = lax.axis_index("expert") % 2
        rows = refs[0].shape[1]
        half = rows // 2
        at = 0
        for i, r in enumerate(refs[:-2]):
            n = r.shape[0]
            out.append(pltpu.make_async_copy(r, full.at[at:at + n, pl.ds(me * rows, rows), :], sems.at[i]))
            at += n
        base = (1 - me) * rows
        k = len(refs) - 2
        out.append(pltpu.make_async_copy(refs[k], full.at[:, pl.ds(base + core * half, half), :], sems.at[k]))
        out.append(pltpu.make_async_copy(refs[k + 1], full.at[:, pl.ds(base + (1 - core) * half, half), :], sems.at[k + 1]))
        return out


def start(copies):
    for c in copies:
        c.start()


def finish(copies):
    for c in copies:
        c.wait()


def call(body, outs, ins, scratch=(), specs=None, flops=0, nbytes=0, **kw):
    return pl.pallas_call(
        body,
        out_shape=outs,
        in_specs=specs or [VM] * len(ins),
        out_specs=[VM] * len(outs),
        scratch_shapes=list(scratch),
        compiler_params=pltpu.CompilerParams(vmem_limit_bytes=VMEM_BYTES),
        cost_estimate=pl.CostEstimate(flops=int(flops), bytes_accessed=int(nbytes), transcendentals=0),
        **kw,
    )(*ins)


def pad_store(ref, block, images, seq, step):
    ref[...] = jnp.zeros(ref.shape, ref.dtype)
    for i in range(images):
        ref[i * step:i * step + seq, :] = block(i).astype(ref.dtype)


def slot_start(expert, local, block):
    owner = jnp.floor((expert.astype(f32) + 0.5) * (1.0 / local))
    return owner * block + (expert.astype(f32) - owner * local) * CAP


def route_body(images, seq, local, block, r_ref, rt_ref, live_ref, cot_ref, dy_ref, dyd_ref, disp_ref, back_ref):
    rows = r_ref.shape[0]
    slots = disp_ref.shape[0]
    step = rows // images
    pad_store(dy_ref, lambda i: cot_ref[i], images, seq, step)
    dy_ref[...] = (dy_ref[...].astype(f32) * live_ref[...]).astype(bf16)
    lane = lax.broadcasted_iota(jnp.int32, (rows, LANES), 1)
    hit = (r_ref[:, 0:1] == lane) | (r_ref[:, 1:2] == lane)
    ti = lax.broadcasted_iota(jnp.int32, (rows, rows), 0)
    tj = lax.broadcasted_iota(jnp.int32, (rows, rows), 1)
    place = nn((ti > tj).astype(f32).astype(bf16), hit.astype(f32).astype(bf16))
    place = jnp.where(hit, place, -1.0).astype(bf16)
    off = lax.broadcasted_iota(jnp.int32, (LANES, slots), 1).astype(f32) - slot_start(
        lax.broadcasted_iota(jnp.int32, (LANES, slots), 0), local, block)
    spread = ((off >= 0) & (off < CAP)).astype(f32)
    within = jnp.sum(spread * off, axis=0, keepdims=True)
    within = jnp.where(jnp.sum(spread, axis=0, keepdims=True) > 0, within, -2.0)
    back_ref[...] = (nn(place, spread.astype(bf16)) == within).astype(f32).astype(bf16)
    sub = lax.broadcasted_iota(jnp.int32, (LANES, rows), 0)
    hit_t = (rt_ref[0:1, :] == sub) | (rt_ref[1:2, :] == sub)
    place_t = nn(hit_t.astype(f32).astype(bf16), (ti < tj).astype(f32).astype(bf16))
    place_t = jnp.where(hit_t, place_t, -1.0).astype(bf16)
    off = lax.broadcasted_iota(jnp.int32, (slots, LANES), 0).astype(f32) - slot_start(
        lax.broadcasted_iota(jnp.int32, (slots, LANES), 1), local, block)
    spread_t = ((off >= 0) & (off < CAP)).astype(f32)
    within_t = jnp.sum(spread_t * off, axis=1, keepdims=True)
    within_t = jnp.where(jnp.sum(spread_t, axis=1, keepdims=True) > 0, within_t, -2.0)
    disp_ref[...] = (nn(spread_t.astype(bf16), place_t) == within_t).astype(f32).astype(bf16)
    dyd_ref[...] = nn(disp_ref[...], dy_ref[...]).astype(bf16)


def attend_forward(step, seq, images, x, gain, wq, wo, qkv_ref, mix_ref):
    width = x.shape[1]
    head = width // HEADS
    scale = head ** -0.5
    xn, _ = norm(x)
    a = (xn * gain).astype(bf16)
    for c in range(3):
        qkv_ref[:, c * width:(c + 1) * width] = nn(a, wq[c][...]).astype(bf16)
    lane = lax.broadcasted_iota(jnp.int32, (1, LANES), 1)
    col = lax.broadcasted_iota(jnp.int32, (1, step), 1)
    per = LANES // head

    def image(i, _):
        at = pl.ds(pl.multiple_of(i * step, step), step)
        for hp in range(width // LANES):
            q = qkv_ref[at, hp * LANES:(hp + 1) * LANES]
            k = qkv_ref[at, width + hp * LANES:width + (hp + 1) * LANES]
            v = qkv_ref[at, 2 * width + hp * LANES:2 * width + (hp + 1) * LANES]
            got = None
            for h in range(per):
                mine = (lane >= h * head) & (lane < (h + 1) * head)
                qm = q * jnp.where(mine, scale, 0.0).astype(bf16)
                s = jnp.where(col < seq, nt(qm, k), NEG)
                e = jnp.exp(s - jnp.max(s, axis=-1, keepdims=True))
                p = (e * (1.0 / jnp.sum(e, axis=-1, keepdims=True))).astype(bf16)
                o = nn(p, v)
                got = o if got is None else jnp.where(mine, o, got)
            mix_ref[at, hp * LANES:(hp + 1) * LANES] = got.astype(bf16)
        return 0

    lax.fori_loop(0, images, image, 0)
    return x + nn(mix_ref[...], wo[...])


def attend_backward(step, seq, images, grad, x, gain, wq, wo, qkv_ref, mix_ref, dmix_ref, dqkv_ref, pack_ref, base):
    width = x.shape[1]
    head = width // HEADS
    scale = head ** -0.5
    shards = pack_ref.shape[0]
    part = width // shards
    low = grad.astype(bf16)
    dwo = tn(mix_ref[...], low).astype(bf16)
    for s in range(shards):
        pack_ref[s, base + 3 * part:base + 4 * part, :] = dwo[s * part:(s + 1) * part]
    dmix_ref[...] = nt(low, wo[...]).astype(bf16)
    lane = lax.broadcasted_iota(jnp.int32, (1, LANES), 1)
    key = lax.broadcasted_iota(jnp.int32, (step, 1), 0)
    per = LANES // head

    def image(i, _):
        at = pl.ds(pl.multiple_of(i * step, step), step)
        for hp in range(width // LANES):
            q = qkv_ref[at, hp * LANES:(hp + 1) * LANES]
            k = qkv_ref[at, width + hp * LANES:width + (hp + 1) * LANES]
            v = qkv_ref[at, 2 * width + hp * LANES:2 * width + (hp + 1) * LANES]
            do = dmix_ref[at, hp * LANES:(hp + 1) * LANES]
            dq = dk = dv = None
            for h in range(per):
                mine = (lane >= h * head) & (lane < (h + 1) * head)
                scaled = jnp.where(mine, scale, 0.0).astype(bf16)
                km = k * scaled
                s = jnp.where(key < seq, nt(km, q), NEG)
                e = jnp.exp(s - jnp.max(s, axis=0, keepdims=True))
                p = e * (1.0 / jnp.sum(e, axis=0, keepdims=True))
                dom = do * jnp.where(mine, 1.0, 0.0).astype(bf16)
                dp = nt(v, dom)
                ds = (p * (dp - jnp.sum(p * dp, axis=0, keepdims=True))).astype(bf16)
                hv = nn(p.astype(bf16), dom)
                hk = nn(ds, q * scaled)
                hq = tn(ds, km)
                dq, dk, dv = (hq, hk, hv) if dq is None else (dq + hq, dk + hk, dv + hv)
            dqkv_ref[at, hp * LANES:(hp + 1) * LANES] = dq.astype(bf16)
            dqkv_ref[at, width + hp * LANES:width + (hp + 1) * LANES] = dk.astype(bf16)
            dqkv_ref[at, 2 * width + hp * LANES:2 * width + (hp + 1) * LANES] = dv.astype(bf16)
        return 0

    lax.fori_loop(0, images, image, 0)
    xn, rs = norm(x)
    a = (xn * gain).astype(bf16)
    da = None
    for c in range(3):
        d = dqkv_ref[:, c * width:(c + 1) * width]
        dw = tn(a, d).astype(bf16)
        for s in range(shards):
            pack_ref[s, base + c * part:base + (c + 1) * part, :] = dw[s * part:(s + 1) * part]
        one = nt(d, wq[c][...])
        da = one if da is None else da + one
    return norm_back(da, xn, rs, gain)


def block1_body(split, images, seq, x_ref, gain_ref, *refs):
    n = split.count(2)
    pieces, (hidden_ref, qkv_ref, mix_ref, w, sems) = refs[:n], refs[n:]
    copies = split.copies(pieces, w, sems)
    start(copies)
    step = hidden_ref.shape[0] // images
    pad_store(hidden_ref, lambda i: x_ref[i], images, seq, step)
    finish(copies)
    hidden_ref[...] = attend_forward(
        step, seq, images, hidden_ref[...], gain_ref[0:1, :], [w.at[c] for c in range(3)], w.at[3], qkv_ref, mix_ref
    )


def mlp_body(split, blocks, hidden_ref, gain_ref, *refs):
    n = 2 * split.count(1)
    pieces, (out_ref, act_ref, slope_ref, w1, w2, sems) = refs[:n], refs[n:]
    half = n // 2
    copies = split.copies(pieces[:half], w1, sems.at[0]) + split.copies(pieces[half:], w2, sems.at[1])
    start(copies)
    hidden = hidden_ref[...]
    xn, _ = norm(hidden)
    u = (xn * gain_ref[1:2, :]).astype(bf16)
    out_ref[...] = hidden
    finish(copies)
    ff = act_ref.shape[1]
    wide = ff // blocks
    for b in range(blocks):
        at = slice(b * wide, (b + 1) * wide)
        act, slope = gelu_pair(nn(u, w1[0, :, at]))
        act = act.astype(bf16)
        act_ref[:, at] = act
        slope_ref[:, at] = slope.astype(bf16)
        out_ref[...] += nn(act, w2[0, at, :])


def router_probs(u, router, experts):
    lane = lax.broadcasted_iota(jnp.int32, (1, LANES), 1)
    logits = jnp.where(lane < experts, nn(u, router), NEG)
    e = jnp.exp(logits - jnp.max(logits, axis=-1, keepdims=True))
    return e * (1.0 / jnp.sum(e, axis=-1, keepdims=True))


def block2_body(split, images, seq, experts, x_ref, gain_ref, router_ref, disp_ref, live_ref, load_ref, *refs):
    n = split.count(2)
    pieces, (hidden_ref, qkv_ref, mix_ref, u_ref, probs_ref, sum_ref, ud_ref, w, sems) = refs[:n], refs[n:]
    copies = split.copies(pieces, w, sems)
    start(copies)
    finish(copies)
    step = hidden_ref.shape[0] // images
    hidden = attend_forward(
        step, seq, images, x_ref[...], gain_ref[2:3, :], [w.at[c] for c in range(3)], w.at[3], qkv_ref, mix_ref
    )
    hidden_ref[...] = hidden
    xn, _ = norm(hidden)
    u = (xn * gain_ref[3:4, :]).astype(bf16)
    u_ref[...] = u
    ud_ref[...] = nn(disp_ref[...], u).astype(bf16)
    probs = router_probs(u, router_ref[...], experts)
    probs_ref[...] = probs
    sums = jnp.sum(probs * live_ref[...], axis=0, keepdims=True)
    sum_ref[...] = jnp.concatenate([load_ref[...], sums, jnp.zeros((6, LANES), f32)], axis=0)


def split_rows(block, local):
    n, r, w = block.shape
    v = block.astype(f32)
    if r != local * CAP:
        v = v[:, :local * CAP]
    v = v.reshape(n, local, CAP, w)
    return [v[:, i].reshape(n * CAP, w) for i in range(local)]


def join_rows(parts, sources, block):
    local = len(parts)
    w = parts[0].shape[1]
    v = jnp.concatenate([p.reshape(sources, 1, CAP, w) for p in parts], axis=1).reshape(sources, local * CAP, w)
    if block != local * CAP:
        v = jnp.concatenate([v, jnp.zeros((sources, block - local * CAP, w), f32)], axis=1)
    return v


def gate_of(u, router, experts, e):
    lane = lax.broadcasted_iota(jnp.int32, (1, LANES), 1)
    return jnp.sum(jnp.where(lane == e, router_probs(u, router, experts), 0.0), axis=-1, keepdims=True)


def xor(a, b, bits):
    out = 0
    for i in range(bits):
        out = out + ((a // (1 << i) + b // (1 << i)) % 2) * (1 << i)
    return out


def expert_body(owners, shards, local, experts, group, uout_ref, dy_ref, router_ref, stat_ref, w1_hbm, w2_hbm,
                uin_ref, served_ref, duback_ref, dgback_ref, total_ref, dyx_ref,
                w1, w2, dusend, dgsend, statx, state, wsem, lsem, us, ur, ds_, dr, gs, gr, xs, xr, ss, sr, ys, yr):
    me, x = lax.axis_index("expert"), lax.axis_index("shard")
    bits = owners.bit_length() - 1
    barrier = pltpu.get_barrier_semaphore()

    def at(e, s):
        return dict(device_id=(e, s), device_id_type=pl.DeviceIdType.MESH)

    def each(lo, hi, f):
        lax.fori_loop(lo, hi, lambda k, c: (f(k), c)[1], 0)

    def peer(k):
        return xor(me, k, bits)

    each(1, owners, lambda k: pl.semaphore_signal(barrier, inc=1, **at(peer(k), x)))
    each(1, shards, lambda k: pl.semaphore_signal(barrier, inc=1, **at(me, (x + k) % shards)))
    weights = [pltpu.make_async_copy(w1_hbm, w1, wsem.at[0]), pltpu.make_async_copy(w2_hbm, w2, wsem.at[1])]
    start(weights)
    own = pltpu.make_async_copy(uout_ref.at[me], uin_ref.at[me], lsem.at[0])
    own.start()
    pl.semaphore_wait(barrier, owners - 1 + shards - 1)

    def send_u(k):
        return pltpu.make_async_remote_copy(uout_ref.at[peer(k)], uin_ref.at[me], us.at[k], ur.at[k], **at(peer(k), x))

    def send_du(k):
        return pltpu.make_async_remote_copy(dusend.at[peer(k)], duback_ref.at[me], ds_.at[k], dr.at[k], **at(peer(k), x))

    def send_dg(k):
        return pltpu.make_async_remote_copy(dgsend.at[peer(k)], dgback_ref.at[me], gs.at[k], gr.at[k], **at(peer(k), x))

    def send_statx(k):
        return pltpu.make_async_remote_copy(stat_ref, statx.at[k], xs.at[k], xr.at[k], **at(me, (x + k) % shards))

    def send_dyx(k):
        return pltpu.make_async_remote_copy(dy_ref, dyx_ref.at[k - 1], ys.at[k], yr.at[k], **at(me, (x + k) % shards))

    def send_state(k):
        return pltpu.make_async_remote_copy(state.at[0], state.at[k], ss.at[k], sr.at[k], **at(peer(k), x))

    each(1, shards, lambda k: send_statx(k).start())
    each(1, owners, lambda k: send_u(owners - k).start())
    each(1, shards, lambda k: send_dyx(k).start())
    each(1, shards, lambda k: send_statx(k).wait())
    sums = stat_ref[...]
    for k in range(1, shards):
        sums = sums + statx[k]
    state[0] = sums
    each(1, owners, lambda k: send_state(k).start())
    finish(weights)

    def work(g):
        base = xor(me // group, g, bits) * group
        rows = pl.ds(base, group)
        us_, dys = split_rows(uin_ref[rows], local), split_rows(dy_ref[rows], local)
        served, dus, prods = [], [], []
        for i in range(local):
            u, dy = us_[i].astype(bf16), dys[i]
            gate = gate_of(u, router_ref[...], experts, me * local + i)
            dsv = (gate * dy).astype(bf16)
            act, slope = gelu_pair(nn(u, w1[i]))
            out = nn(act.astype(bf16), w2[i])
            dz = (slope * nt(dsv, w2[i])).astype(bf16)
            dus.append(nt(dz, w1[i]))
            served.append(gate * out)
            prods.append(dy * out)
        block = uin_ref.shape[1]
        served_ref[rows] = join_rows(served, group, block).astype(bf16)
        dusend[rows] = join_rows(dus, group, block).astype(bf16)
        prod = join_rows(prods, group, block)
        ones = jnp.ones((8, prod.shape[2]), bf16)
        for j in range(group):
            hi = prod[j].astype(bf16)
            lo = (prod[j] - hi.astype(f32)).astype(bf16)
            dgsend[base + j, :, 0:block] = nt(ones, hi) + nt(ones, lo)

    def step(g):
        @pl.when(g == 0)
        def _():
            own.wait()

        for j in range(group):
            k = g * group + j
            if j == 0:
                pl.when(g > 0)(lambda k=k: send_u(k).wait_recv())
            else:
                send_u(k).wait_recv()
        work(g)
        for j in range(group):
            k = g * group + j
            if j == 0:
                @pl.when(g > 0)
                def _(k=k):
                    send_du(k).start()
                    send_dg(k).start()
            else:
                send_du(k).start()
                send_dg(k).start()

    each(0, owners // group, step)
    backs = [pltpu.make_async_copy(dusend.at[me], duback_ref.at[me], lsem.at[0]),
             pltpu.make_async_copy(dgsend.at[me], dgback_ref.at[me], lsem.at[1])]
    start(backs)
    each(1, owners, lambda k: send_state(k).wait())
    total = state[0]
    for k in range(1, owners):
        total = total + state[k]
    total_ref[...] = total
    each(1, owners, lambda k: send_u(k).wait_send())
    finish(backs)
    each(1, shards, lambda k: send_dyx(k).wait())
    each(1, owners, lambda k: send_du(k).wait())
    each(1, owners, lambda k: send_dg(k).wait())


def expert_grad_body(pieces, experts, *refs):
    us, dys = refs[:pieces], refs[pieces:2 * pieces]
    router_ref, w1_ref, w2_ref, g1_ref, g2_ref, urow, drow, stage, sems = refs[2 * pieces:]
    local = pl.num_programs(0)
    e = lax.axis_index("expert") * local + pl.program_id(0)

    @pl.when((pl.program_id(0) == 0) & (pl.program_id(1) == 0))
    def _():
        todo = [(us[i], urow, i) for i in range(pieces)] + [(dys[i], drow, i) for i in range(pieces)]
        copies = [pltpu.make_async_copy(r, stage.at[n % 2], sems.at[n % 2]) for n, (r, _, _) in enumerate(todo)]
        copies[0].start()
        for n, (_, to, i) in enumerate(todo):
            if n + 1 < len(todo):
                copies[n + 1].start()
            copies[n].wait()
            for j, v in enumerate(split_rows(stage[n % 2], urow.shape[1])):
                to[i, j] = v.astype(bf16)

    at = pl.program_id(0)
    for i in range(pieces):
        u = urow[i, at]
        dy = drow[i, at]
        gate = gate_of(u, router_ref[...], experts, e)
        ds = (gate * dy.astype(f32)).astype(bf16)
        act, slope = gelu_pair(nn(u, w1_ref[0]))
        dz = (slope * nt(ds, w2_ref[0])).astype(bf16)
        g1 = tn(u, dz)
        g2 = tn(act.astype(bf16), ds)
        if i == 0:
            g1_ref[0] = g1
            g2_ref[0] = g2
        else:
            g1_ref[0] += g1
            g2_ref[0] += g2


def split3(v):
    hi = v.astype(bf16)
    r = v - hi.astype(f32)
    mid = r.astype(bf16)
    lo = (r - mid.astype(f32)).astype(bf16)
    return hi, mid, lo


def back2_body(split, images, seq, experts, dy_ref, u_ref, probs_ref, hidden_ref, x_ref, gain_ref, router_ref, aux_ref,
               stat_ref, live_ref, back_ref, ret_ref, dgate_ref, qkv_ref, mix_ref, *refs):
    n = split.count(2)
    pieces, (grad_ref, pack_ref, small_ref, w, sems, dmix_ref, dqkv_ref) = refs[:n], refs[n:]
    copies = split.copies(pieces, w, sems)
    start(copies)
    slots = back_ref.shape[1]
    owners = dgate_ref.shape[0]
    local = experts // owners
    block = slots // owners
    off = lax.broadcasted_iota(jnp.int32, (slots, LANES), 0).astype(f32) - slot_start(
        lax.broadcasted_iota(jnp.int32, (slots, LANES), 1), local, block)
    oe = lax.broadcasted_iota(jnp.int32, (owners, LANES), 0).astype(f32)
    ee = lax.broadcasted_iota(jnp.int32, (owners, LANES), 1).astype(f32)
    pick = ((ee >= oe * local) & (ee < oe * local + local)).astype(f32).astype(bf16)
    column = 0.0
    for part in split3(dgate_ref[:, 0, :]):
        column = column + tn(part, pick)
    table = jnp.where((off >= 0) & (off < CAP), jnp.concatenate([column[0:block]] * owners, axis=0), 0.0)
    lane = lax.broadcasted_iota(jnp.int32, (1, LANES), 1)
    stat = stat_ref[0:1, :]
    total = jnp.sum(jnp.where(lane == LANES - 1, stat, 0.0), axis=-1, keepdims=True)
    fraction = jnp.where(lane < experts, stat, 0.0) / (2.0 * total)
    loss = experts * jnp.sum(fraction * stat_ref[1:2, :] / total, axis=-1, keepdims=True)
    small_ref[LANES + 2:LANES + 3, :] = jnp.broadcast_to(loss, (1, small_ref.shape[1]))
    dprobs = (aux_ref[0, 0] * experts * fraction / total) * live_ref[...]
    for part in split3(table):
        dprobs = dprobs + nn(back_ref[...], part)
    probs = probs_ref[...]
    dlog = (probs * (dprobs - jnp.sum(probs * dprobs, axis=-1, keepdims=True))).astype(bf16)
    small_ref[0:LANES, :] = tn(dlog, u_ref[...])
    du = nn(back_ref[...], ret_ref[...]) + nt(dlog, router_ref[...])
    xn, rs = norm(hidden_ref[...])
    dv, dg = norm_back(du, xn, rs, gain_ref[3:4, :])
    small_ref[LANES:LANES + 1, :] = dg
    grad = dy_ref[...].astype(f32) + dv
    grad_ref[...] = grad
    finish(copies)
    step = hidden_ref.shape[0] // images
    dv, dg = attend_backward(
        step, seq, images, grad, x_ref[...], gain_ref[2:3, :], [w.at[c] for c in range(3)], w.at[3],
        qkv_ref, mix_ref, dmix_ref, dqkv_ref, pack_ref, 0,
    )
    small_ref[LANES + 1:LANES + 2, :] = dg
    grad_ref[...] += dv


def mlp_back_body(split, blocks, grad_ref, hidden_ref, gain_ref, act_ref, slope_ref, *refs):
    n = 2 * split.count(1)
    pieces, (out_ref, pack_ref, dgain_ref, w1, w2, sems, du_ref) = refs[:n], refs[n:]
    half = n // 2
    copies = split.copies(pieces[:half], w1, sems.at[0]) + split.copies(pieces[half:], w2, sems.at[1])
    start(copies)
    xn, rs = norm(hidden_ref[...])
    gain = gain_ref[1:2, :]
    u = (xn * gain).astype(bf16)
    grad = grad_ref[...]
    low = grad.astype(bf16)
    finish(copies)
    width = grad.shape[1]
    ff = act_ref.shape[1]
    shards = pack_ref.shape[0]
    part, fpart = width // shards, ff // shards
    blocks = ff // width
    base = part * blocks
    for b in range(blocks):
        at = slice(b * width, (b + 1) * width)
        dz = (slope_ref[:, at].astype(f32) * nt(low, w2[0, at, :])).astype(bf16)
        d = nt(dz, w1[0, :, at])
        if b == 0:
            du_ref[...] = d
        else:
            du_ref[...] += d
        gin = tn(u, dz).astype(bf16)
        for s in range(shards):
            pack_ref[s, b * part:(b + 1) * part, :] = gin[s * part:(s + 1) * part]
        gout = tn(act_ref[:, at], low).astype(bf16)
        per = min(width, fpart)
        for j in range(width // per):
            row = b * width + j * per
            s, off = row // fpart, row % fpart
            pack_ref[s, base + off:base + off + per, :] = gout[j * per:(j + 1) * per]
    dv, dg = norm_back(du_ref[...], xn, rs, gain)
    dgain_ref[...] = dg
    out_ref[...] = grad + dv


def back1_body(split, images, seq, experts, grad_ref, tok_ref, gain_ref, qkv_ref, mix_ref, small_ref, dg2_ref, *refs):
    n = split.count(2)
    pieces, (out_ref, pack_ref, w, sems, x_ref, dmix_ref, dqkv_ref) = refs[:n], refs[n:]
    copies = split.copies(pieces, w, sems)
    start(copies)
    step = x_ref.shape[0] // images
    pad_store(x_ref, lambda i: tok_ref[i], images, seq, step)
    finish(copies)
    width = x_ref.shape[1]
    dv, dg1 = attend_backward(
        step, seq, images, grad_ref[...], x_ref[...], gain_ref[0:1, :], [w.at[c] for c in range(3)], w.at[3],
        qkv_ref, mix_ref, dmix_ref, dqkv_ref, pack_ref, 0,
    )
    x_ref[...] = grad_ref[...] + dv
    for i in range(images):
        out_ref[i] = x_ref[i * step:i * step + seq, :]
    shards = pack_ref.shape[0]
    part = width // shards
    base = 4 * part
    gains = jnp.concatenate(
        [dg1, dg2_ref[...], small_ref[LANES + 1:LANES + 2, :], small_ref[LANES:LANES + 1, :], jnp.zeros((28, width), f32)], axis=0
    )
    both = jnp.concatenate([small_ref[0:32, :], gains], axis=0).astype(bf16)
    for s in range(shards):
        one = both[:, s * part:(s + 1) * part]
        pack_ref[s, base:base + 64, :] = jnp.concatenate([one, jnp.zeros((64, width - part), bf16)], axis=1)


def output_body(images, seq, hidden_ref, back_ref, ret_ref, live_ref, out_ref, tmp_ref):
    step = hidden_ref.shape[0] // images
    tmp_ref[...] = (hidden_ref[...] + nn(back_ref[...], ret_ref[...])) * live_ref[...]
    for i in range(images):
        out_ref[i] = tmp_ref[i * step:i * step + seq, :].astype(bf16)


def swap(owners, bit):
    return [(i, i ^ (1 << bit)) for i in range(owners)]


def reduce_all(g, owners, shards):
    me = lax.axis_index("expert")
    bits = owners.bit_length() - 1

    def add(a, b):
        return (a.astype(f32) + b.astype(f32)).astype(bf16)

    def fold(v, bit, axis):
        own = (me >> bit) & 1
        half = v.shape[axis] // 2
        keep = lax.dynamic_slice_in_dim(v, own * half, half, axis)
        send = lax.dynamic_slice_in_dim(v, (1 - own) * half, half, axis)
        return add(keep, lax.ppermute(send, "expert", swap(owners, bit)))

    v = fold(g, 0, 1)
    if shards == 2:
        x = lax.axis_index("shard")
        keep = lax.dynamic_index_in_dim(v, x, 0, keepdims=False)
        send = lax.dynamic_index_in_dim(v, 1 - x, 0, keepdims=False)
        v = add(keep, lax.ppermute(send, "shard", [(0, 1), (1, 0)]))
    else:
        v = lax.psum_scatter(v, "shard", scatter_dimension=0, tiled=True)[0]
    for bit in range(1, bits):
        v = fold(v, bit, 0)
    for bit in reversed(range(bits)):
        own = (me >> bit) & 1
        other = lax.ppermute(v, "expert", swap(owners, bit))
        v = jnp.where(own == 0, jnp.concatenate([v, other]), jnp.concatenate([other, v]))
    return v


def per_device(
    owners, shards, tokens, cotangent, routes, counts, aux_weight, attn_qkv1, attn_out1, mlp_in, mlp_out, gains1,
    attn_qkv2, attn_out2, router, gains2, expert_in, expert_out,
):
    images, seq, width = tokens.shape
    step = padded(seq)
    rows = images * step
    experts = router.shape[1]
    local = expert_in.shape[0]
    ff = mlp_in.shape[1]
    block_rows = -(-local * CAP // 16) * 16
    slots = owners * block_rows
    split = Split(shards)
    expert_swap = functools.partial(lax.all_to_all, axis_name="expert", split_axis=0, concat_axis=0, tiled=True)

    within = jnp.arange(step, dtype=jnp.int32) < seq
    live = ((jnp.arange(images, dtype=jnp.int32)[:, None] < counts[0]) & within[None, :]).reshape(rows)
    live = live.astype(f32)
    routes_pad = jnp.pad(routes, ((0, 0), (0, step - seq), (0, 0)), constant_values=-1).reshape(rows, 2)
    lanes = jnp.arange(LANES, dtype=jnp.int32)
    loads = jnp.sum(((routes_pad[:, :, None] == lanes) & (live[:, None, None] > 0)).astype(f32), axis=(0, 1))
    loads = jnp.where(lanes == LANES - 1, jnp.sum(live), loads)
    live_col = live[:, None]

    w_one = split.gather([attn_qkv1, attn_out1[None]])
    w_up = split.gather([mlp_in[None]])
    w_down = split.gather([mlp_out[None]])
    w_two = split.gather([attn_qkv2, attn_out2[None]])
    gains = jnp.concatenate([gains1, gains2])
    if shards == 2:
        x = lax.axis_index("shard")
        other = lax.ppermute(gains, "shard", [(0, 1), (1, 0)])
        gains = jnp.where(x == 0, jnp.concatenate([gains, other], 1), jnp.concatenate([other, gains], 1))
        other = lax.ppermute(router, "shard", [(0, 1), (1, 0)])
        router_full = jnp.where(x == 0, jnp.concatenate([router, other]), jnp.concatenate([other, router]))
    else:
        gains = lax.all_gather(gains, "shard", axis=1, tiled=True)
        router_full = lax.all_gather(router, "shard", axis=0, tiled=True)
    gains = gains.astype(f32)
    router_full = jnp.pad(router_full, ((0, 0), (0, LANES - experts)))

    dy, dy_out, disp, back = call(
        functools.partial(route_body, images, seq, local, block_rows),
        [sds((rows, width), bf16), sds((slots, width), bf16), sds((slots, rows), bf16), sds((rows, slots), bf16)],
        [routes_pad, routes_pad.T, live_col, cotangent], flops=2e9, nbytes=6e6,
    )
    block = (owners, block_rows, width)
    dy_in = expert_swap(dy_out.reshape(block))

    sem = pltpu.SemaphoreType.DMA
    attn_scratch = [pltpu.VMEM((4, width, width), bf16), sem((4,))]
    mlp_scratch = [pltpu.VMEM((1, width, ff), bf16), pltpu.VMEM((1, ff, width), bf16), sem((2, 4))]

    def specs(n, ins):
        return [VM] * n + [ANY] * (len(ins) - n)

    ins = [tokens, gains] + w_one
    hidden, qkv_one, mix_one = call(
        functools.partial(block1_body, split, images, seq),
        [sds((rows, width), f32), sds((rows, 3 * width), bf16), sds((rows, width), bf16)],
        ins, attn_scratch, specs(2, ins), flops=4e9, nbytes=8e6,
    )
    ins = [hidden, gains] + w_up + w_down
    block_out, act, slope = call(
        functools.partial(mlp_body, split, 4),
        [sds((rows, width), f32), sds((rows, ff), bf16), sds((rows, ff), bf16)],
        ins, mlp_scratch, specs(2, ins), flops=6e9, nbytes=12e6,
    )
    ins = [block_out, gains, router_full, disp, live_col, loads[None, :]] + w_two
    hidden_two, qkv_two, mix_two, u_two, probs, stat, u_out = call(
        functools.partial(block2_body, split, images, seq, experts),
        [sds((rows, width), f32), sds((rows, 3 * width), bf16), sds((rows, width), bf16), sds((rows, width), bf16),
         sds((rows, LANES), f32), sds((8, LANES), f32), sds((slots, width), bf16)],
        ins, attn_scratch, specs(6, ins), flops=5e9, nbytes=10e6,
    )

    group = min(4, owners)
    u_in, served, du_back, dgate_back, stat, dy_far = pl.pallas_call(
        functools.partial(expert_body, owners, shards, local, experts, group),
        out_shape=[sds(block, bf16), sds(block, bf16), sds(block, bf16), sds((owners, 8, LANES), f32), sds((8, LANES), f32),
                   sds((shards - 1,) + block, bf16)],
        in_specs=[VM] * 4 + [ANY] * 2,
        out_specs=[VM] * 6,
        scratch_shapes=[
            pltpu.VMEM((local, width, ff), bf16), pltpu.VMEM((local, ff, width), bf16), pltpu.VMEM(block, bf16),
            pltpu.VMEM((owners, 8, LANES), f32), pltpu.VMEM((shards, 8, LANES), f32), pltpu.VMEM((owners, 8, LANES), f32),
            sem((2,)), sem((2,)),
        ] + [sem((owners,))] * 6 + [sem((shards,))] * 2 + [sem((owners,))] * 2 + [sem((shards,))] * 2,
        compiler_params=pltpu.CompilerParams(vmem_limit_bytes=VMEM_BYTES, collective_id=0, has_side_effects=True),
        cost_estimate=pl.CostEstimate(flops=int(11e9), bytes_accessed=int(15e6), transcendentals=0),
    )(u_out.reshape(block), dy_in, router_full, stat, expert_in, expert_out)
    served_back = expert_swap(served).reshape(slots, width)

    if shards == 2:
        us = [u_in, lax.ppermute(u_in, "shard", [(0, 1), (1, 0)])]
    else:
        far = lax.all_gather(u_in, "shard")
        us = [u_in] + [lax.dynamic_index_in_dim(far, (lax.axis_index("shard") + shards - k) % shards, 0, False) for k in range(1, shards)]
    dys = [dy_in] + [dy_far[k] for k in range(shards - 1)]
    parts = 4
    wide = ff // parts
    up_spec = pl.BlockSpec((1, width, wide), lambda e, f: (e, 0, f))
    down_spec = pl.BlockSpec((1, wide, width), lambda e, f: (e, f, 0))
    grad_e_in, grad_e_out = pl.pallas_call(
        functools.partial(expert_grad_body, shards, experts),
        grid=(local, parts),
        out_shape=[sds((local, width, ff), f32), sds((local, ff, width), f32)],
        in_specs=[ANY] * (2 * shards) + [VM, up_spec, down_spec],
        out_specs=[up_spec, down_spec],
        scratch_shapes=[pltpu.VMEM((shards, local, owners * CAP, width), bf16)] * 2 + [pltpu.VMEM((2,) + block, bf16), sem((2,))],
        compiler_params=pltpu.CompilerParams(vmem_limit_bytes=VMEM_BYTES),
        cost_estimate=pl.CostEstimate(flops=int(27e9), bytes_accessed=int(40e6), transcendentals=0),
    )(*us, *dys, router_full, expert_in, expert_out)

    part = width // shards
    back_scratch = [pltpu.VMEM((rows, width), bf16), pltpu.VMEM((rows, 3 * width), bf16)]
    ins = [dy, u_two, probs, hidden_two, block_out, gains, router_full, aux_weight.reshape(1, 1), stat, live_col, back,
           du_back.reshape(slots, width), dgate_back,
           qkv_two, mix_two]
    n = len(ins)
    ins = ins + w_two
    grad_block, pack_two, small = call(
        functools.partial(back2_body, split, images, seq, experts),
        [sds((rows, width), f32), sds((shards, 4 * part, width), bf16), sds((LANES + 8, width), f32)],
        ins, attn_scratch + back_scratch, specs(n, ins), flops=9e9, nbytes=16e6,
    )
    balance_loss = small[LANES + 2, 0]
    late = reduce_all(pack_two, owners, shards)
    ins = [grad_block, hidden, gains, act, slope] + w_up + w_down
    grad_hidden, pack_mlp, dg_two = call(
        functools.partial(mlp_back_body, split, 4),
        [sds((rows, width), f32), sds((shards, part * (ff // width) + ff // shards, width), bf16), sds((1, width), f32)],
        ins, mlp_scratch + [pltpu.VMEM((rows, width), f32)], specs(5, ins), flops=11e9, nbytes=16e6,
    )
    middle = reduce_all(pack_mlp, owners, shards)
    ins = [grad_hidden, tokens, gains, qkv_one, mix_one, small, dg_two] + w_one
    grad_tokens, pack_one = call(
        functools.partial(back1_body, split, images, seq, experts),
        [sds((images, seq, width), f32), sds((shards, 4 * part + 64, width), bf16)],
        ins, attn_scratch + [pltpu.VMEM((rows, width), f32)] + back_scratch, specs(7, ins), flops=9e9, nbytes=14e6,
    )
    early = reduce_all(pack_one, owners, shards)
    (output,) = call(
        functools.partial(output_body, images, seq), [sds((images, seq, width), bf16)],
        [hidden_two, back, served_back, live_col], [pltpu.VMEM((rows, width), f32)], flops=1e9, nbytes=5e6,
    )

    late, middle, early = late.astype(f32), middle.astype(f32), early.astype(f32)
    up = middle[:part * (ff // width)].reshape(ff // width, part, width).transpose(1, 0, 2).reshape(part, ff)
    tail = early[4 * part:, :part]
    return (
        output,
        balance_loss,
        grad_tokens,
        early[:3 * part].reshape(3, part, width),
        early[3 * part:4 * part],
        up,
        middle[part * (ff // width):],
        tail[32:34],
        late[:3 * part].reshape(3, part, width),
        late[3 * part:],
        tail[:experts].T,
        tail[34:36],
        grad_e_in,
        grad_e_out,
    )


def solution(mesh):
    owners, shards = mesh.shape["expert"], mesh.shape["shard"]
    both = ("expert", "shard")
    return jax.shard_map(
        functools.partial(per_device, owners, shards),
        mesh=mesh,
        in_specs=(
            P(both, None, None), P(both, None, None), P(both, None, None), P(both), P(),
            P(None, "shard", None), P("shard", None), P("shard", None), P("shard", None), P(None, "shard"),
            P(None, "shard", None), P("shard", None), P("shard", None), P(None, "shard"),
            P("expert", None, None), P("expert", None, None),
        ),
        out_specs=(
            P(both, None, None), P(), P(both, None, None),
            P(None, "shard", None), P("shard", None), P("shard", None), P("shard", None), P(None, "shard"),
            P(None, "shard", None), P("shard", None), P("shard", None), P(None, "shard"),
            P("expert", None, None), P("expert", None, None),
        ),
        check_vma=False,
    )
```

```python
import functools

import jax
import jax.numpy as jnp
from jax import lax
from jax.experimental import pallas as pl
from jax.experimental.pallas import tpu as pltpu
from jax.sharding import PartitionSpec as P

HEADS = 8
CAP = 40
EPS = 1e-06
NEG = -1e30
LANES = 128
f32 = jnp.float32
bf16 = jnp.bfloat16
ANY = pl.BlockSpec(memory_space=pl.ANY)
VM = pl.BlockSpec(memory_space=pltpu.VMEM)
VMEM_BYTES = 58 << 20


def nn(a, b):
    return lax.dot_general(a, b, (((1,), (0,)), ((), ())), preferred_element_type=f32)


def nt(a, b):
    return lax.dot_general(a, b, (((1,), (1,)), ((), ())), preferred_element_type=f32)


def tn(a, b):
    return lax.dot_general(a, b, (((0,), (0,)), ((), ())), preferred_element_type=f32)


def sds(shape, dtype):
    return jax.ShapeDtypeStruct(shape, dtype)


def padded(seq):
    return -(-seq // 16) * 16


def norm(x):
    xc = x - jnp.mean(x, axis=-1, keepdims=True)
    rs = lax.rsqrt(jnp.mean(xc * xc, axis=-1, keepdims=True) + EPS)
    return xc * rs, rs


def norm_back(dyn, xn, rs, gain):
    dgain = jnp.sum(dyn * xn, axis=0, keepdims=True)
    dxn = dyn * gain
    dv = dxn - jnp.mean(dxn, axis=-1, keepdims=True)
    dv = (dv - xn * jnp.mean(dxn * xn, axis=-1, keepdims=True)) * rs
    return dv, dgain


def gelu_pair(z):
    a = jnp.abs(z)
    t = 1.0 / (1.0 + (0.3275911 * 0.7071067811865476) * a)
    e = jnp.exp(-0.5 * (z * z))
    q = t * (0.127414796 + t * (-0.142248368 + t * (0.7107068705 + t * (-0.7265760135 + t * 0.5307027145))))
    q = q * e
    phi = jnp.where(z >= 0.0, 1.0 - q, q)
    return z * phi, phi + z * (e * 0.3989422804014327)


class Split:
    def __init__(self, shards):
        self.pair = shards == 2
        self.shards = shards

    def gather(self, owns):
        if not self.pair:
            whole = [lax.all_gather(o, "shard", axis=1, tiled=True) for o in owns]
            return whole
        core = lax.axis_index("expert") % 2
        owners = lax.axis_size("expert")
        half = owns[0].shape[1] // 2
        send = jnp.concatenate([lax.dynamic_slice_in_dim(o, core * half, half, 1) for o in owns], axis=0)
        far = lax.ppermute(send, "shard", [(0, 1), (1, 0)])
        near = lax.ppermute(far, "expert", [(i, i ^ 1) for i in range(owners)])
        return list(owns) + [far, near]

    def count(self, owns):
        return owns + 2 if self.pair else owns

    def copies(self, refs, full, sems):
        out = []
        if not self.pair:
            at = 0
            for i, r in enumerate(refs):
                n = r.shape[0]
                out.append(pltpu.make_async_copy(r, full.at[at:at + n], sems.at[i]))
                at += n
            return out
        me = lax.axis_index("shard")
        core = lax.axis_index("expert") % 2
        rows = refs[0].shape[1]
        half = rows // 2
        at = 0
        for i, r in enumerate(refs[:-2]):
            n = r.shape[0]
            out.append(pltpu.make_async_copy(r, full.at[at:at + n, pl.ds(me * rows, rows), :], sems.at[i]))
            at += n
        base = (1 - me) * rows
        k = len(refs) - 2
        out.append(pltpu.make_async_copy(refs[k], full.at[:, pl.ds(base + core * half, half), :], sems.at[k]))
        out.append(pltpu.make_async_copy(refs[k + 1], full.at[:, pl.ds(base + (1 - core) * half, half), :], sems.at[k + 1]))
        return out


def start(copies):
    for c in copies:
        c.start()


def finish(copies):
    for c in copies:
        c.wait()


def call(body, outs, ins, scratch=(), specs=None, flops=0, nbytes=0, **kw):
    return pl.pallas_call(
        body,
        out_shape=outs,
        in_specs=specs or [VM] * len(ins),
        out_specs=[VM] * len(outs),
        scratch_shapes=list(scratch),
        compiler_params=pltpu.CompilerParams(vmem_limit_bytes=VMEM_BYTES),
        cost_estimate=pl.CostEstimate(flops=int(flops), bytes_accessed=int(nbytes), transcendentals=0),
        **kw,
    )(*ins)


def pad_store(ref, block, images, seq, step):
    ref[...] = jnp.zeros(ref.shape, ref.dtype)
    for i in range(images):
        ref[i * step:i * step + seq, :] = block(i).astype(ref.dtype)


def slot_start(expert, local, block):
    owner = jnp.floor((expert.astype(f32) + 0.5) * (1.0 / local))
    return owner * block + (expert.astype(f32) - owner * local) * CAP


def route_body(images, seq, local, block, r_ref, rt_ref, live_ref, cot_ref, dy_ref, dyd_ref, disp_ref, back_ref):
    rows = r_ref.shape[0]
    slots = disp_ref.shape[0]
    step = rows // images
    pad_store(dy_ref, lambda i: cot_ref[i], images, seq, step)
    dy_ref[...] = (dy_ref[...].astype(f32) * live_ref[...]).astype(bf16)
    lane = lax.broadcasted_iota(jnp.int32, (rows, LANES), 1)
    hit = (r_ref[:, 0:1] == lane) | (r_ref[:, 1:2] == lane)
    ti = lax.broadcasted_iota(jnp.int32, (rows, rows), 0)
    tj = lax.broadcasted_iota(jnp.int32, (rows, rows), 1)
    place = nn((ti > tj).astype(f32).astype(bf16), hit.astype(f32).astype(bf16))
    place = jnp.where(hit, place, -1.0).astype(bf16)
    off = lax.broadcasted_iota(jnp.int32, (LANES, slots), 1).astype(f32) - slot_start(
        lax.broadcasted_iota(jnp.int32, (LANES, slots), 0), local, block)
    spread = ((off >= 0) & (off < CAP)).astype(f32)
    within = jnp.sum(spread * off, axis=0, keepdims=True)
    within = jnp.where(jnp.sum(spread, axis=0, keepdims=True) > 0, within, -2.0)
    back_ref[...] = (nn(place, spread.astype(bf16)) == within).astype(f32).astype(bf16)
    sub = lax.broadcasted_iota(jnp.int32, (LANES, rows), 0)
    hit_t = (rt_ref[0:1, :] == sub) | (rt_ref[1:2, :] == sub)
    place_t = nn(hit_t.astype(f32).astype(bf16), (ti < tj).astype(f32).astype(bf16))
    place_t = jnp.where(hit_t, place_t, -1.0).astype(bf16)
    off = lax.broadcasted_iota(jnp.int32, (slots, LANES), 0).astype(f32) - slot_start(
        lax.broadcasted_iota(jnp.int32, (slots, LANES), 1), local, block)
    spread_t = ((off >= 0) & (off < CAP)).astype(f32)
    within_t = jnp.sum(spread_t * off, axis=1, keepdims=True)
    within_t = jnp.where(jnp.sum(spread_t, axis=1, keepdims=True) > 0, within_t, -2.0)
    disp_ref[...] = (nn(spread_t.astype(bf16), place_t) == within_t).astype(f32).astype(bf16)
    dyd_ref[...] = nn(disp_ref[...], dy_ref[...]).astype(bf16)


def attend_forward(step, seq, images, x, gain, wq, wo, qkv_ref, mix_ref):
    width = x.shape[1]
    head = width // HEADS
    scale = head ** -0.5
    xn, _ = norm(x)
    a = (xn * gain).astype(bf16)
    for c in range(3):
        qkv_ref[:, c * width:(c + 1) * width] = nn(a, wq[c][...]).astype(bf16)
    lane = lax.broadcasted_iota(jnp.int32, (1, LANES), 1)
    col = lax.broadcasted_iota(jnp.int32, (1, step), 1)
    per = LANES // head

    def image(i, _):
        at = pl.ds(pl.multiple_of(i * step, step), step)
        for hp in range(width // LANES):
            q = qkv_ref[at, hp * LANES:(hp + 1) * LANES]
            k = qkv_ref[at, width + hp * LANES:width + (hp + 1) * LANES]
            v = qkv_ref[at, 2 * width + hp * LANES:2 * width + (hp + 1) * LANES]
            got = None
            for h in range(per):
                mine = (lane >= h * head) & (lane < (h + 1) * head)
                qm = q * jnp.where(mine, scale, 0.0).astype(bf16)
                s = jnp.where(col < seq, nt(qm, k), NEG)
                e = jnp.exp(s - jnp.max(s, axis=-1, keepdims=True))
                p = (e * (1.0 / jnp.sum(e, axis=-1, keepdims=True))).astype(bf16)
                o = nn(p, v)
                got = o if got is None else jnp.where(mine, o, got)
            mix_ref[at, hp * LANES:(hp + 1) * LANES] = got.astype(bf16)
        return 0

    lax.fori_loop(0, images, image, 0)
    return x + nn(mix_ref[...], wo[...])


def attend_backward(step, seq, images, grad, x, gain, wq, wo, qkv_ref, mix_ref, dmix_ref, dqkv_ref, pack_ref, base,
                    tick=None):
    width = x.shape[1]
    head = width // HEADS
    scale = head ** -0.5
    shards = pack_ref.shape[0]
    part = width // shards
    low = grad.astype(bf16)
    dwo = tn(mix_ref[...], low).astype(bf16)
    for s in range(shards):
        pack_ref[s, base + 3 * part:base + 4 * part, :] = dwo[s * part:(s + 1) * part]
    dmix_ref[...] = nt(low, wo[...]).astype(bf16)
    lane = lax.broadcasted_iota(jnp.int32, (1, LANES), 1)
    key = lax.broadcasted_iota(jnp.int32, (step, 1), 0)
    per = LANES // head

    def image(i, _):
        at = pl.ds(pl.multiple_of(i * step, step), step)
        for hp in range(width // LANES):
            q = qkv_ref[at, hp * LANES:(hp + 1) * LANES]
            k = qkv_ref[at, width + hp * LANES:width + (hp + 1) * LANES]
            v = qkv_ref[at, 2 * width + hp * LANES:2 * width + (hp + 1) * LANES]
            do = dmix_ref[at, hp * LANES:(hp + 1) * LANES]
            dq = dk = dv = None
            for h in range(per):
                mine = (lane >= h * head) & (lane < (h + 1) * head)
                scaled = jnp.where(mine, scale, 0.0).astype(bf16)
                km = k * scaled
                s = jnp.where(key < seq, nt(km, q), NEG)
                e = jnp.exp(s - jnp.max(s, axis=0, keepdims=True))
                p = e * (1.0 / jnp.sum(e, axis=0, keepdims=True))
                dom = do * jnp.where(mine, 1.0, 0.0).astype(bf16)
                dp = nt(v, dom)
                ds = (p * (dp - jnp.sum(p * dp, axis=0, keepdims=True))).astype(bf16)
                hv = nn(p.astype(bf16), dom)
                hk = nn(ds, q * scaled)
                hq = tn(ds, km)
                dq, dk, dv = (hq, hk, hv) if dq is None else (dq + hq, dk + hk, dv + hv)
            dqkv_ref[at, hp * LANES:(hp + 1) * LANES] = dq.astype(bf16)
            dqkv_ref[at, width + hp * LANES:width + (hp + 1) * LANES] = dk.astype(bf16)
            dqkv_ref[at, 2 * width + hp * LANES:2 * width + (hp + 1) * LANES] = dv.astype(bf16)
        if tick is not None:
            tick(i)
        return 0

    lax.fori_loop(0, images, image, 0)
    xn, rs = norm(x)
    a = (xn * gain).astype(bf16)
    da = None
    for c in range(3):
        d = dqkv_ref[:, c * width:(c + 1) * width]
        dw = tn(a, d).astype(bf16)
        for s in range(shards):
            pack_ref[s, base + c * part:base + (c + 1) * part, :] = dw[s * part:(s + 1) * part]
        one = nt(d, wq[c][...])
        da = one if da is None else da + one
    return norm_back(da, xn, rs, gain)


def block1_body(split, images, seq, x_ref, gain_ref, *refs):
    n = split.count(2)
    pieces, (hidden_ref, qkv_ref, mix_ref, w, sems) = refs[:n], refs[n:]
    copies = split.copies(pieces, w, sems)
    start(copies)
    step = hidden_ref.shape[0] // images
    pad_store(hidden_ref, lambda i: x_ref[i], images, seq, step)
    finish(copies)
    hidden_ref[...] = attend_forward(
        step, seq, images, hidden_ref[...], gain_ref[0:1, :], [w.at[c] for c in range(3)], w.at[3], qkv_ref, mix_ref
    )


def mlp_body(split, hidden_ref, gain_ref, *refs):
    n = 2 * split.count(1)
    pieces, (out_ref, act_ref, slope_ref, w1, w2, sems) = refs[:n], refs[n:]
    half = n // 2
    copies = split.copies(pieces[:half], w1, sems.at[0]) + split.copies(pieces[half:], w2, sems.at[1])
    start(copies)
    hidden = hidden_ref[...]
    xn, _ = norm(hidden)
    u = (xn * gain_ref[1:2, :]).astype(bf16)
    out_ref[...] = hidden
    finish(copies)
    wide = act_ref.shape[2]
    for b in range(act_ref.shape[0]):
        at = slice(b * wide, (b + 1) * wide)
        act, slope = gelu_pair(nn(u, w1[0, :, at]))
        act = act.astype(bf16)
        act_ref[b] = act
        slope_ref[b] = slope.astype(bf16)
        out_ref[...] += nn(act, w2[0, at, :])


def router_probs(u, router, experts):
    lane = lax.broadcasted_iota(jnp.int32, (1, LANES), 1)
    logits = jnp.where(lane < experts, nn(u, router), NEG)
    e = jnp.exp(logits - jnp.max(logits, axis=-1, keepdims=True))
    return e * (1.0 / jnp.sum(e, axis=-1, keepdims=True))


def block2_body(split, images, seq, experts, x_ref, gain_ref, router_ref, disp_ref, live_ref, load_ref, *refs):
    n = split.count(2)
    pieces, (hidden_ref, qkv_ref, mix_ref, u_ref, probs_ref, sum_ref, ud_ref, w, sems) = refs[:n], refs[n:]
    copies = split.copies(pieces, w, sems)
    start(copies)
    finish(copies)
    step = hidden_ref.shape[0] // images
    hidden = attend_forward(
        step, seq, images, x_ref[...], gain_ref[2:3, :], [w.at[c] for c in range(3)], w.at[3], qkv_ref, mix_ref
    )
    hidden_ref[...] = hidden
    xn, _ = norm(hidden)
    u = (xn * gain_ref[3:4, :]).astype(bf16)
    u_ref[...] = u
    ud_ref[...] = nn(disp_ref[...], u).astype(bf16)
    probs = router_probs(u, router_ref[...], experts)
    probs_ref[...] = probs
    sums = jnp.sum(probs * live_ref[...], axis=0, keepdims=True)
    sum_ref[...] = jnp.concatenate([load_ref[...], sums, jnp.zeros((6, LANES), f32)], axis=0)


def split_rows(block, local):
    n, r, w = block.shape
    v = block.astype(f32)
    if r != local * CAP:
        v = v[:, :local * CAP]
    v = v.reshape(n, local, CAP, w)
    return [v[:, i].reshape(n * CAP, w) for i in range(local)]


def join_rows(parts, sources, block):
    local = len(parts)
    w = parts[0].shape[1]
    v = jnp.concatenate([p.reshape(sources, 1, CAP, w) for p in parts], axis=1).reshape(sources, local * CAP, w)
    if block != local * CAP:
        v = jnp.concatenate([v, jnp.zeros((sources, block - local * CAP, w), f32)], axis=1)
    return v


def gate_of(u, router, experts, e):
    lane = lax.broadcasted_iota(jnp.int32, (1, LANES), 1)
    return jnp.sum(jnp.where(lane == e, router_probs(u, router, experts), 0.0), axis=-1, keepdims=True)


def xor(a, b, bits):
    out = 0
    for i in range(bits):
        out = out + ((a // (1 << i) + b // (1 << i)) % 2) * (1 << i)
    return out


def expert_body(owners, shards, local, experts, group, uout_ref, dy_ref, router_ref, stat_ref, w1_hbm, w2_hbm,
                uin_ref, served_ref, duback_ref, dgback_ref, total_ref, dyx_ref,
                w1, w2, dusend, dgsend, statx, state, wsem, lsem, us, ur, ds_, dr, gs, gr, xs, xr, ss, sr, ys, yr):
    me, x = lax.axis_index("expert"), lax.axis_index("shard")
    bits = owners.bit_length() - 1
    barrier = pltpu.get_barrier_semaphore()

    def at(e, s):
        return dict(device_id=(e, s), device_id_type=pl.DeviceIdType.MESH)

    def each(lo, hi, f):
        lax.fori_loop(lo, hi, lambda k, c: (f(k), c)[1], 0)

    def peer(k):
        return xor(me, k, bits)

    each(1, owners, lambda k: pl.semaphore_signal(barrier, inc=1, **at(peer(k), x)))
    each(1, shards, lambda k: pl.semaphore_signal(barrier, inc=1, **at(me, (x + k) % shards)))
    weights = [pltpu.make_async_copy(w1_hbm, w1, wsem.at[0]), pltpu.make_async_copy(w2_hbm, w2, wsem.at[1])]
    start(weights)
    own = pltpu.make_async_copy(uout_ref.at[me], uin_ref.at[me], lsem.at[0])
    own.start()
    pl.semaphore_wait(barrier, owners - 1 + shards - 1)

    def send_u(k):
        return pltpu.make_async_remote_copy(uout_ref.at[peer(k)], uin_ref.at[me], us.at[k], ur.at[k], **at(peer(k), x))

    def send_du(k):
        return pltpu.make_async_remote_copy(dusend.at[peer(k)], duback_ref.at[me], ds_.at[k], dr.at[k], **at(peer(k), x))

    def send_dg(k):
        return pltpu.make_async_remote_copy(dgsend.at[peer(k)], dgback_ref.at[me], gs.at[k], gr.at[k], **at(peer(k), x))

    def send_statx(k):
        return pltpu.make_async_remote_copy(stat_ref, statx.at[k], xs.at[k], xr.at[k], **at(me, (x + k) % shards))

    def send_dyx(k):
        return pltpu.make_async_remote_copy(dy_ref, dyx_ref.at[k - 1], ys.at[k], yr.at[k], **at(me, (x + k) % shards))

    def send_state(k):
        return pltpu.make_async_remote_copy(state.at[0], state.at[k], ss.at[k], sr.at[k], **at(peer(k), x))

    each(1, shards, lambda k: send_statx(k).start())
    each(1, owners, lambda k: send_u(owners - k).start())
    each(1, shards, lambda k: send_dyx(k).start())
    each(1, shards, lambda k: send_statx(k).wait())
    sums = stat_ref[...]
    for k in range(1, shards):
        sums = sums + statx[k]
    state[0] = sums
    each(1, owners, lambda k: send_state(k).start())
    finish(weights)

    def work(g):
        base = xor(me // group, g, bits) * group
        rows = pl.ds(base, group)
        us_, dys = split_rows(uin_ref[rows], local), split_rows(dy_ref[rows], local)
        served, dus, prods = [], [], []
        for i in range(local):
            u, dy = us_[i].astype(bf16), dys[i]
            gate = gate_of(u, router_ref[...], experts, me * local + i)
            dsv = (gate * dy).astype(bf16)
            act, slope = gelu_pair(nn(u, w1[i]))
            out = nn(act.astype(bf16), w2[i])
            dz = (slope * nt(dsv, w2[i])).astype(bf16)
            dus.append(nt(dz, w1[i]))
            served.append(gate * out)
            prods.append(dy * out)
        block = uin_ref.shape[1]
        served_ref[rows] = join_rows(served, group, block).astype(bf16)
        dusend[rows] = join_rows(dus, group, block).astype(bf16)
        prod = join_rows(prods, group, block)
        ones = jnp.ones((8, prod.shape[2]), bf16)
        for j in range(group):
            hi = prod[j].astype(bf16)
            lo = (prod[j] - hi.astype(f32)).astype(bf16)
            dgsend[base + j, :, 0:block] = nt(ones, hi) + nt(ones, lo)

    def step(g):
        @pl.when(g == 0)
        def _():
            own.wait()

        for j in range(group):
            k = g * group + j
            if j == 0:
                pl.when(g > 0)(lambda k=k: send_u(k).wait_recv())
            else:
                send_u(k).wait_recv()
        work(g)
        for j in range(group):
            k = g * group + j
            if j == 0:
                @pl.when(g > 0)
                def _(k=k):
                    send_du(k).start()
                    send_dg(k).start()
            else:
                send_du(k).start()
                send_dg(k).start()

    each(0, owners // group, step)
    backs = [pltpu.make_async_copy(dusend.at[me], duback_ref.at[me], lsem.at[0]),
             pltpu.make_async_copy(dgsend.at[me], dgback_ref.at[me], lsem.at[1])]
    start(backs)
    each(1, owners, lambda k: send_state(k).wait())
    total = state[0]
    for k in range(1, owners):
        total = total + state[k]
    total_ref[...] = total
    each(1, owners, lambda k: send_u(k).wait_send())
    finish(backs)
    each(1, shards, lambda k: send_dyx(k).wait())
    each(1, owners, lambda k: send_du(k).wait())
    each(1, owners, lambda k: send_dg(k).wait())


def expert_grad_body(pieces, experts, *refs):
    us, dys = refs[:pieces], refs[pieces:2 * pieces]
    router_ref, w1_ref, w2_ref, g1_ref, g2_ref, urow, drow, stage, sems = refs[2 * pieces:]
    local = pl.num_programs(0)
    e = lax.axis_index("expert") * local + pl.program_id(0)

    @pl.when((pl.program_id(0) == 0) & (pl.program_id(1) == 0))
    def _():
        todo = [(us[i], urow, i) for i in range(pieces)] + [(dys[i], drow, i) for i in range(pieces)]
        copies = [pltpu.make_async_copy(r, stage.at[n % 2], sems.at[n % 2]) for n, (r, _, _) in enumerate(todo)]
        copies[0].start()
        for n, (_, to, i) in enumerate(todo):
            if n + 1 < len(todo):
                copies[n + 1].start()
            copies[n].wait()
            for j, v in enumerate(split_rows(stage[n % 2], urow.shape[1])):
                to[i, j] = v.astype(bf16)

    at = pl.program_id(0)
    for i in range(pieces):
        u = urow[i, at]
        dy = drow[i, at]
        gate = gate_of(u, router_ref[...], experts, e)
        ds = (gate * dy.astype(f32)).astype(bf16)
        act, slope = gelu_pair(nn(u, w1_ref[0]))
        dz = (slope * nt(ds, w2_ref[0])).astype(bf16)
        g1 = tn(u, dz)
        g2 = tn(act.astype(bf16), ds)
        if i == 0:
            g1_ref[0] = g1
            g2_ref[0] = g2
        else:
            g1_ref[0] += g1
            g2_ref[0] += g2


def split3(v):
    hi = v.astype(bf16)
    r = v - hi.astype(f32)
    mid = r.astype(bf16)
    lo = (r - mid.astype(f32)).astype(bf16)
    return hi, mid, lo


def router_backward(experts, dy_ref, u_ref, probs_ref, hidden_ref, gain_ref, router_ref, aux_ref, stat_ref, live_ref,
                    back_ref, ret_ref, dgate_ref, small_ref):
    slots = back_ref.shape[1]
    owners = dgate_ref.shape[0]
    local = experts // owners
    block = slots // owners
    off = lax.broadcasted_iota(jnp.int32, (slots, LANES), 0).astype(f32) - slot_start(
        lax.broadcasted_iota(jnp.int32, (slots, LANES), 1), local, block)
    oe = lax.broadcasted_iota(jnp.int32, (owners, LANES), 0).astype(f32)
    ee = lax.broadcasted_iota(jnp.int32, (owners, LANES), 1).astype(f32)
    pick = ((ee >= oe * local) & (ee < oe * local + local)).astype(f32).astype(bf16)
    column = 0.0
    for part in split3(dgate_ref[:, 0, :]):
        column = column + tn(part, pick)
    table = jnp.where((off >= 0) & (off < CAP), jnp.concatenate([column[0:block]] * owners, axis=0), 0.0)
    lane = lax.broadcasted_iota(jnp.int32, (1, LANES), 1)
    stat = stat_ref[0:1, :]
    total = jnp.sum(jnp.where(lane == LANES - 1, stat, 0.0), axis=-1, keepdims=True)
    fraction = jnp.where(lane < experts, stat, 0.0) / (2.0 * total)
    loss = experts * jnp.sum(fraction * stat_ref[1:2, :] / total, axis=-1, keepdims=True)
    small_ref[LANES + 2:LANES + 3, :] = jnp.broadcast_to(loss, (1, small_ref.shape[1]))
    dprobs = (aux_ref[0, 0] * experts * fraction / total) * live_ref[...]
    for part in split3(table):
        dprobs = dprobs + nn(back_ref[...], part)
    probs = probs_ref[...]
    dlog = (probs * (dprobs - jnp.sum(probs * dprobs, axis=-1, keepdims=True))).astype(bf16)
    small_ref[0:LANES, :] = tn(dlog, u_ref[...])
    du = nn(back_ref[...], ret_ref[...].reshape(slots, dy_ref.shape[1])) + nt(dlog, router_ref[...])
    xn, rs = norm(hidden_ref[...])
    dv, dg = norm_back(du, xn, rs, gain_ref[3:4, :])
    small_ref[LANES:LANES + 1, :] = dg
    grad = dy_ref[...].astype(f32) + dv
    return grad


def back2_body(split, images, seq, experts, dy_ref, u_ref, probs_ref, hidden_ref, x_ref, gain_ref, router_ref, aux_ref,
               stat_ref, live_ref, back_ref, ret_ref, dgate_ref, qkv_ref, mix_ref, *refs):
    n = split.count(2)
    pieces, (grad_ref, pack_ref, small_ref, w, sems, dmix_ref, dqkv_ref) = refs[:n], refs[n:]
    copies = split.copies(pieces, w, sems)
    start(copies)
    grad = router_backward(experts, dy_ref, u_ref, probs_ref, hidden_ref, gain_ref, router_ref, aux_ref, stat_ref, live_ref,
                           back_ref, ret_ref, dgate_ref, small_ref)
    grad_ref[...] = grad
    finish(copies)
    step = hidden_ref.shape[0] // images
    dv, dg = attend_backward(
        step, seq, images, grad, x_ref[...], gain_ref[2:3, :], [w.at[c] for c in range(3)], w.at[3],
        qkv_ref, mix_ref, dmix_ref, dqkv_ref, pack_ref, 0,
    )
    small_ref[LANES + 1:LANES + 2, :] = dg
    grad_ref[...] += dv


def mlp_back_body(split, grad_ref, hidden_ref, gain_ref, act_ref, slope_ref, *refs):
    n = 2 * split.count(1)
    pieces, (out_ref, pack_ref, dgain_ref, w1, w2, sems, du_ref) = refs[:n], refs[n:]
    half = n // 2
    copies = split.copies(pieces[:half], w1, sems.at[0]) + split.copies(pieces[half:], w2, sems.at[1])
    start(copies)
    xn, rs = norm(hidden_ref[...])
    gain = gain_ref[1:2, :]
    u = (xn * gain).astype(bf16)
    grad = grad_ref[...]
    low = grad.astype(bf16)
    finish(copies)
    width = grad.shape[1]
    blocks = act_ref.shape[0]
    ff = blocks * width
    shards = pack_ref.shape[0]
    part, fpart = width // shards, ff // shards
    base = part * blocks
    for b in range(blocks):
        at = slice(b * width, (b + 1) * width)
        dz = (slope_ref[b].astype(f32) * nt(low, w2[0, at, :])).astype(bf16)
        d = nt(dz, w1[0, :, at])
        if b == 0:
            du_ref[...] = d
        else:
            du_ref[...] += d
        gin = tn(u, dz).astype(bf16)
        for s in range(shards):
            pack_ref[s, b * part:(b + 1) * part, :] = gin[s * part:(s + 1) * part]
        gout = tn(act_ref[b], low).astype(bf16)
        per = min(width, fpart)
        for j in range(width // per):
            row = b * width + j * per
            s, off = row // fpart, row % fpart
            pack_ref[s, base + off:base + off + per, :] = gout[j * per:(j + 1) * per]
    dv, dg = norm_back(du_ref[...], xn, rs, gain)
    dgain_ref[...] = dg
    out_ref[...] = grad + dv


def back1_body(split, images, seq, experts, grad_ref, tok_ref, gain_ref, qkv_ref, mix_ref, small_ref, dg2_ref, *refs):
    n = split.count(2)
    pieces, (out_ref, pack_ref, w, sems, x_ref, dmix_ref, dqkv_ref) = refs[:n], refs[n:]
    copies = split.copies(pieces, w, sems)
    start(copies)
    step = x_ref.shape[0] // images
    pad_store(x_ref, lambda i: tok_ref[i], images, seq, step)
    finish(copies)
    width = x_ref.shape[1]
    dv, dg1 = attend_backward(
        step, seq, images, grad_ref[...], x_ref[...], gain_ref[0:1, :], [w.at[c] for c in range(3)], w.at[3],
        qkv_ref, mix_ref, dmix_ref, dqkv_ref, pack_ref, 0,
    )
    x_ref[...] = grad_ref[...] + dv
    for i in range(images):
        out_ref[i] = x_ref[i * step:i * step + seq, :]
    shards = pack_ref.shape[0]
    part = width // shards
    base = 4 * part
    gains = jnp.concatenate(
        [dg1, dg2_ref[...], small_ref[LANES + 1:LANES + 2, :], small_ref[LANES:LANES + 1, :], jnp.zeros((28, width), f32)], axis=0
    )
    both = jnp.concatenate([small_ref[0:32, :], gains], axis=0).astype(bf16)
    for s in range(shards):
        one = both[:, s * part:(s + 1) * part]
        pack_ref[s, base:base + 64, :] = jnp.concatenate([one, jnp.zeros((64, width - part), bf16)], axis=1)


def output_body(images, seq, hidden_ref, back_ref, ret_ref, live_ref, out_ref, tmp_ref):
    step = hidden_ref.shape[0] // images
    tmp_ref[...] = (hidden_ref[...] + nn(back_ref[...], ret_ref[...])) * live_ref[...]
    for i in range(images):
        out_ref[i] = tmp_ref[i * step:i * step + seq, :].astype(bf16)


def backward_body(split, images, seq, experts, local, owners, plan, *refs):
    (gain_ref, router_ref, aux_ref, stat_ref, live_ref, back_ref, dgate_ref, tok_ref, dy_h, u_h, probs_h, du_h,
     hid2_h, x2_h, hid1_h, qkv2_h, mix2_h, qkv1_h, mix1_h, act_h, slope_h, served_h, uin_h, dyin_h, dyx_h, we1_h, we2_h,
     *refs) = refs
    na, nm = split.count(2), split.count(1)
    two, refs = refs[:na], refs[na:]
    up, refs = refs[:nm], refs[nm:]
    down, refs = refs[:nm], refs[nm:]
    one, refs = refs[:na], refs[na:]
    (out_ref, gtok_ref, fin, smout_ref, small_ref, ge1_h, ge2_h, sback_h, ux_h,
     hid2, xbuf, grad_ref, dubuf, qkv, mix, dmix, dqkv, watt, w1, w2, big, stage, pack, crecv, xa, yb, ya, xb, zr,
     sm, smr,
     lsem, wsem, vs, vr, xs, xr, gs, gr, ms, mr, esem, osem, tsem) = refs
    me, x = lax.axis_index("expert"), lax.axis_index("shard")
    bits = owners.bit_length() - 1
    bit = [(me // (1 << i)) % 2 for i in range(bits)]
    hop = [me + (1 - 2 * bit[i]) * (1 << i) for i in range(bits)]
    rows, width = grad_ref.shape
    step = rows // images
    blocks = act_h.shape[0]
    whole = pack.shape[2]
    part = width // 2

    def to(e, s):
        return dict(device_id=(e, s), device_id_type=pl.DeviceIdType.MESH)

    def each(lo, hi, f):
        lax.fori_loop(lo, hi, lambda k, c: (f(k), c)[1], 0)

    barrier = pltpu.get_barrier_semaphore()
    each(1, owners, lambda k: pl.semaphore_signal(barrier, inc=1, **to(xor(me, k, bits), x)))
    pl.semaphore_signal(barrier, inc=1, **to(me, 1 - x))

    def load(src, dst, i):
        return pltpu.make_async_copy(src, dst, lsem.at[i])

    count = 4 + 2 * blocks
    dy_ref, u_ref, probs_ref, du_ref = dmix, dqkv.at[:, 0:width], dubuf.at[:, 0:LANES], stage.at[0]
    start_in = [load(hid2_h, hid2, 0), load(du_h, du_ref, count), load(dy_h, dy_ref, count + 1), load(u_h, u_ref, count + 2),
                load(probs_h, probs_ref, count + 3)]
    start(start_in)
    first = [load(x2_h, xbuf, 1), load(qkv2_h, qkv, 2), load(mix2_h, mix, 3)]
    w_two = split.copies(two, watt, wsem.at[0])
    w_mlp = split.copies(up, w1, wsem.at[1]) + split.copies(down, w2, wsem.at[2])
    gelus = [load(act_h.at[b], big.at[b, 0:rows], 4 + b) for b in range(blocks)]
    gelus += [load(slope_h.at[b], big.at[b, big.shape[1] // 2:big.shape[1] // 2 + rows], 4 + blocks + b) for b in range(blocks)]
    start(first + w_two + w_mlp + gelus)
    own = pltpu.make_async_copy(served_h.at[me], sback_h.at[me], tsem.at[0])
    own.start()
    pl.semaphore_wait(barrier, owners)

    def send_served(k):
        p = xor(me, k, bits)
        return pltpu.make_async_remote_copy(served_h.at[p], sback_h.at[me], vs.at[k], vr.at[k], **to(p, x))

    def send_rows():
        return pltpu.make_async_remote_copy(uin_h, ux_h, xs.at[0], xr.at[0], **to(me, 1 - x))

    send_rows().start()
    each(1, owners, lambda k: send_served(owners - k).start())

    def add(ref, at, other):
        ref[at] = (ref[at].astype(f32) + other.astype(f32)).astype(bf16)

    def stages(n):
        def copy(src, dst, i, peer):
            return pltpu.make_async_remote_copy(src, dst, gs.at[n, i], gr.at[n, i], **peer)

        q = whole // 4
        o = bit[0] * (whole // 2)
        out = []
        out.append((
            lambda: [copy(pack.at[n, :, pl.ds((1 - bit[0]) * (whole // 2), whole // 2)], crecv.at[n], 0, to(hop[0], x))],
            lambda: add(pack, (n, slice(None), pl.ds(o, whole // 2)), crecv[n])))
        e = q // 2
        b1 = bit[1] * e

        def after1():
            add(pack, (n, x, pl.ds(o, q)), xa[n])
            add(pack, (n, slice(None), pl.ds(o + q + b1, e)), yb[n])

        out.append((
            lambda: [copy(pack.at[n, 1 - x, pl.ds(o, q)], xa.at[n], 1, to(me, 1 - x)),
                     copy(pack.at[n, :, pl.ds(o + q + e - b1, e)], yb.at[n], 2, to(hop[1], x))],
            after1))

        def after2():
            add(pack, (n, x, pl.ds(o + b1, e)), ya[n])
            add(pack, (n, x, pl.ds(o + q + b1, e)), xb[n])

        out.append((
            lambda: [copy(pack.at[n, x, pl.ds(o + e - b1, e)], ya.at[n], 3, to(hop[1], x)),
                     copy(pack.at[n, 1 - x, pl.ds(o + q + b1, e)], xb.at[n], 4, to(me, 1 - x))],
            after2))
        at, size, sem, starts = o + b1, e, 5, [(o, q), (o + b1, e)]
        zoff = 0
        for i in range(2, bits):
            size //= 2
            keep, give = at + bit[i] * size, at + (1 - bit[i]) * size

            def go(give=give, size=size, sem=sem, i=i, zoff=zoff):
                return [copy(pack.at[n, x, pl.ds(give + j * q, size)], zr.at[n, j, pl.ds(zoff, size)], sem + j, to(hop[i], x))
                        for j in range(2)]

            def after(keep=keep, size=size, zoff=zoff):
                for j in range(2):
                    add(pack, (n, x, pl.ds(keep + j * q, size)), zr[n, j, zoff:zoff + size])

            out.append((go, after))
            at, sem, zoff = keep, sem + 2, zoff + size
            starts.append((at, size))
        last_go, last_after = out[-1]

        def after_last(at=at, size=size):
            last_after()
            for j in range(2):
                fin[n, pl.ds(at + j * q, size)] = pack[n, x, pl.ds(at + j * q, size)]

        out[-1] = (last_go, after_last)
        for i in reversed(range(1, bits)):
            at, size = starts[i]

            def go(at=at, size=size, sem=sem, i=i):
                return [copy(fin.at[n, pl.ds(at + j * q, size)], fin.at[n, pl.ds(at + j * q, size)], sem + j, to(hop[i], x))
                        for j in range(2)]

            out.append((go, lambda: None))
            sem += 2
        out.append((lambda sem=sem: [copy(fin.at[n, pl.ds(o, whole // 2)], fin.at[n, pl.ds(o, whole // 2)], sem, to(hop[0], x))],
                    lambda: None))
        return out

    groups = [stages(n) for n in range(4)]

    def small_stage(i):
        if i == 0:
            src, dst, peer = sm, smr.at[0], to(hop[0], x)
        elif i == 1:
            src, dst, peer = sm.at[1 - x], smr.at[1, 0], to(me, 1 - x)
        else:
            src, dst, peer = sm.at[x], smr.at[i, 0], to(hop[i - 1], x)
        return pltpu.make_async_remote_copy(src, dst, ms.at[i], mr.at[i], **peer)

    def small_after(i):
        if i == 0:
            sm[...] += smr[0]
        else:
            sm[x] += smr[i, 0]

    def tick(n, k):
        table = groups[n]
        if k > 0:
            finish(table[k - 1][0]())
            table[k - 1][1]()
            if n == 3 and k - 1 < bits + 1:
                small_stage(k - 1).wait()
                small_after(k - 1)
        if k < len(table):
            start(table[k][0]())
            if n == 3 and k < bits + 1:
                small_stage(k).start()

    done = [0] * 4

    def at_point(name, index=None):
        for i, n in plan.get(name, ()):
            if index is None:
                tick(n, done[n])
            else:
                pl.when(index == i)(functools.partial(tick, n, done[n]))
            done[n] += 1

    finish(start_in)
    grad_ref[...] = router_backward(experts, dy_ref, u_ref, probs_ref, hid2, gain_ref, router_ref, aux_ref, stat_ref, live_ref,
                                    back_ref, du_ref, dgate_ref, small_ref)
    finish(first + w_two)
    dv, dg = attend_backward(
        step, seq, images, grad_ref[...], xbuf[...], gain_ref[2:3, :], [watt.at[c] for c in range(3)], watt.at[3],
        qkv, mix, dmix, dqkv, pack.at[0], 0,
    )
    small_ref[LANES + 1:LANES + 2, :] = dg
    grad_ref[...] += dv
    at_point("two")
    second = [load(hid1_h, xbuf, 1), load(qkv1_h, qkv, 2), load(mix1_h, mix, 3)]
    w_one = split.copies(one, watt, wsem.at[0])
    start(second + w_one)

    finish(gelus + w_mlp)
    low = grad_ref[...].astype(bf16)
    fpart = blocks * width // 2
    for b in range(blocks):
        s, off = b * width // fpart, b * width % fpart
        pack[1, s, off:off + width, :] = tn(big[b, 0:rows], low).astype(bf16)
    at_point("out")
    finish(second[:1])
    xn, rs = norm(xbuf[...])
    gain = gain_ref[1:2, :]
    u = (xn * gain).astype(bf16)
    half = big.shape[1] // 2
    for b in range(blocks):
        cols = slice(b * width, (b + 1) * width)
        dz = (big[b, half:half + rows].astype(f32) * nt(low, w2[0, cols, :])).astype(bf16)
        d = nt(dz, w1[0, :, cols])
        if b == 0:
            dubuf[...] = d
        else:
            dubuf[...] += d
        gin = tn(u, dz).astype(bf16)
        for s in range(2):
            pack[2, s, b * part:(b + 1) * part, :] = gin[s * part:(s + 1) * part]
        at_point("in%d" % b)
    dv, dg = norm_back(dubuf[...], xn, rs, gain)
    small_ref[LANES + 3:LANES + 4, :] = dg
    grad_ref[...] += dv
    at_point("mlp")

    pad_store(xbuf, lambda i: tok_ref[i], images, seq, step)
    finish(second[1:] + w_one)
    dv, dg = attend_backward(
        step, seq, images, grad_ref[...], xbuf[...], gain_ref[0:1, :], [watt.at[c] for c in range(3)], watt.at[3],
        qkv, mix, dmix, dqkv, pack.at[3], 0, tick=lambda i: at_point("image", i),
    )
    sm[...] = jnp.zeros(sm.shape, f32)
    for s in range(2):
        cols = slice(s * part, (s + 1) * part)
        sm[s, 0:experts] = small_ref[0:experts, cols]
        sm[s, experts:experts + 1] = dg[:, cols]
        sm[s, experts + 1:experts + 2] = small_ref[LANES + 3:LANES + 4, cols]
        sm[s, experts + 2:experts + 3] = small_ref[LANES + 1:LANES + 2, cols]
        sm[s, experts + 3:experts + 4] = small_ref[LANES:LANES + 1, cols]
    at_point("one")
    grad_ref[...] += dv
    for i in range(images):
        gtok_ref[i] = grad_ref[i * step:i * step + seq, :]

    own.wait()
    each(1, owners, lambda k: send_served(k).wait())
    send_rows().wait()
    at_point("rows")

    todo = [(uin_h, 0, 0), (ux_h, 0, 1), (dyin_h, 1, 0), (dyx_h.at[0], 1, 1)]
    moves = [pltpu.make_async_copy(r, stage.at[i % 2], esem.at[i % 2]) for i, (r, _, _) in enumerate(todo)]

    def lane(i):
        return pl.ds(pl.multiple_of(i * width, width), width)

    def chunk(i):
        e, f = i // blocks, i % blocks
        slot = i % 2
        col = pl.ds(pl.multiple_of(f * width, width), width)
        return [pltpu.make_async_copy(we1_h.at[e, :, col], w1.at[0, :, lane(slot)], esem.at[2 + slot]),
                pltpu.make_async_copy(we2_h.at[e, col, :], w2.at[0, lane(slot), :], esem.at[4 + slot])]

    def result(i):
        e, f = i // blocks, i % blocks
        slot = i % 2
        col = pl.ds(pl.multiple_of(f * width, width), width)
        return [pltpu.make_async_copy(w1.at[0, :, lane(2 + slot)], ge1_h.at[e, :, col], osem.at[slot]),
                pltpu.make_async_copy(w2.at[0, lane(2 + slot), :], ge2_h.at[e, col, :], osem.at[2 + slot])]

    moves[0].start()
    start(chunk(0))
    for i, (_, kind, piece) in enumerate(todo):
        if i + 1 < len(todo):
            moves[i + 1].start()
        moves[i].wait()
        for e, v in enumerate(split_rows(stage[i % 2], local)):
            if kind == 1:
                u = big[e, piece * half:(piece + 1) * half]
                v = v * gate_of(u, router_ref[...], experts, me * local + e)
            big[kind * local + e, piece * half:(piece + 1) * half] = v.astype(bf16)
    back = pltpu.make_async_copy(sback_h, stage.at[0], tsem.at[0])
    back.start()
    back.wait()
    grad_ref[...] = (hid2[...] + nn(back_ref[...], stage[0].reshape(back_ref.shape[1], width))) * live_ref[...]
    for i in range(images):
        out_ref[i] = grad_ref[i * step:i * step + seq, :].astype(bf16)
    at_point("output")
    count = local * blocks
    acc1, acc2 = xbuf.at[0:width], dubuf.at[0:width]

    def expert(i, c):
        slot = i % 2
        pl.when(i + 1 < count)(lambda: start(chunk(i + 1)))
        finish(chunk(i))
        e = i // blocks
        for p in range(2):
            u = big[e, p * half:(p + 1) * half]
            dsv = big[local + e, p * half:(p + 1) * half]
            act, slope = gelu_pair(nn(u, w1[0, :, lane(slot)]))
            dz = (slope * nt(dsv, w2[0, lane(slot), :])).astype(bf16)
            g1, g2 = tn(u, dz), tn(act.astype(bf16), dsv)
            if p == 0:
                acc1[...] = g1
                acc2[...] = g2
                at_point("early", i)
            else:
                pl.when(i >= 2)(lambda: finish(result(i - 2)))
                w1[0, :, lane(2 + slot)] = (acc1[...] + g1).astype(bf16)
                w2[0, lane(2 + slot), :] = (acc2[...] + g2).astype(bf16)
        start(result(i))
        at_point("late", i)
        return c

    lax.fori_loop(0, count, expert, 0)
    at_point("end")
    for i in range(max(0, count - 2), count):
        finish(result(i))
    smout_ref[...] = sm[x]


def swap(owners, bit):
    return [(i, i ^ (1 << bit)) for i in range(owners)]


def reduce_all(g, owners, shards):
    me = lax.axis_index("expert")
    bits = owners.bit_length() - 1

    def add(a, b):
        return (a.astype(f32) + b.astype(f32)).astype(bf16)

    def fold(v, bit, axis):
        own = (me >> bit) & 1
        half = v.shape[axis] // 2
        keep = lax.dynamic_slice_in_dim(v, own * half, half, axis)
        send = lax.dynamic_slice_in_dim(v, (1 - own) * half, half, axis)
        return add(keep, lax.ppermute(send, "expert", swap(owners, bit)))

    v = fold(g, 0, 1)
    if shards == 2:
        x = lax.axis_index("shard")
        keep = lax.dynamic_index_in_dim(v, x, 0, keepdims=False)
        send = lax.dynamic_index_in_dim(v, 1 - x, 0, keepdims=False)
        v = add(keep, lax.ppermute(send, "shard", [(0, 1), (1, 0)]))
    else:
        v = lax.psum_scatter(v, "shard", scatter_dimension=0, tiled=True)[0]
    for bit in range(1, bits):
        v = fold(v, bit, 0)
    for bit in reversed(range(bits)):
        own = (me >> bit) & 1
        other = lax.ppermute(v, "expert", swap(owners, bit))
        v = jnp.where(own == 0, jnp.concatenate([v, other]), jnp.concatenate([other, v]))
    return v


def per_device(
    owners, shards, tokens, cotangent, routes, counts, aux_weight, attn_qkv1, attn_out1, mlp_in, mlp_out, gains1,
    attn_qkv2, attn_out2, router, gains2, expert_in, expert_out,
):
    images, seq, width = tokens.shape
    step = padded(seq)
    rows = images * step
    experts = router.shape[1]
    local = expert_in.shape[0]
    ff = mlp_in.shape[1]
    block_rows = -(-local * CAP // 16) * 16
    slots = owners * block_rows
    split = Split(shards)
    expert_swap = functools.partial(lax.all_to_all, axis_name="expert", split_axis=0, concat_axis=0, tiled=True)

    within = jnp.arange(step, dtype=jnp.int32) < seq
    live = ((jnp.arange(images, dtype=jnp.int32)[:, None] < counts[0]) & within[None, :]).reshape(rows)
    live = live.astype(f32)
    routes_pad = jnp.pad(routes, ((0, 0), (0, step - seq), (0, 0)), constant_values=-1).reshape(rows, 2)
    lanes = jnp.arange(LANES, dtype=jnp.int32)
    loads = jnp.sum(((routes_pad[:, :, None] == lanes) & (live[:, None, None] > 0)).astype(f32), axis=(0, 1))
    loads = jnp.where(lanes == LANES - 1, jnp.sum(live), loads)
    live_col = live[:, None]

    w_one = split.gather([attn_qkv1, attn_out1[None]])
    w_up = split.gather([mlp_in[None]])
    w_down = split.gather([mlp_out[None]])
    w_two = split.gather([attn_qkv2, attn_out2[None]])
    gains = jnp.concatenate([gains1, gains2])
    if shards == 2:
        x = lax.axis_index("shard")
        other = lax.ppermute(gains, "shard", [(0, 1), (1, 0)])
        gains = jnp.where(x == 0, jnp.concatenate([gains, other], 1), jnp.concatenate([other, gains], 1))
        other = lax.ppermute(router, "shard", [(0, 1), (1, 0)])
        router_full = jnp.where(x == 0, jnp.concatenate([router, other]), jnp.concatenate([other, router]))
    else:
        gains = lax.all_gather(gains, "shard", axis=1, tiled=True)
        router_full = lax.all_gather(router, "shard", axis=0, tiled=True)
    gains = gains.astype(f32)
    router_full = jnp.pad(router_full, ((0, 0), (0, LANES - experts)))

    dy, dy_out, disp, back = call(
        functools.partial(route_body, images, seq, local, block_rows),
        [sds((rows, width), bf16), sds((slots, width), bf16), sds((slots, rows), bf16), sds((rows, slots), bf16)],
        [routes_pad, routes_pad.T, live_col, cotangent], flops=2e9, nbytes=6e6,
    )
    block = (owners, block_rows, width)
    dy_in = expert_swap(dy_out.reshape(block))

    sem = pltpu.SemaphoreType.DMA
    attn_scratch = [pltpu.VMEM((4, width, width), bf16), sem((4,))]
    mlp_scratch = [pltpu.VMEM((1, width, ff), bf16), pltpu.VMEM((1, ff, width), bf16), sem((2, 4))]

    def specs(n, ins):
        return [VM] * n + [ANY] * (len(ins) - n)

    ins = [tokens, gains] + w_one
    hidden, qkv_one, mix_one = call(
        functools.partial(block1_body, split, images, seq),
        [sds((rows, width), f32), sds((rows, 3 * width), bf16), sds((rows, width), bf16)],
        ins, attn_scratch, specs(2, ins), flops=4e9, nbytes=8e6,
    )
    ins = [hidden, gains] + w_up + w_down
    block_out, act, slope = call(
        functools.partial(mlp_body, split),
        [sds((rows, width), f32)] + [sds((ff // width, rows, width), bf16)] * 2,
        ins, mlp_scratch, specs(2, ins), flops=6e9, nbytes=12e6,
    )
    ins = [block_out, gains, router_full, disp, live_col, loads[None, :]] + w_two
    hidden_two, qkv_two, mix_two, u_two, probs, stat, u_out = call(
        functools.partial(block2_body, split, images, seq, experts),
        [sds((rows, width), f32), sds((rows, 3 * width), bf16), sds((rows, width), bf16), sds((rows, width), bf16),
         sds((rows, LANES), f32), sds((8, LANES), f32), sds((slots, width), bf16)],
        ins, attn_scratch, specs(6, ins), flops=5e9, nbytes=10e6,
    )

    group = min(4, owners)
    u_in, served, du_back, dgate_back, stat, dy_far = pl.pallas_call(
        functools.partial(expert_body, owners, shards, local, experts, group),
        out_shape=[sds(block, bf16), sds(block, bf16), sds(block, bf16), sds((owners, 8, LANES), f32), sds((8, LANES), f32),
                   sds((shards - 1,) + block, bf16)],
        in_specs=[VM] * 4 + [ANY] * 2,
        out_specs=[VM] * 6,
        scratch_shapes=[
            pltpu.VMEM((local, width, ff), bf16), pltpu.VMEM((local, ff, width), bf16), pltpu.VMEM(block, bf16),
            pltpu.VMEM((owners, 8, LANES), f32), pltpu.VMEM((shards, 8, LANES), f32), pltpu.VMEM((owners, 8, LANES), f32),
            sem((2,)), sem((2,)),
        ] + [sem((owners,))] * 6 + [sem((shards,))] * 2 + [sem((owners,))] * 2 + [sem((shards,))] * 2,
        compiler_params=pltpu.CompilerParams(vmem_limit_bytes=VMEM_BYTES, collective_id=0, has_side_effects=True),
        cost_estimate=pl.CostEstimate(flops=int(11e9), bytes_accessed=int(15e6), transcendentals=0),
    )(u_out.reshape(block), dy_in, router_full, stat, expert_in, expert_out)
    parts_of = (gains, router_full, aux_weight.reshape(1, 1), stat, live_col, back, dgate_back, tokens, dy, u_two, probs, du_back)
    if shards == 2:
        return fused_backward(split, experts, tokens, parts_of, hidden_two, block_out, hidden, qkv_two, mix_two, qkv_one, mix_one,
                              act, slope, served, u_in, dy_in, dy_far, expert_in, expert_out, w_two, w_up, w_down, w_one)
    served_back = expert_swap(served).reshape(slots, width)

    if shards == 2:
        us = [u_in, lax.ppermute(u_in, "shard", [(0, 1), (1, 0)])]
    else:
        far = lax.all_gather(u_in, "shard")
        us = [u_in] + [lax.dynamic_index_in_dim(far, (lax.axis_index("shard") + shards - k) % shards, 0, False) for k in range(1, shards)]
    dys = [dy_in] + [dy_far[k] for k in range(shards - 1)]
    parts = 4
    wide = ff // parts
    up_spec = pl.BlockSpec((1, width, wide), lambda e, f: (e, 0, f))
    down_spec = pl.BlockSpec((1, wide, width), lambda e, f: (e, f, 0))
    grad_e_in, grad_e_out = pl.pallas_call(
        functools.partial(expert_grad_body, shards, experts),
        grid=(local, parts),
        out_shape=[sds((local, width, ff), f32), sds((local, ff, width), f32)],
        in_specs=[ANY] * (2 * shards) + [VM, up_spec, down_spec],
        out_specs=[up_spec, down_spec],
        scratch_shapes=[pltpu.VMEM((shards, local, owners * CAP, width), bf16)] * 2 + [pltpu.VMEM((2,) + block, bf16), sem((2,))],
        compiler_params=pltpu.CompilerParams(vmem_limit_bytes=VMEM_BYTES),
        cost_estimate=pl.CostEstimate(flops=int(27e9), bytes_accessed=int(40e6), transcendentals=0),
    )(*us, *dys, router_full, expert_in, expert_out)

    part = width // shards
    back_scratch = [pltpu.VMEM((rows, width), bf16), pltpu.VMEM((rows, 3 * width), bf16)]
    ins = [dy, u_two, probs, hidden_two, block_out, gains, router_full, aux_weight.reshape(1, 1), stat, live_col, back,
           du_back.reshape(slots, width), dgate_back,
           qkv_two, mix_two]
    n = len(ins)
    ins = ins + w_two
    grad_block, pack_two, small = call(
        functools.partial(back2_body, split, images, seq, experts),
        [sds((rows, width), f32), sds((shards, 4 * part, width), bf16), sds((LANES + 8, width), f32)],
        ins, attn_scratch + back_scratch, specs(n, ins), flops=9e9, nbytes=16e6,
    )
    balance_loss = small[LANES + 2, 0]
    late = reduce_all(pack_two, owners, shards)
    ins = [grad_block, hidden, gains, act, slope] + w_up + w_down
    grad_hidden, pack_mlp, dg_two = call(
        functools.partial(mlp_back_body, split),
        [sds((rows, width), f32), sds((shards, part * (ff // width) + ff // shards, width), bf16), sds((1, width), f32)],
        ins, mlp_scratch + [pltpu.VMEM((rows, width), f32)], specs(5, ins), flops=11e9, nbytes=16e6,
    )
    middle = reduce_all(pack_mlp, owners, shards)
    ins = [grad_hidden, tokens, gains, qkv_one, mix_one, small, dg_two] + w_one
    grad_tokens, pack_one = call(
        functools.partial(back1_body, split, images, seq, experts),
        [sds((images, seq, width), f32), sds((shards, 4 * part + 64, width), bf16)],
        ins, attn_scratch + [pltpu.VMEM((rows, width), f32)] + back_scratch, specs(7, ins), flops=9e9, nbytes=14e6,
    )
    early = reduce_all(pack_one, owners, shards)
    (output,) = call(
        functools.partial(output_body, images, seq), [sds((images, seq, width), bf16)],
        [hidden_two, back, served_back, live_col], [pltpu.VMEM((rows, width), f32)], flops=1e9, nbytes=5e6,
    )

    late, middle, early = late.astype(f32), middle.astype(f32), early.astype(f32)
    up = middle[:part * (ff // width)].reshape(ff // width, part, width).transpose(1, 0, 2).reshape(part, ff)
    tail = early[4 * part:, :part]
    return (
        output,
        balance_loss,
        grad_tokens,
        early[:3 * part].reshape(3, part, width),
        early[3 * part:4 * part],
        up,
        middle[part * (ff // width):],
        tail[32:34],
        late[:3 * part].reshape(3, part, width),
        late[3 * part:],
        tail[:experts].T,
        tail[34:36],
        grad_e_in,
        grad_e_out,
    )


PLAN = {
    "two": [(0, 0)],
    "out": [(0, 0), (0, 1)],
    "in0": [(0, 1)],
    "in2": [(0, 0)],
    "mlp": [(0, 2), (0, 1)],
    "image": [(0, 2), (0, 0), (1, 1), (1, 2), (2, 0), (2, 1)],
    "one": [(0, 3), (0, 0)],
    "rows": [(0, 3), (0, 2), (0, 1)],
    "output": [(0, 3), (0, 2), (0, 0)],
    "early": [(0, 1), (1, 3), (1, 1), (2, 3), (2, 1), (3, 3), (4, 3), (5, 3)],
    "late": [(0, 2), (0, 0), (1, 2), (1, 0), (2, 2), (2, 0), (3, 1), (3, 2), (4, 2)],
    "end": [],
}


def fused_backward(split, experts, tokens, parts_of, hidden_two, block_out, hidden, qkv_two, mix_two, qkv_one, mix_one,
                   act, slope, served, u_in, dy_in, dy_far, expert_in, expert_out, w_two, w_up, w_down, w_one):
    images, seq, width = tokens.shape
    rows = hidden.shape[0]
    local, _, ff = expert_in.shape
    block = served.shape
    owners = block[0]
    bits = owners.bit_length() - 1
    whole = 2 * width
    part = width // 2
    blocks = ff // width
    stages = 3 + (bits - 2) + (bits - 1) + 1
    plan = {k: list(v) for k, v in PLAN.items()}
    left = [stages + 1] * 4
    for k in plan:
        for item in list(plan[k]):
            if left[item[1]] > 0:
                left[item[1]] -= 1
            else:
                plan[k].remove(item)
    plan["end"] = plan["end"] + [(0, n) for i in range(max(left)) for n in range(4) if left[n] > i]
    small_rows = -(-(experts + 4) // 8) * 8
    sem = pltpu.SemaphoreType.DMA
    ins = list(parts_of) + [hidden_two, block_out, hidden, qkv_two, mix_two, qkv_one, mix_one, act, slope, served, u_in, dy_in,
                            dy_far, expert_in, expert_out] + w_two + w_up + w_down + w_one
    vmem = 8
    big_rows = 2 * owners * CAP
    nsem = 5 + 4 * (bits - 2) + 3
    V = pltpu.VMEM
    outs = pl.pallas_call(
        functools.partial(backward_body, split, images, seq, experts, local, owners, plan),
        out_shape=[
            sds((images, seq, width), bf16), sds((images, seq, width), f32), sds((4, whole, width), bf16),
            sds((small_rows, part), f32), sds((LANES + 8, width), f32), sds(expert_in.shape, bf16), sds(expert_out.shape, bf16),
            sds(block, bf16), sds(block, bf16),
        ],
        in_specs=[VM] * vmem + [ANY] * (len(ins) - vmem),
        out_specs=[VM] * 5 + [ANY] * 4,
        scratch_shapes=[
            V((rows, width), f32), V((rows, width), f32), V((rows, width), f32), V((rows, width), f32),
            V((rows, 3 * width), bf16), V((rows, width), bf16), V((rows, width), bf16), V((rows, 3 * width), bf16),
            V((4, width, width), bf16), V((1, width, ff), bf16), V((1, ff, width), bf16), V((blocks, big_rows, width), bf16),
            V((2,) + block, bf16),
            V((4, 2, whole, width), bf16), V((4, 2, whole // 2, width), bf16), V((4, whole // 4, width), bf16),
            V((4, 2, whole // 8, width), bf16), V((4, whole // 8, width), bf16), V((4, whole // 8, width), bf16),
            V((4, 2, whole // 8 - whole // (1 << (bits + 1)), width), bf16),
            V((2, small_rows, part), f32), V((bits + 1, 2, small_rows, part), f32),
            sem((8 + 2 * blocks,)), sem((3, 4)), sem((owners,)), sem((owners,)), sem((1,)), sem((1,)),
            sem((4, nsem)), sem((4, nsem)), sem((bits + 1,)), sem((bits + 1,)), sem((6,)), sem((4,)), sem((1,)),
        ],
        compiler_params=pltpu.CompilerParams(vmem_limit_bytes=63 << 20, collective_id=1, has_side_effects=True),
        cost_estimate=pl.CostEstimate(flops=int(60e9), bytes_accessed=int(80e6), transcendentals=0),
    )(*ins)
    output, grad_tokens, fin, tail, small, grad_e_in, grad_e_out = outs[:7]
    return (
        output,
        small[LANES + 2, 0],
        grad_tokens,
        fin[3, :3 * part].astype(f32).reshape(3, part, width),
        fin[3, 3 * part:].astype(f32),
        fin[2].astype(f32).reshape(blocks, part, width).transpose(1, 0, 2).reshape(part, ff),
        fin[1].astype(f32),
        tail[experts:experts + 2],
        fin[0, :3 * part].astype(f32).reshape(3, part, width),
        fin[0, 3 * part:].astype(f32),
        tail[:experts].T,
        tail[experts + 2:experts + 4],
        grad_e_in.astype(f32),
        grad_e_out.astype(f32),
    )


def solution(mesh):
    owners, shards = mesh.shape["expert"], mesh.shape["shard"]
    both = ("expert", "shard")
    return jax.shard_map(
        functools.partial(per_device, owners, shards),
        mesh=mesh,
        in_specs=(
            P(both, None, None), P(both, None, None), P(both, None, None), P(both), P(),
            P(None, "shard", None), P("shard", None), P("shard", None), P("shard", None), P(None, "shard"),
            P(None, "shard", None), P("shard", None), P("shard", None), P(None, "shard"),
            P("expert", None, None), P("expert", None, None),
        ),
        out_specs=(
            P(both, None, None), P(), P(both, None, None),
            P(None, "shard", None), P("shard", None), P("shard", None), P("shard", None), P(None, "shard"),
            P(None, "shard", None), P("shard", None), P("shard", None), P(None, "shard"),
            P("expert", None, None), P("expert", None, None),
        ),
        check_vma=False,
    )
```

```python
import functools

import jax
import jax.numpy as jnp
from jax import lax
from jax.experimental import pallas as pl
from jax.experimental.pallas import tpu as pltpu
from jax.sharding import PartitionSpec as P

HEADS = 8
CAP = 40
EPS = 1e-06
NEG = -1e30
LANES = 128
f32 = jnp.float32
bf16 = jnp.bfloat16
ANY = pl.BlockSpec(memory_space=pl.ANY)
VM = pl.BlockSpec(memory_space=pltpu.VMEM)
VMEM_BYTES = 58 << 20


def nn(a, b):
    return lax.dot_general(a, b, (((1,), (0,)), ((), ())), preferred_element_type=f32)


def nt(a, b):
    return lax.dot_general(a, b, (((1,), (1,)), ((), ())), preferred_element_type=f32)


def tn(a, b):
    return lax.dot_general(a, b, (((0,), (0,)), ((), ())), preferred_element_type=f32)


def sds(shape, dtype):
    return jax.ShapeDtypeStruct(shape, dtype)


def padded(seq):
    return -(-seq // 16) * 16


def norm(x):
    xc = x - jnp.mean(x, axis=-1, keepdims=True)
    rs = lax.rsqrt(jnp.mean(xc * xc, axis=-1, keepdims=True) + EPS)
    return xc * rs, rs


def norm_back(dyn, xn, rs, gain):
    dgain = jnp.sum(dyn * xn, axis=0, keepdims=True)
    dxn = dyn * gain
    dv = dxn - jnp.mean(dxn, axis=-1, keepdims=True)
    dv = (dv - xn * jnp.mean(dxn * xn, axis=-1, keepdims=True)) * rs
    return dv, dgain


def gelu_pair(z):
    a = jnp.abs(z)
    t = 1.0 / (1.0 + (0.3275911 * 0.7071067811865476) * a)
    e = jnp.exp(-0.5 * (z * z))
    q = t * (0.127414796 + t * (-0.142248368 + t * (0.7107068705 + t * (-0.7265760135 + t * 0.5307027145))))
    q = q * e
    phi = jnp.where(z >= 0.0, 1.0 - q, q)
    return z * phi, phi + z * (e * 0.3989422804014327)


class Split:
    def __init__(self, shards):
        self.pair = shards == 2
        self.shards = shards

    def gather(self, owns):
        if not self.pair:
            whole = [lax.all_gather(o, "shard", axis=1, tiled=True) for o in owns]
            return whole
        core = lax.axis_index("expert") % 2
        owners = lax.axis_size("expert")
        half = owns[0].shape[1] // 2
        send = jnp.concatenate([lax.dynamic_slice_in_dim(o, core * half, half, 1) for o in owns], axis=0)
        far = lax.ppermute(send, "shard", [(0, 1), (1, 0)])
        near = lax.ppermute(far, "expert", [(i, i ^ 1) for i in range(owners)])
        return list(owns) + [far, near]

    def count(self, owns):
        return owns + 2 if self.pair else owns

    def copies(self, refs, full, sems):
        out = []
        if not self.pair:
            at = 0
            for i, r in enumerate(refs):
                n = r.shape[0]
                out.append(pltpu.make_async_copy(r, full.at[at:at + n], sems.at[i]))
                at += n
            return out
        me = lax.axis_index("shard")
        core = lax.axis_index("expert") % 2
        rows = refs[0].shape[1]
        half = rows // 2
        at = 0
        for i, r in enumerate(refs[:-2]):
            n = r.shape[0]
            out.append(pltpu.make_async_copy(r, full.at[at:at + n, pl.ds(me * rows, rows), :], sems.at[i]))
            at += n
        base = (1 - me) * rows
        k = len(refs) - 2
        out.append(pltpu.make_async_copy(refs[k], full.at[:, pl.ds(base + core * half, half), :], sems.at[k]))
        out.append(pltpu.make_async_copy(refs[k + 1], full.at[:, pl.ds(base + (1 - core) * half, half), :], sems.at[k + 1]))
        return out


def start(copies):
    for c in copies:
        c.start()


def finish(copies):
    for c in copies:
        c.wait()


def call(body, outs, ins, scratch=(), specs=None, flops=0, nbytes=0, **kw):
    return pl.pallas_call(
        body,
        out_shape=outs,
        in_specs=specs or [VM] * len(ins),
        out_specs=[VM] * len(outs),
        scratch_shapes=list(scratch),
        compiler_params=pltpu.CompilerParams(vmem_limit_bytes=VMEM_BYTES),
        cost_estimate=pl.CostEstimate(flops=int(flops), bytes_accessed=int(nbytes), transcendentals=0),
        **kw,
    )(*ins)


def pad_store(ref, block, images, seq, step):
    ref[...] = jnp.zeros(ref.shape, ref.dtype)
    for i in range(images):
        ref[i * step:i * step + seq, :] = block(i).astype(ref.dtype)


def slot_start(expert, local, block):
    owner = jnp.floor((expert.astype(f32) + 0.5) * (1.0 / local))
    return owner * block + (expert.astype(f32) - owner * local) * CAP


def route_body(images, seq, local, block, r_ref, rt_ref, live_ref, cot_ref, dy_ref, dyd_ref, disp_ref, back_ref):
    step = r_ref.shape[0] // images
    pad_store(dy_ref, lambda i: cot_ref[i], images, seq, step)
    dy_ref[...] = (dy_ref[...].astype(f32) * live_ref[...]).astype(bf16)
    route_tables(local, block, r_ref, rt_ref, disp_ref, back_ref)
    dyd_ref[...] = nn(disp_ref[...], dy_ref[...]).astype(bf16)


def route_tables(local, block, r_ref, rt_ref, disp_ref, back_ref):
    rows = r_ref.shape[0]
    slots = disp_ref.shape[0]
    lane = lax.broadcasted_iota(jnp.int32, (rows, LANES), 1)
    hit = (r_ref[:, 0:1] == lane) | (r_ref[:, 1:2] == lane)
    ti = lax.broadcasted_iota(jnp.int32, (rows, rows), 0)
    tj = lax.broadcasted_iota(jnp.int32, (rows, rows), 1)
    place = nn((ti > tj).astype(f32).astype(bf16), hit.astype(f32).astype(bf16))
    place = jnp.where(hit, place, -1.0).astype(bf16)
    off = lax.broadcasted_iota(jnp.int32, (LANES, slots), 1).astype(f32) - slot_start(
        lax.broadcasted_iota(jnp.int32, (LANES, slots), 0), local, block)
    spread = ((off >= 0) & (off < CAP)).astype(f32)
    within = jnp.sum(spread * off, axis=0, keepdims=True)
    within = jnp.where(jnp.sum(spread, axis=0, keepdims=True) > 0, within, -2.0)
    back_ref[...] = (nn(place, spread.astype(bf16)) == within).astype(f32).astype(bf16)
    sub = lax.broadcasted_iota(jnp.int32, (LANES, rows), 0)
    hit_t = (rt_ref[0:1, :] == sub) | (rt_ref[1:2, :] == sub)
    place_t = nn(hit_t.astype(f32).astype(bf16), (ti < tj).astype(f32).astype(bf16))
    place_t = jnp.where(hit_t, place_t, -1.0).astype(bf16)
    off = lax.broadcasted_iota(jnp.int32, (slots, LANES), 0).astype(f32) - slot_start(
        lax.broadcasted_iota(jnp.int32, (slots, LANES), 1), local, block)
    spread_t = ((off >= 0) & (off < CAP)).astype(f32)
    within_t = jnp.sum(spread_t * off, axis=1, keepdims=True)
    within_t = jnp.where(jnp.sum(spread_t, axis=1, keepdims=True) > 0, within_t, -2.0)
    disp_ref[...] = (nn(spread_t.astype(bf16), place_t) == within_t).astype(f32).astype(bf16)
    return hit.astype(f32)


def attend_forward(step, seq, images, x, gain, wq, wo, qkv_ref, mix_ref, tick=None, image_tick=None):
    width = x.shape[1]
    head = width // HEADS
    scale = head ** -0.5
    xn, _ = norm(x)
    a = (xn * gain).astype(bf16)
    for c in range(3):
        qkv_ref[:, c * width:(c + 1) * width] = nn(a, wq[c][...]).astype(bf16)
    if tick is not None:
        tick()
    lane = lax.broadcasted_iota(jnp.int32, (1, LANES), 1)
    col = lax.broadcasted_iota(jnp.int32, (1, step), 1)
    per = LANES // head

    def image(i, _):
        at = pl.ds(pl.multiple_of(i * step, step), step)
        for hp in range(width // LANES):
            q = qkv_ref[at, hp * LANES:(hp + 1) * LANES]
            k = qkv_ref[at, width + hp * LANES:width + (hp + 1) * LANES]
            v = qkv_ref[at, 2 * width + hp * LANES:2 * width + (hp + 1) * LANES]
            got = None
            for h in range(per):
                mine = (lane >= h * head) & (lane < (h + 1) * head)
                qm = q * jnp.where(mine, scale, 0.0).astype(bf16)
                s = jnp.where(col < seq, nt(qm, k), NEG)
                e = jnp.exp(s - jnp.max(s, axis=-1, keepdims=True))
                p = (e * (1.0 / jnp.sum(e, axis=-1, keepdims=True))).astype(bf16)
                o = nn(p, v)
                got = o if got is None else jnp.where(mine, o, got)
            mix_ref[at, hp * LANES:(hp + 1) * LANES] = got.astype(bf16)
        if image_tick is not None:
            image_tick(i)
        return 0

    lax.fori_loop(0, images, image, 0)
    return x + nn(mix_ref[...], wo[...])


def attend_backward(step, seq, images, grad, x, gain, wq, wo, qkv_ref, mix_ref, dmix_ref, dqkv_ref, pack_ref, base,
                    tick=None):
    width = x.shape[1]
    head = width // HEADS
    scale = head ** -0.5
    shards = pack_ref.shape[0]
    part = width // shards
    low = grad.astype(bf16)
    dwo = tn(mix_ref[...], low).astype(bf16)
    for s in range(shards):
        pack_ref[s, base + 3 * part:base + 4 * part, :] = dwo[s * part:(s + 1) * part]
    dmix_ref[...] = nt(low, wo[...]).astype(bf16)
    lane = lax.broadcasted_iota(jnp.int32, (1, LANES), 1)
    key = lax.broadcasted_iota(jnp.int32, (step, 1), 0)
    per = LANES // head

    def image(i, _):
        at = pl.ds(pl.multiple_of(i * step, step), step)
        for hp in range(width // LANES):
            q = qkv_ref[at, hp * LANES:(hp + 1) * LANES]
            k = qkv_ref[at, width + hp * LANES:width + (hp + 1) * LANES]
            v = qkv_ref[at, 2 * width + hp * LANES:2 * width + (hp + 1) * LANES]
            do = dmix_ref[at, hp * LANES:(hp + 1) * LANES]
            dq = dk = dv = None
            for h in range(per):
                mine = (lane >= h * head) & (lane < (h + 1) * head)
                scaled = jnp.where(mine, scale, 0.0).astype(bf16)
                km = k * scaled
                s = jnp.where(key < seq, nt(km, q), NEG)
                e = jnp.exp(s - jnp.max(s, axis=0, keepdims=True))
                p = e * (1.0 / jnp.sum(e, axis=0, keepdims=True))
                dom = do * jnp.where(mine, 1.0, 0.0).astype(bf16)
                dp = nt(v, dom)
                ds = (p * (dp - jnp.sum(p * dp, axis=0, keepdims=True))).astype(bf16)
                hv = nn(p.astype(bf16), dom)
                hk = nn(ds, q * scaled)
                hq = tn(ds, km)
                dq, dk, dv = (hq, hk, hv) if dq is None else (dq + hq, dk + hk, dv + hv)
            dqkv_ref[at, hp * LANES:(hp + 1) * LANES] = dq.astype(bf16)
            dqkv_ref[at, width + hp * LANES:width + (hp + 1) * LANES] = dk.astype(bf16)
            dqkv_ref[at, 2 * width + hp * LANES:2 * width + (hp + 1) * LANES] = dv.astype(bf16)
        if tick is not None:
            tick(i)
        return 0

    lax.fori_loop(0, images, image, 0)
    xn, rs = norm(x)
    a = (xn * gain).astype(bf16)
    da = None
    for c in range(3):
        d = dqkv_ref[:, c * width:(c + 1) * width]
        dw = tn(a, d).astype(bf16)
        for s in range(shards):
            pack_ref[s, base + c * part:base + (c + 1) * part, :] = dw[s * part:(s + 1) * part]
        one = nt(d, wq[c][...])
        da = one if da is None else da + one
    return norm_back(da, xn, rs, gain)


def block1_body(split, images, seq, x_ref, gain_ref, *refs):
    n = split.count(2)
    pieces, (hidden_ref, qkv_ref, mix_ref, w, sems) = refs[:n], refs[n:]
    copies = split.copies(pieces, w, sems)
    start(copies)
    step = hidden_ref.shape[0] // images
    pad_store(hidden_ref, lambda i: x_ref[i], images, seq, step)
    finish(copies)
    hidden_ref[...] = attend_forward(
        step, seq, images, hidden_ref[...], gain_ref[0:1, :], [w.at[c] for c in range(3)], w.at[3], qkv_ref, mix_ref
    )


def mlp_body(split, hidden_ref, gain_ref, *refs):
    n = 2 * split.count(1)
    pieces, (out_ref, act_ref, slope_ref, w1, w2, sems) = refs[:n], refs[n:]
    half = n // 2
    copies = split.copies(pieces[:half], w1, sems.at[0]) + split.copies(pieces[half:], w2, sems.at[1])
    start(copies)
    hidden = hidden_ref[...]
    xn, _ = norm(hidden)
    u = (xn * gain_ref[1:2, :]).astype(bf16)
    out_ref[...] = hidden
    finish(copies)
    wide = act_ref.shape[2]
    for b in range(act_ref.shape[0]):
        at = slice(b * wide, (b + 1) * wide)
        act, slope = gelu_pair(nn(u, w1[0, :, at]))
        act = act.astype(bf16)
        act_ref[b] = act
        slope_ref[b] = slope.astype(bf16)
        out_ref[...] += nn(act, w2[0, at, :])


def router_probs(u, router, experts):
    lane = lax.broadcasted_iota(jnp.int32, (1, LANES), 1)
    logits = jnp.where(lane < experts, nn(u, router), NEG)
    e = jnp.exp(logits - jnp.max(logits, axis=-1, keepdims=True))
    return e * (1.0 / jnp.sum(e, axis=-1, keepdims=True))


def block2_body(split, images, seq, experts, x_ref, gain_ref, router_ref, disp_ref, live_ref, load_ref, *refs):
    n = split.count(2)
    pieces, (hidden_ref, qkv_ref, mix_ref, u_ref, probs_ref, sum_ref, ud_ref, w, sems) = refs[:n], refs[n:]
    copies = split.copies(pieces, w, sems)
    start(copies)
    finish(copies)
    step = hidden_ref.shape[0] // images
    hidden = attend_forward(
        step, seq, images, x_ref[...], gain_ref[2:3, :], [w.at[c] for c in range(3)], w.at[3], qkv_ref, mix_ref
    )
    hidden_ref[...] = hidden
    xn, _ = norm(hidden)
    u = (xn * gain_ref[3:4, :]).astype(bf16)
    u_ref[...] = u
    ud_ref[...] = nn(disp_ref[...], u).astype(bf16)
    probs = router_probs(u, router_ref[...], experts)
    probs_ref[...] = probs
    sums = jnp.sum(probs * live_ref[...], axis=0, keepdims=True)
    sum_ref[...] = jnp.concatenate([load_ref[...], sums, jnp.zeros((6, LANES), f32)], axis=0)


def forward_body(images, seq, experts, local, owners, *refs):
    (r_ref, rt_ref, counts_ref, tok_ref, cot_ref, gain_ref, router_ref, q1_h, o1_h, up_h, down_h, q2_h, o2_h,
     gains_out, router_out, stat_out, live_out,
     dy_o, uout_o, hid1_o, x2_o, hid2_o, qkv1_o, mix1_o, qkv2_o, mix2_o, act_o, slope_o, u_o, probs_o, back_o,
     wa_o, wu_o, wd_o, wb_o, dyin_o,
     wa, wu, wd, wb, dy, slot_rows, disp, back, hid1, x2, hid2, qkv1, mix1, qkv2, mix2, act, slope, u, probs, gx,
     lsem, osem, ks, kr, vs, vr) = refs
    me, x = lax.axis_index("expert"), lax.axis_index("shard")
    bits = owners.bit_length() - 1
    b0, b1 = me % 2, (me // 2) % 2
    core, side = me + 1 - 2 * b0, me + (1 - 2 * b1) * 2
    rows, width = dy.shape
    step = rows // images
    part = width // 2
    ff = wd.shape[1]
    fpart = ff // 2

    def to(e, s):
        return dict(device_id=(e, s), device_id_type=pl.DeviceIdType.MESH)

    def each(lo, hi, f):
        lax.fori_loop(lo, hi, lambda k, c: (f(k), c)[1], 0)

    barrier = pltpu.get_barrier_semaphore()
    each(1, owners, lambda k: pl.semaphore_signal(barrier, inc=1, **to(xor(me, k, bits), x)))
    pl.semaphore_signal(barrier, inc=1, **to(me, 1 - x))

    def at(first, size):
        return pl.ds(pl.multiple_of(first, 64), size)

    mine, theirs = x * part, (1 - x) * part
    loads = [
        pltpu.make_async_copy(q1_h, wa.at[0:3, at(mine, part)], lsem.at[0]),
        pltpu.make_async_copy(o1_h, wa.at[3, at(mine, part)], lsem.at[1]),
        pltpu.make_async_copy(up_h, wu.at[0, at(mine, part)], lsem.at[2]),
        pltpu.make_async_copy(down_h, wd.at[0, at(x * fpart, fpart)], lsem.at[3]),
        pltpu.make_async_copy(q2_h, wb.at[0:3, at(mine, part)], lsem.at[4]),
        pltpu.make_async_copy(o2_h, wb.at[3, at(mine, part)], lsem.at[5]),
    ]
    start(loads)
    router_out[at(mine, part), :] = router_ref[...]
    pl.semaphore_wait(barrier, owners)

    def remote(src, dst, i, peer):
        return pltpu.make_async_remote_copy(src, dst, ks.at[i], kr.at[i], **peer)

    far, near, over = to(me, 1 - x), to(core, x), to(side, x)
    half, quarter, fquarter = part // 2, part // 4, fpart // 4
    p = b0 * 2 + b1
    h = b0 * half
    here = at(theirs + h, half)
    moves = {
        "small": [lambda: remote(gain_ref, gx, 0, far), lambda: remote(router_ref, router_out.at[at(mine, part), :], 1, far)],
        "ax": [lambda: remote(q1_h.at[:, at(h, half)], wa.at[0:3, at(mine + h, half)], 2, far),
               lambda: remote(o1_h.at[at(h, half)], wa.at[3, at(mine + h, half)], 3, far)],
        "ac": [lambda: remote(wa.at[:, here], wa.at[:, here], 4, near)],
        "ux": [lambda: remote(up_h.at[at(p * quarter, quarter)], wu.at[0, at(mine + p * quarter, quarter)], 5, far)],
        "uy": [lambda: remote(wu.at[0, at(theirs + p * quarter, quarter)], wu.at[0, at(theirs + p * quarter, quarter)], 6, over)],
        "uc": [lambda: remote(wu.at[0, here], wu.at[0, here], 7, near)],
        "dx": [lambda: remote(down_h.at[at(p * fquarter, fquarter)], wd.at[0, at(x * fpart + p * fquarter, fquarter)], 8, far)],
        "dy": [lambda: remote(wd.at[0, at((1 - x) * fpart + p * fquarter, fquarter)],
                              wd.at[0, at((1 - x) * fpart + p * fquarter, fquarter)], 9, over)],
        "dc": [lambda: remote(wd.at[0, at((1 - x) * fpart + b0 * 2 * fquarter, 2 * fquarter)],
                              wd.at[0, at((1 - x) * fpart + b0 * 2 * fquarter, 2 * fquarter)], 10, near)],
        "bx": [lambda: remote(q2_h.at[:, at(p * quarter, quarter)], wb.at[0:3, at(mine + p * quarter, quarter)], 11, far),
               lambda: remote(o2_h.at[at(p * quarter, quarter)], wb.at[3, at(mine + p * quarter, quarter)], 12, far)],
        "by": [lambda: remote(wb.at[:, at(theirs + p * quarter, quarter)], wb.at[:, at(theirs + p * quarter, quarter)], 13, over)],
        "bc": [lambda: remote(wb.at[:, here], wb.at[:, here], 14, near)],
    }

    def go(*names):
        for n in names:
            for m in moves[n]:
                m().start()

    def done(*names):
        for n in names:
            for m in moves[n]:
                m().wait()

    def send_dy(k):
        q = xor(me, k, bits)
        return pltpu.make_async_remote_copy(slot_rows.at[0, q], dyin_o.at[me], vs.at[k], vr.at[k], **to(q, x))

    out = []

    def keep(src, dst):
        c = pltpu.make_async_copy(src, dst, osem.at[len(out)])
        c.start()
        out.append(c)

    go("ax", "small")
    row = lax.broadcasted_iota(jnp.int32, (rows, 1), 0)
    live = ((row < counts_ref[0] * step) & (r_ref[:, 0:1] >= 0)).astype(f32)
    live_out[...] = live
    pad_store(dy, lambda i: cot_ref[i], images, seq, step)
    dy[...] = (dy[...].astype(f32) * live).astype(bf16)
    keep(dy, dy_o)
    hit = route_tables(local, slot_rows.shape[2], r_ref, rt_ref, disp, back)
    keep(back, back_o)
    slot_rows[0] = nn(disp[...], dy[...]).astype(bf16).reshape(slot_rows.shape[1:])
    keep(slot_rows.at[0, me], dyin_o.at[me])
    lane = lax.broadcasted_iota(jnp.int32, (1, LANES), 1)
    load = jnp.where(lane == LANES - 1, jnp.sum(live, axis=0, keepdims=True), jnp.sum(hit * live, axis=0, keepdims=True))
    done("ax")
    go("ac", "ux", "dx")
    each(1, owners, lambda k: send_dy(owners - k).start())
    pad_store(hid1, lambda i: tok_ref[i], images, seq, step)
    done("small")
    own_gain, far_gain = gain_ref[...], gx[...]
    gains = jnp.where(x == 0, jnp.concatenate([own_gain, far_gain], axis=1), jnp.concatenate([far_gain, own_gain], axis=1))
    gains_out[...] = gains
    finish(loads)
    done("ac")
    keep(wa, wa_o)

    def first_tick():
        go("bx")

    def first_image(i):
        @pl.when(i == 0)
        def _():
            done("ux")
            go("uy")

        @pl.when(i == 1)
        def _():
            done("dx", "uy")
            go("dy", "uc")

        @pl.when(i == 2)
        def _():
            done("bx")
            go("by")

    hid1[...] = attend_forward(step, seq, images, hid1[...], gains[0:1], [wa.at[c] for c in range(3)], wa.at[3], qkv1, mix1,
                               first_tick, first_image)
    keep(hid1, hid1_o)
    keep(qkv1, qkv1_o)
    keep(mix1, mix1_o)

    done("uc")
    keep(wu, wu_o)
    xn, _ = norm(hid1[...])
    a = (xn * gains[1:2]).astype(bf16)
    for b in range(act.shape[0]):
        one, two = gelu_pair(nn(a, wu[0, :, b * width:(b + 1) * width]))
        act[b] = one.astype(bf16)
        slope[b] = two.astype(bf16)
        if b == 0:
            done("dy", "by")
            go("dc", "bc")
    keep(slope, slope_o)
    keep(act, act_o)
    done("dc", "bc")
    keep(wd, wd_o)
    keep(wb, wb_o)
    total = hid1[...]
    for b in range(act.shape[0]):
        total = total + nn(act[b], wd[0, b * width:(b + 1) * width, :])
    x2[...] = total
    keep(x2, x2_o)

    hid2[...] = attend_forward(step, seq, images, x2[...], gains[2:3], [wb.at[c] for c in range(3)], wb.at[3], qkv2, mix2)
    keep(qkv2, qkv2_o)
    keep(mix2, mix2_o)
    keep(hid2, hid2_o)
    xn, _ = norm(hid2[...])
    u[...] = (xn * gains[3:4]).astype(bf16)
    keep(u, u_o)
    slot_rows[1] = nn(disp[...], u[...]).astype(bf16).reshape(slot_rows.shape[1:])
    keep(slot_rows.at[1], uout_o)
    probs[...] = router_probs(u[...], router_out[...], experts)
    keep(probs, probs_o)
    sums = jnp.sum(probs[...] * live, axis=0, keepdims=True)
    stat_out[...] = jnp.concatenate([load, sums, jnp.zeros((6, LANES), f32)], axis=0)
    each(1, owners, lambda k: send_dy(k).wait())
    finish(out)


def fused_forward(owners, experts, local, block, tokens, cotangent, routes, counts, gains, router, attn_qkv1, attn_out1, mlp_in, mlp_out,
                  attn_qkv2, attn_out2):
    images, seq, width = tokens.shape
    step = padded(seq)
    rows = images * step
    ff = mlp_in.shape[1]
    slots = owners * block[1]
    blocks = ff // width
    part = width // 2
    routes_pad = jnp.pad(routes, ((0, 0), (0, step - seq), (0, 0)), constant_values=-1).reshape(rows, 2)
    gains = jnp.pad(gains, ((0, 4), (0, 0))).astype(f32)
    router = jnp.pad(router, ((0, 0), (0, LANES - experts)))
    V, sem = pltpu.VMEM, pltpu.SemaphoreType.DMA
    kept = [
        ((rows, width), bf16), (block, bf16), ((rows, width), f32), ((rows, width), f32), ((rows, width), f32),
        ((rows, 3 * width), bf16), ((rows, width), bf16), ((rows, 3 * width), bf16), ((rows, width), bf16),
        ((blocks, rows, width), bf16), ((blocks, rows, width), bf16), ((rows, width), bf16), ((rows, LANES), f32), ((rows, slots), bf16),
        ((4, width, width), bf16), ((1, width, ff), bf16), ((1, ff, width), bf16), ((4, width, width), bf16), (block, bf16),
    ]
    return pl.pallas_call(
        functools.partial(forward_body, images, seq, experts, local, owners),
        out_shape=[sds((8, width), f32), sds((width, LANES), bf16), sds((8, LANES), f32), sds((rows, 1), f32)]
        + [sds(shape, dtype) for shape, dtype in kept],
        in_specs=[VM, VM, pl.BlockSpec(memory_space=pltpu.SMEM)] + [VM] * 4 + [ANY] * 6,
        out_specs=[VM] * 4 + [ANY] * len(kept),
        scratch_shapes=[
            V((4, width, width), bf16), V((1, width, ff), bf16), V((1, ff, width), bf16), V((4, width, width), bf16),
            V((rows, width), bf16), V((2,) + block, bf16), V((slots, rows), bf16), V((rows, slots), bf16),
            V((rows, width), f32), V((rows, width), f32), V((rows, width), f32),
            V((rows, 3 * width), bf16), V((rows, width), bf16), V((rows, 3 * width), bf16), V((rows, width), bf16),
            V((blocks, rows, width), bf16), V((blocks, rows, width), bf16), V((rows, width), bf16), V((rows, LANES), f32),
            V((8, part), f32),
            sem((6,)), sem((len(kept),)), sem((15,)), sem((15,)), sem((owners,)), sem((owners,)),
        ],
        compiler_params=pltpu.CompilerParams(vmem_limit_bytes=VMEM_BYTES, collective_id=2, has_side_effects=True),
        cost_estimate=pl.CostEstimate(flops=int(18e9), bytes_accessed=int(60e6), transcendentals=0),
    )(routes_pad, routes_pad.T, counts, tokens, cotangent, gains, router, attn_qkv1, attn_out1, mlp_in, mlp_out, attn_qkv2, attn_out2)


def split_rows(block, local):
    n, r, w = block.shape
    v = block.astype(f32)
    if r != local * CAP:
        v = v[:, :local * CAP]
    v = v.reshape(n, local, CAP, w)
    return [v[:, i].reshape(n * CAP, w) for i in range(local)]


def join_rows(parts, sources, block):
    local = len(parts)
    w = parts[0].shape[1]
    v = jnp.concatenate([p.reshape(sources, 1, CAP, w) for p in parts], axis=1).reshape(sources, local * CAP, w)
    if block != local * CAP:
        v = jnp.concatenate([v, jnp.zeros((sources, block - local * CAP, w), f32)], axis=1)
    return v


def gate_of(u, router, experts, e):
    lane = lax.broadcasted_iota(jnp.int32, (1, LANES), 1)
    return jnp.sum(jnp.where(lane == e, router_probs(u, router, experts), 0.0), axis=-1, keepdims=True)


def xor(a, b, bits):
    out = 0
    for i in range(bits):
        out = out + ((a // (1 << i) + b // (1 << i)) % 2) * (1 << i)
    return out


def expert_body(owners, shards, local, experts, group, uout_ref, dy_ref, router_ref, stat_ref, w1_hbm, w2_hbm,
                uin_ref, served_ref, duback_ref, dgback_ref, total_ref, dyx_ref, ux_ref,
                w1, w2, dusend, dgsend, statx, state, wsem, lsem, us, ur, ds_, dr, gs, gr, ss, sr, fs, fr, xs, xr, ys, yr):
    me, x = lax.axis_index("expert"), lax.axis_index("shard")
    bits = owners.bit_length() - 1
    barrier = pltpu.get_barrier_semaphore()

    def at(e, s):
        return dict(device_id=(e, s), device_id_type=pl.DeviceIdType.MESH)

    def each(lo, hi, f):
        lax.fori_loop(lo, hi, lambda k, c: (f(k), c)[1], 0)

    def peer(k):
        return xor(me, k, bits)

    each(1, owners, lambda k: pl.semaphore_signal(barrier, inc=1, **at(peer(k), x)))
    each(1, shards, lambda k: pl.semaphore_signal(barrier, inc=1, **at(me, (x + k) % shards)))
    weights = [pltpu.make_async_copy(w1_hbm, w1, wsem.at[0]), pltpu.make_async_copy(w2_hbm, w2, wsem.at[1])]
    start(weights)
    own = pltpu.make_async_copy(uout_ref.at[me], uin_ref.at[me], lsem.at[0])
    own.start()
    pl.semaphore_wait(barrier, owners - 1 + shards - 1)

    def send_u(k):
        return pltpu.make_async_remote_copy(uout_ref.at[peer(k)], uin_ref.at[me], us.at[k], ur.at[k], **at(peer(k), x))

    def send_du(k):
        return pltpu.make_async_remote_copy(dusend.at[peer(k)], duback_ref.at[me], ds_.at[k], dr.at[k], **at(peer(k), x))

    def send_dg(k):
        return pltpu.make_async_remote_copy(dgsend.at[peer(k)], dgback_ref.at[me], gs.at[k], gr.at[k], **at(peer(k), x))

    def send_statx(k):
        return pltpu.make_async_remote_copy(stat_ref, statx.at[k], xs.at[k], xr.at[k], **at(me, (x + k) % shards))

    def send_dyx(k):
        return pltpu.make_async_remote_copy(dy_ref, dyx_ref.at[k - 1], ys.at[k], yr.at[k], **at(me, (x + k) % shards))

    def send_far(g):
        rows = pl.ds(xor(me // group, g, bits) * group, group)
        return pltpu.make_async_remote_copy(uin_ref.at[rows], ux_ref.at[rows], fs.at[g], fr.at[g], **at(me, (x + 1) % shards))

    def send_state(k):
        return pltpu.make_async_remote_copy(state.at[0], state.at[k], ss.at[k], sr.at[k], **at(peer(k), x))

    each(1, shards, lambda k: send_statx(k).start())
    each(1, owners, lambda k: send_u(owners - k).start())
    each(1, shards, lambda k: send_dyx(k).start())
    each(1, shards, lambda k: send_statx(k).wait())
    sums = stat_ref[...]
    for k in range(1, shards):
        sums = sums + statx[k]
    state[0] = sums
    each(1, owners, lambda k: send_state(k).start())
    finish(weights)

    def work(g):
        base = xor(me // group, g, bits) * group
        rows = pl.ds(base, group)
        us_, dys = split_rows(uin_ref[rows], local), split_rows(dy_ref[rows], local)
        served, dus, prods = [], [], []
        for i in range(local):
            u, dy = us_[i].astype(bf16), dys[i]
            gate = gate_of(u, router_ref[...], experts, me * local + i)
            dsv = (gate * dy).astype(bf16)
            act, slope = gelu_pair(nn(u, w1[i]))
            out = nn(act.astype(bf16), w2[i])
            dz = (slope * nt(dsv, w2[i])).astype(bf16)
            dus.append(nt(dz, w1[i]))
            served.append(gate * out)
            prods.append(dy * out)
        block = uin_ref.shape[1]
        served_ref[rows] = join_rows(served, group, block).astype(bf16)
        dusend[rows] = join_rows(dus, group, block).astype(bf16)
        prod = join_rows(prods, group, block)
        ones = jnp.ones((8, prod.shape[2]), bf16)
        for j in range(group):
            hi = prod[j].astype(bf16)
            lo = (prod[j] - hi.astype(f32)).astype(bf16)
            dgsend[base + j, :, 0:block] = nt(ones, hi) + nt(ones, lo)

    def step(g):
        @pl.when(g == 0)
        def _():
            own.wait()

        for j in range(group):
            k = g * group + j
            if j == 0:
                pl.when(g > 0)(lambda k=k: send_u(k).wait_recv())
            else:
                send_u(k).wait_recv()
        if shards == 2:
            send_far(g).start()
        work(g)
        for j in range(group):
            k = g * group + j
            if j == 0:
                @pl.when(g > 0)
                def _(k=k):
                    send_du(k).start()
                    send_dg(k).start()
            else:
                send_du(k).start()
                send_dg(k).start()

    each(0, owners // group, step)
    backs = [pltpu.make_async_copy(dusend.at[me], duback_ref.at[me], lsem.at[0]),
             pltpu.make_async_copy(dgsend.at[me], dgback_ref.at[me], lsem.at[1])]
    start(backs)
    each(1, owners, lambda k: send_state(k).wait())
    total = state[0]
    for k in range(1, owners):
        total = total + state[k]
    total_ref[...] = total
    each(1, owners, lambda k: send_u(k).wait_send())
    finish(backs)
    each(1, shards, lambda k: send_dyx(k).wait())
    if shards == 2:
        each(0, owners // group, lambda g: send_far(g).wait())
    each(1, owners, lambda k: send_du(k).wait())
    each(1, owners, lambda k: send_dg(k).wait())


def expert_grad_body(pieces, experts, *refs):
    us, dys = refs[:pieces], refs[pieces:2 * pieces]
    router_ref, w1_ref, w2_ref, g1_ref, g2_ref, urow, drow, stage, sems = refs[2 * pieces:]
    local = pl.num_programs(0)
    e = lax.axis_index("expert") * local + pl.program_id(0)

    @pl.when((pl.program_id(0) == 0) & (pl.program_id(1) == 0))
    def _():
        todo = [(us[i], urow, i) for i in range(pieces)] + [(dys[i], drow, i) for i in range(pieces)]
        copies = [pltpu.make_async_copy(r, stage.at[n % 2], sems.at[n % 2]) for n, (r, _, _) in enumerate(todo)]
        copies[0].start()
        for n, (_, to, i) in enumerate(todo):
            if n + 1 < len(todo):
                copies[n + 1].start()
            copies[n].wait()
            for j, v in enumerate(split_rows(stage[n % 2], urow.shape[1])):
                to[i, j] = v.astype(bf16)

    at = pl.program_id(0)
    for i in range(pieces):
        u = urow[i, at]
        dy = drow[i, at]
        gate = gate_of(u, router_ref[...], experts, e)
        ds = (gate * dy.astype(f32)).astype(bf16)
        act, slope = gelu_pair(nn(u, w1_ref[0]))
        dz = (slope * nt(ds, w2_ref[0])).astype(bf16)
        g1 = tn(u, dz)
        g2 = tn(act.astype(bf16), ds)
        if i == 0:
            g1_ref[0] = g1
            g2_ref[0] = g2
        else:
            g1_ref[0] += g1
            g2_ref[0] += g2


def split3(v):
    hi = v.astype(bf16)
    r = v - hi.astype(f32)
    mid = r.astype(bf16)
    lo = (r - mid.astype(f32)).astype(bf16)
    return hi, mid, lo


def router_backward(experts, dy_ref, u_ref, probs_ref, hidden_ref, gain_ref, router_ref, aux_ref, stat_ref, live_ref,
                    back_ref, ret_ref, dgate_ref, small_ref):
    slots = back_ref.shape[1]
    owners = dgate_ref.shape[0]
    local = experts // owners
    block = slots // owners
    off = lax.broadcasted_iota(jnp.int32, (slots, LANES), 0).astype(f32) - slot_start(
        lax.broadcasted_iota(jnp.int32, (slots, LANES), 1), local, block)
    oe = lax.broadcasted_iota(jnp.int32, (owners, LANES), 0).astype(f32)
    ee = lax.broadcasted_iota(jnp.int32, (owners, LANES), 1).astype(f32)
    pick = ((ee >= oe * local) & (ee < oe * local + local)).astype(f32).astype(bf16)
    column = 0.0
    for part in split3(dgate_ref[:, 0, :]):
        column = column + tn(part, pick)
    table = jnp.where((off >= 0) & (off < CAP), jnp.concatenate([column[0:block]] * owners, axis=0), 0.0)
    lane = lax.broadcasted_iota(jnp.int32, (1, LANES), 1)
    stat = stat_ref[0:1, :]
    total = jnp.sum(jnp.where(lane == LANES - 1, stat, 0.0), axis=-1, keepdims=True)
    fraction = jnp.where(lane < experts, stat, 0.0) / (2.0 * total)
    loss = experts * jnp.sum(fraction * stat_ref[1:2, :] / total, axis=-1, keepdims=True)
    small_ref[LANES + 2:LANES + 3, :] = jnp.broadcast_to(loss, (1, small_ref.shape[1]))
    dprobs = (aux_ref[0, 0] * experts * fraction / total) * live_ref[...]
    for part in split3(table):
        dprobs = dprobs + nn(back_ref[...], part)
    probs = probs_ref[...]
    dlog = (probs * (dprobs - jnp.sum(probs * dprobs, axis=-1, keepdims=True))).astype(bf16)
    small_ref[0:LANES, :] = tn(dlog, u_ref[...])
    du = nn(back_ref[...], ret_ref[...].reshape(slots, dy_ref.shape[1])) + nt(dlog, router_ref[...])
    xn, rs = norm(hidden_ref[...])
    dv, dg = norm_back(du, xn, rs, gain_ref[3:4, :])
    small_ref[LANES:LANES + 1, :] = dg
    grad = dy_ref[...].astype(f32) + dv
    return grad


def back2_body(split, images, seq, experts, dy_ref, u_ref, probs_ref, hidden_ref, x_ref, gain_ref, router_ref, aux_ref,
               stat_ref, live_ref, back_ref, ret_ref, dgate_ref, qkv_ref, mix_ref, *refs):
    n = split.count(2)
    pieces, (grad_ref, pack_ref, small_ref, w, sems, dmix_ref, dqkv_ref) = refs[:n], refs[n:]
    copies = split.copies(pieces, w, sems)
    start(copies)
    grad = router_backward(experts, dy_ref, u_ref, probs_ref, hidden_ref, gain_ref, router_ref, aux_ref, stat_ref, live_ref,
                           back_ref, ret_ref, dgate_ref, small_ref)
    grad_ref[...] = grad
    finish(copies)
    step = hidden_ref.shape[0] // images
    dv, dg = attend_backward(
        step, seq, images, grad, x_ref[...], gain_ref[2:3, :], [w.at[c] for c in range(3)], w.at[3],
        qkv_ref, mix_ref, dmix_ref, dqkv_ref, pack_ref, 0,
    )
    small_ref[LANES + 1:LANES + 2, :] = dg
    grad_ref[...] += dv


def mlp_back_body(split, grad_ref, hidden_ref, gain_ref, act_ref, slope_ref, *refs):
    n = 2 * split.count(1)
    pieces, (out_ref, pack_ref, dgain_ref, w1, w2, sems, du_ref) = refs[:n], refs[n:]
    half = n // 2
    copies = split.copies(pieces[:half], w1, sems.at[0]) + split.copies(pieces[half:], w2, sems.at[1])
    start(copies)
    xn, rs = norm(hidden_ref[...])
    gain = gain_ref[1:2, :]
    u = (xn * gain).astype(bf16)
    grad = grad_ref[...]
    low = grad.astype(bf16)
    finish(copies)
    width = grad.shape[1]
    blocks = act_ref.shape[0]
    ff = blocks * width
    shards = pack_ref.shape[0]
    part, fpart = width // shards, ff // shards
    base = part * blocks
    for b in range(blocks):
        at = slice(b * width, (b + 1) * width)
        dz = (slope_ref[b].astype(f32) * nt(low, w2[0, at, :])).astype(bf16)
        d = nt(dz, w1[0, :, at])
        if b == 0:
            du_ref[...] = d
        else:
            du_ref[...] += d
        gin = tn(u, dz).astype(bf16)
        for s in range(shards):
            pack_ref[s, b * part:(b + 1) * part, :] = gin[s * part:(s + 1) * part]
        gout = tn(act_ref[b], low).astype(bf16)
        per = min(width, fpart)
        for j in range(width // per):
            row = b * width + j * per
            s, off = row // fpart, row % fpart
            pack_ref[s, base + off:base + off + per, :] = gout[j * per:(j + 1) * per]
    dv, dg = norm_back(du_ref[...], xn, rs, gain)
    dgain_ref[...] = dg
    out_ref[...] = grad + dv


def back1_body(split, images, seq, experts, grad_ref, tok_ref, gain_ref, qkv_ref, mix_ref, small_ref, dg2_ref, *refs):
    n = split.count(2)
    pieces, (out_ref, pack_ref, w, sems, x_ref, dmix_ref, dqkv_ref) = refs[:n], refs[n:]
    copies = split.copies(pieces, w, sems)
    start(copies)
    step = x_ref.shape[0] // images
    pad_store(x_ref, lambda i: tok_ref[i], images, seq, step)
    finish(copies)
    width = x_ref.shape[1]
    dv, dg1 = attend_backward(
        step, seq, images, grad_ref[...], x_ref[...], gain_ref[0:1, :], [w.at[c] for c in range(3)], w.at[3],
        qkv_ref, mix_ref, dmix_ref, dqkv_ref, pack_ref, 0,
    )
    x_ref[...] = grad_ref[...] + dv
    for i in range(images):
        out_ref[i] = x_ref[i * step:i * step + seq, :]
    shards = pack_ref.shape[0]
    part = width // shards
    base = 4 * part
    gains = jnp.concatenate(
        [dg1, dg2_ref[...], small_ref[LANES + 1:LANES + 2, :], small_ref[LANES:LANES + 1, :], jnp.zeros((28, width), f32)], axis=0
    )
    both = jnp.concatenate([small_ref[0:32, :], gains], axis=0).astype(bf16)
    for s in range(shards):
        one = both[:, s * part:(s + 1) * part]
        pack_ref[s, base:base + 64, :] = jnp.concatenate([one, jnp.zeros((64, width - part), bf16)], axis=1)


def output_body(images, seq, hidden_ref, back_ref, ret_ref, live_ref, out_ref, tmp_ref):
    step = hidden_ref.shape[0] // images
    tmp_ref[...] = (hidden_ref[...] + nn(back_ref[...], ret_ref[...])) * live_ref[...]
    for i in range(images):
        out_ref[i] = tmp_ref[i * step:i * step + seq, :].astype(bf16)


def backward_body(split, images, seq, experts, local, owners, plan, *refs):
    (gain_ref, router_ref, aux_ref, stat_ref, live_ref, back_ref, dgate_ref, tok_ref, dy_h, u_h, probs_h, du_h,
     hid2_h, x2_h, hid1_h, qkv2_h, mix2_h, qkv1_h, mix1_h, act_h, slope_h, served_h, uin_h, ux_h, dyin_h, dyx_h, we1_h, we2_h,
     *refs) = refs
    na = nm = 1
    two, refs = refs[:na], refs[na:]
    up, refs = refs[:nm], refs[nm:]
    down, refs = refs[:nm], refs[nm:]
    one, refs = refs[:na], refs[na:]
    (out_ref, gtok_ref, fin, smout_ref, small_ref, ge1_h, ge2_h, sback_h,
     hid2, xbuf, grad_ref, dubuf, qkv, mix, dmix, dqkv, watt, w1, w2, big, stage, pack, crecv, xa, yb, ya, xb, zr,
     sm, smr,
     lsem, wsem, vs, vr, gs, gr, ms, mr, esem, osem, tsem) = refs
    me, x = lax.axis_index("expert"), lax.axis_index("shard")
    bits = owners.bit_length() - 1
    bit = [(me // (1 << i)) % 2 for i in range(bits)]
    hop = [me + (1 - 2 * bit[i]) * (1 << i) for i in range(bits)]
    rows, width = grad_ref.shape
    step = rows // images
    blocks = act_h.shape[0]
    whole = pack.shape[2]
    part = width // 2

    def to(e, s):
        return dict(device_id=(e, s), device_id_type=pl.DeviceIdType.MESH)

    def each(lo, hi, f):
        lax.fori_loop(lo, hi, lambda k, c: (f(k), c)[1], 0)

    barrier = pltpu.get_barrier_semaphore()
    each(1, owners, lambda k: pl.semaphore_signal(barrier, inc=1, **to(xor(me, k, bits), x)))
    pl.semaphore_signal(barrier, inc=1, **to(me, 1 - x))

    def load(src, dst, i):
        return pltpu.make_async_copy(src, dst, lsem.at[i])

    count = 4 + 2 * blocks
    dy_ref, u_ref, probs_ref, du_ref = dmix, dqkv.at[:, 0:width], dubuf.at[:, 0:LANES], stage.at[0]
    start_in = [load(hid2_h, hid2, 0), load(du_h, du_ref, count), load(dy_h, dy_ref, count + 1), load(u_h, u_ref, count + 2),
                load(probs_h, probs_ref, count + 3)]
    start(start_in)
    first = [load(x2_h, xbuf, 1), load(qkv2_h, qkv, 2), load(mix2_h, mix, 3)]
    w_two = split.copies(two, watt, wsem.at[0])
    w_mlp = split.copies(up, w1, wsem.at[1]) + split.copies(down, w2, wsem.at[2])
    gelus = [load(act_h.at[b], big.at[b, 0:rows], 4 + b) for b in range(blocks)]
    gelus += [load(slope_h.at[b], big.at[b, big.shape[1] // 2:big.shape[1] // 2 + rows], 4 + blocks + b) for b in range(blocks)]
    start(first + w_two + w_mlp + gelus)
    own = pltpu.make_async_copy(served_h.at[me], sback_h.at[me], tsem.at[0])
    own.start()
    pl.semaphore_wait(barrier, owners)

    def send_served(k):
        p = xor(me, k, bits)
        return pltpu.make_async_remote_copy(served_h.at[p], sback_h.at[me], vs.at[k], vr.at[k], **to(p, x))

    each(1, owners, lambda k: send_served(owners - k).start())

    planes = owners // 4

    def add(ref, at, other):
        ref[at] = ref[at] + other

    def span(first, size):
        return pl.ds(pl.multiple_of(first, 32), size)

    def stages(n):
        def copy(src, dst, i, peer):
            return pltpu.make_async_remote_copy(src, dst, gs.at[n, i], gr.at[n, i], **peer)

        q = whole // 4
        o = bit[0] * (whole // 2)
        out = []
        out.append((
            lambda: [copy(pack.at[n, :, span((1 - bit[0]) * (whole // 2), whole // 2)], crecv.at[n], 0, to(hop[0], x))],
            lambda: add(pack, (n, slice(None), span(o, whole // 2)), crecv[n])))
        e = q // 2
        b1 = bit[1] * e

        def after1():
            add(pack, (n, x, span(o, q)), xa[n])
            add(pack, (n, slice(None), span(o + q + b1, e)), yb[n])

        out.append((
            lambda: [copy(pack.at[n, 1 - x, span(o, q)], xa.at[n], 1, to(me, 1 - x)),
                     copy(pack.at[n, :, span(o + q + e - b1, e)], yb.at[n], 2, to(hop[1], x))],
            after1))

        def after2():
            add(pack, (n, x, span(o + b1, e)), ya[n])
            add(pack, (n, x, span(o + q + b1, e)), xb[n])

        out.append((
            lambda: [copy(pack.at[n, x, span(o + e - b1, e)], ya.at[n], 3, to(hop[1], x)),
                     copy(pack.at[n, 1 - x, span(o + q + b1, e)], xb.at[n], 4, to(me, 1 - x))],
            after2))
        size = e // planes
        base = o + b1

        def rows_at(p):
            return [span(base + p * size + j * q, size) for j in range(2)]

        def over(make):
            out = []
            for k in range(1, planes):
                p = xor(me // 4, k, bits)
                for j in range(2):
                    out.append(make(k, p, j, 5 + 2 * (k - 1) + j, to(p * 4 + me % 4, x)))
            return out

        mine = me // 4

        def after3():
            for j in range(2):
                at = (n, x, rows_at(mine)[j])
                total = pack[at].astype(f32)
                for k in range(1, planes):
                    total = total + zr[n, 2 * (k - 1) + j].astype(f32)
                fin[(n, rows_at(mine)[j])] = total.astype(bf16)

        out.append((
            lambda: over(lambda k, p, j, i, peer: copy(pack.at[n, x, rows_at(p)[j]], zr.at[n, 2 * (k - 1) + j], i, peer)), after3))
        more = 2 * (planes - 1)
        out.append((
            lambda: over(lambda k, p, j, i, peer: copy(fin.at[n, rows_at(mine)[j]], fin.at[n, rows_at(mine)[j]], i + more, peer)),
            lambda: None))
        out.append((
            lambda: [copy(fin.at[n, span(base + j * q, e)], fin.at[n, span(base + j * q, e)], 5 + 2 * more + j, to(hop[1], x))
                     for j in range(2)],
            lambda: None))
        out.append((
            lambda: [copy(fin.at[n, span(o, whole // 2)], fin.at[n, span(o, whole // 2)], 7 + 2 * more, to(hop[0], x))],
            lambda: None))
        return out

    groups = [stages(n) for n in range(4)]

    def small_stage(i):
        if i == 0:
            src, dst, peer = sm, smr.at[0], to(hop[0], x)
        elif i == 1:
            src, dst, peer = sm.at[1 - x], smr.at[1, 0], to(me, 1 - x)
        else:
            src, dst, peer = sm.at[x], smr.at[i, 0], to(hop[i - 1], x)
        return pltpu.make_async_remote_copy(src, dst, ms.at[i], mr.at[i], **peer)

    def small_after(i):
        if i == 0:
            sm[...] += smr[0]
        else:
            sm[x] += smr[i, 0]

    def tick(n, k):
        table = groups[n]
        if k > 0:
            finish(table[k - 1][0]())
            table[k - 1][1]()
            if n == 3 and k - 1 < bits + 1:
                small_stage(k - 1).wait()
                small_after(k - 1)
        if k < len(table):
            start(table[k][0]())
            if n == 3 and k < bits + 1:
                small_stage(k).start()

    def at_point(name, index=None):
        for i, n, k in plan.get(name, ()):
            if index is None:
                tick(n, k)
            else:
                pl.when(index == i)(functools.partial(tick, n, k))

    finish(start_in)
    grad_ref[...] = router_backward(experts, dy_ref, u_ref, probs_ref, hid2, gain_ref, router_ref, aux_ref, stat_ref, live_ref,
                                    back_ref, du_ref, dgate_ref, small_ref)
    finish(first + w_two)
    dv, dg = attend_backward(
        step, seq, images, grad_ref[...], xbuf[...], gain_ref[2:3, :], [watt.at[c] for c in range(3)], watt.at[3],
        qkv, mix, dmix, dqkv, pack.at[0], 0,
    )
    small_ref[LANES + 1:LANES + 2, :] = dg
    grad_ref[...] += dv
    at_point("two")
    second = [load(hid1_h, xbuf, 1), load(qkv1_h, qkv, 2), load(mix1_h, mix, 3)]
    w_one = split.copies(one, watt, wsem.at[0])
    start(second + w_one)

    finish(gelus + w_mlp)
    low = grad_ref[...].astype(bf16)
    fpart = blocks * width // 2
    for b in range(blocks):
        s, off = b * width // fpart, b * width % fpart
        pack[1, s, off:off + width, :] = tn(big[b, 0:rows], low).astype(bf16)
    at_point("out")
    finish(second[:1])
    xn, rs = norm(xbuf[...])
    gain = gain_ref[1:2, :]
    u = (xn * gain).astype(bf16)
    half = big.shape[1] // 2
    for b in range(blocks):
        cols = slice(b * width, (b + 1) * width)
        dz = (big[b, half:half + rows].astype(f32) * nt(low, w2[0, cols, :])).astype(bf16)
        d = nt(dz, w1[0, :, cols])
        if b == 0:
            dubuf[...] = d
        else:
            dubuf[...] += d
        gin = tn(u, dz).astype(bf16)
        for s in range(2):
            pack[2, s, b * part:(b + 1) * part, :] = gin[s * part:(s + 1) * part]
        at_point("in%d" % b)
    dv, dg = norm_back(dubuf[...], xn, rs, gain)
    small_ref[LANES + 3:LANES + 4, :] = dg
    grad_ref[...] += dv
    at_point("mlp")

    pad_store(xbuf, lambda i: tok_ref[i], images, seq, step)
    finish(second[1:] + w_one)
    dv, dg = attend_backward(
        step, seq, images, grad_ref[...], xbuf[...], gain_ref[0:1, :], [watt.at[c] for c in range(3)], watt.at[3],
        qkv, mix, dmix, dqkv, pack.at[3], 0, tick=lambda i: at_point("image", i),
    )
    sm[...] = jnp.zeros(sm.shape, f32)
    for s in range(2):
        cols = slice(s * part, (s + 1) * part)
        sm[s, 0:experts] = small_ref[0:experts, cols]
        sm[s, experts:experts + 1] = dg[:, cols]
        sm[s, experts + 1:experts + 2] = small_ref[LANES + 3:LANES + 4, cols]
        sm[s, experts + 2:experts + 3] = small_ref[LANES + 1:LANES + 2, cols]
        sm[s, experts + 3:experts + 4] = small_ref[LANES:LANES + 1, cols]
    at_point("one")
    grad_ref[...] += dv
    for i in range(images):
        gtok_ref[i] = grad_ref[i * step:i * step + seq, :]

    own.wait()
    each(1, owners, lambda k: send_served(k).wait())
    at_point("rows")

    todo = [(uin_h, 0, 0), (ux_h, 0, 1), (dyin_h, 1, 0), (dyx_h.at[0], 1, 1)]
    moves = [pltpu.make_async_copy(r, stage.at[i % 2], esem.at[i % 2]) for i, (r, _, _) in enumerate(todo)]

    def lane(i):
        return pl.ds(pl.multiple_of(i * width, width), width)

    def chunk(i):
        e, f = i // blocks, i % blocks
        slot = i % 2
        col = pl.ds(pl.multiple_of(f * width, width), width)
        return [pltpu.make_async_copy(we1_h.at[e, :, col], w1.at[0, :, lane(slot)], esem.at[2 + slot]),
                pltpu.make_async_copy(we2_h.at[e, col, :], w2.at[0, lane(slot), :], esem.at[4 + slot])]

    def result(i):
        e, f = i // blocks, i % blocks
        slot = i % 2
        col = pl.ds(pl.multiple_of(f * width, width), width)
        return [pltpu.make_async_copy(w1.at[0, :, lane(2 + slot)], ge1_h.at[e, :, col], osem.at[slot]),
                pltpu.make_async_copy(w2.at[0, lane(2 + slot), :], ge2_h.at[e, col, :], osem.at[2 + slot])]

    moves[0].start()
    start(chunk(0))
    for i, (_, kind, piece) in enumerate(todo):
        if i + 1 < len(todo):
            moves[i + 1].start()
        moves[i].wait()
        for e, v in enumerate(split_rows(stage[i % 2], local)):
            if kind == 1:
                u = big[e, piece * half:(piece + 1) * half]
                v = v * gate_of(u, router_ref[...], experts, me * local + e)
            big[kind * local + e, piece * half:(piece + 1) * half] = v.astype(bf16)
    back = pltpu.make_async_copy(sback_h, stage.at[0], tsem.at[0])
    back.start()
    back.wait()
    grad_ref[...] = (hid2[...] + nn(back_ref[...], stage[0].reshape(back_ref.shape[1], width))) * live_ref[...]
    for i in range(images):
        out_ref[i] = grad_ref[i * step:i * step + seq, :].astype(bf16)
    at_point("output")
    count = local * blocks
    acc1, acc2 = xbuf.at[0:width], dubuf.at[0:width]

    def expert(i, c):
        slot = i % 2
        pl.when(i + 1 < count)(lambda: start(chunk(i + 1)))
        finish(chunk(i))
        e = i // blocks
        for p in range(2):
            u = big[e, p * half:(p + 1) * half]
            dsv = big[local + e, p * half:(p + 1) * half]
            act, slope = gelu_pair(nn(u, w1[0, :, lane(slot)]))
            dz = (slope * nt(dsv, w2[0, lane(slot), :])).astype(bf16)
            g1, g2 = tn(u, dz), tn(act.astype(bf16), dsv)
            if p == 0:
                acc1[...] = g1
                acc2[...] = g2
                at_point("early", i)
            else:
                pl.when(i >= 2)(lambda: finish(result(i - 2)))
                w1[0, :, lane(2 + slot)] = (acc1[...] + g1).astype(bf16)
                w2[0, lane(2 + slot), :] = (acc2[...] + g2).astype(bf16)
        start(result(i))
        at_point("late", i)
        return c

    lax.fori_loop(0, count, expert, 0)
    at_point("end")
    for i in range(max(0, count - 2), count):
        finish(result(i))
    smout_ref[...] = sm[x]


def swap(owners, bit):
    return [(i, i ^ (1 << bit)) for i in range(owners)]


def reduce_all(g, owners, shards):
    me = lax.axis_index("expert")
    bits = owners.bit_length() - 1

    def add(a, b):
        return (a.astype(f32) + b.astype(f32)).astype(bf16)

    def fold(v, bit, axis):
        own = (me >> bit) & 1
        half = v.shape[axis] // 2
        keep = lax.dynamic_slice_in_dim(v, own * half, half, axis)
        send = lax.dynamic_slice_in_dim(v, (1 - own) * half, half, axis)
        return add(keep, lax.ppermute(send, "expert", swap(owners, bit)))

    v = fold(g, 0, 1)
    if shards == 2:
        x = lax.axis_index("shard")
        keep = lax.dynamic_index_in_dim(v, x, 0, keepdims=False)
        send = lax.dynamic_index_in_dim(v, 1 - x, 0, keepdims=False)
        v = add(keep, lax.ppermute(send, "shard", [(0, 1), (1, 0)]))
    else:
        v = lax.psum_scatter(v, "shard", scatter_dimension=0, tiled=True)[0]
    for bit in range(1, bits):
        v = fold(v, bit, 0)
    for bit in reversed(range(bits)):
        own = (me >> bit) & 1
        other = lax.ppermute(v, "expert", swap(owners, bit))
        v = jnp.where(own == 0, jnp.concatenate([v, other]), jnp.concatenate([other, v]))
    return v


def per_device(
    owners, shards, tokens, cotangent, routes, counts, aux_weight, attn_qkv1, attn_out1, mlp_in, mlp_out, gains1,
    attn_qkv2, attn_out2, router, gains2, expert_in, expert_out,
):
    images, seq, width = tokens.shape
    step = padded(seq)
    rows = images * step
    experts = router.shape[1]
    local = expert_in.shape[0]
    ff = mlp_in.shape[1]
    block_rows = -(-local * CAP // 16) * 16
    slots = owners * block_rows
    split = Split(shards)
    expert_swap = functools.partial(lax.all_to_all, axis_name="expert", split_axis=0, concat_axis=0, tiled=True)

    block = (owners, block_rows, width)
    sem = pltpu.SemaphoreType.DMA
    if shards == 2:
        (gains, router_full, stat, live_col, dy, u_out, hidden, block_out, hidden_two, qkv_one, mix_one, qkv_two, mix_two, act, slope,
         u_two, probs, back, w_one, w_up, w_down, w_two, dy_in) = fused_forward(
            owners, experts, local, block, tokens, cotangent, routes, counts, jnp.concatenate([gains1, gains2]), router,
            attn_qkv1, attn_out1, mlp_in, mlp_out, attn_qkv2, attn_out2)
        w_one, w_up, w_down, w_two = [w_one], [w_up], [w_down], [w_two]
    else:
        within = jnp.arange(step, dtype=jnp.int32) < seq
        live = ((jnp.arange(images, dtype=jnp.int32)[:, None] < counts[0]) & within[None, :]).reshape(rows)
        live = live.astype(f32)
        routes_pad = jnp.pad(routes, ((0, 0), (0, step - seq), (0, 0)), constant_values=-1).reshape(rows, 2)
        lanes = jnp.arange(LANES, dtype=jnp.int32)
        loads = jnp.sum(((routes_pad[:, :, None] == lanes) & (live[:, None, None] > 0)).astype(f32), axis=(0, 1))
        loads = jnp.where(lanes == LANES - 1, jnp.sum(live), loads)
        live_col = live[:, None]

        w_one = split.gather([attn_qkv1, attn_out1[None]])
        w_up = split.gather([mlp_in[None]])
        w_down = split.gather([mlp_out[None]])
        w_two = split.gather([attn_qkv2, attn_out2[None]])
        gains = jnp.concatenate([gains1, gains2])
        if shards == 2:
            x = lax.axis_index("shard")
            other = lax.ppermute(gains, "shard", [(0, 1), (1, 0)])
            gains = jnp.where(x == 0, jnp.concatenate([gains, other], 1), jnp.concatenate([other, gains], 1))
            other = lax.ppermute(router, "shard", [(0, 1), (1, 0)])
            router_full = jnp.where(x == 0, jnp.concatenate([router, other]), jnp.concatenate([other, router]))
        else:
            gains = lax.all_gather(gains, "shard", axis=1, tiled=True)
            router_full = lax.all_gather(router, "shard", axis=0, tiled=True)
        gains = gains.astype(f32)
        router_full = jnp.pad(router_full, ((0, 0), (0, LANES - experts)))

        dy, dy_out, disp, back = call(
            functools.partial(route_body, images, seq, local, block_rows),
            [sds((rows, width), bf16), sds((slots, width), bf16), sds((slots, rows), bf16), sds((rows, slots), bf16)],
            [routes_pad, routes_pad.T, live_col, cotangent], flops=2e9, nbytes=6e6,
        )
        block = (owners, block_rows, width)
        dy_in = expert_swap(dy_out.reshape(block))

        sem = pltpu.SemaphoreType.DMA
        attn_scratch = [pltpu.VMEM((4, width, width), bf16), sem((4,))]
        mlp_scratch = [pltpu.VMEM((1, width, ff), bf16), pltpu.VMEM((1, ff, width), bf16), sem((2, 4))]

        def specs(n, ins):
            return [VM] * n + [ANY] * (len(ins) - n)

        ins = [tokens, gains] + w_one
        hidden, qkv_one, mix_one = call(
            functools.partial(block1_body, split, images, seq),
            [sds((rows, width), f32), sds((rows, 3 * width), bf16), sds((rows, width), bf16)],
            ins, attn_scratch, specs(2, ins), flops=4e9, nbytes=8e6,
        )
        ins = [hidden, gains] + w_up + w_down
        block_out, act, slope = call(
            functools.partial(mlp_body, split),
            [sds((rows, width), f32)] + [sds((ff // width, rows, width), bf16)] * 2,
            ins, mlp_scratch, specs(2, ins), flops=6e9, nbytes=12e6,
        )
        ins = [block_out, gains, router_full, disp, live_col, loads[None, :]] + w_two
        hidden_two, qkv_two, mix_two, u_two, probs, stat, u_out = call(
            functools.partial(block2_body, split, images, seq, experts),
            [sds((rows, width), f32), sds((rows, 3 * width), bf16), sds((rows, width), bf16), sds((rows, width), bf16),
             sds((rows, LANES), f32), sds((8, LANES), f32), sds((slots, width), bf16)],
            ins, attn_scratch, specs(6, ins), flops=5e9, nbytes=10e6,
        )

    group = min(4, owners)
    u_in, served, du_back, dgate_back, stat, dy_far, u_far = pl.pallas_call(
        functools.partial(expert_body, owners, shards, local, experts, group),
        out_shape=[sds(block, bf16), sds(block, bf16), sds(block, bf16), sds((owners, 8, LANES), f32), sds((8, LANES), f32),
                   sds((shards - 1,) + block, bf16), sds(block, bf16)],
        in_specs=[VM] * 4 + [ANY] * 2,
        out_specs=[VM] * 5 + [ANY] * 2,
        scratch_shapes=[
            pltpu.VMEM((local, width, ff), bf16), pltpu.VMEM((local, ff, width), bf16), pltpu.VMEM(block, bf16),
            pltpu.VMEM((owners, 8, LANES), f32), pltpu.VMEM((shards, 8, LANES), f32), pltpu.VMEM((owners, 8, LANES), f32),
            sem((2,)), sem((2,)),
        ] + [sem((owners,))] * 10 + [sem((shards,))] * 4,
        compiler_params=pltpu.CompilerParams(vmem_limit_bytes=VMEM_BYTES, collective_id=0, has_side_effects=True),
        cost_estimate=pl.CostEstimate(flops=int(11e9), bytes_accessed=int(15e6), transcendentals=0),
    )(u_out.reshape(block), dy_in, router_full, stat, expert_in, expert_out)
    parts_of = (gains, router_full, aux_weight.reshape(1, 1), stat, live_col, back, dgate_back, tokens, dy, u_two, probs, du_back)
    if shards == 2:
        return fused_backward(Split(1), experts, tokens, parts_of, hidden_two, block_out, hidden, qkv_two, mix_two, qkv_one, mix_one,
                              act, slope, served, u_in, u_far, dy_in, dy_far, expert_in, expert_out, w_two, w_up, w_down, w_one)
    served_back = expert_swap(served).reshape(slots, width)

    if shards == 2:
        us = [u_in, lax.ppermute(u_in, "shard", [(0, 1), (1, 0)])]
    else:
        far = lax.all_gather(u_in, "shard")
        us = [u_in] + [lax.dynamic_index_in_dim(far, (lax.axis_index("shard") + shards - k) % shards, 0, False) for k in range(1, shards)]
    dys = [dy_in] + [dy_far[k] for k in range(shards - 1)]
    parts = 4
    wide = ff // parts
    up_spec = pl.BlockSpec((1, width, wide), lambda e, f: (e, 0, f))
    down_spec = pl.BlockSpec((1, wide, width), lambda e, f: (e, f, 0))
    grad_e_in, grad_e_out = pl.pallas_call(
        functools.partial(expert_grad_body, shards, experts),
        grid=(local, parts),
        out_shape=[sds((local, width, ff), f32), sds((local, ff, width), f32)],
        in_specs=[ANY] * (2 * shards) + [VM, up_spec, down_spec],
        out_specs=[up_spec, down_spec],
        scratch_shapes=[pltpu.VMEM((shards, local, owners * CAP, width), bf16)] * 2 + [pltpu.VMEM((2,) + block, bf16), sem((2,))],
        compiler_params=pltpu.CompilerParams(vmem_limit_bytes=VMEM_BYTES),
        cost_estimate=pl.CostEstimate(flops=int(27e9), bytes_accessed=int(40e6), transcendentals=0),
    )(*us, *dys, router_full, expert_in, expert_out)

    part = width // shards
    back_scratch = [pltpu.VMEM((rows, width), bf16), pltpu.VMEM((rows, 3 * width), bf16)]
    ins = [dy, u_two, probs, hidden_two, block_out, gains, router_full, aux_weight.reshape(1, 1), stat, live_col, back,
           du_back.reshape(slots, width), dgate_back,
           qkv_two, mix_two]
    n = len(ins)
    ins = ins + w_two
    grad_block, pack_two, small = call(
        functools.partial(back2_body, split, images, seq, experts),
        [sds((rows, width), f32), sds((shards, 4 * part, width), bf16), sds((LANES + 8, width), f32)],
        ins, attn_scratch + back_scratch, specs(n, ins), flops=9e9, nbytes=16e6,
    )
    balance_loss = small[LANES + 2, 0]
    late = reduce_all(pack_two, owners, shards)
    ins = [grad_block, hidden, gains, act, slope] + w_up + w_down
    grad_hidden, pack_mlp, dg_two = call(
        functools.partial(mlp_back_body, split),
        [sds((rows, width), f32), sds((shards, part * (ff // width) + ff // shards, width), bf16), sds((1, width), f32)],
        ins, mlp_scratch + [pltpu.VMEM((rows, width), f32)], specs(5, ins), flops=11e9, nbytes=16e6,
    )
    middle = reduce_all(pack_mlp, owners, shards)
    ins = [grad_hidden, tokens, gains, qkv_one, mix_one, small, dg_two] + w_one
    grad_tokens, pack_one = call(
        functools.partial(back1_body, split, images, seq, experts),
        [sds((images, seq, width), f32), sds((shards, 4 * part + 64, width), bf16)],
        ins, attn_scratch + [pltpu.VMEM((rows, width), f32)] + back_scratch, specs(7, ins), flops=9e9, nbytes=14e6,
    )
    early = reduce_all(pack_one, owners, shards)
    (output,) = call(
        functools.partial(output_body, images, seq), [sds((images, seq, width), bf16)],
        [hidden_two, back, served_back, live_col], [pltpu.VMEM((rows, width), f32)], flops=1e9, nbytes=5e6,
    )

    late, middle, early = late.astype(f32), middle.astype(f32), early.astype(f32)
    up = middle[:part * (ff // width)].reshape(ff // width, part, width).transpose(1, 0, 2).reshape(part, ff)
    tail = early[4 * part:, :part]
    return (
        output,
        balance_loss,
        grad_tokens,
        early[:3 * part].reshape(3, part, width),
        early[3 * part:4 * part],
        up,
        middle[part * (ff // width):],
        tail[32:34],
        late[:3 * part].reshape(3, part, width),
        late[3 * part:],
        tail[:experts].T,
        tail[34:36],
        grad_e_in,
        grad_e_out,
    )


PLAN = [
    ("two", None, 0),
    ("out", None, 0), ("out", None, 1),
    ("in1", None, 1),
    ("mlp", None, 0), ("mlp", None, 2),
    ("image", 0, 2), ("image", 0, 0), ("image", 0, 1), ("image", 1, 1), ("image", 2, 0),
    ("one", None, 3), ("one", None, 2), ("one", None, 1),
    ("rows", None, 3), ("rows", None, 0), ("rows", None, 2),
    ("output", None, 1),
    ("early", 0, 2), ("late", 0, 3), ("late", 0, 0),
    ("early", 1, 1), ("late", 1, 3), ("late", 1, 2), ("late", 1, 0),
    ("early", 2, 1), ("late", 2, 2),
    ("early", 3, 3), ("early", 3, 2),
    ("early", 4, 3), ("late", 5, 3), ("late", 6, 3),
]


def fused_backward(split, experts, tokens, parts_of, hidden_two, block_out, hidden, qkv_two, mix_two, qkv_one, mix_one,
                   act, slope, served, u_in, u_far, dy_in, dy_far, expert_in, expert_out, w_two, w_up, w_down, w_one):
    images, seq, width = tokens.shape
    rows = hidden.shape[0]
    local, _, ff = expert_in.shape
    block = served.shape
    owners = block[0]
    bits = owners.bit_length() - 1
    whole = 2 * width
    part = width // 2
    blocks = ff // width
    stages = 7
    left = [0] * 4
    plan = {}
    for name, index, n in PLAN:
        if left[n] <= stages and (index is None or index < (images if name == "image" else local * blocks)):
            plan.setdefault(name, []).append((index, n, left[n]))
            left[n] += 1
    plan["end"] = [(None, n, k) for k in range(stages + 1) for n in range(4) if k >= left[n]]
    small_rows = -(-(experts + 4) // 8) * 8
    sem = pltpu.SemaphoreType.DMA
    ins = list(parts_of) + [hidden_two, block_out, hidden, qkv_two, mix_two, qkv_one, mix_one, act, slope, served, u_in, u_far, dy_in,
                            dy_far, expert_in, expert_out] + w_two + w_up + w_down + w_one
    vmem = 8
    big_rows = 2 * owners * CAP
    nsem = 8 + 4 * (owners // 4 - 1)
    V = pltpu.VMEM
    outs = pl.pallas_call(
        functools.partial(backward_body, split, images, seq, experts, local, owners, plan),
        out_shape=[
            sds((images, seq, width), bf16), sds((images, seq, width), f32), sds((4, whole, width), bf16),
            sds((small_rows, part), f32), sds((LANES + 8, width), f32), sds(expert_in.shape, bf16), sds(expert_out.shape, bf16),
            sds(block, bf16),
        ],
        in_specs=[VM] * vmem + [ANY] * (len(ins) - vmem),
        out_specs=[VM] * 5 + [ANY] * 3,
        scratch_shapes=[
            V((rows, width), f32), V((rows, width), f32), V((rows, width), f32), V((rows, width), f32),
            V((rows, 3 * width), bf16), V((rows, width), bf16), V((rows, width), bf16), V((rows, 3 * width), bf16),
            V((4, width, width), bf16), V((1, width, ff), bf16), V((1, ff, width), bf16), V((blocks, big_rows, width), bf16),
            V((2,) + block, bf16),
            V((4, 2, whole, width), bf16), V((4, 2, whole // 2, width), bf16), V((4, whole // 4, width), bf16),
            V((4, 2, whole // 8, width), bf16), V((4, whole // 8, width), bf16), V((4, whole // 8, width), bf16),
            V((4, 2 * (owners // 4 - 1), whole // (2 * owners), width), bf16),
            V((2, small_rows, part), f32), V((bits + 1, 2, small_rows, part), f32),
            sem((8 + 2 * blocks,)), sem((3, 4)), sem((owners,)), sem((owners,)),
            sem((4, nsem)), sem((4, nsem)), sem((bits + 1,)), sem((bits + 1,)), sem((6,)), sem((4,)), sem((1,)),
        ],
        compiler_params=pltpu.CompilerParams(vmem_limit_bytes=63 << 20, collective_id=1, has_side_effects=True),
        cost_estimate=pl.CostEstimate(flops=int(60e9), bytes_accessed=int(80e6), transcendentals=0),
    )(*ins)
    output, grad_tokens, fin, tail, small, grad_e_in, grad_e_out = outs[:7]
    qkv1, out1, up, down, qkv2, out2, grad_e_in, grad_e_out = widen(fin, grad_e_in, grad_e_out, part, width, blocks)
    return (
        output, small[LANES + 2, 0], grad_tokens, qkv1, out1, up, down, tail[experts:experts + 2], qkv2, out2, tail[:experts].T,
        tail[experts + 2:experts + 4], grad_e_in, grad_e_out,
    )


def widen_body(sixth, fin_ref, e1_ref, e2_ref, qkv1_ref, out1_ref, up_ref, down_ref, qkv2_ref, out2_ref, g1_ref, g2_ref):
    i = pl.program_id(0)
    g1_ref[...] = e1_ref[...].astype(f32)
    g2_ref[...] = e2_ref[...].astype(f32)
    up_ref[...] = fin_ref[2].astype(f32)
    down_ref[...] = fin_ref[1].astype(f32)

    @pl.when(i < sixth)
    def _():
        qkv1_ref[0] = fin_ref[3].astype(f32)
        qkv2_ref[0] = fin_ref[0].astype(f32)

    @pl.when(i >= sixth)
    def _():
        out1_ref[...] = fin_ref[3].astype(f32)
        out2_ref[...] = fin_ref[0].astype(f32)


def widen(fin, e1, e2, part, width, blocks):
    steps = 2 * blocks
    some = fin.shape[1] // steps
    per = part // some
    sixth = 3 * per
    local, _, ff = e1.shape
    qkv = pl.BlockSpec((1, some, width), lambda i: (jnp.minimum(i, sixth - 1) // per, jnp.minimum(i, sixth - 1) % per, 0))
    out = pl.BlockSpec((some, width), lambda i: (jnp.maximum(i - sixth, 0), 0))
    return pl.pallas_call(
        functools.partial(widen_body, sixth),
        grid=(steps,),
        out_shape=[sds((3, part, width), f32), sds((part, width), f32), sds((part, blocks * width), f32), sds((fin.shape[1], width), f32),
                   sds((3, part, width), f32), sds((part, width), f32), sds(e1.shape, f32), sds(e2.shape, f32)],
        in_specs=[pl.BlockSpec((4, some, width), lambda i: (0, i, 0)),
                  pl.BlockSpec((local, width // steps, ff), lambda i: (0, i, 0)),
                  pl.BlockSpec((local, ff // steps, width), lambda i: (0, i, 0))],
        out_specs=[qkv, out, pl.BlockSpec((some, width), lambda i: (i % per, i // per)), pl.BlockSpec((some, width), lambda i: (i, 0)),
                   qkv, out, pl.BlockSpec((local, width // steps, ff), lambda i: (0, i, 0)),
                   pl.BlockSpec((local, ff // steps, width), lambda i: (0, i, 0))],
        compiler_params=pltpu.CompilerParams(vmem_limit_bytes=VMEM_BYTES),
        cost_estimate=pl.CostEstimate(flops=0, bytes_accessed=int(40e6), transcendentals=0),
    )(fin, e1, e2)


def solution(mesh):
    owners, shards = mesh.shape["expert"], mesh.shape["shard"]
    both = ("expert", "shard")
    return jax.shard_map(
        functools.partial(per_device, owners, shards),
        mesh=mesh,
        in_specs=(
            P(both, None, None), P(both, None, None), P(both, None, None), P(both), P(),
            P(None, "shard", None), P("shard", None), P("shard", None), P("shard", None), P(None, "shard"),
            P(None, "shard", None), P("shard", None), P("shard", None), P(None, "shard"),
            P("expert", None, None), P("expert", None, None),
        ),
        out_specs=(
            P(both, None, None), P(), P(both, None, None),
            P(None, "shard", None), P("shard", None), P("shard", None), P("shard", None), P(None, "shard"),
            P(None, "shard", None), P("shard", None), P("shard", None), P(None, "shard"),
            P("expert", None, None), P("expert", None, None),
        ),
        check_vma=False,
    )
```

```python
import functools

import jax
import jax.numpy as jnp
from jax import lax
from jax.experimental import pallas as pl
from jax.experimental.pallas import tpu as pltpu
from jax.sharding import PartitionSpec as P

HEADS = 8
CAP = 40
EPS = 1e-06
NEG = -1e30
LANES = 128
f32 = jnp.float32
bf16 = jnp.bfloat16
ANY = pl.BlockSpec(memory_space=pl.ANY)
VM = pl.BlockSpec(memory_space=pltpu.VMEM)
VMEM_BYTES = 58 << 20


def nn(a, b):
    return lax.dot_general(a, b, (((1,), (0,)), ((), ())), preferred_element_type=f32)


def nt(a, b):
    return lax.dot_general(a, b, (((1,), (1,)), ((), ())), preferred_element_type=f32)


def tn(a, b):
    return lax.dot_general(a, b, (((0,), (0,)), ((), ())), preferred_element_type=f32)


def sds(shape, dtype):
    return jax.ShapeDtypeStruct(shape, dtype)


def padded(seq):
    return -(-seq // 16) * 16


def norm(x):
    xc = x - jnp.mean(x, axis=-1, keepdims=True)
    rs = lax.rsqrt(jnp.mean(xc * xc, axis=-1, keepdims=True) + EPS)
    return xc * rs, rs


def norm_back(dyn, xn, rs, gain):
    dgain = jnp.sum(dyn * xn, axis=0, keepdims=True)
    dxn = dyn * gain
    dv = dxn - jnp.mean(dxn, axis=-1, keepdims=True)
    dv = (dv - xn * jnp.mean(dxn * xn, axis=-1, keepdims=True)) * rs
    return dv, dgain


def gelu_pair(z):
    a = jnp.abs(z)
    t = 1.0 / (1.0 + (0.3275911 * 0.7071067811865476) * a)
    e = jnp.exp(-0.5 * (z * z))
    q = t * (0.127414796 + t * (-0.142248368 + t * (0.7107068705 + t * (-0.7265760135 + t * 0.5307027145))))
    q = q * e
    phi = jnp.where(z >= 0.0, 1.0 - q, q)
    return z * phi, phi + z * (e * 0.3989422804014327)


class Split:
    def __init__(self, shards):
        self.pair = shards == 2
        self.shards = shards

    def gather(self, owns):
        if not self.pair:
            whole = [lax.all_gather(o, "shard", axis=1, tiled=True) for o in owns]
            return whole
        core = lax.axis_index("expert") % 2
        owners = lax.axis_size("expert")
        half = owns[0].shape[1] // 2
        send = jnp.concatenate([lax.dynamic_slice_in_dim(o, core * half, half, 1) for o in owns], axis=0)
        far = lax.ppermute(send, "shard", [(0, 1), (1, 0)])
        near = lax.ppermute(far, "expert", [(i, i ^ 1) for i in range(owners)])
        return list(owns) + [far, near]

    def count(self, owns):
        return owns + 2 if self.pair else owns

    def copies(self, refs, full, sems):
        out = []
        if not self.pair:
            at = 0
            for i, r in enumerate(refs):
                n = r.shape[0]
                out.append(pltpu.make_async_copy(r, full.at[at:at + n], sems.at[i]))
                at += n
            return out
        me = lax.axis_index("shard")
        core = lax.axis_index("expert") % 2
        rows = refs[0].shape[1]
        half = rows // 2
        at = 0
        for i, r in enumerate(refs[:-2]):
            n = r.shape[0]
            out.append(pltpu.make_async_copy(r, full.at[at:at + n, pl.ds(me * rows, rows), :], sems.at[i]))
            at += n
        base = (1 - me) * rows
        k = len(refs) - 2
        out.append(pltpu.make_async_copy(refs[k], full.at[:, pl.ds(base + core * half, half), :], sems.at[k]))
        out.append(pltpu.make_async_copy(refs[k + 1], full.at[:, pl.ds(base + (1 - core) * half, half), :], sems.at[k + 1]))
        return out


def start(copies):
    for c in copies:
        c.start()


def finish(copies):
    for c in copies:
        c.wait()


def call(body, outs, ins, scratch=(), specs=None, flops=0, nbytes=0, **kw):
    return pl.pallas_call(
        body,
        out_shape=outs,
        in_specs=specs or [VM] * len(ins),
        out_specs=[VM] * len(outs),
        scratch_shapes=list(scratch),
        compiler_params=pltpu.CompilerParams(vmem_limit_bytes=VMEM_BYTES),
        cost_estimate=pl.CostEstimate(flops=int(flops), bytes_accessed=int(nbytes), transcendentals=0),
        **kw,
    )(*ins)


def pad_store(ref, block, images, seq, step):
    ref[...] = jnp.zeros(ref.shape, ref.dtype)
    for i in range(images):
        ref[i * step:i * step + seq, :] = block(i).astype(ref.dtype)


def slot_start(expert, local, block):
    owner = jnp.floor((expert.astype(f32) + 0.5) * (1.0 / local))
    return owner * block + (expert.astype(f32) - owner * local) * CAP


def route_body(images, seq, local, block, r_ref, rt_ref, live_ref, cot_ref, dy_ref, dyd_ref, disp_ref, back_ref):
    step = r_ref.shape[0] // images
    pad_store(dy_ref, lambda i: cot_ref[i], images, seq, step)
    dy_ref[...] = (dy_ref[...].astype(f32) * live_ref[...]).astype(bf16)
    route_tables(local, block, r_ref, rt_ref, disp_ref, back_ref)
    dyd_ref[...] = nn(disp_ref[...], dy_ref[...]).astype(bf16)


def route_tables(local, block, r_ref, rt_ref, disp_ref, back_ref):
    rows = r_ref.shape[0]
    slots = disp_ref.shape[0]
    lane = lax.broadcasted_iota(jnp.int32, (rows, LANES), 1)
    hit = (r_ref[:, 0:1] == lane) | (r_ref[:, 1:2] == lane)
    ti = lax.broadcasted_iota(jnp.int32, (rows, rows), 0)
    tj = lax.broadcasted_iota(jnp.int32, (rows, rows), 1)
    place = nn((ti > tj).astype(f32).astype(bf16), hit.astype(f32).astype(bf16))
    place = jnp.where(hit, place, -1.0).astype(bf16)
    off = lax.broadcasted_iota(jnp.int32, (LANES, slots), 1).astype(f32) - slot_start(
        lax.broadcasted_iota(jnp.int32, (LANES, slots), 0), local, block)
    spread = ((off >= 0) & (off < CAP)).astype(f32)
    within = jnp.sum(spread * off, axis=0, keepdims=True)
    within = jnp.where(jnp.sum(spread, axis=0, keepdims=True) > 0, within, -2.0)
    back_ref[...] = (nn(place, spread.astype(bf16)) == within).astype(f32).astype(bf16)
    sub = lax.broadcasted_iota(jnp.int32, (LANES, rows), 0)
    hit_t = (rt_ref[0:1, :] == sub) | (rt_ref[1:2, :] == sub)
    place_t = nn(hit_t.astype(f32).astype(bf16), (ti < tj).astype(f32).astype(bf16))
    place_t = jnp.where(hit_t, place_t, -1.0).astype(bf16)
    off = lax.broadcasted_iota(jnp.int32, (slots, LANES), 0).astype(f32) - slot_start(
        lax.broadcasted_iota(jnp.int32, (slots, LANES), 1), local, block)
    spread_t = ((off >= 0) & (off < CAP)).astype(f32)
    within_t = jnp.sum(spread_t * off, axis=1, keepdims=True)
    within_t = jnp.where(jnp.sum(spread_t, axis=1, keepdims=True) > 0, within_t, -2.0)
    disp_ref[...] = (nn(spread_t.astype(bf16), place_t) == within_t).astype(f32).astype(bf16)
    return hit.astype(f32)


def attend_forward(step, seq, images, x, gain, wq, wo, qkv_ref, mix_ref, tick=None, image_tick=None):
    width = x.shape[1]
    head = width // HEADS
    scale = head ** -0.5
    xn, _ = norm(x)
    a = (xn * gain).astype(bf16)
    for c in range(3):
        qkv_ref[:, c * width:(c + 1) * width] = nn(a, wq[c][...]).astype(bf16)
    if tick is not None:
        tick()
    lane = lax.broadcasted_iota(jnp.int32, (1, LANES), 1)
    col = lax.broadcasted_iota(jnp.int32, (1, step), 1)
    per = LANES // head

    def image(i, _):
        at = pl.ds(pl.multiple_of(i * step, step), step)
        for hp in range(width // LANES):
            q = qkv_ref[at, hp * LANES:(hp + 1) * LANES]
            k = qkv_ref[at, width + hp * LANES:width + (hp + 1) * LANES]
            v = qkv_ref[at, 2 * width + hp * LANES:2 * width + (hp + 1) * LANES]
            got = None
            for h in range(per):
                mine = (lane >= h * head) & (lane < (h + 1) * head)
                qm = q * jnp.where(mine, scale, 0.0).astype(bf16)
                s = jnp.where(col < seq, nt(qm, k), NEG)
                e = jnp.exp(s - jnp.max(s, axis=-1, keepdims=True))
                p = (e * (1.0 / jnp.sum(e, axis=-1, keepdims=True))).astype(bf16)
                o = nn(p, v)
                got = o if got is None else jnp.where(mine, o, got)
            mix_ref[at, hp * LANES:(hp + 1) * LANES] = got.astype(bf16)
        if image_tick is not None:
            image_tick(i)
        return 0

    lax.fori_loop(0, images, image, 0)
    return x + nn(mix_ref[...], wo[...])


def attend_backward(step, seq, images, grad, x, gain, wq, wo, qkv_ref, mix_ref, dmix_ref, dqkv_ref, pack_ref, base,
                    tick=None):
    width = x.shape[1]
    head = width // HEADS
    scale = head ** -0.5
    shards = pack_ref.shape[0]
    part = width // shards
    low = grad.astype(bf16)
    dwo = tn(mix_ref[...], low).astype(bf16)
    for s in range(shards):
        pack_ref[s, base + 3 * part:base + 4 * part, :] = dwo[s * part:(s + 1) * part]
    dmix_ref[...] = nt(low, wo[...]).astype(bf16)
    lane = lax.broadcasted_iota(jnp.int32, (1, LANES), 1)
    key = lax.broadcasted_iota(jnp.int32, (step, 1), 0)
    per = LANES // head

    def image(i, _):
        at = pl.ds(pl.multiple_of(i * step, step), step)
        for hp in range(width // LANES):
            q = qkv_ref[at, hp * LANES:(hp + 1) * LANES]
            k = qkv_ref[at, width + hp * LANES:width + (hp + 1) * LANES]
            v = qkv_ref[at, 2 * width + hp * LANES:2 * width + (hp + 1) * LANES]
            do = dmix_ref[at, hp * LANES:(hp + 1) * LANES]
            dq = dk = dv = None
            for h in range(per):
                mine = (lane >= h * head) & (lane < (h + 1) * head)
                scaled = jnp.where(mine, scale, 0.0).astype(bf16)
                km = k * scaled
                s = jnp.where(key < seq, nt(km, q), NEG)
                e = jnp.exp(s - jnp.max(s, axis=0, keepdims=True))
                p = e * (1.0 / jnp.sum(e, axis=0, keepdims=True))
                dom = do * jnp.where(mine, 1.0, 0.0).astype(bf16)
                dp = nt(v, dom)
                ds = (p * (dp - jnp.sum(p * dp, axis=0, keepdims=True))).astype(bf16)
                hv = nn(p.astype(bf16), dom)
                hk = nn(ds, q * scaled)
                hq = tn(ds, km)
                dq, dk, dv = (hq, hk, hv) if dq is None else (dq + hq, dk + hk, dv + hv)
            dqkv_ref[at, hp * LANES:(hp + 1) * LANES] = dq.astype(bf16)
            dqkv_ref[at, width + hp * LANES:width + (hp + 1) * LANES] = dk.astype(bf16)
            dqkv_ref[at, 2 * width + hp * LANES:2 * width + (hp + 1) * LANES] = dv.astype(bf16)
        if tick is not None:
            tick(i)
        return 0

    lax.fori_loop(0, images, image, 0)
    xn, rs = norm(x)
    a = (xn * gain).astype(bf16)
    da = None
    for c in range(3):
        d = dqkv_ref[:, c * width:(c + 1) * width]
        dw = tn(a, d).astype(bf16)
        for s in range(shards):
            pack_ref[s, base + c * part:base + (c + 1) * part, :] = dw[s * part:(s + 1) * part]
        one = nt(d, wq[c][...])
        da = one if da is None else da + one
    return norm_back(da, xn, rs, gain)


def block1_body(split, images, seq, x_ref, gain_ref, *refs):
    n = split.count(2)
    pieces, (hidden_ref, qkv_ref, mix_ref, w, sems) = refs[:n], refs[n:]
    copies = split.copies(pieces, w, sems)
    start(copies)
    step = hidden_ref.shape[0] // images
    pad_store(hidden_ref, lambda i: x_ref[i], images, seq, step)
    finish(copies)
    hidden_ref[...] = attend_forward(
        step, seq, images, hidden_ref[...], gain_ref[0:1, :], [w.at[c] for c in range(3)], w.at[3], qkv_ref, mix_ref
    )


def mlp_body(split, hidden_ref, gain_ref, *refs):
    n = 2 * split.count(1)
    pieces, (out_ref, act_ref, slope_ref, w1, w2, sems) = refs[:n], refs[n:]
    half = n // 2
    copies = split.copies(pieces[:half], w1, sems.at[0]) + split.copies(pieces[half:], w2, sems.at[1])
    start(copies)
    hidden = hidden_ref[...]
    xn, _ = norm(hidden)
    u = (xn * gain_ref[1:2, :]).astype(bf16)
    out_ref[...] = hidden
    finish(copies)
    wide = act_ref.shape[2]
    for b in range(act_ref.shape[0]):
        at = slice(b * wide, (b + 1) * wide)
        act, slope = gelu_pair(nn(u, w1[0, :, at]))
        act = act.astype(bf16)
        act_ref[b] = act
        slope_ref[b] = slope.astype(bf16)
        out_ref[...] += nn(act, w2[0, at, :])


def router_probs(u, router, experts):
    lane = lax.broadcasted_iota(jnp.int32, (1, LANES), 1)
    logits = jnp.where(lane < experts, nn(u, router), NEG)
    e = jnp.exp(logits - jnp.max(logits, axis=-1, keepdims=True))
    return e * (1.0 / jnp.sum(e, axis=-1, keepdims=True))


def block2_body(split, images, seq, experts, x_ref, gain_ref, router_ref, disp_ref, live_ref, load_ref, *refs):
    n = split.count(2)
    pieces, (hidden_ref, qkv_ref, mix_ref, u_ref, probs_ref, sum_ref, ud_ref, w, sems) = refs[:n], refs[n:]
    copies = split.copies(pieces, w, sems)
    start(copies)
    finish(copies)
    step = hidden_ref.shape[0] // images
    hidden = attend_forward(
        step, seq, images, x_ref[...], gain_ref[2:3, :], [w.at[c] for c in range(3)], w.at[3], qkv_ref, mix_ref
    )
    hidden_ref[...] = hidden
    xn, _ = norm(hidden)
    u = (xn * gain_ref[3:4, :]).astype(bf16)
    u_ref[...] = u
    ud_ref[...] = nn(disp_ref[...], u).astype(bf16)
    probs = router_probs(u, router_ref[...], experts)
    probs_ref[...] = probs
    sums = jnp.sum(probs * live_ref[...], axis=0, keepdims=True)
    sum_ref[...] = jnp.concatenate([load_ref[...], sums, jnp.zeros((6, LANES), f32)], axis=0)


def forward_body(images, seq, experts, local, owners, *refs):
    (r_ref, rt_ref, counts_ref, tok_ref, cot_ref, gain_ref, router_ref, q1_h, o1_h, up_h, down_h, q2_h, o2_h,
     gains_out, router_out, stat_out, live_out,
     dy_o, uout_o, hid1_o, x2_o, hid2_o, qkv1_o, mix1_o, qkv2_o, mix2_o, act_o, slope_o, u_o, probs_o, back_o,
     wa_o, wu_o, wd_o, wb_o, dyin_o,
     wa, wu, wd, wb, dy, slot_rows, disp, back, hid1, x2, hid2, qkv1, mix1, qkv2, mix2, act, slope, u, probs, gx,
     lsem, osem, ks, kr, vs, vr) = refs
    me, x = lax.axis_index("expert"), lax.axis_index("shard")
    bits = owners.bit_length() - 1
    b0, b1 = me % 2, (me // 2) % 2
    core, side = me + 1 - 2 * b0, me + (1 - 2 * b1) * 2
    rows, width = dy.shape
    step = rows // images
    part = width // 2
    ff = wd.shape[1]
    fpart = ff // 2

    def to(e, s):
        return dict(device_id=(e, s), device_id_type=pl.DeviceIdType.MESH)

    def each(lo, hi, f):
        lax.fori_loop(lo, hi, lambda k, c: (f(k), c)[1], 0)

    barrier = pltpu.get_barrier_semaphore()
    each(1, owners, lambda k: pl.semaphore_signal(barrier, inc=1, **to(xor(me, k, bits), x)))
    pl.semaphore_signal(barrier, inc=1, **to(me, 1 - x))

    def at(first, size):
        return pl.ds(pl.multiple_of(first, 64), size)

    mine, theirs = x * part, (1 - x) * part
    loads = [
        pltpu.make_async_copy(q1_h, wa.at[0:3, at(mine, part)], lsem.at[0]),
        pltpu.make_async_copy(o1_h, wa.at[3, at(mine, part)], lsem.at[1]),
        pltpu.make_async_copy(up_h, wu.at[0, at(mine, part)], lsem.at[2]),
        pltpu.make_async_copy(down_h, wd.at[0, at(x * fpart, fpart)], lsem.at[3]),
        pltpu.make_async_copy(q2_h, wb.at[0:3, at(mine, part)], lsem.at[4]),
        pltpu.make_async_copy(o2_h, wb.at[3, at(mine, part)], lsem.at[5]),
    ]
    start(loads)
    router_out[at(mine, part), :] = router_ref[...]
    pl.semaphore_wait(barrier, owners)

    def remote(src, dst, i, peer):
        return pltpu.make_async_remote_copy(src, dst, ks.at[i], kr.at[i], **peer)

    far, near, over = to(me, 1 - x), to(core, x), to(side, x)
    half, quarter, fquarter = part // 2, part // 4, fpart // 4
    p = b0 * 2 + b1
    h = b0 * half
    here = at(theirs + h, half)
    moves = {
        "small": [lambda: remote(gain_ref, gx, 0, far), lambda: remote(router_ref, router_out.at[at(mine, part), :], 1, far)],
        "ax": [lambda: remote(q1_h.at[:, at(h, half)], wa.at[0:3, at(mine + h, half)], 2, far),
               lambda: remote(o1_h.at[at(h, half)], wa.at[3, at(mine + h, half)], 3, far)],
        "ac": [lambda: remote(wa.at[:, here], wa.at[:, here], 4, near)],
        "ux": [lambda: remote(up_h.at[at(p * quarter, quarter)], wu.at[0, at(mine + p * quarter, quarter)], 5, far)],
        "uy": [lambda: remote(wu.at[0, at(theirs + p * quarter, quarter)], wu.at[0, at(theirs + p * quarter, quarter)], 6, over)],
        "uc": [lambda: remote(wu.at[0, here], wu.at[0, here], 7, near)],
        "dx": [lambda: remote(down_h.at[at(p * fquarter, fquarter)], wd.at[0, at(x * fpart + p * fquarter, fquarter)], 8, far)],
        "dy": [lambda: remote(wd.at[0, at((1 - x) * fpart + p * fquarter, fquarter)],
                              wd.at[0, at((1 - x) * fpart + p * fquarter, fquarter)], 9, over)],
        "dc": [lambda: remote(wd.at[0, at((1 - x) * fpart + b0 * 2 * fquarter, 2 * fquarter)],
                              wd.at[0, at((1 - x) * fpart + b0 * 2 * fquarter, 2 * fquarter)], 10, near)],
        "bx": [lambda: remote(q2_h.at[:, at(p * quarter, quarter)], wb.at[0:3, at(mine + p * quarter, quarter)], 11, far),
               lambda: remote(o2_h.at[at(p * quarter, quarter)], wb.at[3, at(mine + p * quarter, quarter)], 12, far)],
        "by": [lambda: remote(wb.at[:, at(theirs + p * quarter, quarter)], wb.at[:, at(theirs + p * quarter, quarter)], 13, over)],
        "bc": [lambda: remote(wb.at[:, here], wb.at[:, here], 14, near)],
    }

    def go(*names):
        for n in names:
            for m in moves[n]:
                m().start()

    def done(*names):
        for n in names:
            for m in moves[n]:
                m().wait()

    def send_dy(k):
        q = xor(me, k, bits)
        return pltpu.make_async_remote_copy(slot_rows.at[0, q], dyin_o.at[me], vs.at[k], vr.at[k], **to(q, x))

    out = []

    def keep(src, dst):
        c = pltpu.make_async_copy(src, dst, osem.at[len(out)])
        c.start()
        out.append(c)

    go("ax", "small")
    row = lax.broadcasted_iota(jnp.int32, (rows, 1), 0)
    live = ((row < counts_ref[0] * step) & (r_ref[:, 0:1] >= 0)).astype(f32)
    live_out[...] = live
    pad_store(dy, lambda i: cot_ref[i], images, seq, step)
    dy[...] = (dy[...].astype(f32) * live).astype(bf16)
    keep(dy, dy_o)
    hit = route_tables(local, slot_rows.shape[2], r_ref, rt_ref, disp, back)
    keep(back, back_o)
    slot_rows[0] = nn(disp[...], dy[...]).astype(bf16).reshape(slot_rows.shape[1:])
    keep(slot_rows.at[0, me], dyin_o.at[me])
    lane = lax.broadcasted_iota(jnp.int32, (1, LANES), 1)
    load = jnp.where(lane == LANES - 1, jnp.sum(live, axis=0, keepdims=True), jnp.sum(hit * live, axis=0, keepdims=True))
    done("ax")
    go("ac", "ux", "dx")
    planes = owners // 4
    each(0, planes, lambda k: send_dy(4 * (planes - 1 - k) + 1).start())
    each(0, planes - 1, lambda k: send_dy(4 * (planes - 1 - k)).start())
    pad_store(hid1, lambda i: tok_ref[i], images, seq, step)
    done("small")
    own_gain, far_gain = gain_ref[...], gx[...]
    gains = jnp.where(x == 0, jnp.concatenate([own_gain, far_gain], axis=1), jnp.concatenate([far_gain, own_gain], axis=1))
    gains_out[...] = gains
    finish(loads)
    done("ac")
    keep(wa, wa_o)

    def first_tick():
        go("bx")

    def first_image(i):
        @pl.when(i == 0)
        def _():
            done("ux")
            go("uy")

        @pl.when(i == 1)
        def _():
            done("dx")
            go("dy")

        @pl.when(i == 2)
        def _():
            done("uy")
            go("uc")

    hid1[...] = attend_forward(step, seq, images, hid1[...], gains[0:1], [wa.at[c] for c in range(3)], wa.at[3], qkv1, mix1,
                               first_tick, first_image)
    keep(hid1, hid1_o)
    keep(qkv1, qkv1_o)
    keep(mix1, mix1_o)

    done("uc")
    keep(wu, wu_o)
    xn, _ = norm(hid1[...])
    a = (xn * gains[1:2]).astype(bf16)
    for b in range(act.shape[0]):
        one, two = gelu_pair(nn(a, wu[0, :, b * width:(b + 1) * width]))
        act[b] = one.astype(bf16)
        slope[b] = two.astype(bf16)
        if b == 0:
            done("bx")
            go("by")
        if b == 1:
            done("dy")
            go("dc")
            each(0, planes, lambda k: send_dy(4 * (planes - 1 - k) + 3).start())
            each(0, planes, lambda k: send_dy(4 * (planes - 1 - k) + 2).start())
    keep(slope, slope_o)
    keep(act, act_o)
    done("dc")
    keep(wd, wd_o)
    total = hid1[...]
    for b in range(act.shape[0]):
        total = total + nn(act[b], wd[0, b * width:(b + 1) * width, :])
        if b == 0:
            done("by")
            go("bc")
    x2[...] = total
    done("bc")
    keep(wb, wb_o)
    keep(x2, x2_o)

    hid2[...] = attend_forward(step, seq, images, x2[...], gains[2:3], [wb.at[c] for c in range(3)], wb.at[3], qkv2, mix2)
    keep(qkv2, qkv2_o)
    keep(mix2, mix2_o)
    keep(hid2, hid2_o)
    xn, _ = norm(hid2[...])
    u[...] = (xn * gains[3:4]).astype(bf16)
    keep(u, u_o)
    slot_rows[1] = nn(disp[...], u[...]).astype(bf16).reshape(slot_rows.shape[1:])
    keep(slot_rows.at[1], uout_o)
    probs[...] = router_probs(u[...], router_out[...], experts)
    keep(probs, probs_o)
    sums = jnp.sum(probs[...] * live, axis=0, keepdims=True)
    stat_out[...] = jnp.concatenate([load, sums, jnp.zeros((6, LANES), f32)], axis=0)
    each(1, owners, lambda k: send_dy(k).wait())
    finish(out)


def fused_forward(owners, experts, local, block, tokens, cotangent, routes, counts, gains, router, attn_qkv1, attn_out1, mlp_in, mlp_out,
                  attn_qkv2, attn_out2):
    images, seq, width = tokens.shape
    step = padded(seq)
    rows = images * step
    ff = mlp_in.shape[1]
    slots = owners * block[1]
    blocks = ff // width
    part = width // 2
    routes_pad = jnp.pad(routes, ((0, 0), (0, step - seq), (0, 0)), constant_values=-1).reshape(rows, 2)
    gains = jnp.pad(gains, ((0, 4), (0, 0))).astype(f32)
    router = jnp.pad(router, ((0, 0), (0, LANES - experts)))
    V, sem = pltpu.VMEM, pltpu.SemaphoreType.DMA
    kept = [
        ((rows, width), bf16), (block, bf16), ((rows, width), f32), ((rows, width), f32), ((rows, width), f32),
        ((rows, 3 * width), bf16), ((rows, width), bf16), ((rows, 3 * width), bf16), ((rows, width), bf16),
        ((blocks, rows, width), bf16), ((blocks, rows, width), bf16), ((rows, width), bf16), ((rows, LANES), f32), ((rows, slots), bf16),
        ((4, width, width), bf16), ((1, width, ff), bf16), ((1, ff, width), bf16), ((4, width, width), bf16), (block, bf16),
    ]
    return pl.pallas_call(
        functools.partial(forward_body, images, seq, experts, local, owners),
        out_shape=[sds((8, width), f32), sds((width, LANES), bf16), sds((8, LANES), f32), sds((rows, 1), f32)]
        + [sds(shape, dtype) for shape, dtype in kept],
        in_specs=[VM, VM, pl.BlockSpec(memory_space=pltpu.SMEM)] + [VM] * 4 + [ANY] * 6,
        out_specs=[VM] * 4 + [ANY] * len(kept),
        scratch_shapes=[
            V((4, width, width), bf16), V((1, width, ff), bf16), V((1, ff, width), bf16), V((4, width, width), bf16),
            V((rows, width), bf16), V((2,) + block, bf16), V((slots, rows), bf16), V((rows, slots), bf16),
            V((rows, width), f32), V((rows, width), f32), V((rows, width), f32),
            V((rows, 3 * width), bf16), V((rows, width), bf16), V((rows, 3 * width), bf16), V((rows, width), bf16),
            V((blocks, rows, width), bf16), V((blocks, rows, width), bf16), V((rows, width), bf16), V((rows, LANES), f32),
            V((8, part), f32),
            sem((6,)), sem((len(kept),)), sem((15,)), sem((15,)), sem((owners,)), sem((owners,)),
        ],
        compiler_params=pltpu.CompilerParams(vmem_limit_bytes=VMEM_BYTES, collective_id=2, has_side_effects=True),
        cost_estimate=pl.CostEstimate(flops=int(18e9), bytes_accessed=int(60e6), transcendentals=0),
    )(routes_pad, routes_pad.T, counts, tokens, cotangent, gains, router, attn_qkv1, attn_out1, mlp_in, mlp_out, attn_qkv2, attn_out2)


def split_rows(block, local):
    n, r, w = block.shape
    v = block.astype(f32)
    if r != local * CAP:
        v = v[:, :local * CAP]
    v = v.reshape(n, local, CAP, w)
    return [v[:, i].reshape(n * CAP, w) for i in range(local)]


def join_rows(parts, sources, block):
    local = len(parts)
    w = parts[0].shape[1]
    v = jnp.concatenate([p.reshape(sources, 1, CAP, w) for p in parts], axis=1).reshape(sources, local * CAP, w)
    if block != local * CAP:
        v = jnp.concatenate([v, jnp.zeros((sources, block - local * CAP, w), f32)], axis=1)
    return v


def gate_of(u, router, experts, e):
    lane = lax.broadcasted_iota(jnp.int32, (1, LANES), 1)
    return jnp.sum(jnp.where(lane == e, router_probs(u, router, experts), 0.0), axis=-1, keepdims=True)


def xor(a, b, bits):
    out = 0
    for i in range(bits):
        out = out + ((a // (1 << i) + b // (1 << i)) % 2) * (1 << i)
    return out


def expert_body(owners, shards, local, experts, group, uout_ref, dy_ref, router_ref, stat_ref, w1_hbm, w2_hbm,
                uin_ref, served_ref, duback_ref, dgback_ref, total_ref, dyx_ref, ux_ref, *refs):
    if shards == 2:
        p1_h, p2_h, *refs = refs
    (w1, w2, dusend, dgsend, statx, state, acts, dzs, urows, drows, ob1, ob2, wsem, lsem, osem, us, ur, ds_, dr, gs, gr, ss, sr, fs, fr, xs, xr, ys, yr) = refs
    me, x = lax.axis_index("expert"), lax.axis_index("shard")
    bits = owners.bit_length() - 1
    barrier = pltpu.get_barrier_semaphore()

    def at(e, s):
        return dict(device_id=(e, s), device_id_type=pl.DeviceIdType.MESH)

    def each(lo, hi, f):
        lax.fori_loop(lo, hi, lambda k, c: (f(k), c)[1], 0)

    def peer(k):
        return xor(me, k, bits)

    each(1, owners, lambda k: pl.semaphore_signal(barrier, inc=1, **at(peer(k), x)))
    each(1, shards, lambda k: pl.semaphore_signal(barrier, inc=1, **at(me, (x + k) % shards)))
    weights = [pltpu.make_async_copy(w1_hbm, w1, wsem.at[0]), pltpu.make_async_copy(w2_hbm, w2, wsem.at[1])]
    start(weights)
    own = pltpu.make_async_copy(uout_ref.at[me], uin_ref.at[me], lsem.at[0])
    own.start()
    pl.semaphore_wait(barrier, owners - 1 + shards - 1)

    def send_u(k):
        return pltpu.make_async_remote_copy(uout_ref.at[peer(k)], uin_ref.at[me], us.at[k], ur.at[k], **at(peer(k), x))

    def send_du(k):
        return pltpu.make_async_remote_copy(dusend.at[peer(k)], duback_ref.at[me], ds_.at[k], dr.at[k], **at(peer(k), x))

    def send_dg(k):
        return pltpu.make_async_remote_copy(dgsend.at[peer(k)], dgback_ref.at[me], gs.at[k], gr.at[k], **at(peer(k), x))

    def send_statx(k):
        return pltpu.make_async_remote_copy(stat_ref, statx.at[k], xs.at[k], xr.at[k], **at(me, (x + k) % shards))

    def send_dyx(k):
        return pltpu.make_async_remote_copy(dy_ref, dyx_ref.at[k - 1], ys.at[k], yr.at[k], **at(me, (x + k) % shards))

    def send_far(g):
        rows = pl.ds(xor(me // group, g, bits) * group, group)
        return pltpu.make_async_remote_copy(uin_ref.at[rows], ux_ref.at[rows], fs.at[g], fr.at[g], **at(me, (x + 1) % shards))

    def send_state(k):
        return pltpu.make_async_remote_copy(state.at[0], state.at[k], ss.at[k], sr.at[k], **at(peer(k), x))

    each(1, shards, lambda k: send_statx(k).start())
    each(1, owners, lambda k: send_u(owners - k).start())
    each(1, shards, lambda k: send_dyx(k).start())
    each(1, shards, lambda k: send_statx(k).wait())
    sums = stat_ref[...]
    for k in range(1, shards):
        sums = sums + statx[k]
    state[0] = sums
    each(1, owners, lambda k: send_state(k).start())
    finish(weights)

    def work(g):
        base = xor(me // group, g, bits) * group
        rows = pl.ds(base, group)
        us_, dys = split_rows(uin_ref[rows], local), split_rows(dy_ref[rows], local)
        served, dus, prods = [], [], []
        for i in range(local):
            u, dy = us_[i].astype(bf16), dys[i]
            gate = gate_of(u, router_ref[...], experts, me * local + i)
            dsv = (gate * dy).astype(bf16)
            act, slope = gelu_pair(nn(u, w1[i]))
            out = nn(act.astype(bf16), w2[i])
            dz = (slope * nt(dsv, w2[i])).astype(bf16)
            if shards == 2:
                n = group * CAP
                spot = pl.ds(pl.multiple_of(g * n, n), n)
                acts[i, spot] = act.astype(bf16)
                dzs[i, spot] = dz
                urows[i, spot] = u
                drows[i, spot] = dsv
            dus.append(nt(dz, w1[i]))
            served.append(gate * out)
            prods.append(dy * out)
        block = uin_ref.shape[1]
        served_ref[rows] = join_rows(served, group, block).astype(bf16)
        dusend[rows] = join_rows(dus, group, block).astype(bf16)
        prod = join_rows(prods, group, block)
        ones = jnp.ones((8, prod.shape[2]), bf16)
        for j in range(group):
            hi = prod[j].astype(bf16)
            lo = (prod[j] - hi.astype(f32)).astype(bf16)
            dgsend[base + j, :, 0:block] = nt(ones, hi) + nt(ones, lo)

    def step(g):
        @pl.when(g == 0)
        def _():
            own.wait()

        for j in range(group):
            k = g * group + j
            if j == 0:
                pl.when(g > 0)(lambda k=k: send_u(k).wait_recv())
            else:
                send_u(k).wait_recv()
        if shards == 2:
            send_far(g).start()
        work(g)
        for j in range(group):
            k = g * group + j
            if j == 0:
                @pl.when(g > 0)
                def _(k=k):
                    send_du(k).start()
                    send_dg(k).start()
            else:
                send_du(k).start()
                send_dg(k).start()

    each(0, owners // group, step)
    backs = [pltpu.make_async_copy(dusend.at[me], duback_ref.at[me], lsem.at[0]),
             pltpu.make_async_copy(dgsend.at[me], dgback_ref.at[me], lsem.at[1])]
    start(backs)
    if shards == 2:
        width = urows.shape[2]
        blocks = acts.shape[2] // width

        def result(i):
            e, f = i // blocks, i % blocks
            col = pl.ds(pl.multiple_of(f * width, width), width)
            return [pltpu.make_async_copy(ob1.at[i % 2], p1_h.at[e, :, col], osem.at[i % 2]),
                    pltpu.make_async_copy(ob2.at[i % 2], p2_h.at[e, col, :], osem.at[2 + i % 2])]

        def gradient(i):
            e, f = i // blocks, i % blocks
            col = pl.ds(pl.multiple_of(f * width, width), width)
            pl.when(i >= 2)(lambda: finish(result(i - 2)))
            ob1[i % 2] = tn(urows[e], dzs[e, :, col]).astype(bf16)
            ob2[i % 2] = tn(acts[e, :, col], drows[e]).astype(bf16)
            start(result(i))

        count = local * blocks
        each(0, count, gradient)
        for i in range(max(0, count - 2), count):
            finish(result(i))
    each(1, owners, lambda k: send_state(k).wait())
    total = state[0]
    for k in range(1, owners):
        total = total + state[k]
    total_ref[...] = total
    each(1, owners, lambda k: send_u(k).wait_send())
    finish(backs)
    each(1, shards, lambda k: send_dyx(k).wait())
    if shards == 2:
        each(0, owners // group, lambda g: send_far(g).wait())
    each(1, owners, lambda k: send_du(k).wait())
    each(1, owners, lambda k: send_dg(k).wait())


def expert_grad_body(pieces, experts, *refs):
    us, dys = refs[:pieces], refs[pieces:2 * pieces]
    router_ref, w1_ref, w2_ref, g1_ref, g2_ref, urow, drow, stage, sems = refs[2 * pieces:]
    local = pl.num_programs(0)
    e = lax.axis_index("expert") * local + pl.program_id(0)

    @pl.when((pl.program_id(0) == 0) & (pl.program_id(1) == 0))
    def _():
        todo = [(us[i], urow, i) for i in range(pieces)] + [(dys[i], drow, i) for i in range(pieces)]
        copies = [pltpu.make_async_copy(r, stage.at[n % 2], sems.at[n % 2]) for n, (r, _, _) in enumerate(todo)]
        copies[0].start()
        for n, (_, to, i) in enumerate(todo):
            if n + 1 < len(todo):
                copies[n + 1].start()
            copies[n].wait()
            for j, v in enumerate(split_rows(stage[n % 2], urow.shape[1])):
                to[i, j] = v.astype(bf16)

    at = pl.program_id(0)
    for i in range(pieces):
        u = urow[i, at]
        dy = drow[i, at]
        gate = gate_of(u, router_ref[...], experts, e)
        ds = (gate * dy.astype(f32)).astype(bf16)
        act, slope = gelu_pair(nn(u, w1_ref[0]))
        dz = (slope * nt(ds, w2_ref[0])).astype(bf16)
        g1 = tn(u, dz)
        g2 = tn(act.astype(bf16), ds)
        if i == 0:
            g1_ref[0] = g1
            g2_ref[0] = g2
        else:
            g1_ref[0] += g1
            g2_ref[0] += g2


def split3(v):
    hi = v.astype(bf16)
    r = v - hi.astype(f32)
    mid = r.astype(bf16)
    lo = (r - mid.astype(f32)).astype(bf16)
    return hi, mid, lo


def router_backward(experts, dy_ref, u_ref, probs_ref, hidden_ref, gain_ref, router_ref, aux_ref, stat_ref, live_ref,
                    back_ref, ret_ref, dgate_ref, small_ref):
    slots = back_ref.shape[1]
    owners = dgate_ref.shape[0]
    local = experts // owners
    block = slots // owners
    off = lax.broadcasted_iota(jnp.int32, (slots, LANES), 0).astype(f32) - slot_start(
        lax.broadcasted_iota(jnp.int32, (slots, LANES), 1), local, block)
    oe = lax.broadcasted_iota(jnp.int32, (owners, LANES), 0).astype(f32)
    ee = lax.broadcasted_iota(jnp.int32, (owners, LANES), 1).astype(f32)
    pick = ((ee >= oe * local) & (ee < oe * local + local)).astype(f32).astype(bf16)
    column = 0.0
    for part in split3(dgate_ref[:, 0, :]):
        column = column + tn(part, pick)
    table = jnp.where((off >= 0) & (off < CAP), jnp.concatenate([column[0:block]] * owners, axis=0), 0.0)
    lane = lax.broadcasted_iota(jnp.int32, (1, LANES), 1)
    stat = stat_ref[0:1, :]
    total = jnp.sum(jnp.where(lane == LANES - 1, stat, 0.0), axis=-1, keepdims=True)
    fraction = jnp.where(lane < experts, stat, 0.0) / (2.0 * total)
    loss = experts * jnp.sum(fraction * stat_ref[1:2, :] / total, axis=-1, keepdims=True)
    small_ref[LANES + 2:LANES + 3, :] = jnp.broadcast_to(loss, (1, small_ref.shape[1]))
    dprobs = (aux_ref[0, 0] * experts * fraction / total) * live_ref[...]
    for part in split3(table):
        dprobs = dprobs + nn(back_ref[...], part)
    probs = probs_ref[...]
    dlog = (probs * (dprobs - jnp.sum(probs * dprobs, axis=-1, keepdims=True))).astype(bf16)
    small_ref[0:LANES, :] = tn(dlog, u_ref[...])
    du = nn(back_ref[...], ret_ref[...].reshape(slots, dy_ref.shape[1])) + nt(dlog, router_ref[...])
    xn, rs = norm(hidden_ref[...])
    dv, dg = norm_back(du, xn, rs, gain_ref[3:4, :])
    small_ref[LANES:LANES + 1, :] = dg
    grad = dy_ref[...].astype(f32) + dv
    return grad


def back2_body(split, images, seq, experts, dy_ref, u_ref, probs_ref, hidden_ref, x_ref, gain_ref, router_ref, aux_ref,
               stat_ref, live_ref, back_ref, ret_ref, dgate_ref, qkv_ref, mix_ref, *refs):
    n = split.count(2)
    pieces, (grad_ref, pack_ref, small_ref, w, sems, dmix_ref, dqkv_ref) = refs[:n], refs[n:]
    copies = split.copies(pieces, w, sems)
    start(copies)
    grad = router_backward(experts, dy_ref, u_ref, probs_ref, hidden_ref, gain_ref, router_ref, aux_ref, stat_ref, live_ref,
                           back_ref, ret_ref, dgate_ref, small_ref)
    grad_ref[...] = grad
    finish(copies)
    step = hidden_ref.shape[0] // images
    dv, dg = attend_backward(
        step, seq, images, grad, x_ref[...], gain_ref[2:3, :], [w.at[c] for c in range(3)], w.at[3],
        qkv_ref, mix_ref, dmix_ref, dqkv_ref, pack_ref, 0,
    )
    small_ref[LANES + 1:LANES + 2, :] = dg
    grad_ref[...] += dv


def mlp_back_body(split, grad_ref, hidden_ref, gain_ref, act_ref, slope_ref, *refs):
    n = 2 * split.count(1)
    pieces, (out_ref, pack_ref, dgain_ref, w1, w2, sems, du_ref) = refs[:n], refs[n:]
    half = n // 2
    copies = split.copies(pieces[:half], w1, sems.at[0]) + split.copies(pieces[half:], w2, sems.at[1])
    start(copies)
    xn, rs = norm(hidden_ref[...])
    gain = gain_ref[1:2, :]
    u = (xn * gain).astype(bf16)
    grad = grad_ref[...]
    low = grad.astype(bf16)
    finish(copies)
    width = grad.shape[1]
    blocks = act_ref.shape[0]
    ff = blocks * width
    shards = pack_ref.shape[0]
    part, fpart = width // shards, ff // shards
    base = part * blocks
    for b in range(blocks):
        at = slice(b * width, (b + 1) * width)
        dz = (slope_ref[b].astype(f32) * nt(low, w2[0, at, :])).astype(bf16)
        d = nt(dz, w1[0, :, at])
        if b == 0:
            du_ref[...] = d
        else:
            du_ref[...] += d
        gin = tn(u, dz).astype(bf16)
        for s in range(shards):
            pack_ref[s, b * part:(b + 1) * part, :] = gin[s * part:(s + 1) * part]
        gout = tn(act_ref[b], low).astype(bf16)
        per = min(width, fpart)
        for j in range(width // per):
            row = b * width + j * per
            s, off = row // fpart, row % fpart
            pack_ref[s, base + off:base + off + per, :] = gout[j * per:(j + 1) * per]
    dv, dg = norm_back(du_ref[...], xn, rs, gain)
    dgain_ref[...] = dg
    out_ref[...] = grad + dv


def back1_body(split, images, seq, experts, grad_ref, tok_ref, gain_ref, qkv_ref, mix_ref, small_ref, dg2_ref, *refs):
    n = split.count(2)
    pieces, (out_ref, pack_ref, w, sems, x_ref, dmix_ref, dqkv_ref) = refs[:n], refs[n:]
    copies = split.copies(pieces, w, sems)
    start(copies)
    step = x_ref.shape[0] // images
    pad_store(x_ref, lambda i: tok_ref[i], images, seq, step)
    finish(copies)
    width = x_ref.shape[1]
    dv, dg1 = attend_backward(
        step, seq, images, grad_ref[...], x_ref[...], gain_ref[0:1, :], [w.at[c] for c in range(3)], w.at[3],
        qkv_ref, mix_ref, dmix_ref, dqkv_ref, pack_ref, 0,
    )
    x_ref[...] = grad_ref[...] + dv
    for i in range(images):
        out_ref[i] = x_ref[i * step:i * step + seq, :]
    shards = pack_ref.shape[0]
    part = width // shards
    base = 4 * part
    gains = jnp.concatenate(
        [dg1, dg2_ref[...], small_ref[LANES + 1:LANES + 2, :], small_ref[LANES:LANES + 1, :], jnp.zeros((28, width), f32)], axis=0
    )
    both = jnp.concatenate([small_ref[0:32, :], gains], axis=0).astype(bf16)
    for s in range(shards):
        one = both[:, s * part:(s + 1) * part]
        pack_ref[s, base:base + 64, :] = jnp.concatenate([one, jnp.zeros((64, width - part), bf16)], axis=1)


def output_body(images, seq, hidden_ref, back_ref, ret_ref, live_ref, out_ref, tmp_ref):
    step = hidden_ref.shape[0] // images
    tmp_ref[...] = (hidden_ref[...] + nn(back_ref[...], ret_ref[...])) * live_ref[...]
    for i in range(images):
        out_ref[i] = tmp_ref[i * step:i * step + seq, :].astype(bf16)


def backward_body(split, images, seq, experts, local, owners, plan, *refs):
    (gain_ref, router_ref, aux_ref, stat_ref, live_ref, back_ref, dgate_ref, tok_ref, dy_h, u_h, probs_h, du_h,
     hid2_h, x2_h, hid1_h, qkv2_h, mix2_h, qkv1_h, mix1_h, act_h, slope_h, served_h, ux_h, dyx_h, p1_h, p2_h, we1_h, we2_h,
     *refs) = refs
    na = nm = 1
    two, refs = refs[:na], refs[na:]
    up, refs = refs[:nm], refs[nm:]
    down, refs = refs[:nm], refs[nm:]
    one, refs = refs[:na], refs[na:]
    (out_ref, gtok_ref, fin, smout_ref, small_ref, ge1_h, ge2_h, sback_h,
     hid2, xbuf, grad_ref, dubuf, qkv, mix, dmix, dqkv, watt, w1, w2, big, stage, pack, crecv, xa, yb, ya, xb, zr,
     sm, smr,
     lsem, wsem, vs, vr, gs, gr, ms, mr, esem, osem, tsem, psem) = refs
    me, x = lax.axis_index("expert"), lax.axis_index("shard")
    bits = owners.bit_length() - 1
    bit = [(me // (1 << i)) % 2 for i in range(bits)]
    hop = [me + (1 - 2 * bit[i]) * (1 << i) for i in range(bits)]
    rows, width = grad_ref.shape
    step = rows // images
    blocks = act_h.shape[0]
    whole = pack.shape[2]
    part = width // 2

    def to(e, s):
        return dict(device_id=(e, s), device_id_type=pl.DeviceIdType.MESH)

    def each(lo, hi, f):
        lax.fori_loop(lo, hi, lambda k, c: (f(k), c)[1], 0)

    barrier = pltpu.get_barrier_semaphore()
    each(1, owners, lambda k: pl.semaphore_signal(barrier, inc=1, **to(xor(me, k, bits), x)))
    pl.semaphore_signal(barrier, inc=1, **to(me, 1 - x))

    def load(src, dst, i):
        return pltpu.make_async_copy(src, dst, lsem.at[i])

    count = 4 + 2 * blocks
    dy_ref, u_ref, probs_ref, du_ref = dmix, dqkv.at[:, 0:width], dubuf.at[:, 0:LANES], stage.at[0]
    start_in = [load(hid2_h, hid2, 0), load(du_h, du_ref, count), load(dy_h, dy_ref, count + 1), load(u_h, u_ref, count + 2),
                load(probs_h, probs_ref, count + 3)]
    start(start_in)
    first = [load(x2_h, xbuf, 1), load(qkv2_h, qkv, 2), load(mix2_h, mix, 3)]
    w_two = split.copies(two, watt, wsem.at[0])
    w_mlp = split.copies(up, w1, wsem.at[1]) + split.copies(down, w2, wsem.at[2])
    gelus = [load(act_h.at[b], big.at[b, 0:rows], 4 + b) for b in range(blocks)]
    gelus += [load(slope_h.at[b], big.at[b, big.shape[1] // 2:big.shape[1] // 2 + rows], 4 + blocks + b) for b in range(blocks)]
    start(first + w_two + w_mlp + gelus)
    own = pltpu.make_async_copy(served_h.at[me], sback_h.at[me], tsem.at[0])
    own.start()
    pl.semaphore_wait(barrier, owners)

    def send_served(k):
        p = xor(me, k, bits)
        return pltpu.make_async_remote_copy(served_h.at[p], sback_h.at[me], vs.at[k], vr.at[k], **to(p, x))

    each(1, owners, lambda k: send_served(owners - k).start())

    planes = owners // 4

    def add(ref, at, other):
        ref[at] = ref[at] + other

    def span(first, size):
        return pl.ds(pl.multiple_of(first, 32), size)

    def stages(n):
        def copy(src, dst, i, peer):
            return pltpu.make_async_remote_copy(src, dst, gs.at[n, i], gr.at[n, i], **peer)

        q = whole // 4
        o = bit[0] * (whole // 2)
        out = []
        out.append((
            lambda: [copy(pack.at[n, :, span((1 - bit[0]) * (whole // 2), whole // 2)], crecv.at[n], 0, to(hop[0], x))],
            lambda: add(pack, (n, slice(None), span(o, whole // 2)), crecv[n])))
        e = q // 2
        b1 = bit[1] * e

        def after1():
            add(pack, (n, x, span(o, q)), xa[n])
            add(pack, (n, slice(None), span(o + q + b1, e)), yb[n])

        out.append((
            lambda: [copy(pack.at[n, 1 - x, span(o, q)], xa.at[n], 1, to(me, 1 - x)),
                     copy(pack.at[n, :, span(o + q + e - b1, e)], yb.at[n], 2, to(hop[1], x))],
            after1))

        def after2():
            add(pack, (n, x, span(o + b1, e)), ya[n])
            add(pack, (n, x, span(o + q + b1, e)), xb[n])

        out.append((
            lambda: [copy(pack.at[n, x, span(o + e - b1, e)], ya.at[n], 3, to(hop[1], x)),
                     copy(pack.at[n, 1 - x, span(o + q + b1, e)], xb.at[n], 4, to(me, 1 - x))],
            after2))
        size = e // planes
        base = o + b1

        def rows_at(p):
            return [span(base + p * size + j * q, size) for j in range(2)]

        def over(make):
            out = []
            for k in range(1, planes):
                p = xor(me // 4, k, bits)
                for j in range(2):
                    out.append(make(k, p, j, 5 + 2 * (k - 1) + j, to(p * 4 + me % 4, x)))
            return out

        mine = me // 4

        def after3():
            for j in range(2):
                at = (n, x, rows_at(mine)[j])
                total = pack[at].astype(f32)
                for k in range(1, planes):
                    total = total + zr[n, 2 * (k - 1) + j].astype(f32)
                fin[(n, rows_at(mine)[j])] = total.astype(bf16)

        out.append((
            lambda: over(lambda k, p, j, i, peer: copy(pack.at[n, x, rows_at(p)[j]], zr.at[n, 2 * (k - 1) + j], i, peer)), after3))
        more = 2 * (planes - 1)
        out.append((
            lambda: over(lambda k, p, j, i, peer: copy(fin.at[n, rows_at(mine)[j]], fin.at[n, rows_at(mine)[j]], i + more, peer)),
            lambda: None))
        out.append((
            lambda: [copy(fin.at[n, span(base + j * q, e)], fin.at[n, span(base + j * q, e)], 5 + 2 * more + j, to(hop[1], x))
                     for j in range(2)],
            lambda: None))
        out.append((
            lambda: [copy(fin.at[n, span(o, whole // 2)], fin.at[n, span(o, whole // 2)], 7 + 2 * more, to(hop[0], x))],
            lambda: None))
        return out

    groups = [stages(n) for n in range(4)]

    def small_stage(i):
        if i == 0:
            src, dst, peer = sm, smr.at[0], to(hop[0], x)
        elif i == 1:
            src, dst, peer = sm.at[1 - x], smr.at[1, 0], to(me, 1 - x)
        else:
            src, dst, peer = sm.at[x], smr.at[i, 0], to(hop[i - 1], x)
        return pltpu.make_async_remote_copy(src, dst, ms.at[i], mr.at[i], **peer)

    def small_after(i):
        if i == 0:
            sm[...] += smr[0]
        else:
            sm[x] += smr[i, 0]

    def tick(n, k):
        table = groups[n]
        if k > 0:
            finish(table[k - 1][0]())
            table[k - 1][1]()
            if n == 3 and k - 1 < bits + 1:
                small_stage(k - 1).wait()
                small_after(k - 1)
        if k < len(table):
            start(table[k][0]())
            if n == 3 and k < bits + 1:
                small_stage(k).start()

    def at_point(name, index=None):
        for i, n, k in plan.get(name, ()):
            if index is None:
                tick(n, k)
            else:
                pl.when(index == i)(functools.partial(tick, n, k))

    finish(start_in)
    grad_ref[...] = router_backward(experts, dy_ref, u_ref, probs_ref, hid2, gain_ref, router_ref, aux_ref, stat_ref, live_ref,
                                    back_ref, du_ref, dgate_ref, small_ref)
    finish(first + w_two)
    dv, dg = attend_backward(
        step, seq, images, grad_ref[...], xbuf[...], gain_ref[2:3, :], [watt.at[c] for c in range(3)], watt.at[3],
        qkv, mix, dmix, dqkv, pack.at[0], 0,
    )
    small_ref[LANES + 1:LANES + 2, :] = dg
    grad_ref[...] += dv
    at_point("two")
    second = [load(hid1_h, xbuf, 1), load(qkv1_h, qkv, 2), load(mix1_h, mix, 3)]
    w_one = split.copies(one, watt, wsem.at[0])
    start(second + w_one)

    finish(gelus + w_mlp)
    low = grad_ref[...].astype(bf16)
    fpart = blocks * width // 2
    for b in range(blocks):
        s, off = b * width // fpart, b * width % fpart
        pack[1, s, off:off + width, :] = tn(big[b, 0:rows], low).astype(bf16)
    at_point("out")
    finish(second[:1])
    xn, rs = norm(xbuf[...])
    gain = gain_ref[1:2, :]
    u = (xn * gain).astype(bf16)
    half = big.shape[1] // 2
    for b in range(blocks):
        cols = slice(b * width, (b + 1) * width)
        dz = (big[b, half:half + rows].astype(f32) * nt(low, w2[0, cols, :])).astype(bf16)
        d = nt(dz, w1[0, :, cols])
        if b == 0:
            dubuf[...] = d
        else:
            dubuf[...] += d
        gin = tn(u, dz).astype(bf16)
        for s in range(2):
            pack[2, s, b * part:(b + 1) * part, :] = gin[s * part:(s + 1) * part]
        at_point("in%d" % b)
    dv, dg = norm_back(dubuf[...], xn, rs, gain)
    small_ref[LANES + 3:LANES + 4, :] = dg
    grad_ref[...] += dv
    at_point("mlp")

    pad_store(xbuf, lambda i: tok_ref[i], images, seq, step)
    finish(second[1:] + w_one)
    dv, dg = attend_backward(
        step, seq, images, grad_ref[...], xbuf[...], gain_ref[0:1, :], [watt.at[c] for c in range(3)], watt.at[3],
        qkv, mix, dmix, dqkv, pack.at[3], 0, tick=lambda i: at_point("image", i),
    )
    sm[...] = jnp.zeros(sm.shape, f32)
    for s in range(2):
        cols = slice(s * part, (s + 1) * part)
        sm[s, 0:experts] = small_ref[0:experts, cols]
        sm[s, experts:experts + 1] = dg[:, cols]
        sm[s, experts + 1:experts + 2] = small_ref[LANES + 3:LANES + 4, cols]
        sm[s, experts + 2:experts + 3] = small_ref[LANES + 1:LANES + 2, cols]
        sm[s, experts + 3:experts + 4] = small_ref[LANES:LANES + 1, cols]
    at_point("one")
    grad_ref[...] += dv
    for i in range(images):
        gtok_ref[i] = grad_ref[i * step:i * step + seq, :]

    own.wait()
    each(1, owners, lambda k: send_served(k).wait())
    at_point("rows")

    todo = [(ux_h, 0), (dyx_h.at[0], 1)]
    moves = [pltpu.make_async_copy(r, stage.at[i % 2], esem.at[i % 2]) for i, (r, _) in enumerate(todo)]

    def lane(i):
        return pl.ds(pl.multiple_of(i * width, width), width)

    def chunk(i):
        e, f = i // blocks, i % blocks
        slot = i % 2
        col = pl.ds(pl.multiple_of(f * width, width), width)
        return [pltpu.make_async_copy(we1_h.at[e, :, col], w1.at[0, :, lane(slot)], esem.at[2 + slot]),
                pltpu.make_async_copy(we2_h.at[e, col, :], w2.at[0, lane(slot), :], esem.at[4 + slot])]

    def result(i):
        e, f = i // blocks, i % blocks
        slot = i % 2
        col = pl.ds(pl.multiple_of(f * width, width), width)
        return [pltpu.make_async_copy(w1.at[0, :, lane(2 + slot)], ge1_h.at[e, :, col], osem.at[slot]),
                pltpu.make_async_copy(w2.at[0, lane(2 + slot), :], ge2_h.at[e, col, :], osem.at[2 + slot])]

    moves[0].start()
    start(chunk(0))
    for i, (_, kind) in enumerate(todo):
        if i + 1 < len(todo):
            moves[i + 1].start()
        moves[i].wait()
        for e, v in enumerate(split_rows(stage[i % 2], local)):
            if kind == 1:
                u = big[e, 0:half]
                v = v * gate_of(u, router_ref[...], experts, me * local + e)
            big[kind * local + e, 0:half] = v.astype(bf16)
    back = pltpu.make_async_copy(sback_h, stage.at[0], tsem.at[0])
    back.start()
    back.wait()
    grad_ref[...] = (hid2[...] + nn(back_ref[...], stage[0].reshape(back_ref.shape[1], width))) * live_ref[...]
    for i in range(images):
        out_ref[i] = grad_ref[i * step:i * step + seq, :].astype(bf16)
    at_point("output")
    count = local * blocks

    def before(i):
        e, f = i // blocks, i % blocks
        slot = i % 2
        col = pl.ds(pl.multiple_of(f * width, width), width)
        return [pltpu.make_async_copy(p1_h.at[e, :, col], w1.at[0, :, lane(2 + slot)], psem.at[slot]),
                pltpu.make_async_copy(p2_h.at[e, col, :], w2.at[0, lane(2 + slot), :], psem.at[2 + slot])]

    def expert(i, c):
        slot = i % 2
        pl.when(i + 1 < count)(lambda: start(chunk(i + 1)))
        pl.when(i >= 2)(lambda: finish(result(i - 2)))
        start(before(i))
        finish(chunk(i))
        e = i // blocks
        u = big[e, 0:half]
        dsv = big[local + e, 0:half]
        act, slope = gelu_pair(nn(u, w1[0, :, lane(slot)]))
        dz = (slope * nt(dsv, w2[0, lane(slot), :])).astype(bf16)
        act = act.astype(bf16)
        finish(before(i))
        at1, at2 = (0, slice(None), lane(2 + slot)), (0, lane(2 + slot), slice(None))
        w1[at1] = (w1[at1].astype(f32) + tn(u, dz)).astype(bf16)
        at_point("early", i)
        w2[at2] = (w2[at2].astype(f32) + tn(act, dsv)).astype(bf16)
        start(result(i))
        at_point("late", i)
        return c

    lax.fori_loop(0, count, expert, 0)
    at_point("end")
    for i in range(max(0, count - 2), count):
        finish(result(i))
    smout_ref[...] = sm[x]


def swap(owners, bit):
    return [(i, i ^ (1 << bit)) for i in range(owners)]


def reduce_all(g, owners, shards):
    me = lax.axis_index("expert")
    bits = owners.bit_length() - 1

    def add(a, b):
        return (a.astype(f32) + b.astype(f32)).astype(bf16)

    def fold(v, bit, axis):
        own = (me >> bit) & 1
        half = v.shape[axis] // 2
        keep = lax.dynamic_slice_in_dim(v, own * half, half, axis)
        send = lax.dynamic_slice_in_dim(v, (1 - own) * half, half, axis)
        return add(keep, lax.ppermute(send, "expert", swap(owners, bit)))

    v = fold(g, 0, 1)
    if shards == 2:
        x = lax.axis_index("shard")
        keep = lax.dynamic_index_in_dim(v, x, 0, keepdims=False)
        send = lax.dynamic_index_in_dim(v, 1 - x, 0, keepdims=False)
        v = add(keep, lax.ppermute(send, "shard", [(0, 1), (1, 0)]))
    else:
        v = lax.psum_scatter(v, "shard", scatter_dimension=0, tiled=True)[0]
    for bit in range(1, bits):
        v = fold(v, bit, 0)
    for bit in reversed(range(bits)):
        own = (me >> bit) & 1
        other = lax.ppermute(v, "expert", swap(owners, bit))
        v = jnp.where(own == 0, jnp.concatenate([v, other]), jnp.concatenate([other, v]))
    return v


def per_device(
    owners, shards, tokens, cotangent, routes, counts, aux_weight, attn_qkv1, attn_out1, mlp_in, mlp_out, gains1,
    attn_qkv2, attn_out2, router, gains2, expert_in, expert_out,
):
    images, seq, width = tokens.shape
    step = padded(seq)
    rows = images * step
    experts = router.shape[1]
    local = expert_in.shape[0]
    ff = mlp_in.shape[1]
    block_rows = -(-local * CAP // 16) * 16
    slots = owners * block_rows
    split = Split(shards)
    expert_swap = functools.partial(lax.all_to_all, axis_name="expert", split_axis=0, concat_axis=0, tiled=True)

    block = (owners, block_rows, width)
    sem = pltpu.SemaphoreType.DMA
    if shards == 2:
        (gains, router_full, stat, live_col, dy, u_out, hidden, block_out, hidden_two, qkv_one, mix_one, qkv_two, mix_two, act, slope,
         u_two, probs, back, w_one, w_up, w_down, w_two, dy_in) = fused_forward(
            owners, experts, local, block, tokens, cotangent, routes, counts, jnp.concatenate([gains1, gains2]), router,
            attn_qkv1, attn_out1, mlp_in, mlp_out, attn_qkv2, attn_out2)
        w_one, w_up, w_down, w_two = [w_one], [w_up], [w_down], [w_two]
    else:
        within = jnp.arange(step, dtype=jnp.int32) < seq
        live = ((jnp.arange(images, dtype=jnp.int32)[:, None] < counts[0]) & within[None, :]).reshape(rows)
        live = live.astype(f32)
        routes_pad = jnp.pad(routes, ((0, 0), (0, step - seq), (0, 0)), constant_values=-1).reshape(rows, 2)
        lanes = jnp.arange(LANES, dtype=jnp.int32)
        loads = jnp.sum(((routes_pad[:, :, None] == lanes) & (live[:, None, None] > 0)).astype(f32), axis=(0, 1))
        loads = jnp.where(lanes == LANES - 1, jnp.sum(live), loads)
        live_col = live[:, None]

        w_one = split.gather([attn_qkv1, attn_out1[None]])
        w_up = split.gather([mlp_in[None]])
        w_down = split.gather([mlp_out[None]])
        w_two = split.gather([attn_qkv2, attn_out2[None]])
        gains = jnp.concatenate([gains1, gains2])
        if shards == 2:
            x = lax.axis_index("shard")
            other = lax.ppermute(gains, "shard", [(0, 1), (1, 0)])
            gains = jnp.where(x == 0, jnp.concatenate([gains, other], 1), jnp.concatenate([other, gains], 1))
            other = lax.ppermute(router, "shard", [(0, 1), (1, 0)])
            router_full = jnp.where(x == 0, jnp.concatenate([router, other]), jnp.concatenate([other, router]))
        else:
            gains = lax.all_gather(gains, "shard", axis=1, tiled=True)
            router_full = lax.all_gather(router, "shard", axis=0, tiled=True)
        gains = gains.astype(f32)
        router_full = jnp.pad(router_full, ((0, 0), (0, LANES - experts)))

        dy, dy_out, disp, back = call(
            functools.partial(route_body, images, seq, local, block_rows),
            [sds((rows, width), bf16), sds((slots, width), bf16), sds((slots, rows), bf16), sds((rows, slots), bf16)],
            [routes_pad, routes_pad.T, live_col, cotangent], flops=2e9, nbytes=6e6,
        )
        block = (owners, block_rows, width)
        dy_in = expert_swap(dy_out.reshape(block))

        sem = pltpu.SemaphoreType.DMA
        attn_scratch = [pltpu.VMEM((4, width, width), bf16), sem((4,))]
        mlp_scratch = [pltpu.VMEM((1, width, ff), bf16), pltpu.VMEM((1, ff, width), bf16), sem((2, 4))]

        def specs(n, ins):
            return [VM] * n + [ANY] * (len(ins) - n)

        ins = [tokens, gains] + w_one
        hidden, qkv_one, mix_one = call(
            functools.partial(block1_body, split, images, seq),
            [sds((rows, width), f32), sds((rows, 3 * width), bf16), sds((rows, width), bf16)],
            ins, attn_scratch, specs(2, ins), flops=4e9, nbytes=8e6,
        )
        ins = [hidden, gains] + w_up + w_down
        block_out, act, slope = call(
            functools.partial(mlp_body, split),
            [sds((rows, width), f32)] + [sds((ff // width, rows, width), bf16)] * 2,
            ins, mlp_scratch, specs(2, ins), flops=6e9, nbytes=12e6,
        )
        ins = [block_out, gains, router_full, disp, live_col, loads[None, :]] + w_two
        hidden_two, qkv_two, mix_two, u_two, probs, stat, u_out = call(
            functools.partial(block2_body, split, images, seq, experts),
            [sds((rows, width), f32), sds((rows, 3 * width), bf16), sds((rows, width), bf16), sds((rows, width), bf16),
             sds((rows, LANES), f32), sds((8, LANES), f32), sds((slots, width), bf16)],
            ins, attn_scratch, specs(6, ins), flops=5e9, nbytes=10e6,
        )

    group = min(4, owners)
    saved = owners * CAP if shards == 2 else 16
    wide = width if shards == 2 else LANES
    u_in, served, du_back, dgate_back, stat, dy_far, u_far, *partial = pl.pallas_call(
        functools.partial(expert_body, owners, shards, local, experts, group),
        out_shape=[sds(block, bf16), sds(block, bf16), sds(block, bf16), sds((owners, 8, LANES), f32), sds((8, LANES), f32),
                   sds((shards - 1,) + block, bf16), sds(block, bf16)]
        + ([sds(expert_in.shape, bf16), sds(expert_out.shape, bf16)] if shards == 2 else []),
        in_specs=[VM] * 4 + [ANY] * 2,
        out_specs=[VM] * 5 + [ANY] * (4 if shards == 2 else 2),
        scratch_shapes=[
            pltpu.VMEM((local, width, ff), bf16), pltpu.VMEM((local, ff, width), bf16), pltpu.VMEM(block, bf16),
            pltpu.VMEM((owners, 8, LANES), f32), pltpu.VMEM((shards, 8, LANES), f32), pltpu.VMEM((owners, 8, LANES), f32),
            pltpu.VMEM((local, saved, ff if shards == 2 else LANES), bf16), pltpu.VMEM((local, saved, ff if shards == 2 else LANES), bf16),
            pltpu.VMEM((local, saved, wide), bf16), pltpu.VMEM((local, saved, wide), bf16),
            pltpu.VMEM((2, wide, wide), bf16), pltpu.VMEM((2, wide, wide), bf16),
            sem((2,)), sem((2,)), sem((4,)),
        ] + [sem((owners,))] * 10 + [sem((shards,))] * 4,
        compiler_params=pltpu.CompilerParams(vmem_limit_bytes=VMEM_BYTES, collective_id=0, has_side_effects=True),
        cost_estimate=pl.CostEstimate(flops=int(11e9), bytes_accessed=int(15e6), transcendentals=0),
    )(u_out.reshape(block), dy_in, router_full, stat, expert_in, expert_out)
    parts_of = (gains, router_full, aux_weight.reshape(1, 1), stat, live_col, back, dgate_back, tokens, dy, u_two, probs, du_back)
    if shards == 2:
        return fused_backward(Split(1), experts, tokens, parts_of, hidden_two, block_out, hidden, qkv_two, mix_two, qkv_one, mix_one,
                              act, slope, served, u_far, dy_far, *partial, expert_in, expert_out, w_two, w_up, w_down, w_one)
    served_back = expert_swap(served).reshape(slots, width)

    if shards == 2:
        us = [u_in, lax.ppermute(u_in, "shard", [(0, 1), (1, 0)])]
    else:
        far = lax.all_gather(u_in, "shard")
        us = [u_in] + [lax.dynamic_index_in_dim(far, (lax.axis_index("shard") + shards - k) % shards, 0, False) for k in range(1, shards)]
    dys = [dy_in] + [dy_far[k] for k in range(shards - 1)]
    parts = 4
    wide = ff // parts
    up_spec = pl.BlockSpec((1, width, wide), lambda e, f: (e, 0, f))
    down_spec = pl.BlockSpec((1, wide, width), lambda e, f: (e, f, 0))
    grad_e_in, grad_e_out = pl.pallas_call(
        functools.partial(expert_grad_body, shards, experts),
        grid=(local, parts),
        out_shape=[sds((local, width, ff), f32), sds((local, ff, width), f32)],
        in_specs=[ANY] * (2 * shards) + [VM, up_spec, down_spec],
        out_specs=[up_spec, down_spec],
        scratch_shapes=[pltpu.VMEM((shards, local, owners * CAP, width), bf16)] * 2 + [pltpu.VMEM((2,) + block, bf16), sem((2,))],
        compiler_params=pltpu.CompilerParams(vmem_limit_bytes=VMEM_BYTES),
        cost_estimate=pl.CostEstimate(flops=int(27e9), bytes_accessed=int(40e6), transcendentals=0),
    )(*us, *dys, router_full, expert_in, expert_out)

    part = width // shards
    back_scratch = [pltpu.VMEM((rows, width), bf16), pltpu.VMEM((rows, 3 * width), bf16)]
    ins = [dy, u_two, probs, hidden_two, block_out, gains, router_full, aux_weight.reshape(1, 1), stat, live_col, back,
           du_back.reshape(slots, width), dgate_back,
           qkv_two, mix_two]
    n = len(ins)
    ins = ins + w_two
    grad_block, pack_two, small = call(
        functools.partial(back2_body, split, images, seq, experts),
        [sds((rows, width), f32), sds((shards, 4 * part, width), bf16), sds((LANES + 8, width), f32)],
        ins, attn_scratch + back_scratch, specs(n, ins), flops=9e9, nbytes=16e6,
    )
    balance_loss = small[LANES + 2, 0]
    late = reduce_all(pack_two, owners, shards)
    ins = [grad_block, hidden, gains, act, slope] + w_up + w_down
    grad_hidden, pack_mlp, dg_two = call(
        functools.partial(mlp_back_body, split),
        [sds((rows, width), f32), sds((shards, part * (ff // width) + ff // shards, width), bf16), sds((1, width), f32)],
        ins, mlp_scratch + [pltpu.VMEM((rows, width), f32)], specs(5, ins), flops=11e9, nbytes=16e6,
    )
    middle = reduce_all(pack_mlp, owners, shards)
    ins = [grad_hidden, tokens, gains, qkv_one, mix_one, small, dg_two] + w_one
    grad_tokens, pack_one = call(
        functools.partial(back1_body, split, images, seq, experts),
        [sds((images, seq, width), f32), sds((shards, 4 * part + 64, width), bf16)],
        ins, attn_scratch + [pltpu.VMEM((rows, width), f32)] + back_scratch, specs(7, ins), flops=9e9, nbytes=14e6,
    )
    early = reduce_all(pack_one, owners, shards)
    (output,) = call(
        functools.partial(output_body, images, seq), [sds((images, seq, width), bf16)],
        [hidden_two, back, served_back, live_col], [pltpu.VMEM((rows, width), f32)], flops=1e9, nbytes=5e6,
    )

    late, middle, early = late.astype(f32), middle.astype(f32), early.astype(f32)
    up = middle[:part * (ff // width)].reshape(ff // width, part, width).transpose(1, 0, 2).reshape(part, ff)
    tail = early[4 * part:, :part]
    return (
        output,
        balance_loss,
        grad_tokens,
        early[:3 * part].reshape(3, part, width),
        early[3 * part:4 * part],
        up,
        middle[part * (ff // width):],
        tail[32:34],
        late[:3 * part].reshape(3, part, width),
        late[3 * part:],
        tail[:experts].T,
        tail[34:36],
        grad_e_in,
        grad_e_out,
    )


PLAN = [
    ("two", None, 0),
    ("out", None, 1),
    ("out", None, 0),
    ("in1", None, 1),
    ("mlp", None, 2),
    ("mlp", None, 0),
    ("image", 0, 2),
    ("image", 0, 1),
    ("image", 1, 0),
    ("image", 2, 1),
    ("one", None, 3),
    ("one", None, 2),
    ("output", None, 3),
    ("output", None, 0),
    ("early", 0, 2),
    ("early", 0, 1),
    ("late", 3, 3),
    ("early", 4, 0),
    ("late", 4, 2),
    ("late", 4, 1),
    ("early", 6, 3),
]


def fused_backward(split, experts, tokens, parts_of, hidden_two, block_out, hidden, qkv_two, mix_two, qkv_one, mix_one,
                   act, slope, served, u_far, dy_far, part1, part2, expert_in, expert_out, w_two, w_up, w_down, w_one):
    images, seq, width = tokens.shape
    rows = hidden.shape[0]
    local, _, ff = expert_in.shape
    block = served.shape
    owners = block[0]
    bits = owners.bit_length() - 1
    whole = 2 * width
    part = width // 2
    blocks = ff // width
    stages = 7
    left = [0] * 4
    plan = {}
    for name, index, n in PLAN:
        if left[n] <= stages and (index is None or index < (images if name == "image" else local * blocks)):
            plan.setdefault(name, []).append((index, n, left[n]))
            left[n] += 1
    plan["end"] = [(None, n, k) for k in range(stages + 1) for n in range(4) if k >= left[n]]
    small_rows = -(-(experts + 4) // 8) * 8
    sem = pltpu.SemaphoreType.DMA
    ins = list(parts_of) + [hidden_two, block_out, hidden, qkv_two, mix_two, qkv_one, mix_one, act, slope, served, u_far, dy_far,
                            part1, part2, expert_in, expert_out] + w_two + w_up + w_down + w_one
    vmem = 8
    big_rows = 2 * owners * CAP
    nsem = 8 + 4 * (owners // 4 - 1)
    V = pltpu.VMEM
    outs = pl.pallas_call(
        functools.partial(backward_body, split, images, seq, experts, local, owners, plan),
        out_shape=[
            sds((images, seq, width), bf16), sds((images, seq, width), f32), sds((4, whole, width), bf16),
            sds((small_rows, part), f32), sds((LANES + 8, width), f32), sds(expert_in.shape, bf16), sds(expert_out.shape, bf16),
            sds(block, bf16),
        ],
        in_specs=[VM] * vmem + [ANY] * (len(ins) - vmem),
        out_specs=[VM] * 5 + [ANY] * 3,
        scratch_shapes=[
            V((rows, width), f32), V((rows, width), f32), V((rows, width), f32), V((rows, width), f32),
            V((rows, 3 * width), bf16), V((rows, width), bf16), V((rows, width), bf16), V((rows, 3 * width), bf16),
            V((4, width, width), bf16), V((1, width, ff), bf16), V((1, ff, width), bf16), V((blocks, big_rows, width), bf16),
            V((2,) + block, bf16),
            V((4, 2, whole, width), bf16), V((4, 2, whole // 2, width), bf16), V((4, whole // 4, width), bf16),
            V((4, 2, whole // 8, width), bf16), V((4, whole // 8, width), bf16), V((4, whole // 8, width), bf16),
            V((4, 2 * (owners // 4 - 1), whole // (2 * owners), width), bf16),
            V((2, small_rows, part), f32), V((bits + 1, 2, small_rows, part), f32),
            sem((8 + 2 * blocks,)), sem((3, 4)), sem((owners,)), sem((owners,)),
            sem((4, nsem)), sem((4, nsem)), sem((bits + 1,)), sem((bits + 1,)), sem((6,)), sem((4,)), sem((1,)), sem((4,)),
        ],
        compiler_params=pltpu.CompilerParams(vmem_limit_bytes=63 << 20, collective_id=1, has_side_effects=True),
        cost_estimate=pl.CostEstimate(flops=int(60e9), bytes_accessed=int(80e6), transcendentals=0),
    )(*ins)
    output, grad_tokens, fin, tail, small, grad_e_in, grad_e_out = outs[:7]
    qkv1, out1, up, down, qkv2, out2, grad_e_in, grad_e_out = widen(fin, grad_e_in, grad_e_out, part, width, blocks)
    return (
        output, small[LANES + 2, 0], grad_tokens, qkv1, out1, up, down, tail[experts:experts + 2], qkv2, out2, tail[:experts].T,
        tail[experts + 2:experts + 4], grad_e_in, grad_e_out,
    )


def widen_body(sixth, fin_ref, e1_ref, e2_ref, qkv1_ref, out1_ref, up_ref, down_ref, qkv2_ref, out2_ref, g1_ref, g2_ref):
    i = pl.program_id(0)
    g1_ref[...] = e1_ref[...].astype(f32)
    g2_ref[...] = e2_ref[...].astype(f32)
    up_ref[...] = fin_ref[2].astype(f32)
    down_ref[...] = fin_ref[1].astype(f32)

    @pl.when(i < sixth)
    def _():
        qkv1_ref[0] = fin_ref[3].astype(f32)
        qkv2_ref[0] = fin_ref[0].astype(f32)

    @pl.when(i >= sixth)
    def _():
        out1_ref[...] = fin_ref[3].astype(f32)
        out2_ref[...] = fin_ref[0].astype(f32)


def widen(fin, e1, e2, part, width, blocks):
    steps = 2 * blocks
    some = fin.shape[1] // steps
    per = part // some
    sixth = 3 * per
    local, _, ff = e1.shape
    qkv = pl.BlockSpec((1, some, width), lambda i: (jnp.minimum(i, sixth - 1) // per, jnp.minimum(i, sixth - 1) % per, 0))
    out = pl.BlockSpec((some, width), lambda i: (jnp.maximum(i - sixth, 0), 0))
    return pl.pallas_call(
        functools.partial(widen_body, sixth),
        grid=(steps,),
        out_shape=[sds((3, part, width), f32), sds((part, width), f32), sds((part, blocks * width), f32), sds((fin.shape[1], width), f32),
                   sds((3, part, width), f32), sds((part, width), f32), sds(e1.shape, f32), sds(e2.shape, f32)],
        in_specs=[pl.BlockSpec((4, some, width), lambda i: (0, i, 0)),
                  pl.BlockSpec((local, width // steps, ff), lambda i: (0, i, 0)),
                  pl.BlockSpec((local, ff // steps, width), lambda i: (0, i, 0))],
        out_specs=[qkv, out, pl.BlockSpec((some, width), lambda i: (i % per, i // per)), pl.BlockSpec((some, width), lambda i: (i, 0)),
                   qkv, out, pl.BlockSpec((local, width // steps, ff), lambda i: (0, i, 0)),
                   pl.BlockSpec((local, ff // steps, width), lambda i: (0, i, 0))],
        compiler_params=pltpu.CompilerParams(vmem_limit_bytes=VMEM_BYTES),
        cost_estimate=pl.CostEstimate(flops=0, bytes_accessed=int(40e6), transcendentals=0),
    )(fin, e1, e2)


def solution(mesh):
    owners, shards = mesh.shape["expert"], mesh.shape["shard"]
    both = ("expert", "shard")
    return jax.shard_map(
        functools.partial(per_device, owners, shards),
        mesh=mesh,
        in_specs=(
            P(both, None, None), P(both, None, None), P(both, None, None), P(both), P(),
            P(None, "shard", None), P("shard", None), P("shard", None), P("shard", None), P(None, "shard"),
            P(None, "shard", None), P("shard", None), P("shard", None), P(None, "shard"),
            P("expert", None, None), P("expert", None, None),
        ),
        out_specs=(
            P(both, None, None), P(), P(both, None, None),
            P(None, "shard", None), P("shard", None), P("shard", None), P("shard", None), P(None, "shard"),
            P(None, "shard", None), P("shard", None), P("shard", None), P(None, "shard"),
            P("expert", None, None), P("expert", None, None),
        ),
        check_vma=False,
    )
```

```python
import functools

import jax
import jax.numpy as jnp
from jax import lax
from jax.experimental import pallas as pl
from jax.experimental.pallas import tpu as pltpu
from jax.sharding import PartitionSpec as P

HEADS = 8
CAP = 40
EPS = 1e-06
NEG = -1e30
LANES = 128
f32 = jnp.float32
bf16 = jnp.bfloat16
ANY = pl.BlockSpec(memory_space=pl.ANY)
VM = pl.BlockSpec(memory_space=pltpu.VMEM)
VMEM_BYTES = 58 << 20


def nn(a, b):
    return lax.dot_general(a, b, (((1,), (0,)), ((), ())), preferred_element_type=f32)


def nt(a, b):
    return lax.dot_general(a, b, (((1,), (1,)), ((), ())), preferred_element_type=f32)


def tn(a, b):
    return lax.dot_general(a, b, (((0,), (0,)), ((), ())), preferred_element_type=f32)


def sds(shape, dtype):
    return jax.ShapeDtypeStruct(shape, dtype)


def padded(seq):
    return -(-seq // 16) * 16


def norm(x):
    xc = x - jnp.mean(x, axis=-1, keepdims=True)
    rs = lax.rsqrt(jnp.mean(xc * xc, axis=-1, keepdims=True) + EPS)
    return xc * rs, rs


def norm_back(dyn, xn, rs, gain):
    dgain = jnp.sum(dyn * xn, axis=0, keepdims=True)
    dxn = dyn * gain
    dv = dxn - jnp.mean(dxn, axis=-1, keepdims=True)
    dv = (dv - xn * jnp.mean(dxn * xn, axis=-1, keepdims=True)) * rs
    return dv, dgain


def gelu_pair(z):
    a = jnp.abs(z)
    t = 1.0 / (1.0 + (0.3275911 * 0.7071067811865476) * a)
    e = jnp.exp(-0.5 * (z * z))
    q = t * (0.127414796 + t * (-0.142248368 + t * (0.7107068705 + t * (-0.7265760135 + t * 0.5307027145))))
    q = q * e
    phi = jnp.where(z >= 0.0, 1.0 - q, q)
    return z * phi, phi + z * (e * 0.3989422804014327)


class Split:
    def __init__(self, shards):
        self.pair = shards == 2
        self.shards = shards

    def gather(self, owns):
        if not self.pair:
            whole = [lax.all_gather(o, "shard", axis=1, tiled=True) for o in owns]
            return whole
        core = lax.axis_index("expert") % 2
        owners = lax.axis_size("expert")
        half = owns[0].shape[1] // 2
        send = jnp.concatenate([lax.dynamic_slice_in_dim(o, core * half, half, 1) for o in owns], axis=0)
        far = lax.ppermute(send, "shard", [(0, 1), (1, 0)])
        near = lax.ppermute(far, "expert", [(i, i ^ 1) for i in range(owners)])
        return list(owns) + [far, near]

    def count(self, owns):
        return owns + 2 if self.pair else owns

    def copies(self, refs, full, sems):
        out = []
        if not self.pair:
            at = 0
            for i, r in enumerate(refs):
                n = r.shape[0]
                out.append(pltpu.make_async_copy(r, full.at[at:at + n], sems.at[i]))
                at += n
            return out
        me = lax.axis_index("shard")
        core = lax.axis_index("expert") % 2
        rows = refs[0].shape[1]
        half = rows // 2
        at = 0
        for i, r in enumerate(refs[:-2]):
            n = r.shape[0]
            out.append(pltpu.make_async_copy(r, full.at[at:at + n, pl.ds(me * rows, rows), :], sems.at[i]))
            at += n
        base = (1 - me) * rows
        k = len(refs) - 2
        out.append(pltpu.make_async_copy(refs[k], full.at[:, pl.ds(base + core * half, half), :], sems.at[k]))
        out.append(pltpu.make_async_copy(refs[k + 1], full.at[:, pl.ds(base + (1 - core) * half, half), :], sems.at[k + 1]))
        return out


def start(copies):
    for c in copies:
        c.start()


def finish(copies):
    for c in copies:
        c.wait()


def call(body, outs, ins, scratch=(), specs=None, flops=0, nbytes=0, **kw):
    return pl.pallas_call(
        body,
        out_shape=outs,
        in_specs=specs or [VM] * len(ins),
        out_specs=[VM] * len(outs),
        scratch_shapes=list(scratch),
        compiler_params=pltpu.CompilerParams(vmem_limit_bytes=VMEM_BYTES),
        cost_estimate=pl.CostEstimate(flops=int(flops), bytes_accessed=int(nbytes), transcendentals=0),
        **kw,
    )(*ins)


def pad_store(ref, block, images, seq, step):
    ref[...] = jnp.zeros(ref.shape, ref.dtype)
    for i in range(images):
        ref[i * step:i * step + seq, :] = block(i).astype(ref.dtype)


def slot_start(expert, local, block):
    owner = jnp.floor((expert.astype(f32) + 0.5) * (1.0 / local))
    return owner * block + (expert.astype(f32) - owner * local) * CAP


def route_body(images, seq, local, block, r_ref, live_ref, cot_ref, dy_ref, dyd_ref, disp_ref, back_ref):
    step = r_ref.shape[0] // images
    pad_store(dy_ref, lambda i: cot_ref[i], images, seq, step)
    dy_ref[...] = (dy_ref[...].astype(f32) * live_ref[...]).astype(bf16)
    route_tables(local, block, r_ref, disp_ref, back_ref)
    dyd_ref[...] = nn(disp_ref[...], dy_ref[...]).astype(bf16)


def route_tables(local, block, r_ref, disp_ref, back_ref):
    rows = r_ref.shape[0]
    slots = disp_ref.shape[0]
    lane = lax.broadcasted_iota(jnp.int32, (rows, LANES), 1)
    hit = (r_ref[:, 0:1] == lane) | (r_ref[:, 1:2] == lane)
    ti = lax.broadcasted_iota(jnp.int32, (rows, rows), 0)
    tj = lax.broadcasted_iota(jnp.int32, (rows, rows), 1)
    place = nn((ti > tj).astype(f32).astype(bf16), hit.astype(f32).astype(bf16))
    place = jnp.where(hit, place, -1.0).astype(bf16)
    off = lax.broadcasted_iota(jnp.int32, (LANES, slots), 1).astype(f32) - slot_start(
        lax.broadcasted_iota(jnp.int32, (LANES, slots), 0), local, block)
    spread = ((off >= 0) & (off < CAP)).astype(f32)
    within = jnp.sum(spread * off, axis=0, keepdims=True)
    within = jnp.where(jnp.sum(spread, axis=0, keepdims=True) > 0, within, -2.0)
    back_ref[...] = (nn(place, spread.astype(bf16)) == within).astype(f32).astype(bf16)
    off = lax.broadcasted_iota(jnp.int32, (slots, LANES), 0).astype(f32) - slot_start(
        lax.broadcasted_iota(jnp.int32, (slots, LANES), 1), local, block)
    spread_t = ((off >= 0) & (off < CAP)).astype(f32)
    within_t = jnp.sum(spread_t * off, axis=1, keepdims=True)
    within_t = jnp.where(jnp.sum(spread_t, axis=1, keepdims=True) > 0, within_t, -2.0)
    disp_ref[...] = (nt(spread_t.astype(bf16), place) == within_t).astype(f32).astype(bf16)
    return hit.astype(f32)


def attend_forward(step, seq, images, x, gain, wq, wo, qkv_ref, mix_ref, tick=None, image_tick=None):
    width = x.shape[1]
    head = width // HEADS
    scale = head ** -0.5
    xn, _ = norm(x)
    a = (xn * gain).astype(bf16)
    for c in range(3):
        qkv_ref[:, c * width:(c + 1) * width] = nn(a, wq[c][...]).astype(bf16)
    if tick is not None:
        tick()
    lane = lax.broadcasted_iota(jnp.int32, (1, LANES), 1)
    col = lax.broadcasted_iota(jnp.int32, (1, step), 1)
    per = LANES // head

    def image(i, _):
        at = pl.ds(pl.multiple_of(i * step, step), step)
        for hp in range(width // LANES):
            q = qkv_ref[at, hp * LANES:(hp + 1) * LANES]
            k = qkv_ref[at, width + hp * LANES:width + (hp + 1) * LANES]
            v = qkv_ref[at, 2 * width + hp * LANES:2 * width + (hp + 1) * LANES]
            got = None
            for h in range(per):
                mine = (lane >= h * head) & (lane < (h + 1) * head)
                qm = q * jnp.where(mine, scale, 0.0).astype(bf16)
                s = jnp.where(col < seq, nt(qm, k), NEG)
                e = jnp.exp(s - jnp.max(s, axis=-1, keepdims=True))
                p = (e * (1.0 / jnp.sum(e, axis=-1, keepdims=True))).astype(bf16)
                o = nn(p, v)
                got = o if got is None else jnp.where(mine, o, got)
            mix_ref[at, hp * LANES:(hp + 1) * LANES] = got.astype(bf16)
        if image_tick is not None:
            image_tick(i)
        return 0

    lax.fori_loop(0, images, image, 0)
    return x + nn(mix_ref[...], wo[...])


def attend_backward(step, seq, images, grad, x, gain, wq, wo, qkv_ref, mix_ref, dmix_ref, dqkv_ref, pack_ref, base,
                    tick=None):
    width = x.shape[1]
    head = width // HEADS
    scale = head ** -0.5
    shards = pack_ref.shape[0]
    part = width // shards
    low = grad.astype(bf16)
    dwo = tn(mix_ref[...], low).astype(bf16)
    for s in range(shards):
        pack_ref[s, base + 3 * part:base + 4 * part, :] = dwo[s * part:(s + 1) * part]
    dmix_ref[...] = nt(low, wo[...]).astype(bf16)
    lane = lax.broadcasted_iota(jnp.int32, (1, LANES), 1)
    key = lax.broadcasted_iota(jnp.int32, (step, 1), 0)
    per = LANES // head

    def image(i, _):
        at = pl.ds(pl.multiple_of(i * step, step), step)
        for hp in range(width // LANES):
            q = qkv_ref[at, hp * LANES:(hp + 1) * LANES]
            k = qkv_ref[at, width + hp * LANES:width + (hp + 1) * LANES]
            v = qkv_ref[at, 2 * width + hp * LANES:2 * width + (hp + 1) * LANES]
            do = dmix_ref[at, hp * LANES:(hp + 1) * LANES]
            dq = dk = dv = None
            for h in range(per):
                mine = (lane >= h * head) & (lane < (h + 1) * head)
                scaled = jnp.where(mine, scale, 0.0).astype(bf16)
                km = k * scaled
                s = jnp.where(key < seq, nt(km, q), NEG)
                e = jnp.exp(s - jnp.max(s, axis=0, keepdims=True))
                p = e * (1.0 / jnp.sum(e, axis=0, keepdims=True))
                dom = do * jnp.where(mine, 1.0, 0.0).astype(bf16)
                dp = nt(v, dom)
                ds = (p * (dp - jnp.sum(p * dp, axis=0, keepdims=True))).astype(bf16)
                hv = nn(p.astype(bf16), dom)
                hk = nn(ds, q * scaled)
                hq = tn(ds, km)
                dq, dk, dv = (hq, hk, hv) if dq is None else (dq + hq, dk + hk, dv + hv)
            dqkv_ref[at, hp * LANES:(hp + 1) * LANES] = dq.astype(bf16)
            dqkv_ref[at, width + hp * LANES:width + (hp + 1) * LANES] = dk.astype(bf16)
            dqkv_ref[at, 2 * width + hp * LANES:2 * width + (hp + 1) * LANES] = dv.astype(bf16)
        if tick is not None:
            tick(i)
        return 0

    lax.fori_loop(0, images, image, 0)
    xn, rs = norm(x)
    a = (xn * gain).astype(bf16)
    da = None
    for c in range(3):
        d = dqkv_ref[:, c * width:(c + 1) * width]
        dw = tn(a, d).astype(bf16)
        for s in range(shards):
            pack_ref[s, base + c * part:base + (c + 1) * part, :] = dw[s * part:(s + 1) * part]
        one = nt(d, wq[c][...])
        da = one if da is None else da + one
    return norm_back(da, xn, rs, gain)


def block1_body(split, images, seq, x_ref, gain_ref, *refs):
    n = split.count(2)
    pieces, (hidden_ref, qkv_ref, mix_ref, w, sems) = refs[:n], refs[n:]
    copies = split.copies(pieces, w, sems)
    start(copies)
    step = hidden_ref.shape[0] // images
    pad_store(hidden_ref, lambda i: x_ref[i], images, seq, step)
    finish(copies)
    hidden_ref[...] = attend_forward(
        step, seq, images, hidden_ref[...], gain_ref[0:1, :], [w.at[c] for c in range(3)], w.at[3], qkv_ref, mix_ref
    )


def mlp_body(split, hidden_ref, gain_ref, *refs):
    n = 2 * split.count(1)
    pieces, (out_ref, act_ref, slope_ref, w1, w2, sems) = refs[:n], refs[n:]
    half = n // 2
    copies = split.copies(pieces[:half], w1, sems.at[0]) + split.copies(pieces[half:], w2, sems.at[1])
    start(copies)
    hidden = hidden_ref[...]
    xn, _ = norm(hidden)
    u = (xn * gain_ref[1:2, :]).astype(bf16)
    out_ref[...] = hidden
    finish(copies)
    wide = act_ref.shape[2]
    for b in range(act_ref.shape[0]):
        at = slice(b * wide, (b + 1) * wide)
        act, slope = gelu_pair(nn(u, w1[0, :, at]))
        act = act.astype(bf16)
        act_ref[b] = act
        slope_ref[b] = slope.astype(bf16)
        out_ref[...] += nn(act, w2[0, at, :])


def router_probs(u, router, experts):
    lane = lax.broadcasted_iota(jnp.int32, (1, LANES), 1)
    logits = jnp.where(lane < experts, nn(u, router), NEG)
    e = jnp.exp(logits - jnp.max(logits, axis=-1, keepdims=True))
    return e * (1.0 / jnp.sum(e, axis=-1, keepdims=True))


def block2_body(split, images, seq, experts, x_ref, gain_ref, router_ref, disp_ref, live_ref, load_ref, *refs):
    n = split.count(2)
    pieces, (hidden_ref, qkv_ref, mix_ref, u_ref, probs_ref, sum_ref, ud_ref, w, sems) = refs[:n], refs[n:]
    copies = split.copies(pieces, w, sems)
    start(copies)
    finish(copies)
    step = hidden_ref.shape[0] // images
    hidden = attend_forward(
        step, seq, images, x_ref[...], gain_ref[2:3, :], [w.at[c] for c in range(3)], w.at[3], qkv_ref, mix_ref
    )
    hidden_ref[...] = hidden
    xn, _ = norm(hidden)
    u = (xn * gain_ref[3:4, :]).astype(bf16)
    u_ref[...] = u
    ud_ref[...] = nn(disp_ref[...], u).astype(bf16)
    probs = router_probs(u, router_ref[...], experts)
    probs_ref[...] = probs
    sums = jnp.sum(probs * live_ref[...], axis=0, keepdims=True)
    sum_ref[...] = jnp.concatenate([load_ref[...], sums, jnp.zeros((6, LANES), f32)], axis=0)


def forward_body(images, seq, experts, local, owners, *refs):
    (routes_ref, counts_ref, tok_ref, cot_ref, gain1_ref, gain2_ref, small_router_ref, q1_h, o1_h, up_h, down_h, q2_h, o2_h,
     gains_out, router_out, stat_out, live_out,
     dy_o, uout_o, hid1_o, x2_o, hid2_o, qkv1_o, mix1_o, qkv2_o, mix2_o, act_o, slope_o, u_o, probs_o, back_o,
     wa_o, wu_o, wd_o, wb_o, dyin_o,
     wa, wu, wd, wb, dy, slot_rows, disp, back, hid1, x2, hid2, qkv1, mix1, qkv2, mix2, act, slope, u, probs, gx, gain_ref, router_ref, r_ref,
     lsem, osem, ks, kr, vs, vr) = refs
    me, x = lax.axis_index("expert"), lax.axis_index("shard")
    bits = owners.bit_length() - 1
    b0, b1 = me % 2, (me // 2) % 2
    core, side = me + 1 - 2 * b0, me + (1 - 2 * b1) * 2
    rows, width = dy.shape
    step = rows // images
    part = width // 2
    ff = wd.shape[1]
    fpart = ff // 2

    def to(e, s):
        return dict(device_id=(e, s), device_id_type=pl.DeviceIdType.MESH)

    def each(lo, hi, f):
        lax.fori_loop(lo, hi, lambda k, c: (f(k), c)[1], 0)

    barrier = pltpu.get_barrier_semaphore()
    each(1, owners, lambda k: pl.semaphore_signal(barrier, inc=1, **to(xor(me, k, bits), x)))
    pl.semaphore_signal(barrier, inc=1, **to(me, 1 - x))

    def at(first, size):
        return pl.ds(pl.multiple_of(first, 64), size)

    mine, theirs = x * part, (1 - x) * part
    loads = [
        pltpu.make_async_copy(q1_h, wa.at[0:3, at(mine, part)], lsem.at[0]),
        pltpu.make_async_copy(o1_h, wa.at[3, at(mine, part)], lsem.at[1]),
        pltpu.make_async_copy(up_h, wu.at[0, at(mine, part)], lsem.at[2]),
        pltpu.make_async_copy(down_h, wd.at[0, at(x * fpart, fpart)], lsem.at[3]),
        pltpu.make_async_copy(q2_h, wb.at[0:3, at(mine, part)], lsem.at[4]),
        pltpu.make_async_copy(o2_h, wb.at[3, at(mine, part)], lsem.at[5]),
    ]
    start(loads)
    router_ref[...] = jnp.concatenate([small_router_ref[...].astype(f32), jnp.zeros((part, LANES - experts), f32)], axis=1).astype(bf16)
    router_out[at(mine, part), :] = router_ref[...]
    gain_ref[...] = jnp.concatenate([gain1_ref[...].astype(f32), gain2_ref[...].astype(f32), jnp.zeros((4, part), f32)], axis=0)
    pl.semaphore_wait(barrier, owners)

    def remote(src, dst, i, peer):
        return pltpu.make_async_remote_copy(src, dst, ks.at[i], kr.at[i], **peer)

    far, near, over = to(me, 1 - x), to(core, x), to(side, x)
    half, quarter, fquarter = part // 2, part // 4, fpart // 4
    p = b0 * 2 + b1
    h = b0 * half
    here = at(theirs + h, half)
    moves = {
        "small": [lambda: remote(gain_ref, gx, 0, far), lambda: remote(router_ref, router_out.at[at(mine, part), :], 1, far)],
        "ax": [lambda: remote(q1_h.at[:, at(h, half)], wa.at[0:3, at(mine + h, half)], 2, far),
               lambda: remote(o1_h.at[at(h, half)], wa.at[3, at(mine + h, half)], 3, far)],
        "ac": [lambda: remote(wa.at[:, here], wa.at[:, here], 4, near)],
        "ux": [lambda: remote(up_h.at[at(p * quarter, quarter)], wu.at[0, at(mine + p * quarter, quarter)], 5, far)],
        "uy": [lambda: remote(wu.at[0, at(theirs + p * quarter, quarter)], wu.at[0, at(theirs + p * quarter, quarter)], 6, over)],
        "uc": [lambda: remote(wu.at[0, here], wu.at[0, here], 7, near)],
        "dx": [lambda: remote(down_h.at[at(p * fquarter, fquarter)], wd.at[0, at(x * fpart + p * fquarter, fquarter)], 8, far)],
        "dy": [lambda: remote(wd.at[0, at((1 - x) * fpart + p * fquarter, fquarter)],
                              wd.at[0, at((1 - x) * fpart + p * fquarter, fquarter)], 9, over)],
        "dc": [lambda: remote(wd.at[0, at((1 - x) * fpart + b0 * 2 * fquarter, 2 * fquarter)],
                              wd.at[0, at((1 - x) * fpart + b0 * 2 * fquarter, 2 * fquarter)], 10, near)],
        "bx": [lambda: remote(q2_h.at[:, at(p * quarter, quarter)], wb.at[0:3, at(mine + p * quarter, quarter)], 11, far),
               lambda: remote(o2_h.at[at(p * quarter, quarter)], wb.at[3, at(mine + p * quarter, quarter)], 12, far)],
        "by": [lambda: remote(wb.at[:, at(theirs + p * quarter, quarter)], wb.at[:, at(theirs + p * quarter, quarter)], 13, over)],
        "bc": [lambda: remote(wb.at[:, here], wb.at[:, here], 14, near)],
    }

    def go(*names):
        for n in names:
            for m in moves[n]:
                m().start()

    def done(*names):
        for n in names:
            for m in moves[n]:
                m().wait()

    def send_dy(k):
        q = xor(me, k, bits)
        return pltpu.make_async_remote_copy(slot_rows.at[0, q], dyin_o.at[me], vs.at[k], vr.at[k], **to(q, x))

    out = []

    def keep(src, dst):
        c = pltpu.make_async_copy(src, dst, osem.at[len(out)])
        c.start()
        out.append(c)

    go("ax", "small")
    r_ref[...] = jnp.full(r_ref.shape, -1, jnp.int32)
    for i in range(images):
        r_ref[i * step:i * step + seq, :] = routes_ref[i]
    row = lax.broadcasted_iota(jnp.int32, (rows, 1), 0)
    live = ((row < counts_ref[0] * step) & (r_ref[:, 0:1] >= 0)).astype(f32)
    live_out[...] = live
    pad_store(dy, lambda i: cot_ref[i], images, seq, step)
    dy[...] = (dy[...].astype(f32) * live).astype(bf16)
    keep(dy, dy_o)
    hit = route_tables(local, slot_rows.shape[2], r_ref, disp, back)
    keep(back, back_o)
    slot_rows[0] = nn(disp[...], dy[...]).astype(bf16).reshape(slot_rows.shape[1:])
    keep(slot_rows.at[0, me], dyin_o.at[me])
    lane = lax.broadcasted_iota(jnp.int32, (1, LANES), 1)
    load = jnp.where(lane == LANES - 1, jnp.sum(live, axis=0, keepdims=True), jnp.sum(hit * live, axis=0, keepdims=True))
    done("ax")
    go("ac", "ux", "dx")
    planes = owners // 4
    each(0, planes, lambda k: send_dy(4 * (planes - 1 - k) + 1).start())
    each(0, planes - 1, lambda k: send_dy(4 * (planes - 1 - k)).start())
    pad_store(hid1, lambda i: tok_ref[i], images, seq, step)
    done("small")
    own_gain, far_gain = gain_ref[...], gx[...]
    gains = jnp.where(x == 0, jnp.concatenate([own_gain, far_gain], axis=1), jnp.concatenate([far_gain, own_gain], axis=1))
    gains_out[...] = gains
    finish(loads)
    done("ac")
    keep(wa, wa_o)

    def first_tick():
        go("bx")

    def first_image(i):
        @pl.when(i == 0)
        def _():
            done("ux")
            go("uy")

        @pl.when(i == 1)
        def _():
            done("dx")
            go("dy")

        @pl.when(i == 2)
        def _():
            done("uy")
            go("uc")

    hid1[...] = attend_forward(step, seq, images, hid1[...], gains[0:1], [wa.at[c] for c in range(3)], wa.at[3], qkv1, mix1,
                               first_tick, first_image)
    keep(hid1, hid1_o)
    keep(qkv1, qkv1_o)
    keep(mix1, mix1_o)

    done("uc")
    keep(wu, wu_o)
    xn, _ = norm(hid1[...])
    a = (xn * gains[1:2]).astype(bf16)
    for b in range(act.shape[0]):
        one, two = gelu_pair(nn(a, wu[0, :, b * width:(b + 1) * width]))
        act[b] = one.astype(bf16)
        slope[b] = two.astype(bf16)
        if b == 0:
            done("bx")
            go("by")
        if b == 1:
            done("dy")
            go("dc")
            each(0, planes, lambda k: send_dy(4 * (planes - 1 - k) + 3).start())
            each(0, planes, lambda k: send_dy(4 * (planes - 1 - k) + 2).start())
    keep(slope, slope_o)
    keep(act, act_o)
    done("dc")
    keep(wd, wd_o)
    total = hid1[...]
    for b in range(act.shape[0]):
        total = total + nn(act[b], wd[0, b * width:(b + 1) * width, :])
        if b == 0:
            done("by")
            go("bc")
    x2[...] = total
    done("bc")
    keep(wb, wb_o)
    keep(x2, x2_o)

    hid2[...] = attend_forward(step, seq, images, x2[...], gains[2:3], [wb.at[c] for c in range(3)], wb.at[3], qkv2, mix2)
    keep(qkv2, qkv2_o)
    keep(mix2, mix2_o)
    keep(hid2, hid2_o)
    xn, _ = norm(hid2[...])
    u[...] = (xn * gains[3:4]).astype(bf16)
    keep(u, u_o)
    slot_rows[1] = nn(disp[...], u[...]).astype(bf16).reshape(slot_rows.shape[1:])
    keep(slot_rows.at[1], uout_o)
    probs[...] = router_probs(u[...], router_out[...], experts)
    keep(probs, probs_o)
    sums = jnp.sum(probs[...] * live, axis=0, keepdims=True)
    stat_out[...] = jnp.concatenate([load, sums, jnp.zeros((6, LANES), f32)], axis=0)
    each(1, owners, lambda k: send_dy(k).wait())
    finish(out)


def fused_forward(owners, experts, local, block, tokens, cotangent, routes, counts, gains1, gains2, router, attn_qkv1, attn_out1, mlp_in, mlp_out,
                  attn_qkv2, attn_out2):
    images, seq, width = tokens.shape
    step = padded(seq)
    rows = images * step
    ff = mlp_in.shape[1]
    slots = owners * block[1]
    blocks = ff // width
    part = width // 2
    V, sem = pltpu.VMEM, pltpu.SemaphoreType.DMA
    kept = [
        ((rows, width), bf16), (block, bf16), ((rows, width), f32), ((rows, width), f32), ((rows, width), f32),
        ((rows, 3 * width), bf16), ((rows, width), bf16), ((rows, 3 * width), bf16), ((rows, width), bf16),
        ((blocks, rows, width), bf16), ((blocks, rows, width), bf16), ((rows, width), bf16), ((rows, LANES), f32), ((rows, slots), bf16),
        ((4, width, width), bf16), ((1, width, ff), bf16), ((1, ff, width), bf16), ((4, width, width), bf16), (block, bf16),
    ]
    return pl.pallas_call(
        functools.partial(forward_body, images, seq, experts, local, owners),
        out_shape=[sds((8, width), f32), sds((width, LANES), bf16), sds((8, LANES), f32), sds((rows, 1), f32)]
        + [sds(shape, dtype) for shape, dtype in kept],
        in_specs=[VM, pl.BlockSpec(memory_space=pltpu.SMEM)] + [VM] * 5 + [ANY] * 6,
        out_specs=[VM] * 4 + [ANY] * len(kept),
        scratch_shapes=[
            V((4, width, width), bf16), V((1, width, ff), bf16), V((1, ff, width), bf16), V((4, width, width), bf16),
            V((rows, width), bf16), V((2,) + block, bf16), V((slots, rows), bf16), V((rows, slots), bf16),
            V((rows, width), f32), V((rows, width), f32), V((rows, width), f32),
            V((rows, 3 * width), bf16), V((rows, width), bf16), V((rows, 3 * width), bf16), V((rows, width), bf16),
            V((blocks, rows, width), bf16), V((blocks, rows, width), bf16), V((rows, width), bf16), V((rows, LANES), f32),
            V((8, part), f32), V((8, part), f32), V((part, LANES), bf16), V((rows, 2), jnp.int32),
            sem((6,)), sem((len(kept),)), sem((15,)), sem((15,)), sem((owners,)), sem((owners,)),
        ],
        compiler_params=pltpu.CompilerParams(vmem_limit_bytes=VMEM_BYTES, collective_id=2, has_side_effects=True),
        cost_estimate=pl.CostEstimate(flops=int(18e9), bytes_accessed=int(60e6), transcendentals=0),
    )(routes, counts, tokens, cotangent, gains1, gains2, router, attn_qkv1, attn_out1, mlp_in, mlp_out, attn_qkv2, attn_out2)


def split_rows(block, local):
    n, r, w = block.shape
    v = block.astype(f32)
    if r != local * CAP:
        v = v[:, :local * CAP]
    v = v.reshape(n, local, CAP, w)
    return [v[:, i].reshape(n * CAP, w) for i in range(local)]


def join_rows(parts, sources, block):
    local = len(parts)
    w = parts[0].shape[1]
    v = jnp.concatenate([p.reshape(sources, 1, CAP, w) for p in parts], axis=1).reshape(sources, local * CAP, w)
    if block != local * CAP:
        v = jnp.concatenate([v, jnp.zeros((sources, block - local * CAP, w), f32)], axis=1)
    return v


def gate_of(u, router, experts, e):
    lane = lax.broadcasted_iota(jnp.int32, (1, LANES), 1)
    return jnp.sum(jnp.where(lane == e, router_probs(u, router, experts), 0.0), axis=-1, keepdims=True)


def xor(a, b, bits):
    out = 0
    for i in range(bits):
        out = out + ((a // (1 << i) + b // (1 << i)) % 2) * (1 << i)
    return out


def expert_body(owners, shards, local, experts, group, uout_ref, dy_ref, router_ref, stat_ref, w1_hbm, w2_hbm,
                uin_ref, served_ref, duback_ref, dgback_ref, total_ref, dyx_ref, ux_ref, *refs):
    if shards == 2:
        p1_h, p2_h, *refs = refs
    (w1, w2, dusend, dgsend, statx, state, acts, dzs, urows, drows, ob1, ob2, wsem, lsem, osem, us, ur, ds_, dr, gs, gr, ss, sr, fs, fr, xs, xr, ys, yr) = refs
    me, x = lax.axis_index("expert"), lax.axis_index("shard")
    bits = owners.bit_length() - 1
    barrier = pltpu.get_barrier_semaphore()

    def at(e, s):
        return dict(device_id=(e, s), device_id_type=pl.DeviceIdType.MESH)

    def each(lo, hi, f):
        lax.fori_loop(lo, hi, lambda k, c: (f(k), c)[1], 0)

    def peer(k):
        return xor(me, k, bits)

    each(1, owners, lambda k: pl.semaphore_signal(barrier, inc=1, **at(peer(k), x)))
    each(1, shards, lambda k: pl.semaphore_signal(barrier, inc=1, **at(me, (x + k) % shards)))
    weights = [pltpu.make_async_copy(w1_hbm, w1, wsem.at[0]), pltpu.make_async_copy(w2_hbm, w2, wsem.at[1])]
    start(weights)
    own = pltpu.make_async_copy(uout_ref.at[me], uin_ref.at[me], lsem.at[0])
    own.start()
    pl.semaphore_wait(barrier, owners - 1 + shards - 1)

    def send_u(k):
        return pltpu.make_async_remote_copy(uout_ref.at[peer(k)], uin_ref.at[me], us.at[k], ur.at[k], **at(peer(k), x))

    def send_du(k):
        return pltpu.make_async_remote_copy(dusend.at[peer(k)], duback_ref.at[me], ds_.at[k], dr.at[k], **at(peer(k), x))

    def send_dg(k):
        return pltpu.make_async_remote_copy(dgsend.at[peer(k)], dgback_ref.at[me], gs.at[k], gr.at[k], **at(peer(k), x))

    def send_statx(k):
        return pltpu.make_async_remote_copy(stat_ref, statx.at[k], xs.at[k], xr.at[k], **at(me, (x + k) % shards))

    def send_dyx(k):
        return pltpu.make_async_remote_copy(dy_ref, dyx_ref.at[k - 1], ys.at[k], yr.at[k], **at(me, (x + k) % shards))

    def send_far(g):
        rows = pl.ds(xor(me // group, g, bits) * group, group)
        return pltpu.make_async_remote_copy(uin_ref.at[rows], ux_ref.at[rows], fs.at[g], fr.at[g], **at(me, (x + 1) % shards))

    def send_state(k):
        return pltpu.make_async_remote_copy(state.at[0], state.at[k], ss.at[k], sr.at[k], **at(peer(k), x))

    each(1, shards, lambda k: send_statx(k).start())
    each(1, owners, lambda k: send_u(owners - k).start())
    each(1, shards, lambda k: send_dyx(k).start())
    each(1, shards, lambda k: send_statx(k).wait())
    sums = stat_ref[...]
    for k in range(1, shards):
        sums = sums + statx[k]
    state[0] = sums
    each(1, owners, lambda k: send_state(k).start())
    finish(weights)

    def work(g):
        base = xor(me // group, g, bits) * group
        rows = pl.ds(base, group)
        us_, dys = split_rows(uin_ref[rows], local), split_rows(dy_ref[rows], local)
        served, dus, prods = [], [], []
        for i in range(local):
            u, dy = us_[i].astype(bf16), dys[i]
            gate = gate_of(u, router_ref[...], experts, me * local + i)
            dsv = (gate * dy).astype(bf16)
            act, slope = gelu_pair(nn(u, w1[i]))
            out = nn(act.astype(bf16), w2[i])
            dz = (slope * nt(dsv, w2[i])).astype(bf16)
            if shards == 2:
                n = group * CAP
                spot = pl.ds(pl.multiple_of(g * n, n), n)
                acts[i, spot] = act.astype(bf16)
                dzs[i, spot] = dz
                urows[i, spot] = u
                drows[i, spot] = dsv
            dus.append(nt(dz, w1[i]))
            served.append(gate * out)
            prods.append(dy * out)
        block = uin_ref.shape[1]
        served_ref[rows] = join_rows(served, group, block).astype(bf16)
        dusend[rows] = join_rows(dus, group, block).astype(bf16)
        prod = join_rows(prods, group, block)
        ones = jnp.ones((8, prod.shape[2]), bf16)
        for j in range(group):
            hi = prod[j].astype(bf16)
            lo = (prod[j] - hi.astype(f32)).astype(bf16)
            dgsend[base + j, :, 0:block] = nt(ones, hi) + nt(ones, lo)

    def step(g):
        @pl.when(g == 0)
        def _():
            own.wait()

        for j in range(group):
            k = g * group + j
            if j == 0:
                pl.when(g > 0)(lambda k=k: send_u(k).wait_recv())
            else:
                send_u(k).wait_recv()
        if shards == 2:
            send_far(g).start()
        work(g)
        for j in range(group):
            k = g * group + j
            if j == 0:
                @pl.when(g > 0)
                def _(k=k):
                    send_du(k).start()
                    send_dg(k).start()
            else:
                send_du(k).start()
                send_dg(k).start()

    each(0, owners // group, step)
    backs = [pltpu.make_async_copy(dusend.at[me], duback_ref.at[me], lsem.at[0]),
             pltpu.make_async_copy(dgsend.at[me], dgback_ref.at[me], lsem.at[1])]
    start(backs)
    if shards == 2:
        width = urows.shape[2]
        blocks = acts.shape[2] // width

        def result(i):
            e, f = i // blocks, i % blocks
            col = pl.ds(pl.multiple_of(f * width, width), width)
            return [pltpu.make_async_copy(ob1.at[i % 2], p1_h.at[e, :, col], osem.at[i % 2]),
                    pltpu.make_async_copy(ob2.at[i % 2], p2_h.at[e, col, :], osem.at[2 + i % 2])]

        def gradient(i):
            e, f = i // blocks, i % blocks
            col = pl.ds(pl.multiple_of(f * width, width), width)
            pl.when(i >= 2)(lambda: finish(result(i - 2)))
            ob1[i % 2] = tn(urows[e], dzs[e, :, col]).astype(bf16)
            ob2[i % 2] = tn(acts[e, :, col], drows[e]).astype(bf16)
            start(result(i))

        count = local * blocks
        each(0, count, gradient)
        for i in range(max(0, count - 2), count):
            finish(result(i))
    each(1, owners, lambda k: send_state(k).wait())
    total = state[0]
    for k in range(1, owners):
        total = total + state[k]
    total_ref[...] = total
    each(1, owners, lambda k: send_u(k).wait_send())
    finish(backs)
    each(1, shards, lambda k: send_dyx(k).wait())
    if shards == 2:
        each(0, owners // group, lambda g: send_far(g).wait())
    each(1, owners, lambda k: send_du(k).wait())
    each(1, owners, lambda k: send_dg(k).wait())


def expert_grad_body(pieces, experts, *refs):
    us, dys = refs[:pieces], refs[pieces:2 * pieces]
    router_ref, w1_ref, w2_ref, g1_ref, g2_ref, urow, drow, stage, sems = refs[2 * pieces:]
    local = pl.num_programs(0)
    e = lax.axis_index("expert") * local + pl.program_id(0)

    @pl.when((pl.program_id(0) == 0) & (pl.program_id(1) == 0))
    def _():
        todo = [(us[i], urow, i) for i in range(pieces)] + [(dys[i], drow, i) for i in range(pieces)]
        copies = [pltpu.make_async_copy(r, stage.at[n % 2], sems.at[n % 2]) for n, (r, _, _) in enumerate(todo)]
        copies[0].start()
        for n, (_, to, i) in enumerate(todo):
            if n + 1 < len(todo):
                copies[n + 1].start()
            copies[n].wait()
            for j, v in enumerate(split_rows(stage[n % 2], urow.shape[1])):
                to[i, j] = v.astype(bf16)

    at = pl.program_id(0)
    for i in range(pieces):
        u = urow[i, at]
        dy = drow[i, at]
        gate = gate_of(u, router_ref[...], experts, e)
        ds = (gate * dy.astype(f32)).astype(bf16)
        act, slope = gelu_pair(nn(u, w1_ref[0]))
        dz = (slope * nt(ds, w2_ref[0])).astype(bf16)
        g1 = tn(u, dz)
        g2 = tn(act.astype(bf16), ds)
        if i == 0:
            g1_ref[0] = g1
            g2_ref[0] = g2
        else:
            g1_ref[0] += g1
            g2_ref[0] += g2


def split3(v):
    hi = v.astype(bf16)
    r = v - hi.astype(f32)
    mid = r.astype(bf16)
    lo = (r - mid.astype(f32)).astype(bf16)
    return hi, mid, lo


def router_backward(experts, dy_ref, u_ref, probs_ref, hidden_ref, gain_ref, router_ref, aux_ref, stat_ref, live_ref,
                    back_ref, ret_ref, dgate_ref, small_ref):
    slots = back_ref.shape[1]
    owners = dgate_ref.shape[0]
    local = experts // owners
    block = slots // owners
    off = lax.broadcasted_iota(jnp.int32, (slots, LANES), 0).astype(f32) - slot_start(
        lax.broadcasted_iota(jnp.int32, (slots, LANES), 1), local, block)
    oe = lax.broadcasted_iota(jnp.int32, (owners, LANES), 0).astype(f32)
    ee = lax.broadcasted_iota(jnp.int32, (owners, LANES), 1).astype(f32)
    pick = ((ee >= oe * local) & (ee < oe * local + local)).astype(f32).astype(bf16)
    column = 0.0
    for part in split3(dgate_ref[:, 0, :]):
        column = column + tn(part, pick)
    table = jnp.where((off >= 0) & (off < CAP), jnp.concatenate([column[0:block]] * owners, axis=0), 0.0)
    lane = lax.broadcasted_iota(jnp.int32, (1, LANES), 1)
    stat = stat_ref[0:1, :]
    total = jnp.sum(jnp.where(lane == LANES - 1, stat, 0.0), axis=-1, keepdims=True)
    fraction = jnp.where(lane < experts, stat, 0.0) / (2.0 * total)
    loss = experts * jnp.sum(fraction * stat_ref[1:2, :] / total, axis=-1, keepdims=True)
    small_ref[LANES + 2:LANES + 3, :] = jnp.broadcast_to(loss, (1, small_ref.shape[1]))
    dprobs = (aux_ref[0, 0] * experts * fraction / total) * live_ref[...]
    for part in split3(table):
        dprobs = dprobs + nn(back_ref[...], part)
    probs = probs_ref[...]
    dlog = (probs * (dprobs - jnp.sum(probs * dprobs, axis=-1, keepdims=True))).astype(bf16)
    small_ref[0:LANES, :] = tn(dlog, u_ref[...])
    du = nn(back_ref[...], ret_ref[...].reshape(slots, dy_ref.shape[1])) + nt(dlog, router_ref[...])
    xn, rs = norm(hidden_ref[...])
    dv, dg = norm_back(du, xn, rs, gain_ref[3:4, :])
    small_ref[LANES:LANES + 1, :] = dg
    grad = dy_ref[...].astype(f32) + dv
    return grad


def back2_body(split, images, seq, experts, dy_ref, u_ref, probs_ref, hidden_ref, x_ref, gain_ref, router_ref, aux_ref,
               stat_ref, live_ref, back_ref, ret_ref, dgate_ref, qkv_ref, mix_ref, *refs):
    n = split.count(2)
    pieces, (grad_ref, pack_ref, small_ref, w, sems, dmix_ref, dqkv_ref) = refs[:n], refs[n:]
    copies = split.copies(pieces, w, sems)
    start(copies)
    grad = router_backward(experts, dy_ref, u_ref, probs_ref, hidden_ref, gain_ref, router_ref, aux_ref, stat_ref, live_ref,
                           back_ref, ret_ref, dgate_ref, small_ref)
    grad_ref[...] = grad
    finish(copies)
    step = hidden_ref.shape[0] // images
    dv, dg = attend_backward(
        step, seq, images, grad, x_ref[...], gain_ref[2:3, :], [w.at[c] for c in range(3)], w.at[3],
        qkv_ref, mix_ref, dmix_ref, dqkv_ref, pack_ref, 0,
    )
    small_ref[LANES + 1:LANES + 2, :] = dg
    grad_ref[...] += dv


def mlp_back_body(split, grad_ref, hidden_ref, gain_ref, act_ref, slope_ref, *refs):
    n = 2 * split.count(1)
    pieces, (out_ref, pack_ref, dgain_ref, w1, w2, sems, du_ref) = refs[:n], refs[n:]
    half = n // 2
    copies = split.copies(pieces[:half], w1, sems.at[0]) + split.copies(pieces[half:], w2, sems.at[1])
    start(copies)
    xn, rs = norm(hidden_ref[...])
    gain = gain_ref[1:2, :]
    u = (xn * gain).astype(bf16)
    grad = grad_ref[...]
    low = grad.astype(bf16)
    finish(copies)
    width = grad.shape[1]
    blocks = act_ref.shape[0]
    ff = blocks * width
    shards = pack_ref.shape[0]
    part, fpart = width // shards, ff // shards
    base = part * blocks
    for b in range(blocks):
        at = slice(b * width, (b + 1) * width)
        dz = (slope_ref[b].astype(f32) * nt(low, w2[0, at, :])).astype(bf16)
        d = nt(dz, w1[0, :, at])
        if b == 0:
            du_ref[...] = d
        else:
            du_ref[...] += d
        gin = tn(u, dz).astype(bf16)
        for s in range(shards):
            pack_ref[s, b * part:(b + 1) * part, :] = gin[s * part:(s + 1) * part]
        gout = tn(act_ref[b], low).astype(bf16)
        per = min(width, fpart)
        for j in range(width // per):
            row = b * width + j * per
            s, off = row // fpart, row % fpart
            pack_ref[s, base + off:base + off + per, :] = gout[j * per:(j + 1) * per]
    dv, dg = norm_back(du_ref[...], xn, rs, gain)
    dgain_ref[...] = dg
    out_ref[...] = grad + dv


def back1_body(split, images, seq, experts, grad_ref, tok_ref, gain_ref, qkv_ref, mix_ref, small_ref, dg2_ref, *refs):
    n = split.count(2)
    pieces, (out_ref, pack_ref, w, sems, x_ref, dmix_ref, dqkv_ref) = refs[:n], refs[n:]
    copies = split.copies(pieces, w, sems)
    start(copies)
    step = x_ref.shape[0] // images
    pad_store(x_ref, lambda i: tok_ref[i], images, seq, step)
    finish(copies)
    width = x_ref.shape[1]
    dv, dg1 = attend_backward(
        step, seq, images, grad_ref[...], x_ref[...], gain_ref[0:1, :], [w.at[c] for c in range(3)], w.at[3],
        qkv_ref, mix_ref, dmix_ref, dqkv_ref, pack_ref, 0,
    )
    x_ref[...] = grad_ref[...] + dv
    for i in range(images):
        out_ref[i] = x_ref[i * step:i * step + seq, :]
    shards = pack_ref.shape[0]
    part = width // shards
    base = 4 * part
    gains = jnp.concatenate(
        [dg1, dg2_ref[...], small_ref[LANES + 1:LANES + 2, :], small_ref[LANES:LANES + 1, :], jnp.zeros((28, width), f32)], axis=0
    )
    both = jnp.concatenate([small_ref[0:32, :], gains], axis=0).astype(bf16)
    for s in range(shards):
        one = both[:, s * part:(s + 1) * part]
        pack_ref[s, base:base + 64, :] = jnp.concatenate([one, jnp.zeros((64, width - part), bf16)], axis=1)


def output_body(images, seq, hidden_ref, back_ref, ret_ref, live_ref, out_ref, tmp_ref):
    step = hidden_ref.shape[0] // images
    tmp_ref[...] = (hidden_ref[...] + nn(back_ref[...], ret_ref[...])) * live_ref[...]
    for i in range(images):
        out_ref[i] = tmp_ref[i * step:i * step + seq, :].astype(bf16)


def backward_body(split, images, seq, experts, local, owners, plan, *refs):
    (gain_ref, router_ref, aux_ref, stat_ref, live_ref, back_ref, dgate_ref, tok_ref, dy_h, u_h, probs_h, du_h,
     hid2_h, x2_h, hid1_h, qkv2_h, mix2_h, qkv1_h, mix1_h, act_h, slope_h, served_h, ux_h, dyx_h, p1_h, p2_h, we1_h, we2_h,
     *refs) = refs
    na = nm = 1
    two, refs = refs[:na], refs[na:]
    up, refs = refs[:nm], refs[nm:]
    down, refs = refs[:nm], refs[nm:]
    one, refs = refs[:na], refs[na:]
    (out_ref, gtok_ref, fin, smout_ref, small_ref, ge1_h, ge2_h, sback_h,
     hid2, xbuf, grad_ref, dubuf, qkv, mix, dmix, dqkv, watt, w1, w2, big, stage, pack, crecv, xa, yb, ya, xb, zr,
     sm, smr,
     lsem, wsem, vs, vr, gs, gr, ms, mr, esem, osem, tsem, psem) = refs
    me, x = lax.axis_index("expert"), lax.axis_index("shard")
    bits = owners.bit_length() - 1
    bit = [(me // (1 << i)) % 2 for i in range(bits)]
    hop = [me + (1 - 2 * bit[i]) * (1 << i) for i in range(bits)]
    rows, width = grad_ref.shape
    step = rows // images
    blocks = act_h.shape[0]
    whole = pack.shape[2]
    part = width // 2

    def to(e, s):
        return dict(device_id=(e, s), device_id_type=pl.DeviceIdType.MESH)

    def each(lo, hi, f):
        lax.fori_loop(lo, hi, lambda k, c: (f(k), c)[1], 0)

    barrier = pltpu.get_barrier_semaphore()
    each(1, owners, lambda k: pl.semaphore_signal(barrier, inc=1, **to(xor(me, k, bits), x)))
    pl.semaphore_signal(barrier, inc=1, **to(me, 1 - x))

    def load(src, dst, i):
        return pltpu.make_async_copy(src, dst, lsem.at[i])

    count = 4 + 2 * blocks
    dy_ref, u_ref, probs_ref, du_ref = dmix, dqkv.at[:, 0:width], dubuf.at[:, 0:LANES], stage.at[0]
    start_in = [load(hid2_h, hid2, 0), load(du_h, du_ref, count), load(dy_h, dy_ref, count + 1), load(u_h, u_ref, count + 2),
                load(probs_h, probs_ref, count + 3)]
    start(start_in)
    first = [load(x2_h, xbuf, 1), load(qkv2_h, qkv, 2), load(mix2_h, mix, 3)]
    w_two = split.copies(two, watt, wsem.at[0])
    w_mlp = split.copies(up, w1, wsem.at[1]) + split.copies(down, w2, wsem.at[2])
    gelus = [load(act_h.at[b], big.at[b, 0:rows], 4 + b) for b in range(blocks)]
    gelus += [load(slope_h.at[b], big.at[b, big.shape[1] // 2:big.shape[1] // 2 + rows], 4 + blocks + b) for b in range(blocks)]
    start(first + w_two + w_mlp + gelus)
    own = pltpu.make_async_copy(served_h.at[me], sback_h.at[me], tsem.at[0])
    own.start()
    pl.semaphore_wait(barrier, owners)

    def send_served(k):
        p = xor(me, k, bits)
        return pltpu.make_async_remote_copy(served_h.at[p], sback_h.at[me], vs.at[k], vr.at[k], **to(p, x))

    each(1, owners, lambda k: send_served(owners - k).start())

    planes = owners // 4

    def add(ref, at, other):
        ref[at] = ref[at] + other

    def span(first, size):
        return pl.ds(pl.multiple_of(first, 32), size)

    def stages(n):
        def copy(src, dst, i, peer):
            return pltpu.make_async_remote_copy(src, dst, gs.at[n, i], gr.at[n, i], **peer)

        q = whole // 4
        o = bit[0] * (whole // 2)
        out = []
        out.append((
            lambda: [copy(pack.at[n, :, span((1 - bit[0]) * (whole // 2), whole // 2)], crecv.at[n], 0, to(hop[0], x))],
            lambda: add(pack, (n, slice(None), span(o, whole // 2)), crecv[n])))
        e = q // 2
        b1 = bit[1] * e

        def after1():
            add(pack, (n, x, span(o, q)), xa[n])
            add(pack, (n, slice(None), span(o + q + b1, e)), yb[n])

        out.append((
            lambda: [copy(pack.at[n, 1 - x, span(o, q)], xa.at[n], 1, to(me, 1 - x)),
                     copy(pack.at[n, :, span(o + q + e - b1, e)], yb.at[n], 2, to(hop[1], x))],
            after1))

        def after2():
            add(pack, (n, x, span(o + b1, e)), ya[n])
            add(pack, (n, x, span(o + q + b1, e)), xb[n])

        out.append((
            lambda: [copy(pack.at[n, x, span(o + e - b1, e)], ya.at[n], 3, to(hop[1], x)),
                     copy(pack.at[n, 1 - x, span(o + q + b1, e)], xb.at[n], 4, to(me, 1 - x))],
            after2))
        size = e // planes
        base = o + b1

        def rows_at(p):
            return [span(base + p * size + j * q, size) for j in range(2)]

        def over(make):
            out = []
            for k in range(1, planes):
                p = xor(me // 4, k, bits)
                for j in range(2):
                    out.append(make(k, p, j, 5 + 2 * (k - 1) + j, to(p * 4 + me % 4, x)))
            return out

        mine = me // 4

        def after3():
            for j in range(2):
                at = (n, x, rows_at(mine)[j])
                total = pack[at].astype(f32)
                for k in range(1, planes):
                    total = total + zr[n, 2 * (k - 1) + j].astype(f32)
                fin[(n, rows_at(mine)[j])] = total.astype(bf16)

        more = 2 * (planes - 1)
        out.append((
            lambda: over(lambda k, p, j, i, peer: copy(pack.at[n, x, rows_at(p)[j]], zr.at[n, 2 * (k - 1) + j], i, peer)), after3))
        out.append((
            lambda: over(lambda k, p, j, i, peer: copy(fin.at[n, rows_at(mine)[j]], fin.at[n, rows_at(mine)[j]], i + more, peer)),
            lambda: None))
        out.append((
            lambda: [copy(fin.at[n, span(base + j * q, e)], fin.at[n, span(base + j * q, e)], 5 + 2 * more + j, to(hop[1], x))
                     for j in range(2)],
            lambda: None))
        out.append((
            lambda: [copy(fin.at[n, span(o, whole // 2)], fin.at[n, span(o, whole // 2)], 7 + 2 * more, to(hop[0], x))],
            lambda: None))
        return out

    groups = [stages(n) for n in range(4)]

    def small_stage(i):
        if i == 0:
            src, dst, peer = sm, smr.at[0], to(hop[0], x)
        elif i == 1:
            src, dst, peer = sm.at[1 - x], smr.at[1, 0], to(me, 1 - x)
        else:
            src, dst, peer = sm.at[x], smr.at[i, 0], to(hop[i - 1], x)
        return pltpu.make_async_remote_copy(src, dst, ms.at[i], mr.at[i], **peer)

    def small_after(i):
        if i == 0:
            sm[...] += smr[0]
        else:
            sm[x] += smr[i, 0]

    def tick(n, k):
        table = groups[n]
        if k > 0:
            finish(table[k - 1][0]())
            table[k - 1][1]()
            if n == 3 and k - 1 < bits + 1:
                small_stage(k - 1).wait()
                small_after(k - 1)
        if k < len(table):
            start(table[k][0]())
            if n == 3 and k < bits + 1:
                small_stage(k).start()

    def at_point(name, index=None):
        for i, n, k in plan.get(name, ()):
            if index is None:
                tick(n, k)
            else:
                pl.when(index == i)(functools.partial(tick, n, k))

    finish(start_in)
    grad_ref[...] = router_backward(experts, dy_ref, u_ref, probs_ref, hid2, gain_ref, router_ref, aux_ref, stat_ref, live_ref,
                                    back_ref, du_ref, dgate_ref, small_ref)
    finish(first + w_two)
    dv, dg = attend_backward(
        step, seq, images, grad_ref[...], xbuf[...], gain_ref[2:3, :], [watt.at[c] for c in range(3)], watt.at[3],
        qkv, mix, dmix, dqkv, pack.at[0], 0,
    )
    small_ref[LANES + 1:LANES + 2, :] = dg
    grad_ref[...] += dv
    at_point("two")
    second = [load(hid1_h, xbuf, 1), load(qkv1_h, qkv, 2), load(mix1_h, mix, 3)]
    w_one = split.copies(one, watt, wsem.at[0])
    start(second + w_one)

    finish(gelus + w_mlp)
    low = grad_ref[...].astype(bf16)
    fpart = blocks * width // 2
    for b in range(blocks):
        s, off = b * width // fpart, b * width % fpart
        pack[1, s, off:off + width, :] = tn(big[b, 0:rows], low).astype(bf16)
    at_point("out")
    finish(second[:1])
    xn, rs = norm(xbuf[...])
    gain = gain_ref[1:2, :]
    u = (xn * gain).astype(bf16)
    half = big.shape[1] // 2
    for b in range(blocks):
        cols = slice(b * width, (b + 1) * width)
        dz = (big[b, half:half + rows].astype(f32) * nt(low, w2[0, cols, :])).astype(bf16)
        d = nt(dz, w1[0, :, cols])
        if b == 0:
            dubuf[...] = d
        else:
            dubuf[...] += d
        gin = tn(u, dz).astype(bf16)
        for s in range(2):
            pack[2, s, b * part:(b + 1) * part, :] = gin[s * part:(s + 1) * part]
        at_point("in%d" % b)
    dv, dg = norm_back(dubuf[...], xn, rs, gain)
    small_ref[LANES + 3:LANES + 4, :] = dg
    grad_ref[...] += dv
    at_point("mlp")

    pad_store(xbuf, lambda i: tok_ref[i], images, seq, step)
    finish(second[1:] + w_one)
    dv, dg = attend_backward(
        step, seq, images, grad_ref[...], xbuf[...], gain_ref[0:1, :], [watt.at[c] for c in range(3)], watt.at[3],
        qkv, mix, dmix, dqkv, pack.at[3], 0, tick=lambda i: at_point("image", i),
    )
    sm[...] = jnp.zeros(sm.shape, f32)
    for s in range(2):
        cols = slice(s * part, (s + 1) * part)
        sm[s, 0:experts] = small_ref[0:experts, cols]
        sm[s, experts:experts + 1] = dg[:, cols]
        sm[s, experts + 1:experts + 2] = small_ref[LANES + 3:LANES + 4, cols]
        sm[s, experts + 2:experts + 3] = small_ref[LANES + 1:LANES + 2, cols]
        sm[s, experts + 3:experts + 4] = small_ref[LANES:LANES + 1, cols]
    at_point("one")
    grad_ref[...] += dv
    for i in range(images):
        gtok_ref[i] = grad_ref[i * step:i * step + seq, :]

    own.wait()
    each(1, owners, lambda k: send_served(k).wait())
    at_point("rows")

    todo = [(ux_h, 0), (dyx_h.at[0], 1)]
    moves = [pltpu.make_async_copy(r, stage.at[i % 2], esem.at[i % 2]) for i, (r, _) in enumerate(todo)]

    def lane(i):
        return pl.ds(pl.multiple_of(i * width, width), width)

    def chunk(i):
        e, f = i // blocks, i % blocks
        slot = i % 2
        col = pl.ds(pl.multiple_of(f * width, width), width)
        return [pltpu.make_async_copy(we1_h.at[e, :, col], w1.at[0, :, lane(slot)], esem.at[2 + slot]),
                pltpu.make_async_copy(we2_h.at[e, col, :], w2.at[0, lane(slot), :], esem.at[4 + slot])]

    def result(i):
        e, f = i // blocks, i % blocks
        slot = i % 2
        col = pl.ds(pl.multiple_of(f * width, width), width)
        return [pltpu.make_async_copy(w1.at[0, :, lane(2 + slot)], ge1_h.at[e, :, col], osem.at[slot]),
                pltpu.make_async_copy(w2.at[0, lane(2 + slot), :], ge2_h.at[e, col, :], osem.at[2 + slot])]

    moves[0].start()
    start(chunk(0))
    for i, (_, kind) in enumerate(todo):
        if i + 1 < len(todo):
            moves[i + 1].start()
        moves[i].wait()
        for e, v in enumerate(split_rows(stage[i % 2], local)):
            if kind == 1:
                u = big[e, 0:half]
                v = v * gate_of(u, router_ref[...], experts, me * local + e)
            big[kind * local + e, 0:half] = v.astype(bf16)
    back = pltpu.make_async_copy(sback_h, stage.at[0], tsem.at[0])
    back.start()
    back.wait()
    grad_ref[...] = (hid2[...] + nn(back_ref[...], stage[0].reshape(back_ref.shape[1], width))) * live_ref[...]
    for i in range(images):
        out_ref[i] = grad_ref[i * step:i * step + seq, :].astype(bf16)
    at_point("output")
    count = local * blocks

    def before(i):
        e, f = i // blocks, i % blocks
        slot = i % 2
        col = pl.ds(pl.multiple_of(f * width, width), width)
        return [pltpu.make_async_copy(p1_h.at[e, :, col], w1.at[0, :, lane(2 + slot)], psem.at[slot]),
                pltpu.make_async_copy(p2_h.at[e, col, :], w2.at[0, lane(2 + slot), :], psem.at[2 + slot])]

    def expert(i, c):
        slot = i % 2
        pl.when(i + 1 < count)(lambda: start(chunk(i + 1)))
        pl.when(i >= 2)(lambda: finish(result(i - 2)))
        start(before(i))
        finish(chunk(i))
        e = i // blocks
        u = big[e, 0:half]
        dsv = big[local + e, 0:half]
        act, slope = gelu_pair(nn(u, w1[0, :, lane(slot)]))
        dz = (slope * nt(dsv, w2[0, lane(slot), :])).astype(bf16)
        act = act.astype(bf16)
        finish(before(i))
        at1, at2 = (0, slice(None), lane(2 + slot)), (0, lane(2 + slot), slice(None))
        w1[at1] = (w1[at1].astype(f32) + tn(u, dz)).astype(bf16)
        at_point("early", i)
        w2[at2] = (w2[at2].astype(f32) + tn(act, dsv)).astype(bf16)
        start(result(i))
        at_point("late", i)
        return c

    lax.fori_loop(0, count, expert, 0)
    at_point("end")
    for i in range(max(0, count - 2), count):
        finish(result(i))
    smout_ref[...] = sm[x]


def swap(owners, bit):
    return [(i, i ^ (1 << bit)) for i in range(owners)]


def reduce_all(g, owners, shards):
    me = lax.axis_index("expert")
    bits = owners.bit_length() - 1

    def add(a, b):
        return (a.astype(f32) + b.astype(f32)).astype(bf16)

    def fold(v, bit, axis):
        own = (me >> bit) & 1
        half = v.shape[axis] // 2
        keep = lax.dynamic_slice_in_dim(v, own * half, half, axis)
        send = lax.dynamic_slice_in_dim(v, (1 - own) * half, half, axis)
        return add(keep, lax.ppermute(send, "expert", swap(owners, bit)))

    v = fold(g, 0, 1)
    if shards == 2:
        x = lax.axis_index("shard")
        keep = lax.dynamic_index_in_dim(v, x, 0, keepdims=False)
        send = lax.dynamic_index_in_dim(v, 1 - x, 0, keepdims=False)
        v = add(keep, lax.ppermute(send, "shard", [(0, 1), (1, 0)]))
    else:
        v = lax.psum_scatter(v, "shard", scatter_dimension=0, tiled=True)[0]
    for bit in range(1, bits):
        v = fold(v, bit, 0)
    for bit in reversed(range(bits)):
        own = (me >> bit) & 1
        other = lax.ppermute(v, "expert", swap(owners, bit))
        v = jnp.where(own == 0, jnp.concatenate([v, other]), jnp.concatenate([other, v]))
    return v


def per_device(
    owners, shards, tokens, cotangent, routes, counts, aux_weight, attn_qkv1, attn_out1, mlp_in, mlp_out, gains1,
    attn_qkv2, attn_out2, router, gains2, expert_in, expert_out,
):
    images, seq, width = tokens.shape
    step = padded(seq)
    rows = images * step
    experts = router.shape[1]
    local = expert_in.shape[0]
    ff = mlp_in.shape[1]
    block_rows = -(-local * CAP // 16) * 16
    slots = owners * block_rows
    split = Split(shards)
    expert_swap = functools.partial(lax.all_to_all, axis_name="expert", split_axis=0, concat_axis=0, tiled=True)

    block = (owners, block_rows, width)
    sem = pltpu.SemaphoreType.DMA
    if shards == 2:
        (gains, router_full, stat, live_col, dy, u_out, hidden, block_out, hidden_two, qkv_one, mix_one, qkv_two, mix_two, act, slope,
         u_two, probs, back, w_one, w_up, w_down, w_two, dy_in) = fused_forward(
            owners, experts, local, block, tokens, cotangent, routes, counts, gains1, gains2, router,
            attn_qkv1, attn_out1, mlp_in, mlp_out, attn_qkv2, attn_out2)
        w_one, w_up, w_down, w_two = [w_one], [w_up], [w_down], [w_two]
    else:
        within = jnp.arange(step, dtype=jnp.int32) < seq
        live = ((jnp.arange(images, dtype=jnp.int32)[:, None] < counts[0]) & within[None, :]).reshape(rows)
        live = live.astype(f32)
        routes_pad = jnp.pad(routes, ((0, 0), (0, step - seq), (0, 0)), constant_values=-1).reshape(rows, 2)
        lanes = jnp.arange(LANES, dtype=jnp.int32)
        loads = jnp.sum(((routes_pad[:, :, None] == lanes) & (live[:, None, None] > 0)).astype(f32), axis=(0, 1))
        loads = jnp.where(lanes == LANES - 1, jnp.sum(live), loads)
        live_col = live[:, None]

        w_one = split.gather([attn_qkv1, attn_out1[None]])
        w_up = split.gather([mlp_in[None]])
        w_down = split.gather([mlp_out[None]])
        w_two = split.gather([attn_qkv2, attn_out2[None]])
        gains = jnp.concatenate([gains1, gains2])
        if shards == 2:
            x = lax.axis_index("shard")
            other = lax.ppermute(gains, "shard", [(0, 1), (1, 0)])
            gains = jnp.where(x == 0, jnp.concatenate([gains, other], 1), jnp.concatenate([other, gains], 1))
            other = lax.ppermute(router, "shard", [(0, 1), (1, 0)])
            router_full = jnp.where(x == 0, jnp.concatenate([router, other]), jnp.concatenate([other, router]))
        else:
            gains = lax.all_gather(gains, "shard", axis=1, tiled=True)
            router_full = lax.all_gather(router, "shard", axis=0, tiled=True)
        gains = gains.astype(f32)
        router_full = jnp.pad(router_full, ((0, 0), (0, LANES - experts)))

        dy, dy_out, disp, back = call(
            functools.partial(route_body, images, seq, local, block_rows),
            [sds((rows, width), bf16), sds((slots, width), bf16), sds((slots, rows), bf16), sds((rows, slots), bf16)],
            [routes_pad, live_col, cotangent], flops=2e9, nbytes=6e6,
        )
        block = (owners, block_rows, width)
        dy_in = expert_swap(dy_out.reshape(block))

        sem = pltpu.SemaphoreType.DMA
        attn_scratch = [pltpu.VMEM((4, width, width), bf16), sem((4,))]
        mlp_scratch = [pltpu.VMEM((1, width, ff), bf16), pltpu.VMEM((1, ff, width), bf16), sem((2, 4))]

        def specs(n, ins):
            return [VM] * n + [ANY] * (len(ins) - n)

        ins = [tokens, gains] + w_one
        hidden, qkv_one, mix_one = call(
            functools.partial(block1_body, split, images, seq),
            [sds((rows, width), f32), sds((rows, 3 * width), bf16), sds((rows, width), bf16)],
            ins, attn_scratch, specs(2, ins), flops=4e9, nbytes=8e6,
        )
        ins = [hidden, gains] + w_up + w_down
        block_out, act, slope = call(
            functools.partial(mlp_body, split),
            [sds((rows, width), f32)] + [sds((ff // width, rows, width), bf16)] * 2,
            ins, mlp_scratch, specs(2, ins), flops=6e9, nbytes=12e6,
        )
        ins = [block_out, gains, router_full, disp, live_col, loads[None, :]] + w_two
        hidden_two, qkv_two, mix_two, u_two, probs, stat, u_out = call(
            functools.partial(block2_body, split, images, seq, experts),
            [sds((rows, width), f32), sds((rows, 3 * width), bf16), sds((rows, width), bf16), sds((rows, width), bf16),
             sds((rows, LANES), f32), sds((8, LANES), f32), sds((slots, width), bf16)],
            ins, attn_scratch, specs(6, ins), flops=5e9, nbytes=10e6,
        )

    group = min(4, owners)
    saved = owners * CAP if shards == 2 else 16
    wide = width if shards == 2 else LANES
    u_in, served, du_back, dgate_back, stat, dy_far, u_far, *partial = pl.pallas_call(
        functools.partial(expert_body, owners, shards, local, experts, group),
        out_shape=[sds(block, bf16), sds(block, bf16), sds(block, bf16), sds((owners, 8, LANES), f32), sds((8, LANES), f32),
                   sds((shards - 1,) + block, bf16), sds(block, bf16)]
        + ([sds(expert_in.shape, bf16), sds(expert_out.shape, bf16)] if shards == 2 else []),
        in_specs=[VM] * 4 + [ANY] * 2,
        out_specs=[VM] * 5 + [ANY] * (4 if shards == 2 else 2),
        scratch_shapes=[
            pltpu.VMEM((local, width, ff), bf16), pltpu.VMEM((local, ff, width), bf16), pltpu.VMEM(block, bf16),
            pltpu.VMEM((owners, 8, LANES), f32), pltpu.VMEM((shards, 8, LANES), f32), pltpu.VMEM((owners, 8, LANES), f32),
            pltpu.VMEM((local, saved, ff if shards == 2 else LANES), bf16), pltpu.VMEM((local, saved, ff if shards == 2 else LANES), bf16),
            pltpu.VMEM((local, saved, wide), bf16), pltpu.VMEM((local, saved, wide), bf16),
            pltpu.VMEM((2, wide, wide), bf16), pltpu.VMEM((2, wide, wide), bf16),
            sem((2,)), sem((2,)), sem((4,)),
        ] + [sem((owners,))] * 10 + [sem((shards,))] * 4,
        compiler_params=pltpu.CompilerParams(vmem_limit_bytes=VMEM_BYTES, collective_id=0, has_side_effects=True),
        cost_estimate=pl.CostEstimate(flops=int(11e9), bytes_accessed=int(15e6), transcendentals=0),
    )(u_out.reshape(block), dy_in, router_full, stat, expert_in, expert_out)
    parts_of = (gains, router_full, aux_weight.reshape(1, 1), stat, live_col, back, dgate_back, tokens, dy, u_two, probs, du_back)
    if shards == 2:
        return fused_backward(Split(1), experts, tokens, parts_of, hidden_two, block_out, hidden, qkv_two, mix_two, qkv_one, mix_one,
                              act, slope, served, u_far, dy_far, *partial, expert_in, expert_out, w_two, w_up, w_down, w_one)
    served_back = expert_swap(served).reshape(slots, width)

    if shards == 2:
        us = [u_in, lax.ppermute(u_in, "shard", [(0, 1), (1, 0)])]
    else:
        far = lax.all_gather(u_in, "shard")
        us = [u_in] + [lax.dynamic_index_in_dim(far, (lax.axis_index("shard") + shards - k) % shards, 0, False) for k in range(1, shards)]
    dys = [dy_in] + [dy_far[k] for k in range(shards - 1)]
    parts = 4
    wide = ff // parts
    up_spec = pl.BlockSpec((1, width, wide), lambda e, f: (e, 0, f))
    down_spec = pl.BlockSpec((1, wide, width), lambda e, f: (e, f, 0))
    grad_e_in, grad_e_out = pl.pallas_call(
        functools.partial(expert_grad_body, shards, experts),
        grid=(local, parts),
        out_shape=[sds((local, width, ff), f32), sds((local, ff, width), f32)],
        in_specs=[ANY] * (2 * shards) + [VM, up_spec, down_spec],
        out_specs=[up_spec, down_spec],
        scratch_shapes=[pltpu.VMEM((shards, local, owners * CAP, width), bf16)] * 2 + [pltpu.VMEM((2,) + block, bf16), sem((2,))],
        compiler_params=pltpu.CompilerParams(vmem_limit_bytes=VMEM_BYTES),
        cost_estimate=pl.CostEstimate(flops=int(27e9), bytes_accessed=int(40e6), transcendentals=0),
    )(*us, *dys, router_full, expert_in, expert_out)

    part = width // shards
    back_scratch = [pltpu.VMEM((rows, width), bf16), pltpu.VMEM((rows, 3 * width), bf16)]
    ins = [dy, u_two, probs, hidden_two, block_out, gains, router_full, aux_weight.reshape(1, 1), stat, live_col, back,
           du_back.reshape(slots, width), dgate_back,
           qkv_two, mix_two]
    n = len(ins)
    ins = ins + w_two
    grad_block, pack_two, small = call(
        functools.partial(back2_body, split, images, seq, experts),
        [sds((rows, width), f32), sds((shards, 4 * part, width), bf16), sds((LANES + 8, width), f32)],
        ins, attn_scratch + back_scratch, specs(n, ins), flops=9e9, nbytes=16e6,
    )
    balance_loss = small[LANES + 2, 0]
    late = reduce_all(pack_two, owners, shards)
    ins = [grad_block, hidden, gains, act, slope] + w_up + w_down
    grad_hidden, pack_mlp, dg_two = call(
        functools.partial(mlp_back_body, split),
        [sds((rows, width), f32), sds((shards, part * (ff // width) + ff // shards, width), bf16), sds((1, width), f32)],
        ins, mlp_scratch + [pltpu.VMEM((rows, width), f32)], specs(5, ins), flops=11e9, nbytes=16e6,
    )
    middle = reduce_all(pack_mlp, owners, shards)
    ins = [grad_hidden, tokens, gains, qkv_one, mix_one, small, dg_two] + w_one
    grad_tokens, pack_one = call(
        functools.partial(back1_body, split, images, seq, experts),
        [sds((images, seq, width), f32), sds((shards, 4 * part + 64, width), bf16)],
        ins, attn_scratch + [pltpu.VMEM((rows, width), f32)] + back_scratch, specs(7, ins), flops=9e9, nbytes=14e6,
    )
    early = reduce_all(pack_one, owners, shards)
    (output,) = call(
        functools.partial(output_body, images, seq), [sds((images, seq, width), bf16)],
        [hidden_two, back, served_back, live_col], [pltpu.VMEM((rows, width), f32)], flops=1e9, nbytes=5e6,
    )

    late, middle, early = late.astype(f32), middle.astype(f32), early.astype(f32)
    up = middle[:part * (ff // width)].reshape(ff // width, part, width).transpose(1, 0, 2).reshape(part, ff)
    tail = early[4 * part:, :part]
    return (
        output,
        balance_loss,
        grad_tokens,
        early[:3 * part].reshape(3, part, width),
        early[3 * part:4 * part],
        up,
        middle[part * (ff // width):],
        tail[32:34],
        late[:3 * part].reshape(3, part, width),
        late[3 * part:],
        tail[:experts].T,
        tail[34:36],
        grad_e_in,
        grad_e_out,
    )


PLAN = [
    ("two", None, 0),
    ("out", None, 1),
    ("out", None, 0),
    ("in1", None, 1),
    ("mlp", None, 2),
    ("mlp", None, 0),
    ("image", 0, 2),
    ("image", 0, 1),
    ("image", 1, 0),
    ("image", 2, 1),
    ("one", None, 3),
    ("one", None, 2),
    ("output", None, 3),
    ("output", None, 0),
    ("early", 0, 2),
    ("early", 0, 1),
    ("late", 3, 3),
    ("early", 4, 0),
    ("late", 4, 2),
    ("late", 4, 1),
    ("early", 6, 3),
]


def fused_backward(split, experts, tokens, parts_of, hidden_two, block_out, hidden, qkv_two, mix_two, qkv_one, mix_one,
                   act, slope, served, u_far, dy_far, part1, part2, expert_in, expert_out, w_two, w_up, w_down, w_one):
    images, seq, width = tokens.shape
    rows = hidden.shape[0]
    local, _, ff = expert_in.shape
    block = served.shape
    owners = block[0]
    bits = owners.bit_length() - 1
    whole = 2 * width
    part = width // 2
    blocks = ff // width
    steps = [7] * 4
    left = [0] * 4
    plan = {}
    for name, index, n in PLAN:
        if left[n] <= steps[n] and (index is None or index < (images if name == "image" else local * blocks)):
            plan.setdefault(name, []).append((index, n, left[n]))
            left[n] += 1
    plan["end"] = [(None, n, k) for k in range(max(steps) + 1) for n in range(4) if left[n] <= k <= steps[n]]
    small_rows = -(-(experts + 4) // 8) * 8
    sem = pltpu.SemaphoreType.DMA
    ins = list(parts_of) + [hidden_two, block_out, hidden, qkv_two, mix_two, qkv_one, mix_one, act, slope, served, u_far, dy_far,
                            part1, part2, expert_in, expert_out] + w_two + w_up + w_down + w_one
    vmem = 8
    big_rows = 2 * owners * CAP
    nsem = 8 + 4 * (owners // 4 - 1)
    V = pltpu.VMEM
    outs = pl.pallas_call(
        functools.partial(backward_body, split, images, seq, experts, local, owners, plan),
        out_shape=[
            sds((images, seq, width), bf16), sds((images, seq, width), f32), sds((4, whole, width), bf16),
            sds((small_rows, part), f32), sds((LANES + 8, width), f32), sds(expert_in.shape, bf16), sds(expert_out.shape, bf16),
            sds(block, bf16),
        ],
        in_specs=[VM] * vmem + [ANY] * (len(ins) - vmem),
        out_specs=[VM] * 5 + [ANY] * 3,
        scratch_shapes=[
            V((rows, width), f32), V((rows, width), f32), V((rows, width), f32), V((rows, width), f32),
            V((rows, 3 * width), bf16), V((rows, width), bf16), V((rows, width), bf16), V((rows, 3 * width), bf16),
            V((4, width, width), bf16), V((1, width, ff), bf16), V((1, ff, width), bf16), V((blocks, big_rows, width), bf16),
            V((2,) + block, bf16),
            V((4, 2, whole, width), bf16), V((4, 2, whole // 2, width), bf16), V((4, whole // 4, width), bf16),
            V((4, 2, whole // 8, width), bf16), V((4, whole // 8, width), bf16), V((4, whole // 8, width), bf16),
            V((4, 2 * (owners // 4 - 1), whole // (2 * owners), width), bf16),
            V((2, small_rows, part), f32), V((bits + 1, 2, small_rows, part), f32),
            sem((8 + 2 * blocks,)), sem((3, 4)), sem((owners,)), sem((owners,)),
            sem((4, nsem)), sem((4, nsem)), sem((bits + 1,)), sem((bits + 1,)), sem((6,)), sem((4,)), sem((1,)), sem((4,)),
        ],
        compiler_params=pltpu.CompilerParams(vmem_limit_bytes=63 << 20, collective_id=1, has_side_effects=True),
        cost_estimate=pl.CostEstimate(flops=int(60e9), bytes_accessed=int(80e6), transcendentals=0),
    )(*ins)
    output, grad_tokens, fin, tail, small, grad_e_in, grad_e_out = outs[:7]
    qkv1, out1, up, down, qkv2, out2, grad_e_in, grad_e_out, gains1, gains2, router = widen(
        fin, grad_e_in, grad_e_out, tail, part, width, blocks, experts)
    return (
        output, small[LANES + 2, 0], grad_tokens, qkv1, out1, up, down, gains1, qkv2, out2, router, gains2, grad_e_in, grad_e_out,
    )


def widen_body(sixth, experts, fin_ref, e1_ref, e2_ref, tail_ref, qkv1_ref, out1_ref, up_ref, down_ref, qkv2_ref, out2_ref,
               g1_ref, g2_ref, gains1_ref, gains2_ref, router_ref):
    i = pl.program_id(0)

    @pl.when(i == 0)
    def _():
        gains1_ref[...] = tail_ref[experts:experts + 2]
        gains2_ref[...] = tail_ref[experts + 2:experts + 4]
        a = lax.broadcasted_iota(jnp.int32, (experts, experts), 0)
        b = lax.broadcasted_iota(jnp.int32, (experts, experts), 1)
        unit = (a == b).astype(f32).astype(bf16)
        hi, mid, lo = split3(tail_ref[0:experts])
        router_ref[...] = tn(hi, unit) + tn(mid, unit) + tn(lo, unit)

    g1_ref[...] = e1_ref[...].astype(f32)
    g2_ref[...] = e2_ref[...].astype(f32)
    up_ref[...] = fin_ref[2].astype(f32)
    down_ref[...] = fin_ref[1].astype(f32)

    @pl.when(i < sixth)
    def _():
        qkv1_ref[0] = fin_ref[3].astype(f32)
        qkv2_ref[0] = fin_ref[0].astype(f32)

    @pl.when(i >= sixth)
    def _():
        out1_ref[...] = fin_ref[3].astype(f32)
        out2_ref[...] = fin_ref[0].astype(f32)


def widen(fin, e1, e2, tail, part, width, blocks, experts):
    steps = 2 * blocks
    some = fin.shape[1] // steps
    per = part // some
    sixth = 3 * per
    local, _, ff = e1.shape
    qkv = pl.BlockSpec((1, some, width), lambda i: (jnp.minimum(i, sixth - 1) // per, jnp.minimum(i, sixth - 1) % per, 0))
    out = pl.BlockSpec((some, width), lambda i: (jnp.maximum(i - sixth, 0), 0))
    return pl.pallas_call(
        functools.partial(widen_body, sixth, experts),
        grid=(steps,),
        out_shape=[sds((3, part, width), f32), sds((part, width), f32), sds((part, blocks * width), f32), sds((fin.shape[1], width), f32),
                   sds((3, part, width), f32), sds((part, width), f32), sds(e1.shape, f32), sds(e2.shape, f32),
                   sds((2, part), f32), sds((2, part), f32), sds((part, experts), f32)],
        in_specs=[pl.BlockSpec((4, some, width), lambda i: (0, i, 0)),
                  pl.BlockSpec((local, width // steps, ff), lambda i: (0, i, 0)),
                  pl.BlockSpec((local, ff // steps, width), lambda i: (0, i, 0)), pl.BlockSpec(tail.shape, lambda i: (0, 0))],
        out_specs=[qkv, out, pl.BlockSpec((some, width), lambda i: (i % per, i // per)), pl.BlockSpec((some, width), lambda i: (i, 0)),
                   qkv, out, pl.BlockSpec((local, width // steps, ff), lambda i: (0, i, 0)),
                   pl.BlockSpec((local, ff // steps, width), lambda i: (0, i, 0)),
                   pl.BlockSpec((2, part), lambda i: (0, 0)), pl.BlockSpec((2, part), lambda i: (0, 0)),
                   pl.BlockSpec((part, experts), lambda i: (0, 0))],
        compiler_params=pltpu.CompilerParams(vmem_limit_bytes=VMEM_BYTES),
        cost_estimate=pl.CostEstimate(flops=0, bytes_accessed=int(40e6), transcendentals=0),
    )(fin, e1, e2, tail)


def solution(mesh):
    owners, shards = mesh.shape["expert"], mesh.shape["shard"]
    both = ("expert", "shard")
    return jax.shard_map(
        functools.partial(per_device, owners, shards),
        mesh=mesh,
        in_specs=(
            P(both, None, None), P(both, None, None), P(both, None, None), P(both), P(),
            P(None, "shard", None), P("shard", None), P("shard", None), P("shard", None), P(None, "shard"),
            P(None, "shard", None), P("shard", None), P("shard", None), P(None, "shard"),
            P("expert", None, None), P("expert", None, None),
        ),
        out_specs=(
            P(both, None, None), P(), P(both, None, None),
            P(None, "shard", None), P("shard", None), P("shard", None), P("shard", None), P(None, "shard"),
            P(None, "shard", None), P("shard", None), P("shard", None), P(None, "shard"),
            P("expert", None, None), P("expert", None, None),
        ),
        check_vma=False,
    )
```

```python
import functools

import jax
import jax.numpy as jnp
from jax import lax
from jax.experimental import pallas as pl
from jax.experimental.pallas import tpu as pltpu
from jax.sharding import PartitionSpec as P

HEADS = 8
CAP = 40
EPS = 1e-06
NEG = -1e30
LANES = 128
f32 = jnp.float32
bf16 = jnp.bfloat16
ANY = pl.BlockSpec(memory_space=pl.ANY)
VM = pl.BlockSpec(memory_space=pltpu.VMEM)
VMEM_BYTES = 58 << 20


def nn(a, b):
    return lax.dot_general(a, b, (((1,), (0,)), ((), ())), preferred_element_type=f32)


def nt(a, b):
    return lax.dot_general(a, b, (((1,), (1,)), ((), ())), preferred_element_type=f32)


def tn(a, b):
    return lax.dot_general(a, b, (((0,), (0,)), ((), ())), preferred_element_type=f32)


def sds(shape, dtype):
    return jax.ShapeDtypeStruct(shape, dtype)


def padded(seq):
    return -(-seq // 16) * 16


def norm(x):
    xc = x - jnp.mean(x, axis=-1, keepdims=True)
    rs = lax.rsqrt(jnp.mean(xc * xc, axis=-1, keepdims=True) + EPS)
    return xc * rs, rs


def norm_back(dyn, xn, rs, gain):
    dgain = jnp.sum(dyn * xn, axis=0, keepdims=True)
    dxn = dyn * gain
    dv = dxn - jnp.mean(dxn, axis=-1, keepdims=True)
    dv = (dv - xn * jnp.mean(dxn * xn, axis=-1, keepdims=True)) * rs
    return dv, dgain


def gelu_pair(z):
    a = jnp.abs(z)
    t = 1.0 / (1.0 + (0.3275911 * 0.7071067811865476) * a)
    e = jnp.exp(-0.5 * (z * z))
    q = t * (0.127414796 + t * (-0.142248368 + t * (0.7107068705 + t * (-0.7265760135 + t * 0.5307027145))))
    q = q * e
    phi = jnp.where(z >= 0.0, 1.0 - q, q)
    return z * phi, phi + z * (e * 0.3989422804014327)


class Split:
    def __init__(self, shards):
        self.pair = shards == 2
        self.shards = shards

    def gather(self, owns):
        if not self.pair:
            whole = [lax.all_gather(o, "shard", axis=1, tiled=True) for o in owns]
            return whole
        core = lax.axis_index("expert") % 2
        owners = lax.axis_size("expert")
        half = owns[0].shape[1] // 2
        send = jnp.concatenate([lax.dynamic_slice_in_dim(o, core * half, half, 1) for o in owns], axis=0)
        far = lax.ppermute(send, "shard", [(0, 1), (1, 0)])
        near = lax.ppermute(far, "expert", [(i, i ^ 1) for i in range(owners)])
        return list(owns) + [far, near]

    def count(self, owns):
        return owns + 2 if self.pair else owns

    def copies(self, refs, full, sems):
        out = []
        if not self.pair:
            at = 0
            for i, r in enumerate(refs):
                n = r.shape[0]
                out.append(pltpu.make_async_copy(r, full.at[at:at + n], sems.at[i]))
                at += n
            return out
        me = lax.axis_index("shard")
        core = lax.axis_index("expert") % 2
        rows = refs[0].shape[1]
        half = rows // 2
        at = 0
        for i, r in enumerate(refs[:-2]):
            n = r.shape[0]
            out.append(pltpu.make_async_copy(r, full.at[at:at + n, pl.ds(me * rows, rows), :], sems.at[i]))
            at += n
        base = (1 - me) * rows
        k = len(refs) - 2
        out.append(pltpu.make_async_copy(refs[k], full.at[:, pl.ds(base + core * half, half), :], sems.at[k]))
        out.append(pltpu.make_async_copy(refs[k + 1], full.at[:, pl.ds(base + (1 - core) * half, half), :], sems.at[k + 1]))
        return out


def start(copies):
    for c in copies:
        c.start()


def finish(copies):
    for c in copies:
        c.wait()


def call(body, outs, ins, scratch=(), specs=None, flops=0, nbytes=0, **kw):
    return pl.pallas_call(
        body,
        out_shape=outs,
        in_specs=specs or [VM] * len(ins),
        out_specs=[VM] * len(outs),
        scratch_shapes=list(scratch),
        compiler_params=pltpu.CompilerParams(vmem_limit_bytes=VMEM_BYTES),
        cost_estimate=pl.CostEstimate(flops=int(flops), bytes_accessed=int(nbytes), transcendentals=0),
        **kw,
    )(*ins)


def pad_store(ref, block, images, seq, step):
    ref[...] = jnp.zeros(ref.shape, ref.dtype)
    for i in range(images):
        ref[i * step:i * step + seq, :] = block(i).astype(ref.dtype)


def slot_start(expert, local, block):
    owner = jnp.floor((expert.astype(f32) + 0.5) * (1.0 / local))
    return owner * block + (expert.astype(f32) - owner * local) * CAP


def route_body(images, seq, local, block, r_ref, live_ref, cot_ref, dy_ref, dyd_ref, disp_ref, back_ref):
    step = r_ref.shape[0] // images
    pad_store(dy_ref, lambda i: cot_ref[i], images, seq, step)
    dy_ref[...] = (dy_ref[...].astype(f32) * live_ref[...]).astype(bf16)
    route_tables(local, block, r_ref, disp_ref, back_ref)
    dyd_ref[...] = nn(disp_ref[...], dy_ref[...]).astype(bf16)


def route_tables(local, block, r_ref, disp_ref, back_ref):
    rows = r_ref.shape[0]
    slots = disp_ref.shape[0]
    lane = lax.broadcasted_iota(jnp.int32, (rows, LANES), 1)
    hit = (r_ref[:, 0:1] == lane) | (r_ref[:, 1:2] == lane)
    ti = lax.broadcasted_iota(jnp.int32, (rows, rows), 0)
    tj = lax.broadcasted_iota(jnp.int32, (rows, rows), 1)
    place = nn((ti > tj).astype(f32).astype(bf16), hit.astype(f32).astype(bf16))
    place = jnp.where(hit, place, -1.0).astype(bf16)
    off = lax.broadcasted_iota(jnp.int32, (LANES, slots), 1).astype(f32) - slot_start(
        lax.broadcasted_iota(jnp.int32, (LANES, slots), 0), local, block)
    spread = ((off >= 0) & (off < CAP)).astype(f32)
    within = jnp.sum(spread * off, axis=0, keepdims=True)
    within = jnp.where(jnp.sum(spread, axis=0, keepdims=True) > 0, within, -2.0)
    back_ref[...] = (nn(place, spread.astype(bf16)) == within).astype(f32).astype(bf16)
    off = lax.broadcasted_iota(jnp.int32, (slots, LANES), 0).astype(f32) - slot_start(
        lax.broadcasted_iota(jnp.int32, (slots, LANES), 1), local, block)
    spread_t = ((off >= 0) & (off < CAP)).astype(f32)
    within_t = jnp.sum(spread_t * off, axis=1, keepdims=True)
    within_t = jnp.where(jnp.sum(spread_t, axis=1, keepdims=True) > 0, within_t, -2.0)
    disp_ref[...] = (nt(spread_t.astype(bf16), place) == within_t).astype(f32).astype(bf16)
    return hit.astype(f32)


def attend_forward(step, seq, images, x, gain, wq, wo, qkv_ref, mix_ref, tick=None, image_tick=None):
    width = x.shape[1]
    head = width // HEADS
    scale = head ** -0.5
    xn, _ = norm(x)
    a = (xn * gain).astype(bf16)
    for c in range(3):
        qkv_ref[:, c * width:(c + 1) * width] = nn(a, wq[c][...]).astype(bf16)
    if tick is not None:
        tick()
    lane = lax.broadcasted_iota(jnp.int32, (1, LANES), 1)
    col = lax.broadcasted_iota(jnp.int32, (1, step), 1)
    per = LANES // head

    def image(i, _):
        at = pl.ds(pl.multiple_of(i * step, step), step)
        for hp in range(width // LANES):
            q = qkv_ref[at, hp * LANES:(hp + 1) * LANES]
            k = qkv_ref[at, width + hp * LANES:width + (hp + 1) * LANES]
            v = qkv_ref[at, 2 * width + hp * LANES:2 * width + (hp + 1) * LANES]
            got = None
            for h in range(per):
                mine = (lane >= h * head) & (lane < (h + 1) * head)
                qm = q * jnp.where(mine, scale, 0.0).astype(bf16)
                s = jnp.where(col < seq, nt(qm, k), NEG)
                e = jnp.exp(s - jnp.max(s, axis=-1, keepdims=True))
                p = (e * (1.0 / jnp.sum(e, axis=-1, keepdims=True))).astype(bf16)
                o = nn(p, v)
                got = o if got is None else jnp.where(mine, o, got)
            mix_ref[at, hp * LANES:(hp + 1) * LANES] = got.astype(bf16)
        if image_tick is not None:
            image_tick(i)
        return 0

    lax.fori_loop(0, images, image, 0)
    return x + nn(mix_ref[...], wo[...])


def attend_backward(step, seq, images, grad, x, gain, wq, wo, qkv_ref, mix_ref, dmix_ref, dqkv_ref, pack_ref, base,
                    tick=None):
    width = x.shape[1]
    head = width // HEADS
    scale = head ** -0.5
    shards = pack_ref.shape[0]
    part = width // shards
    low = grad.astype(bf16)
    dwo = tn(mix_ref[...], low).astype(bf16)
    for s in range(shards):
        pack_ref[s, base + 3 * part:base + 4 * part, :] = dwo[s * part:(s + 1) * part]
    dmix_ref[...] = nt(low, wo[...]).astype(bf16)
    lane = lax.broadcasted_iota(jnp.int32, (1, LANES), 1)
    key = lax.broadcasted_iota(jnp.int32, (step, 1), 0)
    per = LANES // head

    def image(i, _):
        at = pl.ds(pl.multiple_of(i * step, step), step)
        for hp in range(width // LANES):
            q = qkv_ref[at, hp * LANES:(hp + 1) * LANES]
            k = qkv_ref[at, width + hp * LANES:width + (hp + 1) * LANES]
            v = qkv_ref[at, 2 * width + hp * LANES:2 * width + (hp + 1) * LANES]
            do = dmix_ref[at, hp * LANES:(hp + 1) * LANES]
            dq = dk = dv = None
            for h in range(per):
                mine = (lane >= h * head) & (lane < (h + 1) * head)
                scaled = jnp.where(mine, scale, 0.0).astype(bf16)
                km = k * scaled
                s = jnp.where(key < seq, nt(km, q), NEG)
                e = jnp.exp(s - jnp.max(s, axis=0, keepdims=True))
                p = e * (1.0 / jnp.sum(e, axis=0, keepdims=True))
                dom = do * jnp.where(mine, 1.0, 0.0).astype(bf16)
                dp = nt(v, dom)
                ds = (p * (dp - jnp.sum(p * dp, axis=0, keepdims=True))).astype(bf16)
                hv = nn(p.astype(bf16), dom)
                hk = nn(ds, q * scaled)
                hq = tn(ds, km)
                dq, dk, dv = (hq, hk, hv) if dq is None else (dq + hq, dk + hk, dv + hv)
            dqkv_ref[at, hp * LANES:(hp + 1) * LANES] = dq.astype(bf16)
            dqkv_ref[at, width + hp * LANES:width + (hp + 1) * LANES] = dk.astype(bf16)
            dqkv_ref[at, 2 * width + hp * LANES:2 * width + (hp + 1) * LANES] = dv.astype(bf16)
        if tick is not None:
            tick(i)
        return 0

    lax.fori_loop(0, images, image, 0)
    xn, rs = norm(x)
    a = (xn * gain).astype(bf16)
    da = None
    for c in range(3):
        d = dqkv_ref[:, c * width:(c + 1) * width]
        dw = tn(a, d).astype(bf16)
        for s in range(shards):
            pack_ref[s, base + c * part:base + (c + 1) * part, :] = dw[s * part:(s + 1) * part]
        one = nt(d, wq[c][...])
        da = one if da is None else da + one
    return norm_back(da, xn, rs, gain)


def block1_body(split, images, seq, x_ref, gain_ref, *refs):
    n = split.count(2)
    pieces, (hidden_ref, qkv_ref, mix_ref, w, sems) = refs[:n], refs[n:]
    copies = split.copies(pieces, w, sems)
    start(copies)
    step = hidden_ref.shape[0] // images
    pad_store(hidden_ref, lambda i: x_ref[i], images, seq, step)
    finish(copies)
    hidden_ref[...] = attend_forward(
        step, seq, images, hidden_ref[...], gain_ref[0:1, :], [w.at[c] for c in range(3)], w.at[3], qkv_ref, mix_ref
    )


def mlp_body(split, hidden_ref, gain_ref, *refs):
    n = 2 * split.count(1)
    pieces, (out_ref, act_ref, slope_ref, w1, w2, sems) = refs[:n], refs[n:]
    half = n // 2
    copies = split.copies(pieces[:half], w1, sems.at[0]) + split.copies(pieces[half:], w2, sems.at[1])
    start(copies)
    hidden = hidden_ref[...]
    xn, _ = norm(hidden)
    u = (xn * gain_ref[1:2, :]).astype(bf16)
    out_ref[...] = hidden
    finish(copies)
    wide = act_ref.shape[2]
    for b in range(act_ref.shape[0]):
        at = slice(b * wide, (b + 1) * wide)
        act, slope = gelu_pair(nn(u, w1[0, :, at]))
        act = act.astype(bf16)
        act_ref[b] = act
        slope_ref[b] = slope.astype(bf16)
        out_ref[...] += nn(act, w2[0, at, :])


def router_probs(u, router, experts):
    lane = lax.broadcasted_iota(jnp.int32, (1, LANES), 1)
    logits = jnp.where(lane < experts, nn(u, router), NEG)
    e = jnp.exp(logits - jnp.max(logits, axis=-1, keepdims=True))
    return e * (1.0 / jnp.sum(e, axis=-1, keepdims=True))


def block2_body(split, images, seq, experts, x_ref, gain_ref, router_ref, disp_ref, live_ref, load_ref, *refs):
    n = split.count(2)
    pieces, (hidden_ref, qkv_ref, mix_ref, u_ref, probs_ref, sum_ref, ud_ref, w, sems) = refs[:n], refs[n:]
    copies = split.copies(pieces, w, sems)
    start(copies)
    finish(copies)
    step = hidden_ref.shape[0] // images
    hidden = attend_forward(
        step, seq, images, x_ref[...], gain_ref[2:3, :], [w.at[c] for c in range(3)], w.at[3], qkv_ref, mix_ref
    )
    hidden_ref[...] = hidden
    xn, _ = norm(hidden)
    u = (xn * gain_ref[3:4, :]).astype(bf16)
    u_ref[...] = u
    ud_ref[...] = nn(disp_ref[...], u).astype(bf16)
    probs = router_probs(u, router_ref[...], experts)
    probs_ref[...] = probs
    sums = jnp.sum(probs * live_ref[...], axis=0, keepdims=True)
    sum_ref[...] = jnp.concatenate([load_ref[...], sums, jnp.zeros((6, LANES), f32)], axis=0)


def forward_body(images, seq, experts, local, owners, *refs):
    (routes_ref, counts_ref, tok_ref, cot_ref, gain1_ref, gain2_ref, small_router_ref, q1_h, o1_h, up_h, down_h, q2_h, o2_h,
     gains_out, router_out, stat_out, live_out,
     dy_o, uout_o, hid1_o, x2_o, hid2_o, qkv1_o, mix1_o, qkv2_o, mix2_o, act_o, slope_o, u_o, probs_o, back_o,
     wa_o, wu_o, wd_o, wb_o, dyin_o,
     wa, wu, wd, wb, dy, slot_rows, disp, back, hid1, x2, hid2, qkv1, mix1, qkv2, mix2, act, slope, u, probs, gx, gain_ref, router_ref, r_ref,
     lsem, osem, ks, kr, vs, vr) = refs
    me, x = lax.axis_index("expert"), lax.axis_index("shard")
    bits = owners.bit_length() - 1
    b0, b1 = me % 2, (me // 2) % 2
    core, side = me + 1 - 2 * b0, me + (1 - 2 * b1) * 2
    rows, width = dy.shape
    step = rows // images
    part = width // 2
    ff = wd.shape[1]
    fpart = ff // 2

    def to(e, s):
        return dict(device_id=(e, s), device_id_type=pl.DeviceIdType.MESH)

    def each(lo, hi, f):
        lax.fori_loop(lo, hi, lambda k, c: (f(k), c)[1], 0)

    barrier = pltpu.get_barrier_semaphore()
    each(1, owners, lambda k: pl.semaphore_signal(barrier, inc=1, **to(xor(me, k, bits), x)))
    pl.semaphore_signal(barrier, inc=1, **to(me, 1 - x))

    def at(first, size):
        return pl.ds(pl.multiple_of(first, 64), size)

    mine, theirs = x * part, (1 - x) * part
    loads = [
        pltpu.make_async_copy(q1_h, wa.at[0:3, at(mine, part)], lsem.at[0]),
        pltpu.make_async_copy(o1_h, wa.at[3, at(mine, part)], lsem.at[1]),
        pltpu.make_async_copy(up_h, wu.at[0, at(mine, part)], lsem.at[2]),
        pltpu.make_async_copy(down_h, wd.at[0, at(x * fpart, fpart)], lsem.at[3]),
        pltpu.make_async_copy(q2_h, wb.at[0:3, at(mine, part)], lsem.at[4]),
        pltpu.make_async_copy(o2_h, wb.at[3, at(mine, part)], lsem.at[5]),
    ]
    start(loads)
    router_ref[...] = jnp.concatenate([small_router_ref[...].astype(f32), jnp.zeros((part, LANES - experts), f32)], axis=1).astype(bf16)
    router_out[at(mine, part), :] = router_ref[...]
    gain_ref[...] = jnp.concatenate([gain1_ref[...].astype(f32), gain2_ref[...].astype(f32), jnp.zeros((4, part), f32)], axis=0)
    pl.semaphore_wait(barrier, owners)

    def remote(src, dst, i, peer):
        return pltpu.make_async_remote_copy(src, dst, ks.at[i], kr.at[i], **peer)

    far, near, over = to(me, 1 - x), to(core, x), to(side, x)
    half, quarter, fquarter = part // 2, part // 4, fpart // 4
    p = b0 * 2 + b1
    h = b0 * half
    here = at(theirs + h, half)
    moves = {
        "small": [lambda: remote(gain_ref, gx, 0, far), lambda: remote(router_ref, router_out.at[at(mine, part), :], 1, far)],
        "ax": [lambda: remote(q1_h.at[:, at(h, half)], wa.at[0:3, at(mine + h, half)], 2, far),
               lambda: remote(o1_h.at[at(h, half)], wa.at[3, at(mine + h, half)], 3, far)],
        "ac": [lambda: remote(wa.at[:, here], wa.at[:, here], 4, near)],
        "ux": [lambda: remote(up_h.at[at(p * quarter, quarter)], wu.at[0, at(mine + p * quarter, quarter)], 5, far)],
        "uy": [lambda: remote(wu.at[0, at(theirs + p * quarter, quarter)], wu.at[0, at(theirs + p * quarter, quarter)], 6, over)],
        "uc": [lambda: remote(wu.at[0, here], wu.at[0, here], 7, near)],
        "dx": [lambda: remote(down_h.at[at(p * fquarter, fquarter)], wd.at[0, at(x * fpart + p * fquarter, fquarter)], 8, far)],
        "dy": [lambda: remote(wd.at[0, at((1 - x) * fpart + p * fquarter, fquarter)],
                              wd.at[0, at((1 - x) * fpart + p * fquarter, fquarter)], 9, over)],
        "dc": [lambda: remote(wd.at[0, at((1 - x) * fpart + b0 * 2 * fquarter, 2 * fquarter)],
                              wd.at[0, at((1 - x) * fpart + b0 * 2 * fquarter, 2 * fquarter)], 10, near)],
        "bx": [lambda: remote(q2_h.at[:, at(p * quarter, quarter)], wb.at[0:3, at(mine + p * quarter, quarter)], 11, far),
               lambda: remote(o2_h.at[at(p * quarter, quarter)], wb.at[3, at(mine + p * quarter, quarter)], 12, far)],
        "by": [lambda: remote(wb.at[:, at(theirs + p * quarter, quarter)], wb.at[:, at(theirs + p * quarter, quarter)], 13, over)],
        "bc": [lambda: remote(wb.at[:, here], wb.at[:, here], 14, near)],
    }

    def go(*names):
        for n in names:
            for m in moves[n]:
                m().start()

    def done(*names):
        for n in names:
            for m in moves[n]:
                m().wait()

    def send_dy(k):
        q = xor(me, k, bits)
        return pltpu.make_async_remote_copy(slot_rows.at[0, q], dyin_o.at[me], vs.at[k], vr.at[k], **to(q, x))

    out = []

    def keep(src, dst):
        c = pltpu.make_async_copy(src, dst, osem.at[len(out)])
        c.start()
        out.append(c)

    go("ax", "small")
    r_ref[...] = jnp.full(r_ref.shape, -1, jnp.int32)
    for i in range(images):
        r_ref[i * step:i * step + seq, :] = routes_ref[i]
    row = lax.broadcasted_iota(jnp.int32, (rows, 1), 0)
    live = ((row < counts_ref[0] * step) & (r_ref[:, 0:1] >= 0)).astype(f32)
    live_out[...] = live
    pad_store(dy, lambda i: cot_ref[i], images, seq, step)
    dy[...] = (dy[...].astype(f32) * live).astype(bf16)
    keep(dy, dy_o)
    hit = route_tables(local, slot_rows.shape[2], r_ref, disp, back)
    keep(back, back_o)
    slot_rows[0] = nn(disp[...], dy[...]).astype(bf16).reshape(slot_rows.shape[1:])
    keep(slot_rows.at[0, me], dyin_o.at[me])
    lane = lax.broadcasted_iota(jnp.int32, (1, LANES), 1)
    load = jnp.where(lane == LANES - 1, jnp.sum(live, axis=0, keepdims=True), jnp.sum(hit * live, axis=0, keepdims=True))
    done("ax")
    go("ac", "ux")
    planes = owners // 4
    each(0, planes, lambda k: send_dy(4 * (planes - 1 - k) + 1).start())
    each(0, planes - 1, lambda k: send_dy(4 * (planes - 1 - k)).start())
    pad_store(hid1, lambda i: tok_ref[i], images, seq, step)
    done("small")
    own_gain, far_gain = gain_ref[...], gx[...]
    gains = jnp.where(x == 0, jnp.concatenate([own_gain, far_gain], axis=1), jnp.concatenate([far_gain, own_gain], axis=1))
    gains_out[...] = gains
    finish(loads)
    done("ac")
    keep(wa, wa_o)

    def first_tick():
        go("dx")

    def first_image(i):
        @pl.when(i == 0)
        def _():
            done("ux")
            go("uy")

        @pl.when(i == 1)
        def _():
            go("bx")

        @pl.when(i == 2)
        def _():
            done("uy")
            go("uc")

    hid1[...] = attend_forward(step, seq, images, hid1[...], gains[0:1], [wa.at[c] for c in range(3)], wa.at[3], qkv1, mix1,
                               first_tick, first_image)
    keep(hid1, hid1_o)
    keep(qkv1, qkv1_o)
    keep(mix1, mix1_o)

    done("uc")
    keep(wu, wu_o)
    xn, _ = norm(hid1[...])
    a = (xn * gains[1:2]).astype(bf16)
    for b in range(act.shape[0]):
        one, two = gelu_pair(nn(a, wu[0, :, b * width:(b + 1) * width]))
        act[b] = one.astype(bf16)
        slope[b] = two.astype(bf16)
        if b == 0:
            done("dx")
            go("dy")
        if b == 2:
            done("bx")
            go("by")
        if b == act.shape[0] - 1:
            done("dy")
            go("dc")
            each(0, planes, lambda k: send_dy(4 * (planes - 1 - k) + 3).start())
            each(0, planes, lambda k: send_dy(4 * (planes - 1 - k) + 2).start())
    keep(slope, slope_o)
    keep(act, act_o)
    done("dc")
    keep(wd, wd_o)
    total = hid1[...]
    for b in range(act.shape[0]):
        total = total + nn(act[b], wd[0, b * width:(b + 1) * width, :])
        if b == 0:
            done("by")
            go("bc")
    x2[...] = total
    done("bc")
    keep(wb, wb_o)
    keep(x2, x2_o)

    hid2[...] = attend_forward(step, seq, images, x2[...], gains[2:3], [wb.at[c] for c in range(3)], wb.at[3], qkv2, mix2)
    keep(qkv2, qkv2_o)
    keep(mix2, mix2_o)
    keep(hid2, hid2_o)
    xn, _ = norm(hid2[...])
    u[...] = (xn * gains[3:4]).astype(bf16)
    keep(u, u_o)
    slot_rows[1] = nn(disp[...], u[...]).astype(bf16).reshape(slot_rows.shape[1:])
    keep(slot_rows.at[1], uout_o)
    probs[...] = router_probs(u[...], router_out[...], experts)
    keep(probs, probs_o)
    sums = jnp.sum(probs[...] * live, axis=0, keepdims=True)
    stat_out[...] = jnp.concatenate([load, sums, jnp.zeros((6, LANES), f32)], axis=0)
    each(1, owners, lambda k: send_dy(k).wait())
    finish(out)


def fused_forward(owners, experts, local, block, tokens, cotangent, routes, counts, gains1, gains2, router, attn_qkv1, attn_out1, mlp_in, mlp_out,
                  attn_qkv2, attn_out2):
    images, seq, width = tokens.shape
    step = padded(seq)
    rows = images * step
    ff = mlp_in.shape[1]
    slots = owners * block[1]
    blocks = ff // width
    part = width // 2
    V, sem = pltpu.VMEM, pltpu.SemaphoreType.DMA
    kept = [
        ((rows, width), bf16), (block, bf16), ((rows, width), f32), ((rows, width), f32), ((rows, width), f32),
        ((rows, 3 * width), bf16), ((rows, width), bf16), ((rows, 3 * width), bf16), ((rows, width), bf16),
        ((blocks, rows, width), bf16), ((blocks, rows, width), bf16), ((rows, width), bf16), ((rows, LANES), f32), ((rows, slots), bf16),
        ((4, width, width), bf16), ((1, width, ff), bf16), ((1, ff, width), bf16), ((4, width, width), bf16), (block, bf16),
    ]
    return pl.pallas_call(
        functools.partial(forward_body, images, seq, experts, local, owners),
        out_shape=[sds((8, width), f32), sds((width, LANES), bf16), sds((8, LANES), f32), sds((rows, 1), f32)]
        + [sds(shape, dtype) for shape, dtype in kept],
        in_specs=[VM, pl.BlockSpec(memory_space=pltpu.SMEM)] + [VM] * 5 + [ANY] * 6,
        out_specs=[VM] * 4 + [ANY] * len(kept),
        scratch_shapes=[
            V((4, width, width), bf16), V((1, width, ff), bf16), V((1, ff, width), bf16), V((4, width, width), bf16),
            V((rows, width), bf16), V((2,) + block, bf16), V((slots, rows), bf16), V((rows, slots), bf16),
            V((rows, width), f32), V((rows, width), f32), V((rows, width), f32),
            V((rows, 3 * width), bf16), V((rows, width), bf16), V((rows, 3 * width), bf16), V((rows, width), bf16),
            V((blocks, rows, width), bf16), V((blocks, rows, width), bf16), V((rows, width), bf16), V((rows, LANES), f32),
            V((8, part), f32), V((8, part), f32), V((part, LANES), bf16), V((rows, 2), jnp.int32),
            sem((6,)), sem((len(kept),)), sem((15,)), sem((15,)), sem((owners,)), sem((owners,)),
        ],
        compiler_params=pltpu.CompilerParams(vmem_limit_bytes=VMEM_BYTES, collective_id=2, has_side_effects=True),
        cost_estimate=pl.CostEstimate(flops=int(18e9), bytes_accessed=int(60e6), transcendentals=0),
    )(routes, counts, tokens, cotangent, gains1, gains2, router, attn_qkv1, attn_out1, mlp_in, mlp_out, attn_qkv2, attn_out2)


def split_rows(block, local):
    n, r, w = block.shape
    v = block.astype(f32)
    if r != local * CAP:
        v = v[:, :local * CAP]
    v = v.reshape(n, local, CAP, w)
    return [v[:, i].reshape(n * CAP, w) for i in range(local)]


def join_rows(parts, sources, block):
    local = len(parts)
    w = parts[0].shape[1]
    v = jnp.concatenate([p.reshape(sources, 1, CAP, w) for p in parts], axis=1).reshape(sources, local * CAP, w)
    if block != local * CAP:
        v = jnp.concatenate([v, jnp.zeros((sources, block - local * CAP, w), f32)], axis=1)
    return v


def gate_of(u, router, experts, e):
    lane = lax.broadcasted_iota(jnp.int32, (1, LANES), 1)
    return jnp.sum(jnp.where(lane == e, router_probs(u, router, experts), 0.0), axis=-1, keepdims=True)


def xor(a, b, bits):
    out = 0
    for i in range(bits):
        out = out + ((a // (1 << i) + b // (1 << i)) % 2) * (1 << i)
    return out


def expert_body(owners, shards, local, experts, group, uout_ref, dy_ref, router_ref, stat_ref, w1_hbm, w2_hbm,
                uin_ref, served_ref, duback_ref, dgback_ref, total_ref, dyx_ref, ux_ref, *refs):
    if shards == 2:
        p1_h, p2_h, *refs = refs
    (w1, w2, dusend, dgsend, statx, state, acts, dzs, urows, drows, ob1, ob2, wsem, lsem, osem, us, ur, ds_, dr, gs, gr, ss, sr, fs, fr, xs, xr, ys, yr) = refs
    me, x = lax.axis_index("expert"), lax.axis_index("shard")
    bits = owners.bit_length() - 1
    barrier = pltpu.get_barrier_semaphore()

    def at(e, s):
        return dict(device_id=(e, s), device_id_type=pl.DeviceIdType.MESH)

    def each(lo, hi, f):
        lax.fori_loop(lo, hi, lambda k, c: (f(k), c)[1], 0)

    def peer(k):
        return xor(me, k, bits)

    each(1, owners, lambda k: pl.semaphore_signal(barrier, inc=1, **at(peer(k), x)))
    each(1, shards, lambda k: pl.semaphore_signal(barrier, inc=1, **at(me, (x + k) % shards)))
    weights = [pltpu.make_async_copy(w1_hbm, w1, wsem.at[0]), pltpu.make_async_copy(w2_hbm, w2, wsem.at[1])]
    start(weights)
    own = pltpu.make_async_copy(uout_ref.at[me], uin_ref.at[me], lsem.at[0])
    own.start()
    pl.semaphore_wait(barrier, owners - 1 + shards - 1)

    def send_u(k):
        return pltpu.make_async_remote_copy(uout_ref.at[peer(k)], uin_ref.at[me], us.at[k], ur.at[k], **at(peer(k), x))

    def send_du(k):
        return pltpu.make_async_remote_copy(dusend.at[peer(k)], duback_ref.at[me], ds_.at[k], dr.at[k], **at(peer(k), x))

    def send_dg(k):
        return pltpu.make_async_remote_copy(dgsend.at[peer(k)], dgback_ref.at[me], gs.at[k], gr.at[k], **at(peer(k), x))

    def send_statx(k):
        return pltpu.make_async_remote_copy(stat_ref, statx.at[k], xs.at[k], xr.at[k], **at(me, (x + k) % shards))

    def send_dyx(k):
        return pltpu.make_async_remote_copy(dy_ref, dyx_ref.at[k - 1], ys.at[k], yr.at[k], **at(me, (x + k) % shards))

    def send_far(g):
        rows = pl.ds(xor(me // group, g, bits) * group, group)
        return pltpu.make_async_remote_copy(uin_ref.at[rows], ux_ref.at[rows], fs.at[g], fr.at[g], **at(me, (x + 1) % shards))

    def send_state(k):
        return pltpu.make_async_remote_copy(state.at[0], state.at[k], ss.at[k], sr.at[k], **at(peer(k), x))

    each(1, shards, lambda k: send_statx(k).start())
    each(1, owners, lambda k: send_u(owners - k).start())
    each(1, shards, lambda k: send_dyx(k).start())
    each(1, shards, lambda k: send_statx(k).wait())
    sums = stat_ref[...]
    for k in range(1, shards):
        sums = sums + statx[k]
    state[0] = sums
    each(1, owners, lambda k: send_state(k).start())
    finish(weights)

    def work(g):
        base = xor(me // group, g, bits) * group
        rows = pl.ds(base, group)
        us_, dys = split_rows(uin_ref[rows], local), split_rows(dy_ref[rows], local)
        served, dus, prods = [], [], []
        for i in range(local):
            u, dy = us_[i].astype(bf16), dys[i]
            gate = gate_of(u, router_ref[...], experts, me * local + i)
            dsv = (gate * dy).astype(bf16)
            act, slope = gelu_pair(nn(u, w1[i]))
            out = nn(act.astype(bf16), w2[i])
            dz = (slope * nt(dsv, w2[i])).astype(bf16)
            if shards == 2:
                n = group * CAP
                spot = pl.ds(pl.multiple_of(g * n, n), n)
                acts[i, spot] = act.astype(bf16)
                dzs[i, spot] = dz
                urows[i, spot] = u
                drows[i, spot] = dsv
            dus.append(nt(dz, w1[i]))
            served.append(gate * out)
            prods.append(dy * out)
        block = uin_ref.shape[1]
        served_ref[rows] = join_rows(served, group, block).astype(bf16)
        dusend[rows] = join_rows(dus, group, block).astype(bf16)
        prod = join_rows(prods, group, block)
        ones = jnp.ones((8, prod.shape[2]), bf16)
        for j in range(group):
            hi = prod[j].astype(bf16)
            lo = (prod[j] - hi.astype(f32)).astype(bf16)
            dgsend[base + j, :, 0:block] = nt(ones, hi) + nt(ones, lo)

    def step(g):
        @pl.when(g == 0)
        def _():
            own.wait()

        for j in range(group):
            k = g * group + j
            if j == 0:
                pl.when(g > 0)(lambda k=k: send_u(k).wait_recv())
            else:
                send_u(k).wait_recv()
        if shards == 2:
            send_far(g).start()
        work(g)
        for j in range(group):
            k = g * group + j
            if j == 0:
                @pl.when(g > 0)
                def _(k=k):
                    send_du(k).start()
                    send_dg(k).start()
            else:
                send_du(k).start()
                send_dg(k).start()

    each(0, owners // group, step)
    backs = [pltpu.make_async_copy(dusend.at[me], duback_ref.at[me], lsem.at[0]),
             pltpu.make_async_copy(dgsend.at[me], dgback_ref.at[me], lsem.at[1])]
    start(backs)
    if shards == 2:
        width = urows.shape[2]
        blocks = acts.shape[2] // width

        def result(i):
            e, f = i // blocks, i % blocks
            col = pl.ds(pl.multiple_of(f * width, width), width)
            return [pltpu.make_async_copy(ob1.at[i % 2], p1_h.at[e, :, col], osem.at[i % 2]),
                    pltpu.make_async_copy(ob2.at[i % 2], p2_h.at[e, col, :], osem.at[2 + i % 2])]

        def gradient(i):
            e, f = i // blocks, i % blocks
            col = pl.ds(pl.multiple_of(f * width, width), width)
            pl.when(i >= 2)(lambda: finish(result(i - 2)))
            ob1[i % 2] = tn(urows[e], dzs[e, :, col]).astype(bf16)
            ob2[i % 2] = tn(acts[e, :, col], drows[e]).astype(bf16)
            start(result(i))

        count = local * blocks
        each(0, count, gradient)
        for i in range(max(0, count - 2), count):
            finish(result(i))
    each(1, owners, lambda k: send_state(k).wait())
    total = state[0]
    for k in range(1, owners):
        total = total + state[k]
    total_ref[...] = total
    each(1, owners, lambda k: send_u(k).wait_send())
    finish(backs)
    each(1, shards, lambda k: send_dyx(k).wait())
    if shards == 2:
        each(0, owners // group, lambda g: send_far(g).wait())
    each(1, owners, lambda k: send_du(k).wait())
    each(1, owners, lambda k: send_dg(k).wait())


def expert_grad_body(pieces, experts, *refs):
    us, dys = refs[:pieces], refs[pieces:2 * pieces]
    router_ref, w1_ref, w2_ref, g1_ref, g2_ref, urow, drow, stage, sems = refs[2 * pieces:]
    local = pl.num_programs(0)
    e = lax.axis_index("expert") * local + pl.program_id(0)

    @pl.when((pl.program_id(0) == 0) & (pl.program_id(1) == 0))
    def _():
        todo = [(us[i], urow, i) for i in range(pieces)] + [(dys[i], drow, i) for i in range(pieces)]
        copies = [pltpu.make_async_copy(r, stage.at[n % 2], sems.at[n % 2]) for n, (r, _, _) in enumerate(todo)]
        copies[0].start()
        for n, (_, to, i) in enumerate(todo):
            if n + 1 < len(todo):
                copies[n + 1].start()
            copies[n].wait()
            for j, v in enumerate(split_rows(stage[n % 2], urow.shape[1])):
                to[i, j] = v.astype(bf16)

    at = pl.program_id(0)
    for i in range(pieces):
        u = urow[i, at]
        dy = drow[i, at]
        gate = gate_of(u, router_ref[...], experts, e)
        ds = (gate * dy.astype(f32)).astype(bf16)
        act, slope = gelu_pair(nn(u, w1_ref[0]))
        dz = (slope * nt(ds, w2_ref[0])).astype(bf16)
        g1 = tn(u, dz)
        g2 = tn(act.astype(bf16), ds)
        if i == 0:
            g1_ref[0] = g1
            g2_ref[0] = g2
        else:
            g1_ref[0] += g1
            g2_ref[0] += g2


def split3(v):
    hi = v.astype(bf16)
    r = v - hi.astype(f32)
    mid = r.astype(bf16)
    lo = (r - mid.astype(f32)).astype(bf16)
    return hi, mid, lo


def router_backward(experts, dy_ref, u_ref, probs_ref, hidden_ref, gain_ref, router_ref, aux_ref, stat_ref, live_ref,
                    back_ref, ret_ref, dgate_ref, small_ref):
    slots = back_ref.shape[1]
    owners = dgate_ref.shape[0]
    local = experts // owners
    block = slots // owners
    off = lax.broadcasted_iota(jnp.int32, (slots, LANES), 0).astype(f32) - slot_start(
        lax.broadcasted_iota(jnp.int32, (slots, LANES), 1), local, block)
    oe = lax.broadcasted_iota(jnp.int32, (owners, LANES), 0).astype(f32)
    ee = lax.broadcasted_iota(jnp.int32, (owners, LANES), 1).astype(f32)
    pick = ((ee >= oe * local) & (ee < oe * local + local)).astype(f32).astype(bf16)
    column = 0.0
    for part in split3(dgate_ref[:, 0, :]):
        column = column + tn(part, pick)
    table = jnp.where((off >= 0) & (off < CAP), jnp.concatenate([column[0:block]] * owners, axis=0), 0.0)
    lane = lax.broadcasted_iota(jnp.int32, (1, LANES), 1)
    stat = stat_ref[0:1, :]
    total = jnp.sum(jnp.where(lane == LANES - 1, stat, 0.0), axis=-1, keepdims=True)
    fraction = jnp.where(lane < experts, stat, 0.0) / (2.0 * total)
    loss = experts * jnp.sum(fraction * stat_ref[1:2, :] / total, axis=-1, keepdims=True)
    small_ref[LANES + 2:LANES + 3, :] = jnp.broadcast_to(loss, (1, small_ref.shape[1]))
    dprobs = (aux_ref[0, 0] * experts * fraction / total) * live_ref[...]
    for part in split3(table):
        dprobs = dprobs + nn(back_ref[...], part)
    probs = probs_ref[...]
    dlog = (probs * (dprobs - jnp.sum(probs * dprobs, axis=-1, keepdims=True))).astype(bf16)
    small_ref[0:LANES, :] = tn(dlog, u_ref[...])
    du = nn(back_ref[...], ret_ref[...].reshape(slots, dy_ref.shape[1])) + nt(dlog, router_ref[...])
    xn, rs = norm(hidden_ref[...])
    dv, dg = norm_back(du, xn, rs, gain_ref[3:4, :])
    small_ref[LANES:LANES + 1, :] = dg
    grad = dy_ref[...].astype(f32) + dv
    return grad


def back2_body(split, images, seq, experts, dy_ref, u_ref, probs_ref, hidden_ref, x_ref, gain_ref, router_ref, aux_ref,
               stat_ref, live_ref, back_ref, ret_ref, dgate_ref, qkv_ref, mix_ref, *refs):
    n = split.count(2)
    pieces, (grad_ref, pack_ref, small_ref, w, sems, dmix_ref, dqkv_ref) = refs[:n], refs[n:]
    copies = split.copies(pieces, w, sems)
    start(copies)
    grad = router_backward(experts, dy_ref, u_ref, probs_ref, hidden_ref, gain_ref, router_ref, aux_ref, stat_ref, live_ref,
                           back_ref, ret_ref, dgate_ref, small_ref)
    grad_ref[...] = grad
    finish(copies)
    step = hidden_ref.shape[0] // images
    dv, dg = attend_backward(
        step, seq, images, grad, x_ref[...], gain_ref[2:3, :], [w.at[c] for c in range(3)], w.at[3],
        qkv_ref, mix_ref, dmix_ref, dqkv_ref, pack_ref, 0,
    )
    small_ref[LANES + 1:LANES + 2, :] = dg
    grad_ref[...] += dv


def mlp_back_body(split, grad_ref, hidden_ref, gain_ref, act_ref, slope_ref, *refs):
    n = 2 * split.count(1)
    pieces, (out_ref, pack_ref, dgain_ref, w1, w2, sems, du_ref) = refs[:n], refs[n:]
    half = n // 2
    copies = split.copies(pieces[:half], w1, sems.at[0]) + split.copies(pieces[half:], w2, sems.at[1])
    start(copies)
    xn, rs = norm(hidden_ref[...])
    gain = gain_ref[1:2, :]
    u = (xn * gain).astype(bf16)
    grad = grad_ref[...]
    low = grad.astype(bf16)
    finish(copies)
    width = grad.shape[1]
    blocks = act_ref.shape[0]
    ff = blocks * width
    shards = pack_ref.shape[0]
    part, fpart = width // shards, ff // shards
    base = part * blocks
    for b in range(blocks):
        at = slice(b * width, (b + 1) * width)
        dz = (slope_ref[b].astype(f32) * nt(low, w2[0, at, :])).astype(bf16)
        d = nt(dz, w1[0, :, at])
        if b == 0:
            du_ref[...] = d
        else:
            du_ref[...] += d
        gin = tn(u, dz).astype(bf16)
        for s in range(shards):
            pack_ref[s, b * part:(b + 1) * part, :] = gin[s * part:(s + 1) * part]
        gout = tn(act_ref[b], low).astype(bf16)
        per = min(width, fpart)
        for j in range(width // per):
            row = b * width + j * per
            s, off = row // fpart, row % fpart
            pack_ref[s, base + off:base + off + per, :] = gout[j * per:(j + 1) * per]
    dv, dg = norm_back(du_ref[...], xn, rs, gain)
    dgain_ref[...] = dg
    out_ref[...] = grad + dv


def back1_body(split, images, seq, experts, grad_ref, tok_ref, gain_ref, qkv_ref, mix_ref, small_ref, dg2_ref, *refs):
    n = split.count(2)
    pieces, (out_ref, pack_ref, w, sems, x_ref, dmix_ref, dqkv_ref) = refs[:n], refs[n:]
    copies = split.copies(pieces, w, sems)
    start(copies)
    step = x_ref.shape[0] // images
    pad_store(x_ref, lambda i: tok_ref[i], images, seq, step)
    finish(copies)
    width = x_ref.shape[1]
    dv, dg1 = attend_backward(
        step, seq, images, grad_ref[...], x_ref[...], gain_ref[0:1, :], [w.at[c] for c in range(3)], w.at[3],
        qkv_ref, mix_ref, dmix_ref, dqkv_ref, pack_ref, 0,
    )
    x_ref[...] = grad_ref[...] + dv
    for i in range(images):
        out_ref[i] = x_ref[i * step:i * step + seq, :]
    shards = pack_ref.shape[0]
    part = width // shards
    base = 4 * part
    gains = jnp.concatenate(
        [dg1, dg2_ref[...], small_ref[LANES + 1:LANES + 2, :], small_ref[LANES:LANES + 1, :], jnp.zeros((28, width), f32)], axis=0
    )
    both = jnp.concatenate([small_ref[0:32, :], gains], axis=0).astype(bf16)
    for s in range(shards):
        one = both[:, s * part:(s + 1) * part]
        pack_ref[s, base:base + 64, :] = jnp.concatenate([one, jnp.zeros((64, width - part), bf16)], axis=1)


def output_body(images, seq, hidden_ref, back_ref, ret_ref, live_ref, out_ref, tmp_ref):
    step = hidden_ref.shape[0] // images
    tmp_ref[...] = (hidden_ref[...] + nn(back_ref[...], ret_ref[...])) * live_ref[...]
    for i in range(images):
        out_ref[i] = tmp_ref[i * step:i * step + seq, :].astype(bf16)


def backward_body(split, images, seq, experts, local, owners, plan, *refs):
    (gain_ref, router_ref, aux_ref, stat_ref, live_ref, back_ref, dgate_ref, tok_ref, dy_h, u_h, probs_h, du_h,
     hid2_h, x2_h, hid1_h, qkv2_h, mix2_h, qkv1_h, mix1_h, act_h, slope_h, served_h, ux_h, dyx_h, p1_h, p2_h, we1_h, we2_h,
     *refs) = refs
    na = nm = 1
    two, refs = refs[:na], refs[na:]
    up, refs = refs[:nm], refs[nm:]
    down, refs = refs[:nm], refs[nm:]
    one, refs = refs[:na], refs[na:]
    (out_ref, gtok_ref, fin, smout_ref, small_ref, ge1_h, ge2_h, sback_h,
     hid2, xbuf, grad_ref, dubuf, qkv, mix, dmix, dqkv, watt, w1, w2, big, stage, pack, crecv, xa, yb, ya, xb, zr,
     sm, smr,
     lsem, wsem, vs, vr, gs, gr, ms, mr, esem, osem, tsem, psem) = refs
    me, x = lax.axis_index("expert"), lax.axis_index("shard")
    bits = owners.bit_length() - 1
    bit = [(me // (1 << i)) % 2 for i in range(bits)]
    hop = [me + (1 - 2 * bit[i]) * (1 << i) for i in range(bits)]
    rows, width = grad_ref.shape
    step = rows // images
    blocks = act_h.shape[0]
    whole = pack.shape[2]
    part = width // 2

    def to(e, s):
        return dict(device_id=(e, s), device_id_type=pl.DeviceIdType.MESH)

    def each(lo, hi, f):
        lax.fori_loop(lo, hi, lambda k, c: (f(k), c)[1], 0)

    barrier = pltpu.get_barrier_semaphore()
    each(1, owners, lambda k: pl.semaphore_signal(barrier, inc=1, **to(xor(me, k, bits), x)))
    pl.semaphore_signal(barrier, inc=1, **to(me, 1 - x))

    def load(src, dst, i):
        return pltpu.make_async_copy(src, dst, lsem.at[i])

    count = 4 + 2 * blocks
    dy_ref, u_ref, probs_ref, du_ref = dmix, dqkv.at[:, 0:width], dubuf.at[:, 0:LANES], stage.at[0]
    start_in = [load(hid2_h, hid2, 0), load(du_h, du_ref, count), load(dy_h, dy_ref, count + 1), load(u_h, u_ref, count + 2),
                load(probs_h, probs_ref, count + 3)]
    start(start_in)
    first = [load(x2_h, xbuf, 1), load(qkv2_h, qkv, 2), load(mix2_h, mix, 3)]
    w_two = split.copies(two, watt, wsem.at[0])
    w_mlp = split.copies(up, w1, wsem.at[1]) + split.copies(down, w2, wsem.at[2])
    gelus = [load(act_h.at[b], big.at[b, 0:rows], 4 + b) for b in range(blocks)]
    gelus += [load(slope_h.at[b], big.at[b, big.shape[1] // 2:big.shape[1] // 2 + rows], 4 + blocks + b) for b in range(blocks)]
    start(first + w_two + w_mlp + gelus)
    own = pltpu.make_async_copy(served_h.at[me], sback_h.at[me], tsem.at[0])
    own.start()
    pl.semaphore_wait(barrier, owners)

    def send_served(k):
        p = xor(me, k, bits)
        return pltpu.make_async_remote_copy(served_h.at[p], sback_h.at[me], vs.at[k], vr.at[k], **to(p, x))

    each(1, owners, lambda k: send_served(owners - k).start())

    planes = owners // 4

    def add(ref, at, other):
        ref[at] = ref[at] + other

    def span(first, size):
        return pl.ds(pl.multiple_of(first, 32), size)

    def stages(n):
        def copy(src, dst, i, peer):
            return pltpu.make_async_remote_copy(src, dst, gs.at[n, i], gr.at[n, i], **peer)

        q = whole // 4
        o = bit[0] * (whole // 2)
        out = []
        out.append((
            lambda: [copy(pack.at[n, :, span((1 - bit[0]) * (whole // 2), whole // 2)], crecv.at[n], 0, to(hop[0], x))],
            lambda: add(pack, (n, slice(None), span(o, whole // 2)), crecv[n])))
        e = q // 2
        b1 = bit[1] * e

        def after1():
            add(pack, (n, x, span(o, q)), xa[n])
            add(pack, (n, slice(None), span(o + q + b1, e)), yb[n])

        out.append((
            lambda: [copy(pack.at[n, 1 - x, span(o, q)], xa.at[n], 1, to(me, 1 - x)),
                     copy(pack.at[n, :, span(o + q + e - b1, e)], yb.at[n], 2, to(hop[1], x))],
            after1))

        def after2():
            add(pack, (n, x, span(o + b1, e)), ya[n])
            add(pack, (n, x, span(o + q + b1, e)), xb[n])

        out.append((
            lambda: [copy(pack.at[n, x, span(o + e - b1, e)], ya.at[n], 3, to(hop[1], x)),
                     copy(pack.at[n, 1 - x, span(o + q + b1, e)], xb.at[n], 4, to(me, 1 - x))],
            after2))
        size = e // planes
        base = o + b1

        def rows_at(p):
            return [span(base + p * size + j * q, size) for j in range(2)]

        def over(make):
            out = []
            for k in range(1, planes):
                p = xor(me // 4, k, bits)
                for j in range(2):
                    out.append(make(k, p, j, 5 + 2 * (k - 1) + j, to(p * 4 + me % 4, x)))
            return out

        mine = me // 4

        def after3():
            for j in range(2):
                at = (n, x, rows_at(mine)[j])
                total = pack[at].astype(f32)
                for k in range(1, planes):
                    total = total + zr[n, 2 * (k - 1) + j].astype(f32)
                fin[(n, rows_at(mine)[j])] = total.astype(bf16)

        more = 2 * (planes - 1)
        out.append((
            lambda: over(lambda k, p, j, i, peer: copy(pack.at[n, x, rows_at(p)[j]], zr.at[n, 2 * (k - 1) + j], i, peer)), after3))
        out.append((
            lambda: over(lambda k, p, j, i, peer: copy(fin.at[n, rows_at(mine)[j]], fin.at[n, rows_at(mine)[j]], i + more, peer)),
            lambda: None))
        out.append((
            lambda: [copy(fin.at[n, span(base + j * q, e)], fin.at[n, span(base + j * q, e)], 5 + 2 * more + j, to(hop[1], x))
                     for j in range(2)],
            lambda: None))
        out.append((
            lambda: [copy(fin.at[n, span(o, whole // 2)], fin.at[n, span(o, whole // 2)], 7 + 2 * more, to(hop[0], x))],
            lambda: None))
        return out

    groups = [stages(n) for n in range(4)]

    def small_stage(i):
        if i == 0:
            src, dst, peer = sm, smr.at[0], to(hop[0], x)
        elif i == 1:
            src, dst, peer = sm.at[1 - x], smr.at[1, 0], to(me, 1 - x)
        else:
            src, dst, peer = sm.at[x], smr.at[i, 0], to(hop[i - 1], x)
        return pltpu.make_async_remote_copy(src, dst, ms.at[i], mr.at[i], **peer)

    def small_after(i):
        if i == 0:
            sm[...] += smr[0]
        else:
            sm[x] += smr[i, 0]

    def tick(n, k):
        table = groups[n]
        if k > 0:
            finish(table[k - 1][0]())
            table[k - 1][1]()
            if n == 3 and k - 1 < bits + 1:
                small_stage(k - 1).wait()
                small_after(k - 1)
        if k < len(table):
            start(table[k][0]())
            if n == 3 and k < bits + 1:
                small_stage(k).start()

    def at_point(name, index=None):
        for i, n, k in plan.get(name, ()):
            if index is None:
                tick(n, k)
            else:
                pl.when(index == i)(functools.partial(tick, n, k))

    finish(start_in)
    grad_ref[...] = router_backward(experts, dy_ref, u_ref, probs_ref, hid2, gain_ref, router_ref, aux_ref, stat_ref, live_ref,
                                    back_ref, du_ref, dgate_ref, small_ref)
    finish(first + w_two)
    dv, dg = attend_backward(
        step, seq, images, grad_ref[...], xbuf[...], gain_ref[2:3, :], [watt.at[c] for c in range(3)], watt.at[3],
        qkv, mix, dmix, dqkv, pack.at[0], 0,
    )
    small_ref[LANES + 1:LANES + 2, :] = dg
    grad_ref[...] += dv
    at_point("two")
    second = [load(hid1_h, xbuf, 1), load(qkv1_h, qkv, 2), load(mix1_h, mix, 3)]
    w_one = split.copies(one, watt, wsem.at[0])
    start(second + w_one)

    finish(gelus + w_mlp)
    low = grad_ref[...].astype(bf16)
    fpart = blocks * width // 2
    for b in range(blocks):
        s, off = b * width // fpart, b * width % fpart
        pack[1, s, off:off + width, :] = tn(big[b, 0:rows], low).astype(bf16)
    at_point("out")
    finish(second[:1])
    xn, rs = norm(xbuf[...])
    gain = gain_ref[1:2, :]
    u = (xn * gain).astype(bf16)
    half = big.shape[1] // 2
    for b in range(blocks):
        cols = slice(b * width, (b + 1) * width)
        dz = (big[b, half:half + rows].astype(f32) * nt(low, w2[0, cols, :])).astype(bf16)
        d = nt(dz, w1[0, :, cols])
        if b == 0:
            dubuf[...] = d
        else:
            dubuf[...] += d
        gin = tn(u, dz).astype(bf16)
        for s in range(2):
            pack[2, s, b * part:(b + 1) * part, :] = gin[s * part:(s + 1) * part]
        at_point("in%d" % b)
    dv, dg = norm_back(dubuf[...], xn, rs, gain)
    small_ref[LANES + 3:LANES + 4, :] = dg
    grad_ref[...] += dv
    at_point("mlp")

    pad_store(xbuf, lambda i: tok_ref[i], images, seq, step)
    finish(second[1:] + w_one)
    dv, dg = attend_backward(
        step, seq, images, grad_ref[...], xbuf[...], gain_ref[0:1, :], [watt.at[c] for c in range(3)], watt.at[3],
        qkv, mix, dmix, dqkv, pack.at[3], 0, tick=lambda i: at_point("image", i),
    )
    sm[...] = jnp.zeros(sm.shape, f32)
    for s in range(2):
        cols = slice(s * part, (s + 1) * part)
        sm[s, 0:experts] = small_ref[0:experts, cols]
        sm[s, experts:experts + 1] = dg[:, cols]
        sm[s, experts + 1:experts + 2] = small_ref[LANES + 3:LANES + 4, cols]
        sm[s, experts + 2:experts + 3] = small_ref[LANES + 1:LANES + 2, cols]
        sm[s, experts + 3:experts + 4] = small_ref[LANES:LANES + 1, cols]
    at_point("one")
    grad_ref[...] += dv
    for i in range(images):
        gtok_ref[i] = grad_ref[i * step:i * step + seq, :]

    own.wait()
    each(1, owners, lambda k: send_served(k).wait())
    at_point("rows")

    todo = [(ux_h, 0), (dyx_h.at[0], 1)]
    moves = [pltpu.make_async_copy(r, stage.at[i % 2], esem.at[i % 2]) for i, (r, _) in enumerate(todo)]

    def lane(i):
        return pl.ds(pl.multiple_of(i * width, width), width)

    def chunk(i):
        e, f = i // blocks, i % blocks
        slot = i % 2
        col = pl.ds(pl.multiple_of(f * width, width), width)
        return [pltpu.make_async_copy(we1_h.at[e, :, col], w1.at[0, :, lane(slot)], esem.at[2 + slot]),
                pltpu.make_async_copy(we2_h.at[e, col, :], w2.at[0, lane(slot), :], esem.at[4 + slot])]

    def result(i):
        e, f = i // blocks, i % blocks
        slot = i % 2
        col = pl.ds(pl.multiple_of(f * width, width), width)
        return [pltpu.make_async_copy(w1.at[0, :, lane(2 + slot)], ge1_h.at[e, :, col], osem.at[slot]),
                pltpu.make_async_copy(w2.at[0, lane(2 + slot), :], ge2_h.at[e, col, :], osem.at[2 + slot])]

    moves[0].start()
    start(chunk(0))
    for i, (_, kind) in enumerate(todo):
        if i + 1 < len(todo):
            moves[i + 1].start()
        moves[i].wait()
        for e, v in enumerate(split_rows(stage[i % 2], local)):
            if kind == 1:
                u = big[e, 0:half]
                v = v * gate_of(u, router_ref[...], experts, me * local + e)
            big[kind * local + e, 0:half] = v.astype(bf16)
    back = pltpu.make_async_copy(sback_h, stage.at[0], tsem.at[0])
    back.start()
    back.wait()
    grad_ref[...] = (hid2[...] + nn(back_ref[...], stage[0].reshape(back_ref.shape[1], width))) * live_ref[...]
    for i in range(images):
        out_ref[i] = grad_ref[i * step:i * step + seq, :].astype(bf16)
    at_point("output")
    count = local * blocks

    def before(i):
        e, f = i // blocks, i % blocks
        slot = i % 2
        col = pl.ds(pl.multiple_of(f * width, width), width)
        return [pltpu.make_async_copy(p1_h.at[e, :, col], w1.at[0, :, lane(2 + slot)], psem.at[slot]),
                pltpu.make_async_copy(p2_h.at[e, col, :], w2.at[0, lane(2 + slot), :], psem.at[2 + slot])]

    def expert(i, c):
        slot = i % 2
        pl.when(i + 1 < count)(lambda: start(chunk(i + 1)))
        pl.when(i >= 2)(lambda: finish(result(i - 2)))
        start(before(i))
        finish(chunk(i))
        e = i // blocks
        u = big[e, 0:half]
        dsv = big[local + e, 0:half]
        act, slope = gelu_pair(nn(u, w1[0, :, lane(slot)]))
        dz = (slope * nt(dsv, w2[0, lane(slot), :])).astype(bf16)
        act = act.astype(bf16)
        finish(before(i))
        at1, at2 = (0, slice(None), lane(2 + slot)), (0, lane(2 + slot), slice(None))
        w1[at1] = (w1[at1].astype(f32) + tn(u, dz)).astype(bf16)
        at_point("early", i)
        w2[at2] = (w2[at2].astype(f32) + tn(act, dsv)).astype(bf16)
        start(result(i))
        at_point("late", i)
        return c

    lax.fori_loop(0, count, expert, 0)
    at_point("end")
    for i in range(max(0, count - 2), count):
        finish(result(i))
    smout_ref[...] = sm[x]


def swap(owners, bit):
    return [(i, i ^ (1 << bit)) for i in range(owners)]


def reduce_all(g, owners, shards):
    me = lax.axis_index("expert")
    bits = owners.bit_length() - 1

    def add(a, b):
        return (a.astype(f32) + b.astype(f32)).astype(bf16)

    def fold(v, bit, axis):
        own = (me >> bit) & 1
        half = v.shape[axis] // 2
        keep = lax.dynamic_slice_in_dim(v, own * half, half, axis)
        send = lax.dynamic_slice_in_dim(v, (1 - own) * half, half, axis)
        return add(keep, lax.ppermute(send, "expert", swap(owners, bit)))

    v = fold(g, 0, 1)
    if shards == 2:
        x = lax.axis_index("shard")
        keep = lax.dynamic_index_in_dim(v, x, 0, keepdims=False)
        send = lax.dynamic_index_in_dim(v, 1 - x, 0, keepdims=False)
        v = add(keep, lax.ppermute(send, "shard", [(0, 1), (1, 0)]))
    else:
        v = lax.psum_scatter(v, "shard", scatter_dimension=0, tiled=True)[0]
    for bit in range(1, bits):
        v = fold(v, bit, 0)
    for bit in reversed(range(bits)):
        own = (me >> bit) & 1
        other = lax.ppermute(v, "expert", swap(owners, bit))
        v = jnp.where(own == 0, jnp.concatenate([v, other]), jnp.concatenate([other, v]))
    return v


def per_device(
    owners, shards, tokens, cotangent, routes, counts, aux_weight, attn_qkv1, attn_out1, mlp_in, mlp_out, gains1,
    attn_qkv2, attn_out2, router, gains2, expert_in, expert_out,
):
    images, seq, width = tokens.shape
    step = padded(seq)
    rows = images * step
    experts = router.shape[1]
    local = expert_in.shape[0]
    ff = mlp_in.shape[1]
    block_rows = -(-local * CAP // 16) * 16
    slots = owners * block_rows
    split = Split(shards)
    expert_swap = functools.partial(lax.all_to_all, axis_name="expert", split_axis=0, concat_axis=0, tiled=True)

    block = (owners, block_rows, width)
    sem = pltpu.SemaphoreType.DMA
    if shards == 2:
        (gains, router_full, stat, live_col, dy, u_out, hidden, block_out, hidden_two, qkv_one, mix_one, qkv_two, mix_two, act, slope,
         u_two, probs, back, w_one, w_up, w_down, w_two, dy_in) = fused_forward(
            owners, experts, local, block, tokens, cotangent, routes, counts, gains1, gains2, router,
            attn_qkv1, attn_out1, mlp_in, mlp_out, attn_qkv2, attn_out2)
        w_one, w_up, w_down, w_two = [w_one], [w_up], [w_down], [w_two]
    else:
        within = jnp.arange(step, dtype=jnp.int32) < seq
        live = ((jnp.arange(images, dtype=jnp.int32)[:, None] < counts[0]) & within[None, :]).reshape(rows)
        live = live.astype(f32)
        routes_pad = jnp.pad(routes, ((0, 0), (0, step - seq), (0, 0)), constant_values=-1).reshape(rows, 2)
        lanes = jnp.arange(LANES, dtype=jnp.int32)
        loads = jnp.sum(((routes_pad[:, :, None] == lanes) & (live[:, None, None] > 0)).astype(f32), axis=(0, 1))
        loads = jnp.where(lanes == LANES - 1, jnp.sum(live), loads)
        live_col = live[:, None]

        w_one = split.gather([attn_qkv1, attn_out1[None]])
        w_up = split.gather([mlp_in[None]])
        w_down = split.gather([mlp_out[None]])
        w_two = split.gather([attn_qkv2, attn_out2[None]])
        gains = jnp.concatenate([gains1, gains2])
        if shards == 2:
            x = lax.axis_index("shard")
            other = lax.ppermute(gains, "shard", [(0, 1), (1, 0)])
            gains = jnp.where(x == 0, jnp.concatenate([gains, other], 1), jnp.concatenate([other, gains], 1))
            other = lax.ppermute(router, "shard", [(0, 1), (1, 0)])
            router_full = jnp.where(x == 0, jnp.concatenate([router, other]), jnp.concatenate([other, router]))
        else:
            gains = lax.all_gather(gains, "shard", axis=1, tiled=True)
            router_full = lax.all_gather(router, "shard", axis=0, tiled=True)
        gains = gains.astype(f32)
        router_full = jnp.pad(router_full, ((0, 0), (0, LANES - experts)))

        dy, dy_out, disp, back = call(
            functools.partial(route_body, images, seq, local, block_rows),
            [sds((rows, width), bf16), sds((slots, width), bf16), sds((slots, rows), bf16), sds((rows, slots), bf16)],
            [routes_pad, live_col, cotangent], flops=2e9, nbytes=6e6,
        )
        block = (owners, block_rows, width)
        dy_in = expert_swap(dy_out.reshape(block))

        sem = pltpu.SemaphoreType.DMA
        attn_scratch = [pltpu.VMEM((4, width, width), bf16), sem((4,))]
        mlp_scratch = [pltpu.VMEM((1, width, ff), bf16), pltpu.VMEM((1, ff, width), bf16), sem((2, 4))]

        def specs(n, ins):
            return [VM] * n + [ANY] * (len(ins) - n)

        ins = [tokens, gains] + w_one
        hidden, qkv_one, mix_one = call(
            functools.partial(block1_body, split, images, seq),
            [sds((rows, width), f32), sds((rows, 3 * width), bf16), sds((rows, width), bf16)],
            ins, attn_scratch, specs(2, ins), flops=4e9, nbytes=8e6,
        )
        ins = [hidden, gains] + w_up + w_down
        block_out, act, slope = call(
            functools.partial(mlp_body, split),
            [sds((rows, width), f32)] + [sds((ff // width, rows, width), bf16)] * 2,
            ins, mlp_scratch, specs(2, ins), flops=6e9, nbytes=12e6,
        )
        ins = [block_out, gains, router_full, disp, live_col, loads[None, :]] + w_two
        hidden_two, qkv_two, mix_two, u_two, probs, stat, u_out = call(
            functools.partial(block2_body, split, images, seq, experts),
            [sds((rows, width), f32), sds((rows, 3 * width), bf16), sds((rows, width), bf16), sds((rows, width), bf16),
             sds((rows, LANES), f32), sds((8, LANES), f32), sds((slots, width), bf16)],
            ins, attn_scratch, specs(6, ins), flops=5e9, nbytes=10e6,
        )

    group = min(4, owners)
    saved = owners * CAP if shards == 2 else 16
    wide = width if shards == 2 else LANES
    u_in, served, du_back, dgate_back, stat, dy_far, u_far, *partial = pl.pallas_call(
        functools.partial(expert_body, owners, shards, local, experts, group),
        out_shape=[sds(block, bf16), sds(block, bf16), sds(block, bf16), sds((owners, 8, LANES), f32), sds((8, LANES), f32),
                   sds((shards - 1,) + block, bf16), sds(block, bf16)]
        + ([sds(expert_in.shape, bf16), sds(expert_out.shape, bf16)] if shards == 2 else []),
        in_specs=[VM] * 4 + [ANY] * 2,
        out_specs=[VM] * 5 + [ANY] * (4 if shards == 2 else 2),
        scratch_shapes=[
            pltpu.VMEM((local, width, ff), bf16), pltpu.VMEM((local, ff, width), bf16), pltpu.VMEM(block, bf16),
            pltpu.VMEM((owners, 8, LANES), f32), pltpu.VMEM((shards, 8, LANES), f32), pltpu.VMEM((owners, 8, LANES), f32),
            pltpu.VMEM((local, saved, ff if shards == 2 else LANES), bf16), pltpu.VMEM((local, saved, ff if shards == 2 else LANES), bf16),
            pltpu.VMEM((local, saved, wide), bf16), pltpu.VMEM((local, saved, wide), bf16),
            pltpu.VMEM((2, wide, wide), bf16), pltpu.VMEM((2, wide, wide), bf16),
            sem((2,)), sem((2,)), sem((4,)),
        ] + [sem((owners,))] * 10 + [sem((shards,))] * 4,
        compiler_params=pltpu.CompilerParams(vmem_limit_bytes=VMEM_BYTES, collective_id=0, has_side_effects=True),
        cost_estimate=pl.CostEstimate(flops=int(11e9), bytes_accessed=int(15e6), transcendentals=0),
    )(u_out.reshape(block), dy_in, router_full, stat, expert_in, expert_out)
    parts_of = (gains, router_full, aux_weight.reshape(1, 1), stat, live_col, back, dgate_back, tokens, dy, u_two, probs, du_back)
    if shards == 2:
        return fused_backward(Split(1), experts, tokens, parts_of, hidden_two, block_out, hidden, qkv_two, mix_two, qkv_one, mix_one,
                              act, slope, served, u_far, dy_far, *partial, expert_in, expert_out, w_two, w_up, w_down, w_one)
    served_back = expert_swap(served).reshape(slots, width)

    if shards == 2:
        us = [u_in, lax.ppermute(u_in, "shard", [(0, 1), (1, 0)])]
    else:
        far = lax.all_gather(u_in, "shard")
        us = [u_in] + [lax.dynamic_index_in_dim(far, (lax.axis_index("shard") + shards - k) % shards, 0, False) for k in range(1, shards)]
    dys = [dy_in] + [dy_far[k] for k in range(shards - 1)]
    parts = 4
    wide = ff // parts
    up_spec = pl.BlockSpec((1, width, wide), lambda e, f: (e, 0, f))
    down_spec = pl.BlockSpec((1, wide, width), lambda e, f: (e, f, 0))
    grad_e_in, grad_e_out = pl.pallas_call(
        functools.partial(expert_grad_body, shards, experts),
        grid=(local, parts),
        out_shape=[sds((local, width, ff), f32), sds((local, ff, width), f32)],
        in_specs=[ANY] * (2 * shards) + [VM, up_spec, down_spec],
        out_specs=[up_spec, down_spec],
        scratch_shapes=[pltpu.VMEM((shards, local, owners * CAP, width), bf16)] * 2 + [pltpu.VMEM((2,) + block, bf16), sem((2,))],
        compiler_params=pltpu.CompilerParams(vmem_limit_bytes=VMEM_BYTES),
        cost_estimate=pl.CostEstimate(flops=int(27e9), bytes_accessed=int(40e6), transcendentals=0),
    )(*us, *dys, router_full, expert_in, expert_out)

    part = width // shards
    back_scratch = [pltpu.VMEM((rows, width), bf16), pltpu.VMEM((rows, 3 * width), bf16)]
    ins = [dy, u_two, probs, hidden_two, block_out, gains, router_full, aux_weight.reshape(1, 1), stat, live_col, back,
           du_back.reshape(slots, width), dgate_back,
           qkv_two, mix_two]
    n = len(ins)
    ins = ins + w_two
    grad_block, pack_two, small = call(
        functools.partial(back2_body, split, images, seq, experts),
        [sds((rows, width), f32), sds((shards, 4 * part, width), bf16), sds((LANES + 8, width), f32)],
        ins, attn_scratch + back_scratch, specs(n, ins), flops=9e9, nbytes=16e6,
    )
    balance_loss = small[LANES + 2, 0]
    late = reduce_all(pack_two, owners, shards)
    ins = [grad_block, hidden, gains, act, slope] + w_up + w_down
    grad_hidden, pack_mlp, dg_two = call(
        functools.partial(mlp_back_body, split),
        [sds((rows, width), f32), sds((shards, part * (ff // width) + ff // shards, width), bf16), sds((1, width), f32)],
        ins, mlp_scratch + [pltpu.VMEM((rows, width), f32)], specs(5, ins), flops=11e9, nbytes=16e6,
    )
    middle = reduce_all(pack_mlp, owners, shards)
    ins = [grad_hidden, tokens, gains, qkv_one, mix_one, small, dg_two] + w_one
    grad_tokens, pack_one = call(
        functools.partial(back1_body, split, images, seq, experts),
        [sds((images, seq, width), f32), sds((shards, 4 * part + 64, width), bf16)],
        ins, attn_scratch + [pltpu.VMEM((rows, width), f32)] + back_scratch, specs(7, ins), flops=9e9, nbytes=14e6,
    )
    early = reduce_all(pack_one, owners, shards)
    (output,) = call(
        functools.partial(output_body, images, seq), [sds((images, seq, width), bf16)],
        [hidden_two, back, served_back, live_col], [pltpu.VMEM((rows, width), f32)], flops=1e9, nbytes=5e6,
    )

    late, middle, early = late.astype(f32), middle.astype(f32), early.astype(f32)
    up = middle[:part * (ff // width)].reshape(ff // width, part, width).transpose(1, 0, 2).reshape(part, ff)
    tail = early[4 * part:, :part]
    return (
        output,
        balance_loss,
        grad_tokens,
        early[:3 * part].reshape(3, part, width),
        early[3 * part:4 * part],
        up,
        middle[part * (ff // width):],
        tail[32:34],
        late[:3 * part].reshape(3, part, width),
        late[3 * part:],
        tail[:experts].T,
        tail[34:36],
        grad_e_in,
        grad_e_out,
    )


PLAN = [
    ("two", None, 0),
    ("out", None, 1),
    ("out", None, 0),
    ("in1", None, 1),
    ("mlp", None, 2),
    ("mlp", None, 0),
    ("image", 0, 2),
    ("image", 0, 1),
    ("image", 1, 0),
    ("image", 2, 1),
    ("one", None, 3),
    ("one", None, 2),
    ("output", None, 3),
    ("output", None, 0),
    ("early", 0, 2),
    ("early", 0, 1),
    ("late", 3, 3),
    ("early", 4, 0),
    ("late", 4, 2),
    ("late", 4, 1),
    ("early", 6, 3),
]


def fused_backward(split, experts, tokens, parts_of, hidden_two, block_out, hidden, qkv_two, mix_two, qkv_one, mix_one,
                   act, slope, served, u_far, dy_far, part1, part2, expert_in, expert_out, w_two, w_up, w_down, w_one):
    images, seq, width = tokens.shape
    rows = hidden.shape[0]
    local, _, ff = expert_in.shape
    block = served.shape
    owners = block[0]
    bits = owners.bit_length() - 1
    whole = 2 * width
    part = width // 2
    blocks = ff // width
    steps = [7] * 4
    left = [0] * 4
    plan = {}
    for name, index, n in PLAN:
        if left[n] <= steps[n] and (index is None or index < (images if name == "image" else local * blocks)):
            plan.setdefault(name, []).append((index, n, left[n]))
            left[n] += 1
    plan["end"] = [(None, n, k) for k in range(max(steps) + 1) for n in range(4) if left[n] <= k <= steps[n]]
    small_rows = -(-(experts + 4) // 8) * 8
    sem = pltpu.SemaphoreType.DMA
    ins = list(parts_of) + [hidden_two, block_out, hidden, qkv_two, mix_two, qkv_one, mix_one, act, slope, served, u_far, dy_far,
                            part1, part2, expert_in, expert_out] + w_two + w_up + w_down + w_one
    vmem = 8
    big_rows = 2 * owners * CAP
    nsem = 8 + 4 * (owners // 4 - 1)
    V = pltpu.VMEM
    outs = pl.pallas_call(
        functools.partial(backward_body, split, images, seq, experts, local, owners, plan),
        out_shape=[
            sds((images, seq, width), bf16), sds((images, seq, width), f32), sds((4, whole, width), bf16),
            sds((small_rows, part), f32), sds((LANES + 8, width), f32), sds(expert_in.shape, bf16), sds(expert_out.shape, bf16),
            sds(block, bf16),
        ],
        in_specs=[VM] * vmem + [ANY] * (len(ins) - vmem),
        out_specs=[VM] * 5 + [ANY] * 3,
        scratch_shapes=[
            V((rows, width), f32), V((rows, width), f32), V((rows, width), f32), V((rows, width), f32),
            V((rows, 3 * width), bf16), V((rows, width), bf16), V((rows, width), bf16), V((rows, 3 * width), bf16),
            V((4, width, width), bf16), V((1, width, ff), bf16), V((1, ff, width), bf16), V((blocks, big_rows, width), bf16),
            V((2,) + block, bf16),
            V((4, 2, whole, width), bf16), V((4, 2, whole // 2, width), bf16), V((4, whole // 4, width), bf16),
            V((4, 2, whole // 8, width), bf16), V((4, whole // 8, width), bf16), V((4, whole // 8, width), bf16),
            V((4, 2 * (owners // 4 - 1), whole // (2 * owners), width), bf16),
            V((2, small_rows, part), f32), V((bits + 1, 2, small_rows, part), f32),
            sem((8 + 2 * blocks,)), sem((3, 4)), sem((owners,)), sem((owners,)),
            sem((4, nsem)), sem((4, nsem)), sem((bits + 1,)), sem((bits + 1,)), sem((6,)), sem((4,)), sem((1,)), sem((4,)),
        ],
        compiler_params=pltpu.CompilerParams(vmem_limit_bytes=63 << 20, collective_id=1, has_side_effects=True),
        cost_estimate=pl.CostEstimate(flops=int(60e9), bytes_accessed=int(80e6), transcendentals=0),
    )(*ins)
    output, grad_tokens, fin, tail, small, grad_e_in, grad_e_out = outs[:7]
    qkv1, out1, up, down, qkv2, out2, grad_e_in, grad_e_out, gains1, gains2, router = widen(
        fin, grad_e_in, grad_e_out, tail, part, width, blocks, experts)
    return (
        output, small[LANES + 2, 0], grad_tokens, qkv1, out1, up, down, gains1, qkv2, out2, router, gains2, grad_e_in, grad_e_out,
    )


def widen_body(sixth, experts, fin_ref, e1_ref, e2_ref, tail_ref, qkv1_ref, out1_ref, up_ref, down_ref, qkv2_ref, out2_ref,
               g1_ref, g2_ref, gains1_ref, gains2_ref, router_ref):
    i = pl.program_id(0)

    @pl.when(i == 0)
    def _():
        gains1_ref[...] = tail_ref[experts:experts + 2]
        gains2_ref[...] = tail_ref[experts + 2:experts + 4]
        a = lax.broadcasted_iota(jnp.int32, (experts, experts), 0)
        b = lax.broadcasted_iota(jnp.int32, (experts, experts), 1)
        unit = (a == b).astype(f32).astype(bf16)
        hi, mid, lo = split3(tail_ref[0:experts])
        router_ref[...] = tn(hi, unit) + tn(mid, unit) + tn(lo, unit)

    g1_ref[...] = e1_ref[...].astype(f32)
    g2_ref[...] = e2_ref[...].astype(f32)
    up_ref[...] = fin_ref[2].astype(f32)
    down_ref[...] = fin_ref[1].astype(f32)

    @pl.when(i < sixth)
    def _():
        qkv1_ref[0] = fin_ref[3].astype(f32)
        qkv2_ref[0] = fin_ref[0].astype(f32)

    @pl.when(i >= sixth)
    def _():
        out1_ref[...] = fin_ref[3].astype(f32)
        out2_ref[...] = fin_ref[0].astype(f32)


def widen(fin, e1, e2, tail, part, width, blocks, experts):
    steps = 2 * blocks
    some = fin.shape[1] // steps
    per = part // some
    sixth = 3 * per
    local, _, ff = e1.shape
    qkv = pl.BlockSpec((1, some, width), lambda i: (jnp.minimum(i, sixth - 1) // per, jnp.minimum(i, sixth - 1) % per, 0))
    out = pl.BlockSpec((some, width), lambda i: (jnp.maximum(i - sixth, 0), 0))
    return pl.pallas_call(
        functools.partial(widen_body, sixth, experts),
        grid=(steps,),
        out_shape=[sds((3, part, width), f32), sds((part, width), f32), sds((part, blocks * width), f32), sds((fin.shape[1], width), f32),
                   sds((3, part, width), f32), sds((part, width), f32), sds(e1.shape, f32), sds(e2.shape, f32),
                   sds((2, part), f32), sds((2, part), f32), sds((part, experts), f32)],
        in_specs=[pl.BlockSpec((4, some, width), lambda i: (0, i, 0)),
                  pl.BlockSpec((local, width // steps, ff), lambda i: (0, i, 0)),
                  pl.BlockSpec((local, ff // steps, width), lambda i: (0, i, 0)), pl.BlockSpec(tail.shape, lambda i: (0, 0))],
        out_specs=[qkv, out, pl.BlockSpec((some, width), lambda i: (i % per, i // per)), pl.BlockSpec((some, width), lambda i: (i, 0)),
                   qkv, out, pl.BlockSpec((local, width // steps, ff), lambda i: (0, i, 0)),
                   pl.BlockSpec((local, ff // steps, width), lambda i: (0, i, 0)),
                   pl.BlockSpec((2, part), lambda i: (0, 0)), pl.BlockSpec((2, part), lambda i: (0, 0)),
                   pl.BlockSpec((part, experts), lambda i: (0, 0))],
        compiler_params=pltpu.CompilerParams(vmem_limit_bytes=VMEM_BYTES),
        cost_estimate=pl.CostEstimate(flops=0, bytes_accessed=int(40e6), transcendentals=0),
    )(fin, e1, e2, tail)


def solution(mesh):
    owners, shards = mesh.shape["expert"], mesh.shape["shard"]
    both = ("expert", "shard")
    return jax.shard_map(
        functools.partial(per_device, owners, shards),
        mesh=mesh,
        in_specs=(
            P(both, None, None), P(both, None, None), P(both, None, None), P(both), P(),
            P(None, "shard", None), P("shard", None), P("shard", None), P("shard", None), P(None, "shard"),
            P(None, "shard", None), P("shard", None), P("shard", None), P(None, "shard"),
            P("expert", None, None), P("expert", None, None),
        ),
        out_specs=(
            P(both, None, None), P(), P(both, None, None),
            P(None, "shard", None), P("shard", None), P("shard", None), P("shard", None), P(None, "shard"),
            P(None, "shard", None), P("shard", None), P("shard", None), P(None, "shard"),
            P("expert", None, None), P("expert", None, None),
        ),
        check_vma=False,
    )
```
